32 devices in a mesh: seq: 8 (over z, x), mp: 4 (over y, core).
Axes of the slice: x: 2, y: 2, z: 4, core: 2. Of those that a mesh axis runs over, the one named last changes fastest.
Arguments:
- qkv: bfloat16 [4, 1024, 12288], P('mp', 'seq'), may hold values from -8 to 8
- readout: bfloat16 [2, 4096, 64], replicated, may hold values from -0.375 to 0.375
- step_weight: float32 [1000], replicated, may hold values from 0.3 to 3
- timestep: int32 [2], replicated, may hold values from 0 to 999
- span_frames: int32 [4], replicated, may hold values from 1 to 8, as said below
Outputs:
- grad: float32 [1024, 64], P('seq')
The draws below stay inside these ranges and needn't reach their ends.
Inputs may be any that keep to these rules, and one draw needn't show every extreme that they name: `span_frames`: they sum to 16; one span has exactly 8 frames.
All inputs are finite; a program needn't handle non-finite values.
Results may differ from the reference program's by a relative error of at most 0.0037.
Values may be sent and summed in bfloat16 or wider, within the bound.
No kernel may reach another device: no remote copies, remote signals or barrier semaphores. Data moves between devices by JAX's collectives and lax.ppermute only.
A program may use at most 64 MiB of HBM per device.

```python
import math
import jax
import jax.numpy as jnp
from jax import lax

HEADS = 32
HD = 128
LAT = 64
STEPS = 1000
TOKENS = 1024
FRAME_TOK = 64
FRAMES = 16
SPANS = 4
SAMPLES = 2
N_MP = 4


def draw_qkv(key, part):
    key = jax.random.fold_in(key, 11)
    array_shape = (N_MP, TOKENS, HEADS, 3, HD)
    values_drawn = jnp.clip(jax.random.normal(key, array_shape, jnp.float32), -6.0, 6.0)
    return values_drawn.reshape(N_MP, TOKENS, HEADS * 3 * HD).astype(jnp.bfloat16)


def draw_span_frames(key, part):
    key = jax.random.fold_in(key, 23)
    longest = FRAMES // 2
    remaining = FRAMES - longest
    place_key = jax.random.fold_in(key, 1)
    cut_key = jax.random.fold_in(key, 2)
    long_place = jax.random.randint(place_key, (), 0, SPANS).astype(jnp.int32)
    order = jax.random.permutation(cut_key, remaining - 1).astype(jnp.int32) + 1
    cuts = jnp.sort(order[:SPANS - 2])
    edges = jnp.concatenate([jnp.zeros((1,), jnp.int32), cuts, jnp.full((1,), remaining, jnp.int32)])
    pieces = (edges[1:] - edges[:-1]).astype(jnp.int32)
    slots = jnp.arange(SPANS, dtype=jnp.int32)
    below = jnp.where(slots < long_place, slots, slots - 1)
    below = jnp.clip(below, 0, SPANS - 2)
    taken = pieces[below]
    return jnp.where(slots == long_place, longest, taken).astype(jnp.int32)


def gaussian(own_key, extent, width, reach, held_as=jnp.bfloat16):
    return jnp.clip(width * jax.random.normal(own_key, extent, jnp.float32), -reach, reach).astype(held_as)


def setup_inputs(seed: int = 0) -> dict:
    seeds = jax.random.split(jax.random.key(seed), 6)
    return {
        "qkv": draw_qkv(jax.random.fold_in(seeds[5], 71), 0),
        "readout": gaussian(seeds[1], (2, HEADS * HD, LAT), (2 * HD) ** -0.5, 0.375),
        "step_weight": jnp.clip(jnp.exp(jax.random.uniform(seeds[2], (STEPS,), jnp.float32, math.log(0.3), math.log(3.0))), 0.3, 3.0),
        "timestep": jax.random.randint(seeds[3], (SAMPLES,), 0, STEPS).astype(jnp.int32),
        "span_frames": draw_span_frames(jax.random.fold_in(seeds[5], 71), 0),
    }


def span_limits(span_frames, token_count):
    span_ends = jnp.cumsum(span_frames).astype(jnp.int32) * FRAME_TOK
    places = jnp.arange(token_count, dtype=jnp.int32)
    owner_span = lax.optimization_barrier(jnp.sum((places[:, None] >= span_ends[None, :]).astype(jnp.int32), axis=1)).astype(jnp.int32)
    span_ids = jnp.arange(span_ends.shape[0], dtype=jnp.int32)
    picked = jnp.where(span_ids[None, :] == owner_span[:, None], span_ends[None, :], 0)
    return lax.optimization_barrier(jnp.sum(picked, axis=1)).astype(jnp.int32)

def attend_head(queries, keyset, valueset, key_limits):
    block_size = min(512, TOKENS)
    score_scale = 1.0 / math.sqrt(HD)
    key_places = jnp.arange(TOKENS, dtype=jnp.int32)

    def one_block(block_index):
        row_start = (block_index * block_size).astype(jnp.int32)
        query_rows = lax.dynamic_slice_in_dim(queries, row_start, block_size, 0)
        bounds = lax.dynamic_slice_in_dim(key_limits, row_start, block_size, 0)
        scores = jnp.dot(query_rows, keyset.T, preferred_element_type=jnp.float32) * score_scale
        scores = jnp.where(key_places[None, :] < bounds[:, None], scores, -jnp.inf)
        row_peak = lax.optimization_barrier(jnp.max(scores, axis=1, keepdims=True))
        raw_weights = jnp.exp(scores - row_peak)
        row_total = lax.optimization_barrier(jnp.sum(raw_weights, axis=1, keepdims=True))
        weights = raw_weights.astype(jnp.bfloat16)
        summed = jnp.dot(weights, valueset, preferred_element_type=jnp.float32)
        return (summed / row_total).astype(jnp.bfloat16)
    blocks = lax.map(one_block, jnp.arange(TOKENS // block_size, dtype=jnp.int32))
    return blocks.reshape(TOKENS, HD)

def reference(qkv, readout, step_weight, timestep, span_frames):
    key_limits = span_limits(span_frames, TOKENS)

    def member_step(carried, member):
        member_rows = lax.dynamic_index_in_dim(qkv, member, 0, keepdims=False).reshape(TOKENS, HEADS, 3 * HD)
        model_index = member // SAMPLES
        readout_rows = lax.dynamic_index_in_dim(readout, model_index, 0, keepdims=False)

        def head_step(prediction, head_index):
            head_group = lax.dynamic_index_in_dim(member_rows, head_index, 1, keepdims=False)
            attended = attend_head(head_group[:, :HD], head_group[:, HD:2 * HD], head_group[:, 2 * HD:], key_limits)
            head_rows = lax.dynamic_slice_in_dim(readout_rows, (head_index * HD).astype(jnp.int32), HD, 0)
            return (prediction + jnp.dot(attended, head_rows, preferred_element_type=jnp.float32), None)
        prediction, _ = lax.scan(head_step, jnp.zeros((TOKENS, LAT), jnp.float32), jnp.arange(HEADS, dtype=jnp.int32))
        signed = jnp.where(model_index == 1, 1.0, -1.0).astype(jnp.float32)
        factor = signed * step_weight[timestep[member % SAMPLES]]
        return (carried + factor * prediction, None)
    grad, _ = lax.scan(member_step, jnp.zeros((TOKENS, LAT), jnp.float32), jnp.arange(N_MP, dtype=jnp.int32))
    return grad
```

```python
import functools
import math

import jax
import jax.numpy as jnp
from jax import lax
from jax.experimental import pallas as pl
from jax.experimental.pallas import tpu as pltpu
from jax.sharding import PartitionSpec as P

HEADS = 32
HD = 128
FRAME_TOK = 64
NT = (((1,), (1,)), ((), ()))
VMEM_LIMIT = 48 * 1024 * 1024


def pack_kernel(chunks, qkv_ref, readout_ref, *out_refs):
    lat = readout_ref.shape[1]
    head = 0
    for out_ref, count in zip(out_refs, chunks):
        for i in range(count):
            base = (head + i) * 3 * HD
            out_ref[0, :, i * 2 * HD : (i + 1) * 2 * HD] = qkv_ref[0, :, base : base + 2 * HD]
            values = qkv_ref[0, :, base + 2 * HD : base + 3 * HD]
            rows = readout_ref[0, :, (head + i) * HD : (head + i + 1) * HD]
            folded = lax.dot_general(rows, values, NT, preferred_element_type=jnp.float32)
            column = count * 2 * HD + (i * lat // HD) * HD
            row = (i * lat) % HD
            out_ref[0, row : row + lat, column : column + HD] = folded.astype(jnp.bfloat16)
        head += count


def pack(qkv, readout_t, model_index, seq_count, chunks):
    _, rows, _ = qkv.shape
    lat = readout_t.shape[1]
    heads_local = HEADS // seq_count
    widths = [c * 2 * HD + -(-c * lat // HD) * HD for c in chunks]

    def kernel(index_ref, *refs):
        pack_kernel(chunks, *refs)

    return pl.pallas_call(
        kernel,
        grid_spec=pltpu.PrefetchScalarGridSpec(
            num_scalar_prefetch=1,
            grid=(seq_count,),
            in_specs=[
                pl.BlockSpec((1, rows, heads_local * 3 * HD), lambda d, m: (0, 0, d)),
                pl.BlockSpec((1, lat, heads_local * HD), lambda d, m: (m[0], 0, d)),
            ],
            out_specs=[pl.BlockSpec((1, rows, w), lambda d, m: (d, 0, 0)) for w in widths],
        ),
        out_shape=[jax.ShapeDtypeStruct((seq_count, rows, w), jnp.bfloat16) for w in widths],
        compiler_params=pltpu.CompilerParams(vmem_limit_bytes=VMEM_LIMIT),
        name="pack",
    )(model_index, qkv, readout_t)


def attend_kernel(count, lat, block, last, frames_ref, factor_ref, packed_ref, *refs):
    seq_count, rows, _ = packed_ref.shape
    tokens = seq_count * rows
    spans = frames_ref.shape[0]
    out_ref = refs[-1]
    log2_scale = math.log2(math.e) / math.sqrt(HD)
    per_block = block // rows

    def one_block(b, carry):
        places = b * block + lax.broadcasted_iota(jnp.int32, (1, block), 1)
        end = frames_ref[0] * FRAME_TOK
        bound = jnp.full((1, block), end, jnp.int32)
        for c in range(1, spans):
            later = end + frames_ref[c] * FRAME_TOK
            bound = jnp.where(places >= end, later, bound)
            end = later
        key_places = lax.broadcasted_iota(jnp.int32, (tokens, 1), 0)
        allowed = key_places < bound
        total = None
        for i in range(count):
            queries = packed_ref[pl.ds(b * per_block, per_block), :, i * 2 * HD : i * 2 * HD + HD]
            queries = queries.reshape(block, HD)
            keys = packed_ref[:, :, i * 2 * HD + HD : (i + 1) * 2 * HD].reshape(tokens, HD)
            scores = lax.dot_general(keys, queries, NT, preferred_element_type=jnp.float32)
            scores = jnp.where(allowed, scores, -jnp.inf)
            peak = jnp.max(scores, axis=0, keepdims=True)
            raw = jnp.exp2((scores - peak) * log2_scale)
            row_total = jnp.sum(raw, axis=0, keepdims=True)
            weights = raw.astype(jnp.bfloat16)
            column = count * 2 * HD + (i * lat // HD) * HD
            row = (i * lat) % HD
            folded = jnp.concatenate(
                [packed_ref[s, row : row + lat, column : column + HD] for s in range(seq_count)], axis=1
            )
            summed = jnp.dot(folded, weights, preferred_element_type=jnp.float32) / row_total
            total = summed if total is None else total + summed
        for j in range(per_block):
            part = total[:, j * rows : (j + 1) * rows]
            if len(refs) > 1:
                part = part + refs[0][b * per_block + j]
            if last:
                part = part * factor_ref[0]
            out_ref[b * per_block + j] = part.astype(out_ref.dtype)
        return carry

    lax.fori_loop(0, tokens // block, one_block, 0)


def attend(packed, earlier, span_frames, factor, count, lat, last):
    seq_count, rows, _ = packed.shape
    tokens = seq_count * rows
    block = 256
    smem = pl.BlockSpec(memory_space=pltpu.SMEM)
    vmem = pl.BlockSpec(memory_space=pltpu.VMEM)
    operands = [span_frames, factor, packed] + ([] if earlier is None else [earlier])
    return pl.pallas_call(
        functools.partial(attend_kernel, count, lat, block, last),
        in_specs=[smem, smem] + [vmem] * (len(operands) - 2),
        out_specs=vmem,
        out_shape=jax.ShapeDtypeStruct((seq_count, lat, rows), jnp.bfloat16 if last else jnp.float32),
        compiler_params=pltpu.CompilerParams(vmem_limit_bytes=VMEM_LIMIT),
        cost_estimate=pl.CostEstimate(
            flops=count * tokens * tokens * 2 * (HD + lat),
            bytes_accessed=packed.size * 2,
            transcendentals=count * tokens * tokens,
        ),
        name="attend",
    )(*operands)


def body(qkv, readout, step_weight, timestep, span_frames):
    seq_count = lax.axis_size("seq")
    heads_local = HEADS // seq_count
    lat = readout.shape[2]
    mp_index = lax.axis_index("mp")
    sample_count = lax.axis_size("mp") // 2
    model_index = mp_index // sample_count
    sample_index = mp_index % sample_count
    signed = jnp.where(model_index == 1, 1.0, -1.0).astype(jnp.float32)
    factor = (signed * step_weight[timestep[sample_index]]).reshape(1)
    chunks = [2] * (heads_local // 2) if heads_local % 2 == 0 else [heads_local]
    readout_t = jnp.swapaxes(readout, 1, 2)
    packed = pack(qkv, readout_t, model_index.astype(jnp.int32).reshape(1), seq_count, chunks)
    arrived = [lax.all_to_all(p, "seq", split_axis=0, concat_axis=0, tiled=True) for p in packed]
    result = None
    for n, (array, count) in enumerate(zip(arrived, chunks)):
        result = attend(array, result, span_frames, factor, count, lat, n == len(chunks) - 1)
    parts = lax.all_to_all(result, "seq", split_axis=0, concat_axis=0, tiled=True)
    own = jnp.sum(parts.astype(jnp.float32), axis=0)
    return lax.psum(own, "mp").T


def solution(mesh):
    return jax.shard_map(
        body,
        mesh=mesh,
        in_specs=(P("mp", "seq", None), P(), P(), P(), P()),
        out_specs=P("seq", None),
        check_vma=False,
    )
```

```python
import functools
import math

import jax
import jax.numpy as jnp
from jax import lax
from jax.experimental import pallas as pl
from jax.experimental.pallas import tpu as pltpu
from jax.sharding import PartitionSpec as P

HEADS = 32
HD = 128
FRAME_TOK = 64
NT = (((1,), (1,)), ((), ()))
VMEM_LIMIT = 48 * 1024 * 1024


def pack_kernel(chunks, place_ref, qkv_ref, readout_ref, *out_refs):
    lat = readout_ref.shape[1]
    head = 0
    for out_ref, count in zip(out_refs, chunks):
        for i in range(count):
            base = (head + i) * 3 * HD
            out_ref[:, i * 2 * HD : (i + 1) * 2 * HD] = qkv_ref[0, :, base : base + 2 * HD]
        head += count
    for i in range(head):
        base = i * 3 * HD
        values = qkv_ref[0, :, base + 2 * HD : base + 3 * HD]
        rows = readout_ref[0, :, i * HD : (i + 1) * HD]
        folded = lax.dot_general(rows, values, NT, preferred_element_type=jnp.float32)
        column = chunks[0] * 2 * HD + (i * lat // HD) * HD
        row = (i * lat) % HD
        out_refs[0][row : row + lat, column : column + HD] = folded.astype(jnp.bfloat16)


def pack(place, qkv, readout_t, chunks, widths):
    rows = qkv.shape[1]
    lat = readout_t.shape[1]
    heads_local = sum(chunks)
    return pl.pallas_call(
        functools.partial(pack_kernel, chunks),
        grid_spec=pltpu.PrefetchScalarGridSpec(
            num_scalar_prefetch=1,
            grid=(1,),
            in_specs=[
                pl.BlockSpec((1, rows, heads_local * 3 * HD), lambda g, m: (0, 0, m[0])),
                pl.BlockSpec((1, lat, heads_local * HD), lambda g, m: (m[1], 0, m[0])),
            ],
            out_specs=[pl.BlockSpec((rows, w), lambda g, m: (0, 0)) for w in widths],
        ),
        out_shape=[jax.ShapeDtypeStruct((rows, w), jnp.bfloat16) for w in widths],
        compiler_params=pltpu.CompilerParams(vmem_limit_bytes=VMEM_LIMIT),
        cost_estimate=pl.CostEstimate(
            flops=2 * rows * lat * heads_local * HD,
            bytes_accessed=rows * heads_local * HD * 12,
            transcendentals=0,
        ),
        name="pack",
    )(place, qkv, readout_t)


def attend_kernel(seq_count, count, value_head, lat, block, last, frames_ref, factor_ref, me_ref, *refs):
    pieces = refs[:seq_count]
    others = refs[seq_count:-4]
    held, kept, total_ref, sems = refs[-4:]
    rows = pieces[0].shape[0]
    tokens = seq_count * rows
    spans = frames_ref.shape[0]
    log2_scale = math.log2(math.e) / math.sqrt(HD)
    per_block = block // rows
    own = value_head == 0
    if own:
        value_refs, earlier, outs = None, None, others
        value_column = count * 2 * HD
    else:
        value_refs, earlier, outs = others[:seq_count], others[seq_count], others[seq_count + 1 :]
        value_column = 0

    copies = [pltpu.make_async_copy(pieces[k], held.at[k], sems.at[k]) for k in range(seq_count)]
    if not own:
        width = kept.shape[2]
        start = value_refs[0].shape[1] - width
        copies += [
            pltpu.make_async_copy(value_refs[k].at[:, start:], kept.at[k], sems.at[seq_count + k])
            for k in range(seq_count)
        ]
    for copy in copies:
        copy.start()
    for copy in copies:
        copy.wait()
    value_source = held if own else kept

    def ends_of():
        end = frames_ref[0] * FRAME_TOK
        ends = [end]
        for c in range(1, spans):
            end = end + frames_ref[c] * FRAME_TOK
            ends.append(end)
        return ends

    ends = ends_of()
    me = me_ref[0]
    row_places = lax.broadcasted_iota(jnp.int32, (rows, 1), 0)
    key_places = jnp.concatenate([(me ^ k) * rows + row_places for k in range(seq_count)], axis=0)
    column_places = lax.broadcasted_iota(jnp.int32, (1, rows), 1)

    def one_block(b, carry):
        first = b * per_block
        places = jnp.concatenate(
            [(me ^ (first + j)) * rows + column_places for j in range(per_block)], axis=1
        )
        bound = jnp.full((1, block), ends[0], jnp.int32)
        for c in range(1, spans):
            bound = jnp.where(places >= ends[c - 1], ends[c], bound)
        allowed = key_places < bound
        total = None
        for i in range(count):
            queries = held[pl.ds(first, per_block), :, i * 2 * HD : i * 2 * HD + HD]
            queries = queries.reshape(block, HD)
            keys = held[:, :, i * 2 * HD + HD : (i + 1) * 2 * HD].reshape(tokens, HD)
            scores = lax.dot_general(keys, queries, NT, preferred_element_type=jnp.float32)
            scores = jnp.where(allowed, scores, -jnp.inf)
            peak = jnp.max(scores, axis=0, keepdims=True)
            raw = jnp.exp2((scores - peak) * log2_scale)
            row_total = jnp.sum(raw, axis=0, keepdims=True)
            weights = raw.astype(jnp.bfloat16)
            h = value_head + i
            column = value_column + (h * lat // HD) * HD
            row = (h * lat) % HD
            folded = jnp.concatenate(
                [value_source[s, row : row + lat, column : column + HD] for s in range(seq_count)], axis=1
            )
            summed = jnp.dot(folded, weights, preferred_element_type=jnp.float32) / row_total
            total = summed if total is None else total + summed
        for j in range(per_block):
            part = total[:, j * rows : (j + 1) * rows]
            if earlier is not None:
                part = part + earlier[first + j]
            total_ref[first + j] = part
        return carry

    lax.fori_loop(0, seq_count // per_block, one_block, 0)
    if last:
        for k in range(seq_count):
            outs[k][...] = (total_ref[k] * factor_ref[0]).astype(jnp.bfloat16)
    else:
        outs[0][...] = total_ref[...]


def attend(pieces, value_pieces, earlier, span_frames, factor, me, count, value_head, lat, last):
    seq_count = len(pieces)
    rows, width = pieces[0].shape
    tokens = seq_count * rows
    smem = pl.BlockSpec(memory_space=pltpu.SMEM)
    vmem = pl.BlockSpec(memory_space=pltpu.VMEM)
    anywhere = pl.BlockSpec(memory_space=pl.ANY)
    operands = [span_frames, factor, me] + list(pieces)
    in_specs = [smem] * 3 + [anywhere] * seq_count
    value_width = HD
    if value_head:
        operands += list(value_pieces) + [earlier]
        in_specs += [anywhere] * seq_count + [vmem]
        value_width = -(-(value_head + count) * lat // HD) * HD
    if last:
        out_shape = [jax.ShapeDtypeStruct((lat, rows), jnp.bfloat16)] * seq_count
    else:
        out_shape = [jax.ShapeDtypeStruct((seq_count, lat, rows), jnp.float32)]
    return pl.pallas_call(
        functools.partial(attend_kernel, seq_count, count, value_head, lat, 2 * rows, last),
        in_specs=in_specs,
        out_specs=[vmem] * len(out_shape),
        out_shape=out_shape,
        scratch_shapes=[
            pltpu.VMEM((seq_count, rows, width), jnp.bfloat16),
            pltpu.VMEM((seq_count, rows, value_width), jnp.bfloat16),
            pltpu.VMEM((seq_count, lat, rows), jnp.float32),
            pltpu.SemaphoreType.DMA((2 * seq_count,)),
        ],
        compiler_params=pltpu.CompilerParams(vmem_limit_bytes=VMEM_LIMIT),
        cost_estimate=pl.CostEstimate(
            flops=count * tokens * tokens * 2 * (HD + lat),
            bytes_accessed=tokens * width * 2,
            transcendentals=count * tokens * tokens,
        ),
        name="attend",
    )(*operands)


def swap(array, axis, offset):
    size = lax.axis_size(axis)
    return lax.ppermute(array, axis, [(i, i ^ offset) for i in range(size)])


def body(qkv, readout, step_weight, timestep, span_frames):
    seq_count = lax.axis_size("seq")
    mp_count = lax.axis_size("mp")
    heads_local = HEADS // seq_count
    lat = readout.shape[2]
    me = lax.axis_index("seq").astype(jnp.int32)
    mp_index = lax.axis_index("mp")
    sample_count = mp_count // 2
    model_index = (mp_index // sample_count).astype(jnp.int32)
    sample_index = mp_index % sample_count
    signed = jnp.where(model_index == 1, 1.0, -1.0).astype(jnp.float32)
    factor = (signed * step_weight[timestep[sample_index]]).reshape(1)
    chunks = [heads_local - 1, 1] if heads_local > 1 else [1]
    widths = [c * 2 * HD for c in chunks]
    widths[0] += -(-heads_local * lat // HD) * HD
    readout_t = jnp.swapaxes(readout, 1, 2)

    arrived = [[None] * seq_count for _ in chunks]
    for k in range(seq_count - 1, -1, -1):
        packed = pack(jnp.stack([me ^ k, model_index]), qkv, readout_t, chunks, widths)
        for c, array in enumerate(packed):
            arrived[c][k] = swap(array, "seq", k) if k else array

    result, head = None, 0
    for c, count in enumerate(chunks):
        result = attend(
            arrived[c], arrived[0], result, span_frames, factor, me.reshape(1), count, head, lat, c == len(chunks) - 1
        )
        head += count
        if c < len(chunks) - 1:
            result = result[0]
    own = result[0].astype(jnp.float32)
    for k in range(seq_count - 1, 0, -1):
        own = own + swap(result[k], "seq", k).astype(jnp.float32)
    whole = own
    for k in range(mp_count - 1, 0, -1):
        whole = whole + swap(own, "mp", k)
    return whole.T


def solution(mesh):
    return jax.shard_map(
        body,
        mesh=mesh,
        in_specs=(P("mp", "seq", None), P(), P(), P(), P()),
        out_specs=P("seq", None),
        check_vma=False,
    )
```

```python
import functools
import math

import jax
import jax.numpy as jnp
from jax import lax
from jax.experimental import pallas as pl
from jax.experimental.pallas import tpu as pltpu
from jax.sharding import PartitionSpec as P

HEADS = 32
HD = 128
FRAME_TOK = 64
NT = (((1,), (1,)), ((), ()))
VMEM_LIMIT = 32 * 1024 * 1024


def pack_first_kernel(count, place_ref, qkv_ref, readout_ref, *refs):
    out_ref = refs[-1]
    lat = readout_ref.shape[1]
    heads_local = readout_ref.shape[2] // HD
    for i in range(heads_local):
        base = i * 3 * HD
        if i < count:
            out_ref[:, i * 2 * HD : (i + 1) * 2 * HD] = qkv_ref[0, :, base : base + 2 * HD]
        values = qkv_ref[0, :, base + 2 * HD : base + 3 * HD]
        rows = readout_ref[0, :, i * HD : (i + 1) * HD]
        folded = lax.dot_general(rows, values, NT, preferred_element_type=jnp.float32)
        column = count * 2 * HD + (i * lat // HD) * HD
        row = (i * lat) % HD
        out_ref[row : row + lat, column : column + HD] = folded.astype(jnp.bfloat16)


def pack_last_kernel(place_ref, queries_ref, keys_ref, *refs):
    refs[-1][:, :HD] = queries_ref[0]
    refs[-1][:, HD:] = keys_ref[0]


def pack(place, qkv, readout_t, k, heads_local, chunk, count, width, after):
    rows = qkv.shape[1]
    lat = readout_t.shape[1]
    operands = [place, qkv]
    if chunk == 0:
        kernel = functools.partial(pack_first_kernel, count)
        in_specs = [
            pl.BlockSpec((1, rows, heads_local * 3 * HD), lambda g, m: (0, 0, m[0] ^ k)),
            pl.BlockSpec((1, lat, heads_local * HD), lambda g, m: (m[1], 0, m[0] ^ k)),
        ]
        operands += [readout_t]
    else:
        kernel = pack_last_kernel
        in_specs = [
            pl.BlockSpec((1, rows, HD), lambda g, m: (0, 0, ((m[0] ^ k) * heads_local + heads_local - 1) * 3)),
            pl.BlockSpec((1, rows, HD), lambda g, m: (0, 0, ((m[0] ^ k) * heads_local + heads_local - 1) * 3 + 1)),
        ]
        operands += [qkv]
    if after is not None:
        operands += [after]
        in_specs += [pl.BlockSpec(memory_space=pl.ANY)]
    return pl.pallas_call(
        kernel,
        grid_spec=pltpu.PrefetchScalarGridSpec(
            num_scalar_prefetch=1,
            grid=(1,),
            in_specs=in_specs,
            out_specs=pl.BlockSpec((rows, width), lambda g, m: (0, 0)),
        ),
        out_shape=jax.ShapeDtypeStruct((rows, width), jnp.bfloat16),
        compiler_params=pltpu.CompilerParams(vmem_limit_bytes=VMEM_LIMIT),
        cost_estimate=pl.CostEstimate(
            flops=2 * rows * lat * heads_local * HD if chunk == 0 else 0,
            bytes_accessed=rows * width * 4,
            transcendentals=0,
        ),
        name="pack",
    )(*operands)


def attend_kernel(seq_count, count, value_head, value_column, lat, order, last, frames_ref, factor_ref, me_ref, *refs):
    pieces = refs[:seq_count]
    refs = refs[seq_count:]
    value_refs, earlier = pieces, None
    if value_head:
        value_refs, earlier = refs[:seq_count], refs[seq_count]
        refs = refs[seq_count + 1 :]
    out_refs = refs[-3:-1] if last else refs[-2:-1]
    asked = refs[-1]
    rows = pieces[0].shape[0]
    tokens = seq_count * rows
    spans = frames_ref.shape[0]
    log2_scale = math.log2(math.e) / math.sqrt(HD)
    half = seq_count // 2

    end = frames_ref[0] * FRAME_TOK
    ends = [end]
    for c in range(1, spans):
        end = end + frames_ref[c] * FRAME_TOK
        ends.append(end)
    me = me_ref[0]
    row_places = lax.broadcasted_iota(jnp.int32, (rows, 1), 0)
    key_places = jnp.concatenate([(me ^ k) * rows + row_places for k in range(seq_count)], axis=0)
    column_places = lax.broadcasted_iota(jnp.int32, (1, rows), 1)
    for n, k in enumerate(order):
        for i in range(count):
            asked[n, i] = pieces[k][:, i * 2 * HD : i * 2 * HD + HD]
    reversed_bits = seq_count.bit_length() - 1

    def place_of(n):
        k = jnp.int32(0)
        for bit in range(reversed_bits):
            k = k | (((n >> bit) & 1) << (reversed_bits - 1 - bit))
        return me ^ k

    def one_block(b, carry):
        first = b * 2
        places = jnp.concatenate([place_of(first + j) * rows + column_places for j in range(2)], axis=1)
        bound = jnp.full((1, 2 * rows), ends[0], jnp.int32)
        for c in range(1, spans):
            bound = jnp.where(places >= ends[c - 1], ends[c], bound)
        allowed = key_places < bound
        total = None
        for i in range(count):
            queries = asked[pl.ds(first, 2), i].reshape(2 * rows, HD)
            keys = jnp.concatenate([p[:, i * 2 * HD + HD : (i + 1) * 2 * HD] for p in pieces], axis=0)
            scores = lax.dot_general(keys, queries, NT, preferred_element_type=jnp.float32)
            scores = jnp.where(allowed, scores, -jnp.inf)
            peak = jnp.max(scores, axis=0, keepdims=True)
            raw = jnp.exp2((scores - peak) * log2_scale)
            row_total = jnp.sum(raw, axis=0, keepdims=True)
            weights = raw.astype(jnp.bfloat16)
            h = value_head + i
            column = value_column + (h * lat // HD) * HD
            row = (h * lat) % HD
            folded = jnp.concatenate([v[row : row + lat, column : column + HD] for v in value_refs], axis=1)
            summed = jnp.dot(folded, weights, preferred_element_type=jnp.float32) / row_total
            total = summed if total is None else total + summed
        for j in range(2):
            part = total[:, j * rows : (j + 1) * rows]
            n = first + j
            if earlier is not None:
                part = part + earlier[n]
            if last:
                part = part * factor_ref[0]

                @pl.when(n < half)
                def _():
                    out_refs[0][n] = part

                @pl.when(n >= half)
                def _():
                    out_refs[1][n - half] = part.astype(jnp.bfloat16)
            else:
                out_refs[0][n] = part
        return carry

    lax.fori_loop(0, half, one_block, 0)


def attend(pieces, value_pieces, earlier, after, span_frames, factor, me, count, value_head, value_column, lat, order, last):
    seq_count = len(pieces)
    rows, width = pieces[0].shape
    tokens = seq_count * rows
    smem = pl.BlockSpec(memory_space=pltpu.SMEM)
    vmem = pl.BlockSpec(memory_space=pltpu.VMEM)
    operands = [span_frames, factor, me] + list(pieces)
    in_specs = [smem] * 3 + [vmem] * seq_count
    if value_head:
        operands += list(value_pieces) + [earlier]
        in_specs += [vmem] * (seq_count + 1)
    if after is not None:
        operands += [after]
        in_specs += [pl.BlockSpec(memory_space=pl.ANY)]
    if last:
        out_shape = [
            jax.ShapeDtypeStruct((seq_count // 2, lat, rows), jnp.float32),
            jax.ShapeDtypeStruct((seq_count // 2, lat, rows), jnp.bfloat16),
        ]
    else:
        out_shape = [jax.ShapeDtypeStruct((seq_count, lat, rows), jnp.float32)]
    return pl.pallas_call(
        functools.partial(attend_kernel, seq_count, count, value_head, value_column, lat, order, last),
        in_specs=in_specs,
        out_specs=[vmem] * len(out_shape),
        out_shape=out_shape,
        scratch_shapes=[pltpu.VMEM((seq_count, count, rows, HD), jnp.bfloat16)],
        compiler_params=pltpu.CompilerParams(vmem_limit_bytes=VMEM_LIMIT),
        cost_estimate=pl.CostEstimate(
            flops=count * tokens * tokens * 2 * (HD + lat),
            bytes_accessed=tokens * width * 2,
            transcendentals=count * tokens * tokens,
        ),
        name="attend",
    )(*operands)


def swap(array, axis, offset):
    size = lax.axis_size(axis)
    return lax.ppermute(array, axis, [(i, i ^ offset) for i in range(size)])


def body(qkv, readout, step_weight, timestep, span_frames):
    seq_count = lax.axis_size("seq")
    mp_count = lax.axis_size("mp")
    heads_local = HEADS // seq_count
    lat = readout.shape[2]
    me = lax.axis_index("seq").astype(jnp.int32)
    mp_index = lax.axis_index("mp")
    sample_count = mp_count // 2
    model_index = (mp_index // sample_count).astype(jnp.int32)
    sample_index = mp_index % sample_count
    signed = jnp.where(model_index == 1, 1.0, -1.0).astype(jnp.float32)
    factor = (signed * step_weight[timestep[sample_index]]).reshape(1)
    chunks = [heads_local - 1, 1] if heads_local > 1 else [1]
    value_column = chunks[0] * 2 * HD
    widths = [value_column + -(-heads_local * lat // HD) * HD, 2 * HD]
    readout_t = jnp.swapaxes(readout, 1, 2)
    place = jnp.stack([me, model_index])
    bits = seq_count.bit_length() - 1
    order = [sum(((n >> b) & 1) << (bits - 1 - b) for b in range(bits)) for n in range(seq_count)]

    half = seq_count // 2
    far = list(range(seq_count - 1, half - 1, -1))
    near = list(range(half - 1, 0, -1))
    arrived = [[None] * seq_count for _ in chunks]

    def send(c, k, after):
        packed = pack(place, qkv, readout_t, k, heads_local, c, chunks[c], widths[c], after)
        arrived[c][k] = swap(packed, "seq", k) if k else packed
        return packed

    before = None
    for k in far:
        before = send(0, k, before)
    for k in near:
        send(0, k, before)
        before = arrived[0][k]
    send(0, 0, before)
    hold = None
    if len(chunks) > 1:
        for k in near:
            send(1, k, before)
            before = arrived[1][k]
        send(1, 0, before)
        for k in far:
            hold = send(1, k, before)
            before = arrived[0][k]

    result, head = None, 0
    for c, count in enumerate(chunks):
        last = c == len(chunks) - 1
        result = attend(
            arrived[c], arrived[0], result, None if last else hold, span_frames, factor, me.reshape(1),
            count, head, value_column, lat, order, last,
        )
        head += count
        if not last:
            result = result[0]
    keep, give = result
    offset = 1
    while True:
        keep = keep + swap(give, "seq", offset).astype(jnp.float32)
        offset *= 2
        if offset == seq_count:
            break
        size = keep.shape[0] // 2
        keep, give = keep[:size], keep[size:]
    whole = keep[0]
    offset = 1
    while offset < mp_count:
        whole = whole + swap(whole, "mp", offset)
        offset *= 2
    return whole.T


def solution(mesh):
    return jax.shard_map(
        body,
        mesh=mesh,
        in_specs=(P("mp", "seq", None), P(), P(), P(), P()),
        out_specs=P("seq", None),
        check_vma=False,
    )
```

```python
import functools
import math

import jax
import jax.numpy as jnp
from jax import lax
from jax.experimental import pallas as pl
from jax.experimental.pallas import tpu as pltpu
from jax.sharding import PartitionSpec as P

HEADS = 32
HD = 128
FRAME_TOK = 64
NT = (((1,), (1,)), ((), ()))
VMEM_LIMIT = 32 * 1024 * 1024


def fold(out_ref, column, lat, heads, qkv_ref, readout_ref):
    for i in range(heads):
        base = i * 3 * HD + 2 * HD
        values = qkv_ref[0, :, base : base + HD]
        rows = readout_ref[0, :, i * HD : (i + 1) * HD]
        folded = lax.dot_general(rows, values, NT, preferred_element_type=jnp.float32)
        row, c = (i * lat) % HD, column + (i * lat // HD) * HD
        out_ref[row : row + lat, c : c + HD] = folded.astype(jnp.bfloat16)


def pack_first_kernel(count, place_ref, qkv_ref, readout_ref, *refs):
    out_ref = refs[-1].at[0]
    for i in range(count):
        out_ref[:, i * 2 * HD : (i + 1) * 2 * HD] = qkv_ref[0, :, i * 3 * HD : i * 3 * HD + 2 * HD]
    heads = readout_ref.shape[2] // HD
    fold(out_ref, count * 2 * HD, readout_ref.shape[1], heads, qkv_ref, readout_ref)


def pack_last_kernel(place_ref, queries_ref, keys_ref, *refs):
    refs[-1][0, :, :HD] = queries_ref[0]
    refs[-1][0, :, HD:] = keys_ref[0]


def pack(place, qkv, readout_t, steps, target, heads_local, first, count, width, after):
    rows = qkv.shape[1]
    lat = readout_t.shape[1]
    operands = [place, qkv]
    if first:
        kernel = functools.partial(pack_first_kernel, count)
        in_specs = [
            pl.BlockSpec((1, rows, heads_local * 3 * HD), lambda g, m: (0, 0, target(g, m[0]))),
            pl.BlockSpec((1, lat, heads_local * HD), lambda g, m: (m[1], 0, target(g, m[0]))),
        ]
        operands += [readout_t]
    else:
        kernel = pack_last_kernel
        in_specs = [
            pl.BlockSpec((1, rows, HD), lambda g, m: (0, 0, (target(g, m[0]) * heads_local + heads_local - 1) * 3)),
            pl.BlockSpec((1, rows, HD), lambda g, m: (0, 0, (target(g, m[0]) * heads_local + heads_local - 1) * 3 + 1)),
        ]
        operands += [qkv]
    if after is not None:
        operands += [after]
        in_specs += [pl.BlockSpec(memory_space=pl.ANY)]
    return pl.pallas_call(
        kernel,
        grid_spec=pltpu.PrefetchScalarGridSpec(
            num_scalar_prefetch=1,
            grid=(steps,),
            in_specs=in_specs,
            out_specs=pl.BlockSpec((1, rows, width), lambda g, m: (g, 0, 0)),
        ),
        out_shape=jax.ShapeDtypeStruct((steps, rows, width), jnp.bfloat16),
        compiler_params=pltpu.CompilerParams(vmem_limit_bytes=VMEM_LIMIT),
        cost_estimate=pl.CostEstimate(
            flops=2 * steps * rows * lat * heads_local * HD if first else 0,
            bytes_accessed=steps * rows * width * 4,
            transcendentals=0,
        ),
        name="pack",
    )(*operands)


def attend_kernel(
    seq_count, head, count, near_value_column, far_value_column, lat, order, last, frames_ref, factor_ref, me_ref, near_ref, *refs
):
    half = seq_count // 2
    far_refs, refs = refs[:half], refs[half:]
    far_values, earlier = far_refs, None
    if head:
        far_values, earlier, refs = refs[:half], refs[half], refs[half + 1 :]
    out_refs = refs[-3:-1] if last else refs[-2:-1]
    asked = refs[-1]
    me = me_ref[0]
    rows = near_ref.shape[1]

    def near(k, i):
        return near_ref[(me & (half - 1)) ^ k, :, i * HD : (i + 1) * HD]

    def far(k, i):
        return far_refs[k - half][0, :, i * HD : (i + 1) * HD]

    def cell(k, i, what):
        return near(k, 2 * (head + i) + what) if k < half else far(k, 2 * i + what)

    def value(k, h):
        row, column = (h * lat) % HD, (h * lat // HD) * HD
        if k < half:
            column += near_value_column
            return near_ref[(me & (half - 1)) ^ k, row : row + lat, column : column + HD]
        column += far_value_column
        return far_values[k - half][0, row : row + lat, column : column + HD]

    tokens = seq_count * rows
    spans = frames_ref.shape[0]
    log2_scale = math.log2(math.e) / math.sqrt(HD)

    end = frames_ref[0] * FRAME_TOK
    ends = [end]
    for c in range(1, spans):
        end = end + frames_ref[c] * FRAME_TOK
        ends.append(end)
    row_places = lax.broadcasted_iota(jnp.int32, (rows, 1), 0)
    key_places = jnp.concatenate([(me ^ k) * rows + row_places for k in range(seq_count)], axis=0)
    column_places = lax.broadcasted_iota(jnp.int32, (1, rows), 1)
    for n, k in enumerate(order):
        for i in range(count):
            asked[n, i] = cell(k, i, 0)
    reversed_bits = seq_count.bit_length() - 1

    def place_of(n):
        k = jnp.int32(0)
        for bit in range(reversed_bits):
            k = k | (((n >> bit) & 1) << (reversed_bits - 1 - bit))
        return me ^ k

    def one_block(b, carry):
        first = b * 2
        places = jnp.concatenate([place_of(first + j) * rows + column_places for j in range(2)], axis=1)
        bound = jnp.full((1, 2 * rows), ends[0], jnp.int32)
        for c in range(1, spans):
            bound = jnp.where(places >= ends[c - 1], ends[c], bound)
        allowed = key_places < bound
        total = None
        for i in range(count):
            queries = asked[pl.ds(first, 2), i].reshape(2 * rows, HD)
            keys = jnp.concatenate([cell(k, i, 1) for k in range(seq_count)], axis=0)
            scores = lax.dot_general(keys, queries, NT, preferred_element_type=jnp.float32)
            scores = jnp.where(allowed, scores, -jnp.inf)
            peak = jnp.max(scores, axis=0, keepdims=True)
            raw = jnp.exp2((scores - peak) * log2_scale)
            row_total = jnp.sum(raw, axis=0, keepdims=True)
            weights = raw.astype(jnp.bfloat16)
            folded = jnp.concatenate([value(k, head + i) for k in range(seq_count)], axis=1)
            summed = jnp.dot(folded, weights, preferred_element_type=jnp.float32) / row_total
            total = summed if total is None else total + summed
        for j in range(2):
            part = total[:, j * rows : (j + 1) * rows]
            n = first + j
            if earlier is not None:
                part = part + earlier[n]
            if last:
                part = part * factor_ref[0]

                @pl.when(n < half)
                def _():
                    out_refs[0][n] = part

                @pl.when(n >= half)
                def _():
                    out_refs[1][n - half] = part.astype(jnp.bfloat16)
            else:
                out_refs[0][n] = part
        return carry

    lax.fori_loop(0, half, one_block, 0)


def attend(
    near, far, far_values, earlier, after, span_frames, factor, me, head, count, columns, lat, order, last
):
    half, rows, _ = near.shape
    seq_count = 2 * half
    tokens = seq_count * rows
    smem = pl.BlockSpec(memory_space=pltpu.SMEM)
    vmem = pl.BlockSpec(memory_space=pltpu.VMEM)
    operands = [span_frames, factor, me, near] + list(far)
    if head:
        operands += list(far_values) + [earlier]
    in_specs = [smem] * 3 + [vmem] * (len(operands) - 3)
    if after is not None:
        operands += [after]
        in_specs += [pl.BlockSpec(memory_space=pl.ANY)]
    if last:
        out_shape = [
            jax.ShapeDtypeStruct((seq_count // 2, lat, rows), jnp.float32),
            jax.ShapeDtypeStruct((seq_count // 2, lat, rows), jnp.bfloat16),
        ]
    else:
        out_shape = [jax.ShapeDtypeStruct((seq_count, lat, rows), jnp.float32)]
    return pl.pallas_call(
        functools.partial(attend_kernel, seq_count, head, count, *columns, lat, order, last),
        in_specs=in_specs,
        out_specs=[vmem] * len(out_shape),
        out_shape=out_shape,
        scratch_shapes=[pltpu.VMEM((seq_count, count, rows, HD), jnp.bfloat16)],
        compiler_params=pltpu.CompilerParams(vmem_limit_bytes=VMEM_LIMIT),
        cost_estimate=pl.CostEstimate(
            flops=count * tokens * tokens * 2 * (HD + lat),
            bytes_accessed=tokens * count * 3 * HD * 2,
            transcendentals=count * tokens * tokens,
        ),
        name="attend",
    )(*operands)


def swap(array, axis, offset):
    size = lax.axis_size(axis)
    return lax.ppermute(array, axis, [(i, i ^ offset) for i in range(size)])


def body(qkv, readout, step_weight, timestep, span_frames):
    seq_count = lax.axis_size("seq")
    mp_count = lax.axis_size("mp")
    heads_local = HEADS // seq_count
    lat = readout.shape[2]
    me = lax.axis_index("seq").astype(jnp.int32)
    mp_index = lax.axis_index("mp")
    sample_count = mp_count // 2
    model_index = (mp_index // sample_count).astype(jnp.int32)
    sample_index = mp_index % sample_count
    signed = jnp.where(model_index == 1, 1.0, -1.0).astype(jnp.float32)
    factor = (signed * step_weight[timestep[sample_index]]).reshape(1)
    chunks = [heads_local - 1, 1] if heads_local > 1 else [1]
    value_width = -(-heads_local * lat // HD) * HD
    columns = (heads_local * 2 * HD, chunks[0] * 2 * HD)
    widths = [columns[1] + value_width, 2 * HD]
    readout_t = jnp.swapaxes(readout, 1, 2)
    place = jnp.stack([me, model_index])
    bits = seq_count.bit_length() - 1
    order = [sum(((n >> b) & 1) << (bits - 1 - b) for b in range(bits)) for n in range(seq_count)]
    half = seq_count // 2

    def send(c, k, after):
        packed = pack(
            place, qkv, readout_t, 1, lambda g, m: m ^ k, heads_local, c == 0, chunks[c], widths[c], after
        )
        return packed, swap(packed, "seq", k)

    far = [[None] * half for _ in chunks]
    before = None
    for k in range(seq_count - 1, half - 1, -1):
        before, far[0][k - half] = send(0, k, before)
    near = pack(
        place, qkv, readout_t, half, lambda g, m: (m & -half) | g, heads_local, True, heads_local,
        columns[0] + value_width, before,
    )
    groups = [list(range(half)), list(range(half, seq_count))]
    near = lax.all_to_all(near, "seq", split_axis=0, concat_axis=0, axis_index_groups=groups, tiled=True)
    hold = None
    if len(chunks) > 1:
        for k in range(seq_count - 1, half - 1, -1):
            hold, far[1][k - half] = send(1, k, far[0][k - half])

    result, head = None, 0
    for c, count in enumerate(chunks):
        last = c == len(chunks) - 1
        result = attend(
            near, far[c], far[0], result, None if last else hold, span_frames, factor, me.reshape(1),
            head, count, columns, lat, order, last,
        )
        head += count
        if not last:
            result = result[0]
    keep, give = result
    offset = 1
    while True:
        keep = keep + swap(give, "seq", offset).astype(jnp.float32)
        offset *= 2
        if offset == seq_count:
            break
        size = keep.shape[0] // 2
        keep, give = keep[:size], keep[size:]
    whole = keep[0]
    offset = 1
    while offset < mp_count:
        whole = whole + swap(whole, "mp", offset)
        offset *= 2
    return whole.T


def solution(mesh):
    return jax.shard_map(
        body,
        mesh=mesh,
        in_specs=(P("mp", "seq", None), P(), P(), P(), P()),
        out_specs=P("seq", None),
        check_vma=False,
    )
```

```python
import functools
import math

import jax
import jax.numpy as jnp
from jax import lax
from jax.experimental import pallas as pl
from jax.experimental.pallas import tpu as pltpu
from jax.sharding import PartitionSpec as P

HEADS = 32
HD = 128
FRAME_TOK = 64
NT = (((1,), (1,)), ((), ()))
VMEM_LIMIT = 32 * 1024 * 1024


def layout(score_heads, value_heads, lat):
    scores = {h: n * 2 * HD for n, h in enumerate(score_heads)}
    start = len(score_heads) * 2 * HD
    values = {h: ((n * lat) % HD, start + (n * lat // HD) * HD) for n, h in enumerate(value_heads)}
    return scores, values, start + -(-len(value_heads) * lat // HD) * HD


def pack_kernel(scores, values, place_ref, qkv_ref, readout_ref, *refs):
    out_ref = refs[-1]
    lat = readout_ref.shape[1]
    for h, column in scores.items():
        out_ref[:, column : column + 2 * HD] = qkv_ref[0, :, h * 3 * HD : h * 3 * HD + 2 * HD]
    for h, (row, column) in values.items():
        own = qkv_ref[0, :, h * 3 * HD + 2 * HD : (h + 1) * 3 * HD]
        rows = readout_ref[0, :, h * HD : (h + 1) * HD]
        folded = lax.dot_general(rows, own, NT, preferred_element_type=jnp.float32)
        out_ref[row : row + lat, column : column + HD] = folded.astype(jnp.bfloat16)


def pack(place, qkv, readout_t, k, heads_local, piece, after):
    rows = qkv.shape[1]
    lat = readout_t.shape[1]
    scores, values, width = piece
    operands = [place, qkv, readout_t]
    in_specs = [
        pl.BlockSpec((1, rows, heads_local * 3 * HD), lambda g, m: (0, 0, m[0] ^ k)),
        pl.BlockSpec((1, lat, heads_local * HD), lambda g, m: (m[1], 0, m[0] ^ k)),
    ]
    if after is not None:
        operands += [after]
        in_specs += [pl.BlockSpec(memory_space=pl.ANY)]
    return pl.pallas_call(
        functools.partial(pack_kernel, scores, values),
        grid_spec=pltpu.PrefetchScalarGridSpec(
            num_scalar_prefetch=1,
            grid=(1,),
            in_specs=in_specs,
            out_specs=pl.BlockSpec((rows, width), lambda g, m: (0, 0)),
        ),
        out_shape=jax.ShapeDtypeStruct((rows, width), jnp.bfloat16),
        compiler_params=pltpu.CompilerParams(vmem_limit_bytes=VMEM_LIMIT),
        cost_estimate=pl.CostEstimate(
            flops=2 * rows * lat * len(values) * HD, bytes_accessed=rows * width * 4, transcendentals=0
        ),
        name="pack",
    )(*operands)


def attend_kernel(seq_count, heads, near_piece, far_pieces, lat, order, last, later, frames_ref, factor_ref, me_ref, *refs):
    half = seq_count // 2
    count = len(heads)
    near_refs, refs = refs[:half], refs[half:]
    far_refs, refs = refs[: half * len(far_pieces)], refs[half * len(far_pieces) :]
    earlier = refs[0] if later else None
    out_refs = refs[-3:-1] if last else refs[-2:-1]
    asked = refs[-1]
    me = me_ref[0]
    rows = near_refs[0].shape[0]

    def sources(k):
        if k < half:
            return [(near_refs[k], near_piece)]
        return [(far_refs[c * half + k - half], piece) for c, piece in enumerate(far_pieces)]

    def cell(k, h, what):
        for ref, (scores, _, _) in sources(k):
            if h in scores:
                column = scores[h] + what * HD
                return ref[:, column : column + HD]

    def value(k, h):
        for ref, (_, values, _) in sources(k):
            if h in values:
                row, column = values[h]
                return ref[row : row + lat, column : column + HD]

    tokens = seq_count * rows
    spans = frames_ref.shape[0]
    log2_scale = math.log2(math.e) / math.sqrt(HD)

    end = frames_ref[0] * FRAME_TOK
    ends = [end]
    for c in range(1, spans):
        end = end + frames_ref[c] * FRAME_TOK
        ends.append(end)
    row_places = lax.broadcasted_iota(jnp.int32, (rows, 1), 0)
    key_places = jnp.concatenate([(me ^ k) * rows + row_places for k in range(seq_count)], axis=0)
    column_places = lax.broadcasted_iota(jnp.int32, (1, rows), 1)
    for n, k in enumerate(order):
        for i in range(count):
            asked[n, i] = cell(k, heads[i], 0)
    reversed_bits = seq_count.bit_length() - 1

    def place_of(n):
        k = jnp.int32(0)
        for bit in range(reversed_bits):
            k = k | (((n >> bit) & 1) << (reversed_bits - 1 - bit))
        return me ^ k

    def one_block(b, carry):
        first = b * 2
        places = jnp.concatenate([place_of(first + j) * rows + column_places for j in range(2)], axis=1)
        bound = jnp.full((1, 2 * rows), ends[0], jnp.int32)
        for c in range(1, spans):
            bound = jnp.where(places >= ends[c - 1], ends[c], bound)
        allowed = key_places < bound
        total = None
        for i in range(count):
            queries = asked[pl.ds(first, 2), i].reshape(2 * rows, HD)
            keys = jnp.concatenate([cell(k, heads[i], 1) for k in range(seq_count)], axis=0)
            scores = lax.dot_general(keys, queries, NT, preferred_element_type=jnp.float32)
            scores = jnp.where(allowed, scores, -jnp.inf)
            peak = jnp.max(scores, axis=0, keepdims=True)
            raw = jnp.exp2((scores - peak) * log2_scale)
            row_total = jnp.sum(raw, axis=0, keepdims=True)
            weights = raw.astype(jnp.bfloat16)
            folded = jnp.concatenate([value(k, heads[i]) for k in range(seq_count)], axis=1)
            summed = jnp.dot(folded, weights, preferred_element_type=jnp.float32) / row_total
            total = summed if total is None else total + summed
        for j in range(2):
            part = total[:, j * rows : (j + 1) * rows]
            n = first + j
            if earlier is not None:
                part = part + earlier[n]
            if last:
                part = part * factor_ref[0]

                @pl.when(n < half)
                def _():
                    out_refs[0][n] = part

                @pl.when(n >= half)
                def _():
                    out_refs[1][n - half] = part.astype(jnp.bfloat16)
            else:
                out_refs[0][n] = part
        return carry

    lax.fori_loop(0, half, one_block, 0)


def attend(near, far, earlier, after, span_frames, factor, me, heads, near_piece, far_pieces, lat, order, last):
    half = len(near)
    rows = near[0].shape[0]
    seq_count = 2 * half
    tokens = seq_count * rows
    count = len(heads)
    smem = pl.BlockSpec(memory_space=pltpu.SMEM)
    vmem = pl.BlockSpec(memory_space=pltpu.VMEM)
    operands = [span_frames, factor, me] + list(near) + [p for pieces in far for p in pieces]
    if earlier is not None:
        operands += [earlier]
    in_specs = [smem] * 3 + [vmem] * (len(operands) - 3)
    for array in after:
        operands += [array]
        in_specs += [pl.BlockSpec(memory_space=pl.ANY)]
    if last:
        out_shape = [
            jax.ShapeDtypeStruct((seq_count // 2, lat, rows), jnp.float32),
            jax.ShapeDtypeStruct((seq_count // 2, lat, rows), jnp.bfloat16),
        ]
    else:
        out_shape = [jax.ShapeDtypeStruct((seq_count, lat, rows), jnp.float32)]
    return pl.pallas_call(
        functools.partial(
            attend_kernel, seq_count, heads, near_piece, far_pieces, lat, order, last, earlier is not None
        ),
        in_specs=in_specs,
        out_specs=[vmem] * len(out_shape),
        out_shape=out_shape,
        scratch_shapes=[pltpu.VMEM((seq_count, count, rows, HD), jnp.bfloat16)],
        compiler_params=pltpu.CompilerParams(vmem_limit_bytes=VMEM_LIMIT),
        cost_estimate=pl.CostEstimate(
            flops=count * tokens * tokens * 2 * (HD + lat),
            bytes_accessed=tokens * count * 3 * HD * 2,
            transcendentals=count * tokens * tokens,
        ),
        name="attend",
    )(*operands)


def swap(array, axis, offset):
    size = lax.axis_size(axis)
    return lax.ppermute(array, axis, [(i, i ^ offset) for i in range(size)])


def body(qkv, readout, step_weight, timestep, span_frames):
    seq_count = lax.axis_size("seq")
    mp_count = lax.axis_size("mp")
    heads_local = HEADS // seq_count
    lat = readout.shape[2]
    me = lax.axis_index("seq").astype(jnp.int32)
    mp_index = lax.axis_index("mp")
    sample_count = mp_count // 2
    model_index = (mp_index // sample_count).astype(jnp.int32)
    sample_index = mp_index % sample_count
    signed = jnp.where(model_index == 1, 1.0, -1.0).astype(jnp.float32)
    factor = (signed * step_weight[timestep[sample_index]]).reshape(1)
    readout_t = jnp.swapaxes(readout, 1, 2)
    place = jnp.stack([me, model_index])
    bits = seq_count.bit_length() - 1
    order = [sum(((n >> b) & 1) << (bits - 1 - b) for b in range(bits)) for n in range(seq_count)]
    half = seq_count // 2
    every = list(range(heads_local))
    chunks = [[0,1,2],[3]] if heads_local > 1 else [[0]]
    near_piece = layout(every, every, lat)
    far_pieces = [layout(heads, every if c == 0 else [], lat) for c, heads in enumerate(chunks)]

    def send(k, piece, after):
        packed = pack(place, qkv, readout_t, k, heads_local, piece, after)
        return packed, (swap(packed, "seq", k) if k else packed)

    far = [[None] * half for _ in chunks]
    near = [None] * half
    holds = [[] for _ in chunks]
    gates = [None, None]
    for c in range(len(chunks)):
        for n in range(half):
            k = seq_count - 1 - n
            packed, far[c][k - half] = send(k, far_pieces[c], gates[n % 2])
            if c:
                holds[c - 1].append(packed)
            else:
                gates[n % 2] = far[c][k - half]
        if c:
            gates = [far[c][1 % half], far[c][0]]
    for k in range(half):
        _, near[k] = send(k, near_piece, None)

    result = None
    for c, heads in enumerate(chunks):
        last = c == len(chunks) - 1
        result = attend(
            near, far[: c + 1], result, holds[c], span_frames, factor, me.reshape(1),
            heads, near_piece, far_pieces[: c + 1], lat, order, last,
        )
        if not last:
            result = result[0]
    keep, give = result
    keep = keep + swap(give, "seq", 1).astype(jnp.float32)
    offset = 2
    while offset < seq_count:
        radix = min(4, seq_count // offset)
        size = keep.shape[0] // radix
        parts = [keep[n * size : (n + 1) * size] for n in range(radix)]
        keep = parts[0]
        for n in range(radix - 1, 0, -1):
            bits_n = (n >> 1) | ((n & 1) << 1) if radix == 4 else n
            keep = keep + swap(parts[n], "seq", offset * bits_n)
        offset *= radix
    whole = keep[0]
    offset = 1
    while offset < mp_count:
        radix = min(4, mp_count // offset)
        own = whole
        for n in range(radix - 1, 0, -1):
            whole = whole + swap(own, "mp", offset * n)
        offset *= radix
    return whole.T


def solution(mesh):
    return jax.shard_map(
        body,
        mesh=mesh,
        in_specs=(P("mp", "seq", None), P(), P(), P(), P()),
        out_specs=P("seq", None),
        check_vma=False,
    )
```

```python
import functools
import math

import jax
import jax.numpy as jnp
from jax import lax
from jax.experimental import pallas as pl
from jax.experimental.pallas import tpu as pltpu
from jax.sharding import PartitionSpec as P

HEADS = 32
HD = 128
FRAME_TOK = 64
NT = (((1,), (1,)), ((), ()))
VMEM_LIMIT = 32 * 1024 * 1024
WHOLE_VMEM = 60 * 1024 * 1024


def layout(score_heads, value_heads, lat):
    scores = {h: n * 2 * HD for n, h in enumerate(score_heads)}
    start = len(score_heads) * 2 * HD
    values = {h: ((n * lat) % HD, start + (n * lat // HD) * HD) for n, h in enumerate(value_heads)}
    return scores, values, start + -(-len(value_heads) * lat // HD) * HD


def pack_kernel(scores, values, place_ref, qkv_ref, readout_ref, *refs):
    out_ref = refs[-1]
    lat = readout_ref.shape[1]
    for h, column in scores.items():
        out_ref[:, column : column + 2 * HD] = qkv_ref[0, :, h * 3 * HD : h * 3 * HD + 2 * HD]
    for h, (row, column) in values.items():
        own = qkv_ref[0, :, h * 3 * HD + 2 * HD : (h + 1) * 3 * HD]
        rows = readout_ref[0, :, h * HD : (h + 1) * HD]
        folded = lax.dot_general(rows, own, NT, preferred_element_type=jnp.float32)
        out_ref[row : row + lat, column : column + HD] = folded.astype(jnp.bfloat16)


def pack(place, qkv, readout_t, k, heads_local, piece, after, limit=VMEM_LIMIT):
    rows = qkv.shape[1]
    lat = readout_t.shape[1]
    scores, values, width = piece
    operands = [place, qkv, readout_t]
    in_specs = [
        pl.BlockSpec((1, rows, heads_local * 3 * HD), lambda g, m: (0, 0, m[0] ^ k)),
        pl.BlockSpec((1, lat, heads_local * HD), lambda g, m: (m[1], 0, m[0] ^ k)),
    ]
    if after is not None:
        operands += [after]
        in_specs += [pl.BlockSpec(memory_space=pl.ANY)]
    return pl.pallas_call(
        functools.partial(pack_kernel, scores, values),
        grid_spec=pltpu.PrefetchScalarGridSpec(
            num_scalar_prefetch=1,
            grid=(1,),
            in_specs=in_specs,
            out_specs=pl.BlockSpec((rows, width), lambda g, m: (0, 0)),
        ),
        out_shape=jax.ShapeDtypeStruct((rows, width), jnp.bfloat16),
        compiler_params=pltpu.CompilerParams(vmem_limit_bytes=limit),
        cost_estimate=pl.CostEstimate(
            flops=2 * rows * lat * len(values) * HD, bytes_accessed=rows * width * 4, transcendentals=0
        ),
        name="pack",
    )(*operands)


def attend_kernel(seq_count, heads, near_piece, far_pieces, lat, order, last, later, frames_ref, factor_ref, me_ref, *refs):
    half = seq_count // 2
    count = len(heads)
    near_refs, refs = refs[:half], refs[half:]
    far_refs, refs = refs[: half * len(far_pieces)], refs[half * len(far_pieces) :]
    earlier = refs[0] if later else None
    out_refs = refs[-4:-2] if last else refs[-3:-2]
    asked, folded = refs[-2:]
    me = me_ref[0]
    rows = near_refs[0].shape[0]

    def sources(k):
        if k < half:
            return [(near_refs[k], near_piece)]
        return [(far_refs[c * half + k - half], piece) for c, piece in enumerate(far_pieces)]

    def cell(k, h, what):
        for ref, (scores, _, _) in sources(k):
            if h in scores:
                column = scores[h] + what * HD
                return ref[:, column : column + HD]

    def value(k, h):
        for ref, (_, values, _) in sources(k):
            if h in values:
                row, column = values[h]
                return ref[row : row + lat, column : column + HD]

    spans = frames_ref.shape[0]
    log2_scale = math.log2(math.e) / math.sqrt(HD)
    reversed_bits = seq_count.bit_length() - 1
    block = 2 * rows

    end = frames_ref[0] * FRAME_TOK
    ends = [end]
    for c in range(1, spans):
        end = end + frames_ref[c] * FRAME_TOK
        ends.append(end)
    column_places = lax.broadcasted_iota(jnp.int32, (1, rows), 1)
    for n, k in enumerate(order):
        for i, h in enumerate(heads):
            asked[n, i] = cell(k, h, 0)
    for i, h in enumerate(heads):
        for k in range(seq_count):
            folded[i, :lat, k * rows : (k + 1) * rows] = value(k, h)
        folded[i, lat:] = jnp.ones_like(folded[i, lat:])

    def place_of(n):
        k = jnp.int32(0)
        for bit in range(reversed_bits):
            k = k | (((n >> bit) & 1) << (reversed_bits - 1 - bit))
        return me ^ k

    def one_block(b):
        first = b * 2
        places = jnp.concatenate([place_of(first + j) * rows + column_places for j in range(2)], axis=1)
        bound = jnp.full((1, block), ends[0], jnp.int32)
        for c in range(1, spans):
            bound = jnp.where(places >= ends[c - 1], ends[c], bound)
        bias = [
            jnp.where((me ^ k) * rows + start < bound, 0.0, -jnp.inf)
            for k in range(seq_count)
            for start in range(0, rows, FRAME_TOK)
        ]
        total = None
        for i, h in enumerate(heads):
            queries = asked[pl.ds(first, 2), i].reshape(block, HD)
            keys = jnp.concatenate([cell(k, h, 1) for k in range(seq_count)], axis=0)
            scores = lax.dot_general(keys, queries, NT, preferred_element_type=jnp.float32)
            frames = [scores[g * FRAME_TOK : (g + 1) * FRAME_TOK] for g in range(len(bias))]
            peaks = [jnp.max(f, axis=0, keepdims=True) + shift for f, shift in zip(frames, bias)]
            peak = functools.reduce(jnp.maximum, peaks)
            weights = [
                jnp.exp2((f + (shift - peak)) * log2_scale).astype(jnp.bfloat16) for f, shift in zip(frames, bias)
            ]
            summed = jnp.dot(folded[i], jnp.concatenate(weights, axis=0), preferred_element_type=jnp.float32)
            part = summed[:lat] / summed[lat : lat + 1]
            total = part if total is None else total + part
        for j in range(2):
            part = total[:, j * rows : (j + 1) * rows]
            n = first + j
            if earlier is not None:
                part = part + earlier[n]
            if last:
                part = part * factor_ref[0]

                @pl.when(n < half)
                def _():
                    out_refs[0][n] = part

                @pl.when(n >= half)
                def _():
                    out_refs[1][n - half] = part.astype(jnp.bfloat16)
            else:
                out_refs[0][n] = part

    together = 2 if count == 1 and half % 2 == 0 else 1

    def some_blocks(b, carry):
        for j in range(together):
            one_block(b * together + j)
        return carry

    lax.fori_loop(0, half // together, some_blocks, 0)


def attend(near, far, earlier, after, span_frames, factor, me, heads, near_piece, far_pieces, lat, order, last):
    half = len(near)
    rows = near[0].shape[0]
    seq_count = 2 * half
    tokens = seq_count * rows
    count = len(heads)
    smem = pl.BlockSpec(memory_space=pltpu.SMEM)
    vmem = pl.BlockSpec(memory_space=pltpu.VMEM)
    operands = [span_frames, factor, me] + list(near) + [p for pieces in far for p in pieces]
    if earlier is not None:
        operands += [earlier]
    in_specs = [smem] * 3 + [vmem] * (len(operands) - 3)
    for array in after:
        operands += [array]
        in_specs += [pl.BlockSpec(memory_space=pl.ANY)]
    if last:
        out_shape = [
            jax.ShapeDtypeStruct((seq_count // 2, lat, rows), jnp.float32),
            jax.ShapeDtypeStruct((seq_count // 2, lat, rows), jnp.bfloat16),
        ]
    else:
        out_shape = [jax.ShapeDtypeStruct((seq_count, lat, rows), jnp.float32)]
    return pl.pallas_call(
        functools.partial(
            attend_kernel, seq_count, heads, near_piece, far_pieces, lat, order, last, earlier is not None
        ),
        in_specs=in_specs,
        out_specs=[vmem] * len(out_shape),
        out_shape=out_shape,
        scratch_shapes=[
            pltpu.VMEM((seq_count, count, rows, HD), jnp.bfloat16),
            pltpu.VMEM((count, lat + 16, tokens), jnp.bfloat16),
        ],
        compiler_params=pltpu.CompilerParams(vmem_limit_bytes=VMEM_LIMIT),
        cost_estimate=pl.CostEstimate(
            flops=count * tokens * tokens * 2 * (HD + lat),
            bytes_accessed=tokens * count * 3 * HD * 2,
            transcendentals=count * tokens * tokens,
        ),
        name="attend",
    )(*operands)


def swap(array, axis, offset):
    size = lax.axis_size(axis)
    return lax.ppermute(array, axis, [(i, i ^ offset) for i in range(size)])


def body(qkv, readout, step_weight, timestep, span_frames):
    seq_count = lax.axis_size("seq")
    mp_count = lax.axis_size("mp")
    heads_local = HEADS // seq_count
    lat = readout.shape[2]
    me = lax.axis_index("seq").astype(jnp.int32)
    mp_index = lax.axis_index("mp")
    sample_count = mp_count // 2
    model_index = (mp_index // sample_count).astype(jnp.int32)
    sample_index = mp_index % sample_count
    signed = jnp.where(model_index == 1, 1.0, -1.0).astype(jnp.float32)
    factor = (signed * step_weight[timestep[sample_index]]).reshape(1)
    readout_t = jnp.swapaxes(readout, 1, 2)
    place = jnp.stack([me, model_index])
    bits = seq_count.bit_length() - 1
    order = [sum(((n >> b) & 1) << (bits - 1 - b) for b in range(bits)) for n in range(seq_count)]
    half = seq_count // 2
    every = list(range(heads_local))
    chunks = [[0,1,2],[3]] if heads_local > 1 else [[0]]
    near_piece = layout(every, every, lat)
    far_pieces = [layout(heads, every if c == 0 else [], lat) for c, heads in enumerate(chunks)]

    def send(k, piece, after, limit=VMEM_LIMIT):
        packed = pack(place, qkv, readout_t, k, heads_local, piece, after, limit)
        return packed, (swap(packed, "seq", k) if k else packed)

    far = [[None] * half for _ in chunks]
    near = [None] * half
    holds = [[] for _ in chunks]
    gates = [None, None]
    for c in range(len(chunks)):
        for n in range(half):
            k = seq_count - 1 - n
            packed, far[c][k - half] = send(k, far_pieces[c], gates[n % 2], VMEM_LIMIT if c or n else WHOLE_VMEM)
            if c:
                holds[c - 1].append(packed)
            else:
                gates[n % 2] = far[c][k - half]
        if c:
            gates = [far[c][1 % half], far[c][0]]
    for k in range(half):
        _, near[k] = send(k, near_piece, None)

    result = None
    for c, heads in enumerate(chunks):
        last = c == len(chunks) - 1
        result = attend(
            near, far[: c + 1], result, holds[c], span_frames, factor, me.reshape(1),
            heads, near_piece, far_pieces[: c + 1], lat, order, last,
        )
        if not last:
            result = result[0]
    keep, give = result
    keep = keep + swap(give, "seq", 1).astype(jnp.float32)
    offset = 2
    while offset < seq_count:
        radix = min(4, seq_count // offset)
        size = keep.shape[0] // radix
        parts = [keep[n * size : (n + 1) * size] for n in range(radix)]
        keep = parts[0]
        for n in range(radix - 1, 0, -1):
            bits_n = (n >> 1) | ((n & 1) << 1) if radix == 4 else n
            keep = keep + swap(parts[n], "seq", offset * bits_n)
        offset *= radix
    whole = keep[0]
    offset = 1
    while offset < mp_count:
        radix = min(4, mp_count // offset)
        own = whole
        for n in range(radix - 1, 0, -1):
            whole = whole + swap(own, "mp", offset * n)
        offset *= radix
    return whole.T


def solution(mesh):
    return jax.shard_map(
        body,
        mesh=mesh,
        in_specs=(P("mp", "seq", None), P(), P(), P(), P()),
        out_specs=P("seq", None),
        check_vma=False,
    )
```

```python
import functools
import math

import jax
import jax.numpy as jnp
from jax import lax
from jax.experimental import pallas as pl
from jax.experimental.pallas import tpu as pltpu
from jax.sharding import PartitionSpec as P

HEADS = 32
HD = 128
FRAME_TOK = 64
NT = (((1,), (1,)), ((), ()))
VMEM_LIMIT = 8 * 1024 * 1024
ATTEND_VMEM = 20 * 1024 * 1024
WHOLE_VMEM = 60 * 1024 * 1024


def layout(score_heads, value_heads, lat):
    scores = {h: n * 2 * HD for n, h in enumerate(score_heads)}
    start = len(score_heads) * 2 * HD
    values = {h: ((n * lat) % HD, start + (n * lat // HD) * HD) for n, h in enumerate(value_heads)}
    return scores, values, start + -(-len(value_heads) * lat // HD) * HD


def pack_kernel(scores, values, place_ref, qkv_ref, readout_ref, *refs):
    out_ref = refs[-1]
    lat = readout_ref.shape[1]
    for h, column in scores.items():
        out_ref[:, column : column + 2 * HD] = qkv_ref[0, :, h * 3 * HD : h * 3 * HD + 2 * HD]
    for h, (row, column) in values.items():
        own = qkv_ref[0, :, h * 3 * HD + 2 * HD : (h + 1) * 3 * HD]
        rows = readout_ref[0, :, h * HD : (h + 1) * HD]
        folded = lax.dot_general(rows, own, NT, preferred_element_type=jnp.float32)
        out_ref[row : row + lat, column : column + HD] = folded.astype(jnp.bfloat16)


def pack(place, qkv, readout_t, k, heads_local, piece, after):
    rows = qkv.shape[1]
    lat = readout_t.shape[1]
    scores, values, width = piece
    operands = [place, qkv, readout_t]
    in_specs = [
        pl.BlockSpec((1, rows, heads_local * 3 * HD), lambda g, m: (0, 0, m[0] ^ k)),
        pl.BlockSpec((1, lat, heads_local * HD), lambda g, m: (m[1], 0, m[0] ^ k)),
    ]
    if after is not None:
        operands += [after]
        in_specs += [pl.BlockSpec(memory_space=pl.ANY)]
    return pl.pallas_call(
        functools.partial(pack_kernel, scores, values),
        grid_spec=pltpu.PrefetchScalarGridSpec(
            num_scalar_prefetch=1,
            grid=(1,),
            in_specs=in_specs,
            out_specs=pl.BlockSpec((rows, width), lambda g, m: (0, 0)),
        ),
        out_shape=jax.ShapeDtypeStruct((rows, width), jnp.bfloat16),
        compiler_params=pltpu.CompilerParams(vmem_limit_bytes=VMEM_LIMIT),
        cost_estimate=pl.CostEstimate(
            flops=2 * rows * lat * len(values) * HD, bytes_accessed=rows * width * 4, transcendentals=0
        ),
        name="pack",
    )(*operands)


def attend_kernel(seq_count, heads, near_piece, far_pieces, lat, order, last, later, frames_ref, factor_ref, me_ref, *refs):
    half = seq_count // 2
    count = len(heads)
    near_refs, refs = refs[:half], refs[half:]
    far_refs, refs = refs[: half * len(far_pieces)], refs[half * len(far_pieces) :]
    earlier = refs[0] if later else None
    out_refs = refs[-4:-2] if last else refs[-3:-2]
    asked, folded = refs[-2:]
    me = me_ref[0]
    rows = near_refs[0].shape[0]

    def sources(k):
        if k < half:
            return [(near_refs[k], near_piece)]
        return [(far_refs[c * half + k - half], piece) for c, piece in enumerate(far_pieces)]

    def cell(k, h, what):
        for ref, (scores, _, _) in sources(k):
            if h in scores:
                column = scores[h] + what * HD
                return ref[:, column : column + HD]

    def value(k, h):
        for ref, (_, values, _) in sources(k):
            if h in values:
                row, column = values[h]
                return ref[row : row + lat, column : column + HD]

    spans = frames_ref.shape[0]
    log2_scale = math.log2(math.e) / math.sqrt(HD)
    reversed_bits = seq_count.bit_length() - 1
    block = 2 * rows

    end = frames_ref[0] * FRAME_TOK
    ends = [end]
    for c in range(1, spans):
        end = end + frames_ref[c] * FRAME_TOK
        ends.append(end)
    column_places = lax.broadcasted_iota(jnp.int32, (1, rows), 1)
    for n, k in enumerate(order):
        for i, h in enumerate(heads):
            asked[n, i] = cell(k, h, 0)
    for i, h in enumerate(heads):
        for k in range(seq_count):
            folded[i, :lat, k * rows : (k + 1) * rows] = value(k, h)
        folded[i, lat:] = jnp.ones_like(folded[i, lat:])

    def place_of(n):
        k = jnp.int32(0)
        for bit in range(reversed_bits):
            k = k | (((n >> bit) & 1) << (reversed_bits - 1 - bit))
        return me ^ k

    tile = 2 * rows
    tiles = seq_count // 2

    def bounds_of(b):
        places = jnp.concatenate([place_of(b * 2 + j) * rows + column_places for j in range(2)], axis=1)
        bound = jnp.full((1, block), ends[0], jnp.int32)
        for c in range(1, spans):
            bound = jnp.where(places >= ends[c - 1], ends[c], bound)
        return [
            jnp.where((me ^ k) * rows + start < bound, 0.0, -jnp.inf)
            for k in range(seq_count)
            for start in range(0, rows, FRAME_TOK)
        ]

    def score_tile(b, i, t):
        queries = asked[pl.ds(b * 2, 2), i].reshape(block, HD)
        keys = jnp.concatenate([cell(2 * t + j, heads[i], 1) for j in range(2)], axis=0)
        scores = lax.dot_general(keys, queries, NT, preferred_element_type=jnp.float32)
        return [scores[start : start + FRAME_TOK] for start in range(0, tile, FRAME_TOK)]

    def finish(b, total):
        for j in range(2):
            part = total[:, j * rows : (j + 1) * rows]
            n = b * 2 + j
            if earlier is not None:
                part = part + earlier[n]
            if last:
                part = part * factor_ref[0]

                @pl.when(n < half)
                def _():
                    out_refs[0][n] = part

                @pl.when(n >= half)
                def _():
                    out_refs[1][n - half] = part.astype(jnp.bfloat16)
            else:
                out_refs[0][n] = part

    def units(work):
        biases = {}
        frames = [score_tile(*work[0], t) for t in range(tiles)]
        total = None
        for u, (b, i) in enumerate(work):
            if i == 0:
                biases = bounds_of(b)
            each = len(frames[0])
            flat = [f for t in frames for f in t]
            peaks = [jnp.max(f, axis=0, keepdims=True) + shift for f, shift in zip(flat, biases)]
            peak = functools.reduce(jnp.maximum, peaks)
            following, summed = [], None
            for t in range(tiles):
                if u + 1 < len(work):
                    following.append(score_tile(*work[u + 1], t))
                weights = [
                    jnp.exp2((f + (shift - peak)) * log2_scale).astype(jnp.bfloat16)
                    for f, shift in zip(frames[t], biases[t * each : (t + 1) * each])
                ]
                part = jnp.dot(
                    folded[i, :, t * tile : (t + 1) * tile],
                    jnp.concatenate(weights, axis=0),
                    preferred_element_type=jnp.float32,
                )
                summed = part if summed is None else summed + part
            part = summed[:lat] / summed[lat : lat + 1]
            total = part if i == 0 else total + part
            if i == count - 1:
                finish(b, total)
            frames = following

    together = min(half, 4 if count == 1 else 1)

    def some_blocks(b, carry):
        units([(b * together + j, i) for j in range(together) for i in range(count)])
        return carry

    lax.fori_loop(0, half // together, some_blocks, 0)


def attend(near, far, earlier, after, span_frames, factor, me, heads, near_piece, far_pieces, lat, order, last):
    half = len(near)
    rows = near[0].shape[0]
    seq_count = 2 * half
    tokens = seq_count * rows
    count = len(heads)
    smem = pl.BlockSpec(memory_space=pltpu.SMEM)
    vmem = pl.BlockSpec(memory_space=pltpu.VMEM)
    operands = [span_frames, factor, me] + list(near) + [p for pieces in far for p in pieces]
    if earlier is not None:
        operands += [earlier]
    in_specs = [smem] * 3 + [vmem] * (len(operands) - 3)
    for array in after:
        operands += [array]
        in_specs += [pl.BlockSpec(memory_space=pl.ANY)]
    if last:
        out_shape = [
            jax.ShapeDtypeStruct((seq_count // 2, lat, rows), jnp.float32),
            jax.ShapeDtypeStruct((seq_count // 2, lat, rows), jnp.bfloat16),
        ]
    else:
        out_shape = [jax.ShapeDtypeStruct((seq_count, lat, rows), jnp.float32)]
    return pl.pallas_call(
        functools.partial(
            attend_kernel, seq_count, heads, near_piece, far_pieces, lat, order, last, earlier is not None
        ),
        in_specs=in_specs,
        out_specs=[vmem] * len(out_shape),
        out_shape=out_shape,
        scratch_shapes=[
            pltpu.VMEM((seq_count, count, rows, HD), jnp.bfloat16),
            pltpu.VMEM((count, lat + 16, tokens), jnp.bfloat16),
        ],
        compiler_params=pltpu.CompilerParams(vmem_limit_bytes=ATTEND_VMEM if seq_count <= 8 else WHOLE_VMEM),
        cost_estimate=pl.CostEstimate(
            flops=count * tokens * tokens * 2 * (HD + lat),
            bytes_accessed=tokens * count * 3 * HD * 2,
            transcendentals=count * tokens * tokens,
        ),
        name="attend",
    )(*operands)


def swap(array, axis, offset):
    size = lax.axis_size(axis)
    return lax.ppermute(array, axis, [(i, i ^ offset) for i in range(size)])


def body(qkv, readout, step_weight, timestep, span_frames):
    seq_count = lax.axis_size("seq")
    mp_count = lax.axis_size("mp")
    heads_local = HEADS // seq_count
    lat = readout.shape[2]
    me = lax.axis_index("seq").astype(jnp.int32)
    mp_index = lax.axis_index("mp")
    sample_count = mp_count // 2
    model_index = (mp_index // sample_count).astype(jnp.int32)
    sample_index = mp_index % sample_count
    signed = jnp.where(model_index == 1, 1.0, -1.0).astype(jnp.float32)
    factor = (signed * step_weight[timestep[sample_index]]).reshape(1)
    readout_t = jnp.swapaxes(readout, 1, 2)
    place = jnp.stack([me, model_index])
    bits = seq_count.bit_length() - 1
    order = [sum(((n >> b) & 1) << (bits - 1 - b) for b in range(bits)) for n in range(seq_count)]
    half = seq_count // 2
    every = list(range(heads_local))
    chunks = [[0,1,2],[3]] if heads_local > 1 else [[0]]
    near_piece = layout(every, every, lat)
    far_pieces = [layout(heads, every if c == 0 else [], lat) for c, heads in enumerate(chunks)]

    def send(k, piece, after):
        packed = pack(place, qkv, readout_t, k, heads_local, piece, after)
        return packed, (swap(packed, "seq", k) if k else packed)

    far = [[None] * half for _ in chunks]
    near = [None] * half
    holds = [[] for _ in chunks]
    def far_send(c, n, after):
        k = seq_count - 1 - n
        packed, far[c][k - half] = send(k, far_pieces[c], after)
        if c:
            holds[c - 1].append(packed)

    for n in range(half):
        far_send(0, n, far[0][half + 1 - n] if n > 1 else None)
    for k in range(half):
        _, near[k] = send(k, near_piece, None)
    for c in range(1, len(chunks)):
        for n in range(half):
            far_send(c, n, near[1 + n] if n < 2 and c == 1 else far[c - 1][half - 1 - n])

    result = None
    for c, heads in enumerate(chunks):
        last = c == len(chunks) - 1
        result = attend(
            near, far[: c + 1], result, holds[c], span_frames, factor, me.reshape(1),
            heads, near_piece, far_pieces[: c + 1], lat, order, last,
        )
        if not last:
            result = result[0]
    keep, give = result
    keep = keep + swap(give, "seq", 1).astype(jnp.float32)
    offset = 2
    while offset < seq_count:
        radix = min(4, seq_count // offset)
        size = keep.shape[0] // radix
        parts = [keep[n * size : (n + 1) * size] for n in range(radix)]
        keep = parts[0]
        for n in range(radix - 1, 0, -1):
            bits_n = (n >> 1) | ((n & 1) << 1) if radix == 4 else n
            keep = keep + swap(parts[n], "seq", offset * bits_n)
        offset *= radix
    whole = keep[0]
    offset = 1
    while offset < mp_count:
        radix = min(4, mp_count // offset)
        own = whole
        for n in range(radix - 1, 0, -1):
            whole = whole + swap(own, "mp", offset * n)
        offset *= radix
    return whole.T


def solution(mesh):
    return jax.shard_map(
        body,
        mesh=mesh,
        in_specs=(P("mp", "seq", None), P(), P(), P(), P()),
        out_specs=P("seq", None),
        check_vma=False,
    )
```

```python
import functools
import math

import jax
import jax.numpy as jnp
from jax import lax
from jax.experimental import pallas as pl
from jax.experimental.pallas import tpu as pltpu
from jax.sharding import PartitionSpec as P

HEADS = 32
HD = 128
FRAME_TOK = 64
NT = (((1,), (1,)), ((), ()))
LOG2_SCALE = math.log2(math.e) / math.sqrt(HD)
LOWEST = -1e30
SECOND_WAVE = 3000000000
PACK_VMEM = 8 * 1024 * 1024
ATTEND_VMEM = 20 * 1024 * 1024
WHOLE_VMEM = 60 * 1024 * 1024
SMEM = pl.BlockSpec(memory_space=pltpu.SMEM)
VMEM = pl.BlockSpec(memory_space=pltpu.VMEM)
ANYWHERE = pl.BlockSpec(memory_space=pl.ANY)


def fold(readout, values):
    return lax.dot_general(readout, values, NT, preferred_element_type=jnp.float32).astype(jnp.bfloat16)


def value_place(h, count, lat):
    return (h * lat) % HD, count * 2 * HD + (h * lat // HD) * HD


def pack_near_kernel(split, place_ref, qkv_ref, readout_ref, whole_qkv_ref, whole_readout_ref, *refs):
    out_ref = refs[-1]
    lat = readout_ref.shape[1]
    for h in range(split + 1):
        source, rows, base = (qkv_ref, readout_ref, h) if h < split else (whole_qkv_ref, whole_readout_ref, 0)
        out_ref[:, h * 2 * HD : (h + 1) * 2 * HD] = source[0, :, base * 3 * HD : base * 3 * HD + 2 * HD]
        row, column = value_place(h, split + 1, lat)
        out_ref[row : row + lat, column : column + HD] = fold(
            rows[0, :, base * HD : (base + 1) * HD], source[0, :, base * 3 * HD + 2 * HD : (base + 1) * 3 * HD]
        )


def pack_far_kernel(count, place_ref, qkv_ref, *refs):
    for h in range(count):
        refs[-1][:, h * HD : (h + 1) * HD] = qkv_ref[0, :, h * 3 * HD : h * 3 * HD + HD]


def pack_whole_kernel(place_ref, qkv_ref, readout_ref, *refs):
    out_ref = refs[-1]
    rows = qkv_ref.shape[1]
    lat = readout_ref.shape[1]
    out_ref[:rows] = qkv_ref[0, :, : 2 * HD]
    folded = fold(readout_ref[0], qkv_ref[0, :, 2 * HD :])
    out_ref[rows:, :HD] = folded[: lat // 2]
    out_ref[rows:, HD:] = folded[lat // 2 :]


def pack(kind, place, qkv, readout_t, k, half, pair_heads, split, after):
    rows = qkv.shape[1]
    lat = readout_t.shape[1]

    def pair(m):
        return (m[0] ^ k) & (half - 1)

    def whole(m):
        return pair(m) * pair_heads + split + (m[0] ^ k) // half

    slab = pl.BlockSpec((1, rows, pair_heads * 3 * HD), lambda g, m: (0, 0, pair(m)))
    whole_specs = [
        pl.BlockSpec((1, rows, 3 * HD), lambda g, m: (0, 0, whole(m))),
        pl.BlockSpec((1, lat, HD), lambda g, m: (m[1], 0, whole(m))),
    ]
    if kind == "near":
        kernel = functools.partial(pack_near_kernel, split)
        shape = (rows, (split + 1) * 2 * HD + -(-(split + 1) * lat // HD) * HD)
        in_specs = [slab, pl.BlockSpec((1, lat, pair_heads * HD), lambda g, m: (m[1], 0, pair(m)))] + whole_specs
    elif kind == "far":
        kernel = functools.partial(pack_far_kernel, split)
        shape = (rows, split * HD)
        in_specs = [slab]
    else:
        kernel = pack_whole_kernel
        shape = (rows + lat // 2, 2 * HD)
        in_specs = whole_specs
    operands = [place] + ([qkv, readout_t] * 2)[: len(in_specs)]
    if after is not None:
        operands += [after]
        in_specs += [ANYWHERE]
    return pl.pallas_call(
        kernel,
        grid_spec=pltpu.PrefetchScalarGridSpec(
            num_scalar_prefetch=1,
            grid=(1,),
            in_specs=in_specs,
            out_specs=pl.BlockSpec(shape, lambda g, m: (0, 0)),
        ),
        out_shape=jax.ShapeDtypeStruct(shape, jnp.bfloat16),
        compiler_params=pltpu.CompilerParams(vmem_limit_bytes=PACK_VMEM),
        cost_estimate=pl.CostEstimate(
            flops=SECOND_WAVE if kind == "far" and after is not None else 0,
            bytes_accessed=shape[0] * shape[1] * 4,
            transcendentals=0,
        ),
        name="pack",
    )(*operands)


def place_of(me, n, bits):
    k = jnp.int32(0)
    for bit in range(bits):
        k = k | (((n >> bit) & 1) << (bits - 1 - bit))
    return me ^ k


def mask_rows(frames_ref, me, rows, bits, key_count, b):
    columns = lax.broadcasted_iota(jnp.int32, (1, rows), 1)
    places = jnp.concatenate([place_of(me, b * 2 + j, bits) * rows + columns for j in range(2)], axis=1)
    end = frames_ref[0] * FRAME_TOK
    bound = jnp.full((1, 2 * rows), end, jnp.int32)
    for c in range(1, frames_ref.shape[0]):
        later = end + frames_ref[c] * FRAME_TOK
        bound = jnp.where(places >= end, later, bound)
        end = later
    return [
        jnp.where((me ^ k) * rows + start < bound, 0.0, -jnp.inf)
        for k in range(key_count)
        for start in range(0, rows, FRAME_TOK)
    ]


def run_units(work, tiles, tile, score_tile, masks, folded, finish):
    lat = folded.shape[1] - 16
    frames = [score_tile(*work[0], t) for t in range(tiles)]
    shifts = None
    for u, (b, i) in enumerate(work):
        if u == 0 or b is not work[u - 1][0]:
            shifts = masks(b)
        each = len(frames[0])
        peaks = [jnp.max(f, axis=0, keepdims=True) + s for f, s in zip(sum(frames, []), shifts)]
        peak = jnp.maximum(functools.reduce(jnp.maximum, peaks), LOWEST)
        following, summed = [], None
        for t in range(tiles):
            if u + 1 < len(work):
                following.append(score_tile(*work[u + 1], t))
            weights = [
                jnp.exp2((f + (s - peak)) * LOG2_SCALE).astype(jnp.bfloat16)
                for f, s in zip(frames[t], shifts[t * each : (t + 1) * each])
            ]
            part = jnp.dot(
                folded[i, :, t * tile : (t + 1) * tile],
                jnp.concatenate(weights, axis=0),
                preferred_element_type=jnp.float32,
            )
            summed = part if summed is None else summed + part
        finish(b, i, summed[:lat], summed[lat : lat + 1], peak)
        frames = following


def score_tiles(asked, keys_of, rows):
    def score_tile(b, i, t):
        queries = asked[pl.ds(b * 2, 2), i].reshape(2 * rows, HD)
        keys = jnp.concatenate([keys_of(2 * t + j, i) for j in range(2)], axis=0)
        scores = lax.dot_general(keys, queries, NT, preferred_element_type=jnp.float32)
        return [scores[start : start + FRAME_TOK] for start in range(0, 2 * rows, FRAME_TOK)]

    return score_tile


def split_kernel(seq_count, count, order, frames_ref, me_ref, *refs):
    half = seq_count // 2
    near_refs, far_refs = refs[:half], refs[half:seq_count]
    sums_ref, stats_ref, asked, folded = refs[-4:]
    me = me_ref[0]
    rows = near_refs[0].shape[0]
    lat = sums_ref.shape[2]
    bits = seq_count.bit_length() - 1
    for n, k in enumerate(order):
        for i in range(count):
            if k < half:
                asked[n, i] = near_refs[k][:, i * 2 * HD : i * 2 * HD + HD]
            else:
                asked[n, i] = far_refs[k - half][:, i * HD : (i + 1) * HD]
    for i in range(count):
        row, column = value_place(i, count + 1, lat)
        for k in range(half):
            folded[i, :lat, k * rows : (k + 1) * rows] = near_refs[k][row : row + lat, column : column + HD]
        folded[i, lat:] = jnp.ones_like(folded[i, lat:])

    def keys_of(k, i):
        return near_refs[k][:, i * 2 * HD + HD : (i + 1) * 2 * HD]

    def some_blocks(b, carry):
        peaks, totals = [], []

        def finish(b, i, summed, total, peak):
            sums_ref[b, i] = summed
            peaks.append(peak)
            totals.append(total)

        work = [(b, i) for i in range(count)]
        run_units(
            work, half // 2, 2 * rows, score_tiles(asked, keys_of, rows),
            lambda b: mask_rows(frames_ref, me, rows, bits, half, b), folded, finish,
        )
        rest = [jnp.ones_like(peaks[0])] * (stats_ref.shape[2] - count)
        stats_ref[b, 0] = jnp.concatenate(peaks + rest, axis=0)
        stats_ref[b, 1] = jnp.concatenate(totals + rest, axis=0)
        return carry

    lax.fori_loop(0, half, some_blocks, 0)


def attend_split(near, far, after, span_frames, me, count, lat, order):
    half = len(near)
    rows = near[0].shape[0]
    seq_count = 2 * half
    tokens = seq_count * rows
    padded = -(-count // 8) * 8
    return pl.pallas_call(
        functools.partial(split_kernel, seq_count, count, order),
        in_specs=[SMEM, SMEM] + [VMEM] * seq_count + [ANYWHERE] * len(after),
        out_specs=[VMEM, VMEM],
        out_shape=[
            jax.ShapeDtypeStruct((half, count, lat, 2 * rows), jnp.float32),
            jax.ShapeDtypeStruct((half, 2, padded, 2 * rows), jnp.float32),
        ],
        scratch_shapes=[
            pltpu.VMEM((seq_count, count, rows, HD), jnp.bfloat16),
            pltpu.VMEM((count, lat + 16, half * rows), jnp.bfloat16),
        ],
        compiler_params=pltpu.CompilerParams(vmem_limit_bytes=ATTEND_VMEM),
        cost_estimate=pl.CostEstimate(
            flops=0, bytes_accessed=tokens * count * 3 * HD * 2, transcendentals=0
        ),
        name="attend_split",
    )(span_frames, me, *near, *far, *after)


def combine_kernel(count, sums_ref, stats_ref, other_ref, out_ref):
    rows = out_ref.shape[2]

    def one_block(b, carry):
        peak, total = stats_ref[b, 0], stats_ref[b, 1]
        swapped = [jnp.concatenate([other_ref[b, w, :, rows:], other_ref[b, w, :, :rows]], axis=1) for w in range(2)]
        highest = jnp.maximum(peak, swapped[0])
        own = jnp.exp2((peak - highest) * LOG2_SCALE)
        both = total * own + swapped[1] * jnp.exp2((swapped[0] - highest) * LOG2_SCALE)
        weight = own / both
        result = sums_ref[b, 0] * weight[:1]
        for i in range(1, count):
            result = result + sums_ref[b, i] * weight[i : i + 1]
        for j in range(2):
            out_ref[b * 2 + j] = result[:, j * rows : (j + 1) * rows]
        return carry

    lax.fori_loop(0, sums_ref.shape[0], one_block, 0)


def combine(sums, stats, other):
    half, count, lat, block = sums.shape
    return pl.pallas_call(
        functools.partial(combine_kernel, count),
        in_specs=[VMEM] * 3,
        out_specs=VMEM,
        out_shape=jax.ShapeDtypeStruct((2 * half, lat, block // 2), jnp.float32),
        compiler_params=pltpu.CompilerParams(vmem_limit_bytes=PACK_VMEM),
        cost_estimate=pl.CostEstimate(flops=0, bytes_accessed=sums.size * 4, transcendentals=0),
        name="combine",
    )(sums, stats, other)


def whole_kernel(seq_count, split, order, frames_ref, factor_ref, me_ref, *refs):
    half = seq_count // 2
    pieces = refs[:seq_count]
    earlier = refs[seq_count] if len(refs) > seq_count + 4 else None
    keep_ref, give_ref, asked, folded = refs[-4:]
    me = me_ref[0]
    rows = keep_ref.shape[2]
    lat = keep_ref.shape[1]
    bits = seq_count.bit_length() - 1
    start = split * 2 * HD

    def cell(k, what):
        column = what * HD + (start if k < half else 0)
        return pieces[k][:rows, column : column + HD]

    for n, k in enumerate(order):
        asked[n, 0] = cell(k, 0)
    for k in range(seq_count):
        if k < half:
            row, column = value_place(split, split + 1, lat)
            folded[0, :lat, k * rows : (k + 1) * rows] = pieces[k][row : row + lat, column : column + HD]
        else:
            folded[0, : lat // 2, k * rows : (k + 1) * rows] = pieces[k][rows:, :HD]
            folded[0, lat // 2 : lat, k * rows : (k + 1) * rows] = pieces[k][rows:, HD:]
    folded[0, lat:] = jnp.ones_like(folded[0, lat:])

    def finish(b, i, summed, total, peak):
        result = summed / total
        for j in range(2):
            part = result[:, j * rows : (j + 1) * rows]
            n = b * 2 + j
            if earlier is not None:
                part = part + earlier[n]
            part = part * factor_ref[0]

            @pl.when(n < half)
            def _():
                keep_ref[n] = part

            @pl.when(n >= half)
            def _():
                give_ref[n - half] = part.astype(jnp.bfloat16)

    together = min(half, 4)

    def some_blocks(b, carry):
        run_units(
            [(b * together + j, 0) for j in range(together)], half, 2 * rows,
            score_tiles(asked, lambda k, i: cell(k, 1), rows),
            lambda b: mask_rows(frames_ref, me, rows, bits, seq_count, b), folded, finish,
        )
        return carry

    lax.fori_loop(0, half // together, some_blocks, 0)


def attend_whole(pieces, earlier, span_frames, factor, me, split, rows, lat, order):
    seq_count = len(pieces)
    tokens = seq_count * rows
    operands = [span_frames, factor, me] + list(pieces) + ([] if earlier is None else [earlier])
    return pl.pallas_call(
        functools.partial(whole_kernel, seq_count, split, order),
        in_specs=[SMEM] * 3 + [VMEM] * (len(operands) - 3),
        out_specs=[VMEM, VMEM],
        out_shape=[
            jax.ShapeDtypeStruct((seq_count // 2, lat, rows), jnp.float32),
            jax.ShapeDtypeStruct((seq_count // 2, lat, rows), jnp.bfloat16),
        ],
        scratch_shapes=[
            pltpu.VMEM((seq_count, 1, rows, HD), jnp.bfloat16),
            pltpu.VMEM((1, lat + 16, tokens), jnp.bfloat16),
        ],
        compiler_params=pltpu.CompilerParams(vmem_limit_bytes=ATTEND_VMEM if seq_count <= 8 else WHOLE_VMEM),
        cost_estimate=pl.CostEstimate(
            flops=tokens * tokens * 2 * (HD + lat),
            bytes_accessed=tokens * 3 * HD * 2,
            transcendentals=tokens * tokens,
        ),
        name="attend_whole",
    )(*operands)


def swap(array, axis, offset):
    size = lax.axis_size(axis)
    return lax.ppermute(array, axis, [(i, i ^ offset) for i in range(size)])


def body(qkv, readout, step_weight, timestep, span_frames):
    seq_count = lax.axis_size("seq")
    mp_count = lax.axis_size("mp")
    half = seq_count // 2
    pair_heads = 2 * HEADS // seq_count
    split = pair_heads - 2
    rows = qkv.shape[1]
    lat = readout.shape[2]
    me = lax.axis_index("seq").astype(jnp.int32)
    mp_index = lax.axis_index("mp")
    sample_count = mp_count // 2
    model_index = (mp_index // sample_count).astype(jnp.int32)
    sample_index = mp_index % sample_count
    signed = jnp.where(model_index == 1, 1.0, -1.0).astype(jnp.float32)
    factor = (signed * step_weight[timestep[sample_index]]).reshape(1)
    readout_t = jnp.swapaxes(readout, 1, 2)
    place = jnp.stack([me, model_index])
    bits = seq_count.bit_length() - 1
    order = [sum(((n >> b) & 1) << (bits - 1 - b) for b in range(bits)) for n in range(seq_count)]

    def send(kind, k, after=None):
        packed = pack(kind, place, qkv, readout_t, k, half, pair_heads, split, after)
        return packed, (swap(packed, "seq", k) if k else packed)

    near, far, whole, holds = [None] * half, [None] * half, [None] * half, []
    for n in range(half):
        k = seq_count - 1 - n
        if split:
            _, far[k - half] = send("far", k, far[k - half + 2] if n > 1 else None)
    for k in range(half):
        _, near[k] = send("near", k)
    for n in range(half):
        k = seq_count - 1 - n
        packed, whole[k - half] = send("whole", k, far[k - half] if split else None)
        holds.append(packed)
    earlier = None
    if split:
        sums, stats = attend_split(near, far, holds, span_frames, me.reshape(1), split, lat, order)
        earlier = combine(sums, stats, swap(stats, "seq", half))
    keep, give = attend_whole(near + whole, earlier, span_frames, factor, me.reshape(1), split, rows, lat, order)

    keep = keep + swap(give, "seq", 1).astype(jnp.float32)
    offset = 2
    while offset < seq_count:
        radix = min(4, seq_count // offset)
        size = keep.shape[0] // radix
        parts = [keep[n * size : (n + 1) * size] for n in range(radix)]
        keep = parts[0]
        for n in range(radix - 1, 0, -1):
            bits_n = (n >> 1) | ((n & 1) << 1) if radix == 4 else n
            keep = keep + swap(parts[n], "seq", offset * bits_n)
        offset *= radix
    total = keep[0]
    offset = 1
    while offset < mp_count:
        radix = min(4, mp_count // offset)
        own = total
        for n in range(radix - 1, 0, -1):
            total = total + swap(own, "mp", offset * n)
        offset *= radix
    return total.T


def solution(mesh):
    return jax.shard_map(
        body,
        mesh=mesh,
        in_specs=(P("mp", "seq", None), P(), P(), P(), P()),
        out_specs=P("seq", None),
        check_vma=False,
    )
```

```python
import functools
import math

import jax
import jax.numpy as jnp
from jax import lax
from jax.experimental import pallas as pl
from jax.experimental.pallas import tpu as pltpu
from jax.sharding import PartitionSpec as P

HEADS = 32
HD = 128
FRAME_TOK = 64
NT = (((1,), (1,)), ((), ()))
LOG2_SCALE = math.log2(math.e) / math.sqrt(HD)
LOWEST = -1e30
PACK_VMEM = 8 * 1024 * 1024
ATTEND_VMEM = 20 * 1024 * 1024
WHOLE_VMEM = 60 * 1024 * 1024
SMEM = pl.BlockSpec(memory_space=pltpu.SMEM)
VMEM = pl.BlockSpec(memory_space=pltpu.VMEM)
ANYWHERE = pl.BlockSpec(memory_space=pl.ANY)


def fold(readout, values):
    return lax.dot_general(readout, values, NT, preferred_element_type=jnp.float32).astype(jnp.bfloat16)


def value_place(h, count, lat):
    return (h * lat) % HD, count * 2 * HD + (h * lat // HD) * HD


def pack_kernel(place_ref, qkv_ref, readout_ref, *refs):
    out_ref = refs[-1]
    lat = readout_ref.shape[1]
    count = readout_ref.shape[2] // HD
    for h in range(count):
        base = h * 3 * HD
        out_ref[:, h * 2 * HD : (h + 1) * 2 * HD] = qkv_ref[0, :, base : base + 2 * HD]
        row, column = value_place(h, count, lat)
        out_ref[row : row + lat, column : column + HD] = fold(
            readout_ref[0, :, h * HD : (h + 1) * HD], qkv_ref[0, :, base + 2 * HD : base + 3 * HD]
        )


def pack(place, qkv, readout_t, k, count, after):
    rows = qkv.shape[1]
    lat = readout_t.shape[1]
    width = count * 2 * HD + -(-count * lat // HD) * HD
    operands = [place, qkv, readout_t]
    in_specs = [
        pl.BlockSpec((1, rows, count * 3 * HD), lambda g, m: (0, 0, m[0] ^ k)),
        pl.BlockSpec((1, lat, count * HD), lambda g, m: (m[1], 0, m[0] ^ k)),
    ]
    if after is not None:
        operands += [after]
        in_specs += [ANYWHERE]
    return pl.pallas_call(
        pack_kernel,
        grid_spec=pltpu.PrefetchScalarGridSpec(
            num_scalar_prefetch=1,
            grid=(1,),
            in_specs=in_specs,
            out_specs=pl.BlockSpec((rows, width), lambda g, m: (0, 0)),
        ),
        out_shape=jax.ShapeDtypeStruct((rows, width), jnp.bfloat16),
        compiler_params=pltpu.CompilerParams(vmem_limit_bytes=PACK_VMEM),
        cost_estimate=pl.CostEstimate(flops=0, bytes_accessed=rows * width * 4, transcendentals=0),
        name="pack",
    )(*operands)


def mask_rows(frames_ref, me, rows, query_offsets, key_offsets):
    columns = lax.broadcasted_iota(jnp.int32, (1, rows), 1)
    places = jnp.concatenate([(me ^ k) * rows + columns for k in query_offsets], axis=1)
    end = frames_ref[0] * FRAME_TOK
    bound = jnp.full(places.shape, end, jnp.int32)
    for c in range(1, frames_ref.shape[0]):
        later = end + frames_ref[c] * FRAME_TOK
        bound = jnp.where(places >= end, later, bound)
        end = later
    return [
        jnp.where((me ^ k) * rows + start < bound, 0.0, -jnp.inf)
        for k in key_offsets
        for start in range(0, rows, FRAME_TOK)
    ]


def run_units(units, lat):
    frames = [tile() for tile in units[0][0]]
    for u, (_, values, shifts, finish) in enumerate(units):
        ahead = list(units[u + 1][0]) if u + 1 < len(units) else []
        peaks = [jnp.max(f, axis=0, keepdims=True) + s for f, s in zip(sum(frames, []), shifts)]
        peak = jnp.maximum(functools.reduce(jnp.maximum, peaks), LOWEST)
        following, summed, start = [], None, 0
        for t, tile in enumerate(frames):
            for _ in range(-(-(len(ahead) - len(following)) // (len(frames) - t))):
                following.append(ahead[len(following)]())
            weights = [
                jnp.exp2((f + (s - peak)) * LOG2_SCALE).astype(jnp.bfloat16)
                for f, s in zip(tile, shifts[start : start + len(tile)])
            ]
            start += len(tile)
            part = jnp.dot(values[t](), jnp.concatenate(weights, axis=0), preferred_element_type=jnp.float32)
            summed = part if summed is None else summed + part
        finish(summed[:lat], summed[lat : lat + 1], peak)
        frames = following


def score_tile(keys, queries):
    scores = lax.dot_general(keys(), queries(), NT, preferred_element_type=jnp.float32)
    return [scores[start : start + FRAME_TOK] for start in range(0, scores.shape[0], FRAME_TOK)]


def stage_values(folded, pieces, lat):
    count = folded.shape[0]
    rows = pieces[0].shape[0]
    for i in range(count):
        row, column = value_place(i, count, lat)
        for n, piece in enumerate(pieces):
            folded[i, :lat, n * rows : (n + 1) * rows] = piece[row : row + lat, column : column + HD]
        folded[i, lat:] = jnp.ones_like(folded[i, lat:])


def pairs_of(pieces, i, what):
    column = (2 * i + what) * HD

    def read(n):
        return lambda: jnp.concatenate([pieces[n][:, column : column + HD], pieces[n + 1][:, column : column + HD]], axis=0)

    return [read(n) for n in range(0, len(pieces), 2)]


def early_kernel(offsets, frames_ref, factor_ref, me_ref, *refs):
    count_pieces = len(offsets)
    pieces = refs[:count_pieces]
    sums_ref, stats_ref, asked, folded = refs[-4:]
    me = me_ref[0]
    rows = pieces[0].shape[0]
    lat = sums_ref.shape[2]
    count = folded.shape[0]
    blocks = count_pieces // 2
    stage_values(folded, pieces, lat)
    for i in range(count):
        for b, read in enumerate(pairs_of(pieces, i, 0)):
            asked[b, i] = read()
    half = count_pieces // 2 + 1

    def some_blocks(b, carry):
        q = [2 * b, 2 * b + 1]
        shifts = mask_rows(frames_ref, me, rows, [jnp.where(n < half, n, n + 2) for n in q], offsets)
        peaks, totals, units = [], [], []
        for i in range(count):

            def finish(summed, total, peak, i=i):
                sums_ref[b, i] = summed
                peaks.append(peak)
                totals.append(total)

            tiles = [
                functools.partial(score_tile, keys, lambda i=i: asked[b, i]) for keys in pairs_of(pieces, i, 1)
            ]
            values = [lambda i=i, t=t: folded[i, :, t * 2 * rows : (t + 1) * 2 * rows] for t in range(blocks)]
            units.append((tiles, values, shifts, finish))
        run_units(units, lat)
        rest = [jnp.ones_like(peaks[0])] * (stats_ref.shape[2] - count)
        stats_ref[b, 0] = jnp.concatenate(peaks + rest, axis=0)
        stats_ref[b, 1] = jnp.concatenate(totals + rest, axis=0)
        return carry

    lax.fori_loop(0, blocks, some_blocks, 0)


def late_kernel(offsets, late, frames_ref, factor_ref, me_ref, *refs):
    early = len(offsets)
    pieces = refs[: early + 2]
    sums_ref, stats_ref, keep_ref, give_ref, folded = refs[early + 2 :]
    me = me_ref[0]
    half, lat, rows = keep_ref.shape
    bits = half.bit_length()
    count = folded.shape[0]
    stage_values(folded, pieces, lat)
    every = list(offsets) + list(late)
    results = {}

    def add(b, part):
        results[b] = part if b not in results else results[b] + part

    def write(b):
        for j in range(2):
            k = every[2 * b + j]
            n = sum(((k >> bit) & 1) << (bits - 1 - bit) for bit in range(bits))
            part = results[b][:, j * rows : (j + 1) * rows] * factor_ref[0]
            if n < half:
                keep_ref[n] = part
            else:
                give_ref[n - half] = part.astype(jnp.bfloat16)

    units = []
    blocks = early // 2
    for b in [blocks] + list(range(blocks)):
        keys_in = range(blocks + 1) if b == blocks else [blocks]
        key_offsets = [every[2 * t + j] for t in keys_in for j in range(2)]
        shifts = mask_rows(frames_ref, me, rows, every[2 * b : 2 * b + 2], key_offsets)
        for i in range(count):

            def finish(summed, total, peak, b=b, i=i):
                if b < blocks:
                    before = stats_ref[b, 0, i : i + 1]
                    highest = jnp.maximum(before, peak)
                    old = jnp.exp2((before - highest) * LOG2_SCALE)
                    new = jnp.exp2((peak - highest) * LOG2_SCALE)
                    both = stats_ref[b, 1, i : i + 1] * old + total * new
                    add(b, sums_ref[b, i] * (old / both) + summed * (new / both))
                else:
                    add(b, summed / total)
                if i == count - 1:
                    write(b)

            queries = pairs_of(pieces, i, 0)[b]
            keys = pairs_of(pieces, i, 1)
            tiles = [functools.partial(score_tile, keys[t], queries) for t in keys_in]
            values = [lambda i=i, t=t: folded[i, :, t * 2 * rows : (t + 1) * 2 * rows] for t in keys_in]
            units.append((tiles, values, shifts, finish))
    run_units(units, lat)


def attend_early(pieces, offsets, span_frames, factor, me, count, lat):
    rows = pieces[0].shape[0]
    blocks = len(pieces) // 2
    tokens = len(pieces) * rows
    return pl.pallas_call(
        functools.partial(early_kernel, offsets),
        in_specs=[SMEM] * 3 + [VMEM] * len(pieces),
        out_specs=[VMEM, VMEM],
        out_shape=[
            jax.ShapeDtypeStruct((blocks, count, lat, 2 * rows), jnp.float32),
            jax.ShapeDtypeStruct((blocks, 2, 8, 2 * rows), jnp.float32),
        ],
        scratch_shapes=[
            pltpu.VMEM((blocks, count, 2 * rows, HD), jnp.bfloat16),
            pltpu.VMEM((count, lat + 16, tokens), jnp.bfloat16),
        ],
        compiler_params=pltpu.CompilerParams(vmem_limit_bytes=ATTEND_VMEM if len(pieces) <= 8 else WHOLE_VMEM),
        cost_estimate=pl.CostEstimate(
            flops=count * tokens * tokens * 2 * (HD + lat),
            bytes_accessed=tokens * count * 3 * HD * 2,
            transcendentals=count * tokens * tokens,
        ),
        name="attend_early",
    )(span_frames, factor, me, *pieces)


def attend_late(pieces, offsets, late, sums, stats, span_frames, factor, me, count, lat):
    rows = pieces[0].shape[0]
    tokens = len(pieces) * rows
    half = len(pieces) // 2
    return pl.pallas_call(
        functools.partial(late_kernel, offsets, late),
        in_specs=[SMEM] * 3 + [VMEM] * (len(pieces) + 2),
        out_specs=[VMEM, VMEM],
        out_shape=[
            jax.ShapeDtypeStruct((half, lat, rows), jnp.float32),
            jax.ShapeDtypeStruct((half, lat, rows), jnp.bfloat16),
        ],
        scratch_shapes=[pltpu.VMEM((count, lat + 16, tokens), jnp.bfloat16)],
        compiler_params=pltpu.CompilerParams(vmem_limit_bytes=ATTEND_VMEM if len(pieces) <= 8 else WHOLE_VMEM),
        cost_estimate=pl.CostEstimate(
            flops=count * tokens * rows * 4 * (HD + lat),
            bytes_accessed=tokens * count * 3 * HD * 2,
            transcendentals=count * tokens * rows * 2,
        ),
        name="attend_late",
    )(span_frames, factor, me, *pieces, sums, stats)


def swap(array, axis, offset):
    size = lax.axis_size(axis)
    return lax.ppermute(array, axis, [(i, i ^ offset) for i in range(size)])


def body(qkv, readout, step_weight, timestep, span_frames):
    seq_count = lax.axis_size("seq")
    mp_count = lax.axis_size("mp")
    half = seq_count // 2
    count = HEADS // seq_count
    lat = readout.shape[2]
    me = lax.axis_index("seq").astype(jnp.int32)
    mp_index = lax.axis_index("mp")
    sample_count = mp_count // 2
    model_index = (mp_index // sample_count).astype(jnp.int32)
    sample_index = mp_index % sample_count
    signed = jnp.where(model_index == 1, 1.0, -1.0).astype(jnp.float32)
    factor = (signed * step_weight[timestep[sample_index]]).reshape(1)
    readout_t = jnp.swapaxes(readout, 1, 2)
    place = jnp.stack([me, model_index])

    pieces = [None] * seq_count
    for n in range(half):
        k = seq_count - 1 - n
        pieces[k] = swap(pack(place, qkv, readout_t, k, count, pieces[k + 2] if n > 1 else None), "seq", k)
    for k in range(half):
        packed = pack(place, qkv, readout_t, k, count, None)
        pieces[k] = swap(packed, "seq", k) if k else packed
    late = [half, half + 1]
    early = [k for k in range(seq_count) if k not in late]
    sums, stats = attend_early([pieces[k] for k in early], early, span_frames, factor, me.reshape(1), count, lat)
    keep, give = attend_late(
        [pieces[k] for k in early + late], early, late, sums, stats, span_frames, factor, me.reshape(1), count, lat
    )

    keep = keep + swap(give, "seq", 1).astype(jnp.float32)
    offset = 2
    while offset < seq_count:
        radix = min(4, seq_count // offset)
        size = keep.shape[0] // radix
        parts = [keep[n * size : (n + 1) * size] for n in range(radix)]
        keep = parts[0]
        for n in range(radix - 1, 0, -1):
            bits_n = (n >> 1) | ((n & 1) << 1) if radix == 4 else n
            keep = keep + swap(parts[n], "seq", offset * bits_n)
        offset *= radix
    total = keep[0]
    offset = 1
    while offset < mp_count:
        radix = min(4, mp_count // offset)
        own = total
        for n in range(radix - 1, 0, -1):
            total = total + swap(own, "mp", offset * n)
        offset *= radix
    return total.T


def solution(mesh):
    return jax.shard_map(
        body,
        mesh=mesh,
        in_specs=(P("mp", "seq", None), P(), P(), P(), P()),
        out_specs=P("seq", None),
        check_vma=False,
    )
```

```python
import functools
import math

import jax
import jax.numpy as jnp
from jax import lax
from jax.experimental import pallas as pl
from jax.experimental.pallas import tpu as pltpu
from jax.sharding import PartitionSpec as P

HEADS = 32
HD = 128
FRAME_TOK = 64
NT = (((1,), (1,)), ((), ()))
LOG2_SCALE = math.log2(math.e) / math.sqrt(HD)
LOWEST = -1e30
NEXT_WAVE = 5000000000
PACK_VMEM = 8 * 1024 * 1024
ATTEND_VMEM = 20 * 1024 * 1024
WHOLE_VMEM = 60 * 1024 * 1024
SMEM = pl.BlockSpec(memory_space=pltpu.SMEM)
VMEM = pl.BlockSpec(memory_space=pltpu.VMEM)
ANYWHERE = pl.BlockSpec(memory_space=pl.ANY)


def fold(readout, values):
    return lax.dot_general(readout, values, NT, preferred_element_type=jnp.float32).astype(jnp.bfloat16)


def value_place(h, count, lat):
    return (h * lat) % HD, count * 2 * HD + (h * lat // HD) * HD


def pack_kernel(place_ref, qkv_ref, readout_ref, *refs):
    out_ref = refs[-1]
    lat = readout_ref.shape[1]
    count = readout_ref.shape[2] // HD
    for h in range(count):
        base = h * 3 * HD
        out_ref[:, h * 2 * HD : (h + 1) * 2 * HD] = qkv_ref[0, :, base : base + 2 * HD]
        row, column = value_place(h, count, lat)
        out_ref[row : row + lat, column : column + HD] = fold(
            readout_ref[0, :, h * HD : (h + 1) * HD], qkv_ref[0, :, base + 2 * HD : base + 3 * HD]
        )


def pack(place, qkv, readout_t, k, count, after):
    rows = qkv.shape[1]
    lat = readout_t.shape[1]
    width = count * 2 * HD + -(-count * lat // HD) * HD
    operands = [place, qkv, readout_t]
    in_specs = [
        pl.BlockSpec((1, rows, count * 3 * HD), lambda g, m: (0, 0, m[0] ^ k)),
        pl.BlockSpec((1, lat, count * HD), lambda g, m: (m[1], 0, m[0] ^ k)),
    ]
    if after is not None:
        operands += [after]
        in_specs += [ANYWHERE]
    return pl.pallas_call(
        pack_kernel,
        grid_spec=pltpu.PrefetchScalarGridSpec(
            num_scalar_prefetch=1,
            grid=(1,),
            in_specs=in_specs,
            out_specs=pl.BlockSpec((rows, width), lambda g, m: (0, 0)),
        ),
        out_shape=jax.ShapeDtypeStruct((rows, width), jnp.bfloat16),
        compiler_params=pltpu.CompilerParams(vmem_limit_bytes=PACK_VMEM),
        cost_estimate=pl.CostEstimate(
            flops=NEXT_WAVE if after is not None and k >= 4 else 0, bytes_accessed=rows * width * 4, transcendentals=0
        ),
        name="pack",
    )(*operands)


def mask_rows(frames_ref, me, rows, query_offsets, key_offsets):
    columns = lax.broadcasted_iota(jnp.int32, (1, rows), 1)
    places = jnp.concatenate([(me ^ k) * rows + columns for k in query_offsets], axis=1)
    end = frames_ref[0] * FRAME_TOK
    bound = jnp.full(places.shape, end, jnp.int32)
    for c in range(1, frames_ref.shape[0]):
        later = end + frames_ref[c] * FRAME_TOK
        bound = jnp.where(places >= end, later, bound)
        end = later
    return [
        jnp.where((me ^ k) * rows + start < bound, 0.0, -jnp.inf)
        for k in key_offsets
        for start in range(0, rows, FRAME_TOK)
    ]


def run_units(units, lat):
    frames = [tile() for tile in units[0][0]]
    for u, (_, values, shifts, finish) in enumerate(units):
        ahead = list(units[u + 1][0]) if u + 1 < len(units) else []
        peaks = [jnp.max(f, axis=0, keepdims=True) + s for f, s in zip(sum(frames, []), shifts)]
        peak = jnp.maximum(functools.reduce(jnp.maximum, peaks), LOWEST)
        following, summed, start = [], None, 0
        for t, tile in enumerate(frames):
            for _ in range(-(-(len(ahead) - len(following)) // (len(frames) - t))):
                following.append(ahead[len(following)]())
            weights = [
                jnp.exp2((f + (s - peak)) * LOG2_SCALE).astype(jnp.bfloat16)
                for f, s in zip(tile, shifts[start : start + len(tile)])
            ]
            start += len(tile)
            part = jnp.dot(values[t](), jnp.concatenate(weights, axis=0), preferred_element_type=jnp.float32)
            summed = part if summed is None else summed + part
        finish(summed[:lat], summed[lat : lat + 1], peak)
        frames = following


def score_tile(keys, queries):
    scores = lax.dot_general(keys(), queries(), NT, preferred_element_type=jnp.float32)
    return [scores[start : start + FRAME_TOK] for start in range(0, scores.shape[0], FRAME_TOK)]


def stage_values(folded, pieces, lat):
    count = folded.shape[0]
    rows = pieces[0].shape[0]
    for i in range(count):
        row, column = value_place(i, count, lat)
        for n, piece in enumerate(pieces):
            folded[i, :lat, n * rows : (n + 1) * rows] = piece[row : row + lat, column : column + HD]
        folded[i, lat:] = jnp.ones_like(folded[i, lat:])


def pairs_of(pieces, i, what):
    column = (2 * i + what) * HD

    def read(n):
        return lambda: jnp.concatenate([pieces[n][:, column : column + HD], pieces[n + 1][:, column : column + HD]], axis=0)

    return [read(n) for n in range(0, len(pieces), 2)]


def early_kernel(offsets, frames_ref, factor_ref, me_ref, *refs):
    count_pieces = len(offsets)
    pieces = refs[:count_pieces]
    sums_ref, stats_ref, asked, folded = refs[-4:]
    me = me_ref[0]
    rows = pieces[0].shape[0]
    lat = sums_ref.shape[2]
    count = folded.shape[0]
    blocks = count_pieces // 2
    stage_values(folded, pieces, lat)
    for i in range(count):
        for b, read in enumerate(pairs_of(pieces, i, 0)):
            asked[b, i] = read()
    half = count_pieces // 2 + 1

    def some_blocks(b, carry):
        q = [2 * b, 2 * b + 1]
        shifts = mask_rows(frames_ref, me, rows, [jnp.where(n < half, n, n + 2) for n in q], offsets)
        peaks, totals, units = [], [], []
        for i in range(count):

            def finish(summed, total, peak, i=i):
                sums_ref[b, i] = summed
                peaks.append(peak)
                totals.append(total)

            tiles = [
                functools.partial(score_tile, keys, lambda i=i: asked[b, i]) for keys in pairs_of(pieces, i, 1)
            ]
            values = [lambda i=i, t=t: folded[i, :, t * 2 * rows : (t + 1) * 2 * rows] for t in range(blocks)]
            units.append((tiles, values, shifts, finish))
        run_units(units, lat)
        rest = [jnp.ones_like(peaks[0])] * (stats_ref.shape[2] - count)
        stats_ref[b, 0] = jnp.concatenate(peaks + rest, axis=0)
        stats_ref[b, 1] = jnp.concatenate(totals + rest, axis=0)
        return carry

    lax.fori_loop(0, blocks, some_blocks, 0)


def late_kernel(offsets, late, frames_ref, factor_ref, me_ref, *refs):
    early = len(offsets)
    pieces = refs[: early + 2]
    sums_ref, stats_ref, keep_ref, give_ref, folded = refs[early + 2 :]
    me = me_ref[0]
    half, lat, rows = keep_ref.shape
    bits = half.bit_length()
    count = folded.shape[0]
    stage_values(folded, pieces, lat)
    every = list(offsets) + list(late)
    results = {}

    def add(b, part):
        results[b] = part if b not in results else results[b] + part

    def write(b):
        for j in range(2):
            k = every[2 * b + j]
            n = sum(((k >> bit) & 1) << (bits - 1 - bit) for bit in range(bits))
            part = results[b][:, j * rows : (j + 1) * rows] * factor_ref[0]
            if n < half:
                keep_ref[n] = part
            else:
                give_ref[n - half] = part.astype(jnp.bfloat16)

    units = []
    blocks = early // 2
    for b in [blocks] + list(range(blocks)):
        keys_in = range(blocks + 1) if b == blocks else [blocks]
        key_offsets = [every[2 * t + j] for t in keys_in for j in range(2)]
        shifts = mask_rows(frames_ref, me, rows, every[2 * b : 2 * b + 2], key_offsets)
        for i in range(count):

            def finish(summed, total, peak, b=b, i=i):
                if b < blocks:
                    before = stats_ref[b, 0, i : i + 1]
                    highest = jnp.maximum(before, peak)
                    old = jnp.exp2((before - highest) * LOG2_SCALE)
                    new = jnp.exp2((peak - highest) * LOG2_SCALE)
                    both = stats_ref[b, 1, i : i + 1] * old + total * new
                    add(b, sums_ref[b, i] * (old / both) + summed * (new / both))
                else:
                    add(b, summed / total)
                if i == count - 1:
                    write(b)

            queries = pairs_of(pieces, i, 0)[b]
            keys = pairs_of(pieces, i, 1)
            tiles = [functools.partial(score_tile, keys[t], queries) for t in keys_in]
            values = [lambda i=i, t=t: folded[i, :, t * 2 * rows : (t + 1) * 2 * rows] for t in keys_in]
            units.append((tiles, values, shifts, finish))
    run_units(units, lat)


def attend_early(pieces, offsets, span_frames, factor, me, count, lat):
    rows = pieces[0].shape[0]
    blocks = len(pieces) // 2
    tokens = len(pieces) * rows
    return pl.pallas_call(
        functools.partial(early_kernel, offsets),
        in_specs=[SMEM] * 3 + [VMEM] * len(pieces),
        out_specs=[VMEM, VMEM],
        out_shape=[
            jax.ShapeDtypeStruct((blocks, count, lat, 2 * rows), jnp.float32),
            jax.ShapeDtypeStruct((blocks, 2, 8, 2 * rows), jnp.float32),
        ],
        scratch_shapes=[
            pltpu.VMEM((blocks, count, 2 * rows, HD), jnp.bfloat16),
            pltpu.VMEM((count, lat + 16, tokens), jnp.bfloat16),
        ],
        compiler_params=pltpu.CompilerParams(vmem_limit_bytes=ATTEND_VMEM if len(pieces) <= 8 else WHOLE_VMEM),
        cost_estimate=pl.CostEstimate(
            flops=count * tokens * tokens * 2 * (HD + lat),
            bytes_accessed=tokens * count * 3 * HD * 2,
            transcendentals=count * tokens * tokens,
        ),
        name="attend_early",
    )(span_frames, factor, me, *pieces)


def attend_late(pieces, offsets, late, sums, stats, span_frames, factor, me, count, lat):
    rows = pieces[0].shape[0]
    tokens = len(pieces) * rows
    half = len(pieces) // 2
    return pl.pallas_call(
        functools.partial(late_kernel, offsets, late),
        in_specs=[SMEM] * 3 + [VMEM] * (len(pieces) + 2),
        out_specs=[VMEM, VMEM],
        out_shape=[
            jax.ShapeDtypeStruct((half, lat, rows), jnp.float32),
            jax.ShapeDtypeStruct((half, lat, rows), jnp.bfloat16),
        ],
        scratch_shapes=[pltpu.VMEM((count, lat + 16, tokens), jnp.bfloat16)],
        compiler_params=pltpu.CompilerParams(vmem_limit_bytes=ATTEND_VMEM if len(pieces) <= 8 else WHOLE_VMEM),
        cost_estimate=pl.CostEstimate(
            flops=count * tokens * rows * 4 * (HD + lat),
            bytes_accessed=tokens * count * 3 * HD * 2,
            transcendentals=count * tokens * rows * 2,
        ),
        name="attend_late",
    )(span_frames, factor, me, *pieces, sums, stats)


def swap(array, axis, offset):
    size = lax.axis_size(axis)
    return lax.ppermute(array, axis, [(i, i ^ offset) for i in range(size)])


def body(qkv, readout, step_weight, timestep, span_frames):
    seq_count = lax.axis_size("seq")
    mp_count = lax.axis_size("mp")
    half = seq_count // 2
    count = HEADS // seq_count
    lat = readout.shape[2]
    me = lax.axis_index("seq").astype(jnp.int32)
    mp_index = lax.axis_index("mp")
    sample_count = mp_count // 2
    model_index = (mp_index // sample_count).astype(jnp.int32)
    sample_index = mp_index % sample_count
    signed = jnp.where(model_index == 1, 1.0, -1.0).astype(jnp.float32)
    factor = (signed * step_weight[timestep[sample_index]]).reshape(1)
    readout_t = jnp.swapaxes(readout, 1, 2)
    place = jnp.stack([me, model_index])

    pieces = [None] * seq_count
    for n in range(half):
        k = seq_count - 1 - n
        pieces[k] = swap(pack(place, qkv, readout_t, k, count, pieces[k + 2] if n > 1 else None), "seq", k)
    before = None
    for k in range(1, half):
        before = pieces[k] = swap(pack(place, qkv, readout_t, k, count, before), "seq", k)
    pieces[0] = pack(place, qkv, readout_t, 0, count, None)
    late = [half, half + 1]
    early = [k for k in range(seq_count) if k not in late]
    sums, stats = attend_early([pieces[k] for k in early], early, span_frames, factor, me.reshape(1), count, lat)
    keep, give = attend_late(
        [pieces[k] for k in early + late], early, late, sums, stats, span_frames, factor, me.reshape(1), count, lat
    )

    keep = keep + swap(give, "seq", 1).astype(jnp.float32)
    offset = 2
    while offset < seq_count:
        radix = min(4, seq_count // offset)
        size = keep.shape[0] // radix
        parts = [keep[n * size : (n + 1) * size] for n in range(radix)]
        keep = parts[0]
        for n in range(radix - 1, 0, -1):
            bits_n = (n >> 1) | ((n & 1) << 1) if radix == 4 else n
            keep = keep + swap(parts[n], "seq", offset * bits_n)
        offset *= radix
    total = keep[0]
    offset = 1
    while offset < mp_count:
        radix = min(4, mp_count // offset)
        own = total
        for n in range(radix - 1, 0, -1):
            total = total + swap(own, "mp", offset * n)
        offset *= radix
    return total.T


def solution(mesh):
    return jax.shard_map(
        body,
        mesh=mesh,
        in_specs=(P("mp", "seq", None), P(), P(), P(), P()),
        out_specs=P("seq", None),
        check_vma=False,
    )
```

```python
import functools
import math

import jax
import jax.numpy as jnp
from jax import lax
from jax.experimental import pallas as pl
from jax.experimental.pallas import tpu as pltpu
from jax.sharding import PartitionSpec as P

HEADS = 32
HD = 128
FRAME_TOK = 64
NT = (((1,), (1,)), ((), ()))
LOG2_SCALE = math.log2(math.e) / math.sqrt(HD)
LOWEST = -1e30
NEXT_WAVE = 3000000000
SMALL_VMEM = 24 * 1024 * 1024
LARGE_VMEM = 60 * 1024 * 1024
SMEM = pl.BlockSpec(memory_space=pltpu.SMEM)
VMEM = pl.BlockSpec(memory_space=pltpu.VMEM)
HBM = pl.BlockSpec(memory_space=pltpu.HBM)


def fold(readout, values):
    return lax.dot_general(readout, values, NT, preferred_element_type=jnp.float32).astype(jnp.bfloat16)


def value_place(h, count, lat):
    return (h * lat) % HD, count * 2 * HD + (h * lat // HD) * HD


def pack_kernel(k, me_ref, model_ref, qkv_ref, readout_ref, *refs):
    out_ref, values, readout, sems = refs[-4:]
    rows = out_ref.shape[0]
    count, lat = values.shape[0], readout.shape[0]
    first = (me_ref[0] ^ k) * count

    def columns(h, part, width):
        return pl.ds(pl.multiple_of(((first + h) * 3 + part) * HD, HD), width)

    copies = [
        pltpu.make_async_copy(
            readout_ref.at[model_ref[0], :, pl.ds(pl.multiple_of(first * HD, HD), count * HD)], readout, sems.at[2 * count]
        )
    ]
    for h in range(count):
        copies.append(pltpu.make_async_copy(qkv_ref.at[0, :, columns(h, 2, HD)], values.at[h], sems.at[h]))
    for h in range(count):
        target = out_ref.at[:, h * 2 * HD : (h + 1) * 2 * HD]
        copies.append(pltpu.make_async_copy(qkv_ref.at[0, :, columns(h, 0, 2 * HD)], target, sems.at[count + h]))
    for copy in copies:
        copy.start()
    copies[0].wait()
    for h in range(count):
        copies[1 + h].wait()
        row, column = value_place(h, count, lat)
        out_ref[row : row + lat, column : column + HD] = fold(readout[:, h * HD : (h + 1) * HD], values[h])
    for copy in copies[1 + count :]:
        copy.wait()


def pack(me, model, qkv, readout_t, k, count, after, wave=False):
    rows = qkv.shape[1]
    lat = readout_t.shape[1]
    width = count * 2 * HD + -(-count * lat // HD) * HD
    return pl.pallas_call(
        functools.partial(pack_kernel, k),
        in_specs=[SMEM, SMEM] + [HBM] * (2 + len(after)),
        out_specs=VMEM,
        out_shape=jax.ShapeDtypeStruct((rows, width), jnp.bfloat16),
        scratch_shapes=[
            pltpu.VMEM((count, rows, HD), jnp.bfloat16),
            pltpu.VMEM((lat, count * HD), jnp.bfloat16),
            pltpu.SemaphoreType.DMA((2 * count + 1,)),
        ],
        compiler_params=pltpu.CompilerParams(vmem_limit_bytes=SMALL_VMEM),
        cost_estimate=pl.CostEstimate(
            flops=NEXT_WAVE if wave else 0, bytes_accessed=rows * width * 4, transcendentals=0
        ),
        name="pack",
    )(me, model, qkv, readout_t, *after)


def mask_rows(frames_ref, me, rows, query_offsets, key_offsets):
    columns = lax.broadcasted_iota(jnp.int32, (1, rows), 1)
    places = jnp.concatenate([(me ^ k) * rows + columns for k in query_offsets], axis=1)
    end = frames_ref[0] * FRAME_TOK
    bound = jnp.full(places.shape, end, jnp.int32)
    for c in range(1, frames_ref.shape[0]):
        later = end + frames_ref[c] * FRAME_TOK
        bound = jnp.where(places >= end, later, bound)
        end = later
    return [
        jnp.where((me ^ k) * rows + start < bound, 0.0, -jnp.inf)
        for k in key_offsets
        for start in range(0, rows, FRAME_TOK)
    ]


def run_units(units, lat):
    frames = [tile() for tile in units[0][0]]
    for u, (_, values, shifts, finish) in enumerate(units):
        ahead = list(units[u + 1][0]) if u + 1 < len(units) else []
        peaks = [jnp.max(f, axis=0, keepdims=True) + s for f, s in zip(sum(frames, []), shifts)]
        peak = jnp.maximum(functools.reduce(jnp.maximum, peaks), LOWEST)
        following, summed, start = [], None, 0
        for t, tile in enumerate(frames):
            for _ in range(-(-(len(ahead) - len(following)) // (len(frames) - t))):
                following.append(ahead[len(following)]())
            weights = [
                jnp.exp2((f + (s - peak)) * LOG2_SCALE).astype(jnp.bfloat16)
                for f, s in zip(tile, shifts[start : start + len(tile)])
            ]
            start += len(tile)
            part = jnp.dot(values[t](), jnp.concatenate(weights, axis=0), preferred_element_type=jnp.float32)
            summed = part if summed is None else summed + part
        finish(summed[:lat], summed[lat : lat + 1], peak)
        frames = following


def score_tile(keys, queries):
    scores = lax.dot_general(keys(), queries(), NT, preferred_element_type=jnp.float32)
    return [scores[start : start + FRAME_TOK] for start in range(0, scores.shape[0], FRAME_TOK)]


def stage_values(folded, pieces, lat):
    count = folded.shape[0]
    rows = pieces[0].shape[0]
    for i in range(count):
        row, column = value_place(i, count, lat)
        for n, piece in enumerate(pieces):
            folded[i, :lat, n * rows : (n + 1) * rows] = piece[row : row + lat, column : column + HD]
        folded[i, lat:] = jnp.ones_like(folded[i, lat:])


def pairs_of(pieces, i, what):
    column = (2 * i + what) * HD

    def read(n):
        return lambda: jnp.concatenate([pieces[n][:, column : column + HD], pieces[n + 1][:, column : column + HD]], axis=0)

    return [read(n) for n in range(0, len(pieces), 2)]


def early_kernel(offsets, frames_ref, me_ref, timestep_ref, step_weight_ref, sign_ref, sample_ref, *refs):
    count_pieces = len(offsets)
    arrived = refs[:count_pieces]
    sums_ref, stats_ref, factor_ref, pieces, folded, asked, sems = refs[-7:]
    me = me_ref[0]
    rows = pieces.shape[1]
    lat = sums_ref.shape[2]
    count = folded.shape[0]
    blocks = count_pieces // 2
    copies = [pltpu.make_async_copy(arrived[n], pieces.at[n], sems.at[n]) for n in range(count_pieces)]
    for copy in copies:
        copy.start()
    factor_ref[...] = jnp.full(factor_ref.shape, sign_ref[0] * step_weight_ref[timestep_ref[sample_ref[0]]])
    for copy in copies:
        copy.wait()
    pieces = [pieces.at[n] for n in range(count_pieces)]
    stage_values(folded, pieces, lat)
    for i in range(count):
        for b, read in enumerate(pairs_of(pieces, i, 0)):
            asked[b, i] = read()
    half = count_pieces // 2 + 1

    def some_blocks(b, carry):
        q = [2 * b, 2 * b + 1]
        shifts = mask_rows(frames_ref, me, rows, [jnp.where(n < half, n, n + 2) for n in q], offsets)
        peaks, totals, units = [], [], []
        for i in range(count):

            def finish(summed, total, peak, i=i):
                sums_ref[b, i] = summed
                peaks.append(peak)
                totals.append(total)

            tiles = [
                functools.partial(score_tile, keys, lambda i=i: asked[b, i]) for keys in pairs_of(pieces, i, 1)
            ]
            values = [lambda i=i, t=t: folded[i, :, t * 2 * rows : (t + 1) * 2 * rows] for t in range(blocks)]
            units.append((tiles, values, shifts, finish))
        run_units(units, lat)
        rest = [jnp.ones_like(peaks[0])] * (stats_ref.shape[2] - count)
        stats_ref[b, 0] = jnp.concatenate(peaks + rest, axis=0)
        stats_ref[b, 1] = jnp.concatenate(totals + rest, axis=0)
        return carry

    lax.fori_loop(0, blocks, some_blocks, 0)


def late_kernel(offsets, late, frames_ref, me_ref, *refs):
    early = len(offsets)
    arrived = refs[:2]
    sums_ref, stats_ref, factor_ref, early_ref, early_folded, keep_ref, give_ref, late_pieces, folded, sems = refs[2:]
    copies = [pltpu.make_async_copy(arrived[n], late_pieces.at[n], sems.at[n]) for n in range(2)]
    for copy in copies:
        copy.start()
    me = me_ref[0]
    half, lat, rows = keep_ref.shape
    bits = half.bit_length()
    count = folded.shape[0]
    for copy in copies:
        copy.wait()
    pieces = [early_ref.at[n] for n in range(early)] + [late_pieces.at[n] for n in range(2)]
    stage_values(folded, pieces[early:], lat)
    factor = factor_ref[:1]
    every = list(offsets) + list(late)
    results = {}

    def add(b, part):
        results[b] = part if b not in results else results[b] + part

    def write(b):
        for j in range(2):
            k = every[2 * b + j]
            n = sum(((k >> bit) & 1) << (bits - 1 - bit) for bit in range(bits))
            part = results[b][:, j * rows : (j + 1) * rows] * factor
            if n < half:
                keep_ref[n] = part
            else:
                give_ref[n - half] = part.astype(jnp.bfloat16)

    units = []
    blocks = early // 2
    for b in [blocks] + list(range(blocks)):
        keys_in = range(blocks + 1) if b == blocks else [blocks]
        key_offsets = [every[2 * t + j] for t in keys_in for j in range(2)]
        shifts = mask_rows(frames_ref, me, rows, every[2 * b : 2 * b + 2], key_offsets)
        for i in range(count):

            def finish(summed, total, peak, b=b, i=i):
                if b < blocks:
                    before = stats_ref[b, 0, i : i + 1]
                    highest = jnp.maximum(before, peak)
                    old = jnp.exp2((before - highest) * LOG2_SCALE)
                    new = jnp.exp2((peak - highest) * LOG2_SCALE)
                    both = stats_ref[b, 1, i : i + 1] * old + total * new
                    add(b, sums_ref[b, i] * (old / both) + summed * (new / both))
                else:
                    add(b, summed / total)
                if i == count - 1:
                    write(b)

            queries = pairs_of(pieces, i, 0)[b]
            keys = pairs_of(pieces, i, 1)
            tiles = [functools.partial(score_tile, keys[t], queries) for t in keys_in]
            values = [
                lambda i=i, t=t: folded[i] if t == blocks else early_folded[i, :, t * 2 * rows : (t + 1) * 2 * rows]
                for t in keys_in
            ]
            units.append((tiles, values, shifts, finish))
    run_units(units, lat)


def attend_early(pieces, offsets, span_frames, me, timestep, step_weight, sign, sample, count, lat):
    rows, width = pieces[0].shape
    blocks = len(pieces) // 2
    tokens = len(pieces) * rows
    return pl.pallas_call(
        functools.partial(early_kernel, offsets),
        in_specs=[SMEM] * 6 + [HBM] * len(pieces),
        out_specs=[VMEM] * 5,
        out_shape=[
            jax.ShapeDtypeStruct((blocks, count, lat, 2 * rows), jnp.float32),
            jax.ShapeDtypeStruct((blocks, 2, 8, 2 * rows), jnp.float32),
            jax.ShapeDtypeStruct((8, rows), jnp.float32),
            jax.ShapeDtypeStruct((len(pieces), rows, width), jnp.bfloat16),
            jax.ShapeDtypeStruct((count, lat + 16, tokens), jnp.bfloat16),
        ],
        scratch_shapes=[
            pltpu.VMEM((blocks, count, 2 * rows, HD), jnp.bfloat16),
            pltpu.SemaphoreType.DMA((len(pieces),)),
        ],
        compiler_params=pltpu.CompilerParams(vmem_limit_bytes=SMALL_VMEM if len(pieces) <= 8 else LARGE_VMEM),
        cost_estimate=pl.CostEstimate(
            flops=count * tokens * tokens * 2 * (HD + lat),
            bytes_accessed=tokens * count * 3 * HD * 2,
            transcendentals=count * tokens * tokens,
        ),
        name="attend_early",
    )(span_frames, me, timestep, step_weight, sign, sample, *pieces)


def attend_late(pieces, offsets, late, early, span_frames, me, count, lat):
    rows, width = pieces[0].shape
    half = len(offsets) // 2 + 1
    tokens = 2 * half * rows
    return pl.pallas_call(
        functools.partial(late_kernel, offsets, late),
        in_specs=[SMEM] * 2 + [HBM] * 2 + [VMEM] * len(early),
        out_specs=[VMEM, VMEM],
        out_shape=[
            jax.ShapeDtypeStruct((half, lat, rows), jnp.float32),
            jax.ShapeDtypeStruct((half, lat, rows), jnp.bfloat16),
        ],
        scratch_shapes=[
            pltpu.VMEM((2, rows, width), jnp.bfloat16),
            pltpu.VMEM((count, lat + 16, 2 * rows), jnp.bfloat16),
            pltpu.SemaphoreType.DMA((2,)),
        ],
        compiler_params=pltpu.CompilerParams(vmem_limit_bytes=SMALL_VMEM if half <= 4 else LARGE_VMEM),
        cost_estimate=pl.CostEstimate(
            flops=count * tokens * rows * 4 * (HD + lat),
            bytes_accessed=tokens * count * 3 * HD * 2,
            transcendentals=count * tokens * rows * 2,
        ),
        name="attend_late",
    )(span_frames, me, *pieces, *early)


def swap(array, axis, offset):
    size = lax.axis_size(axis)
    return lax.ppermute(array, axis, [(i, i ^ offset) for i in range(size)])


def body(qkv, readout, step_weight, timestep, span_frames):
    seq_count = lax.axis_size("seq")
    mp_count = lax.axis_size("mp")
    half = seq_count // 2
    count = HEADS // seq_count
    lat = readout.shape[2]
    me = lax.axis_index("seq").astype(jnp.int32).reshape(1)
    mp_index = lax.axis_index("mp").astype(jnp.int32)
    sample_count = mp_count // 2
    model_index = mp_index // sample_count
    sample = (mp_index % sample_count).reshape(1)
    sign = jnp.where(model_index == 1, 1.0, -1.0).astype(jnp.float32).reshape(1)
    model = model_index.reshape(1)
    readout_t = jnp.swapaxes(readout, 1, 2)

    pieces = [None] * seq_count
    packed = {}
    for n in range(half):
        k = seq_count - 1 - n
        after = [pieces[k + 2]] if n > 1 else []
        packed[k] = pack(me, model, qkv, readout_t, k, count, after, n > 1)
        pieces[k] = swap(packed[k], "seq", k)
    for k in range(1, half):
        after = [pieces[k - 1]] if k > 2 else []
        pieces[k] = swap(pack(me, model, qkv, readout_t, k, count, after), "seq", k)
    pieces[0] = pack(me, model, qkv, readout_t, 0, count, [packed[seq_count - 2]])
    late = [half, half + 1]
    early = [k for k in range(seq_count) if k not in late]
    merged = attend_early(
        [pieces[k] for k in early], early, span_frames, me, timestep, step_weight, sign, sample, count, lat
    )
    keep, give = attend_late([pieces[k] for k in late], early, late, merged, span_frames, me, count, lat)

    keep = keep + swap(give, "seq", 1).astype(jnp.float32)
    offset = 2
    while offset < seq_count:
        radix = min(4, seq_count // offset)
        size = keep.shape[0] // radix
        parts = [keep[n * size : (n + 1) * size] for n in range(radix)]
        keep = parts[0]
        for n in range(radix - 1, 0, -1):
            bits_n = (n >> 1) | ((n & 1) << 1) if radix == 4 else n
            keep = keep + swap(parts[n], "seq", offset * bits_n)
        offset *= radix
    total = keep[0]
    offset = 1
    while offset < mp_count:
        radix = min(4, mp_count // offset)
        own = total
        for n in range(radix - 1, 0, -1):
            total = total + swap(own, "mp", offset * n)
        offset *= radix
    return total.T


def solution(mesh):
    return jax.shard_map(
        body,
        mesh=mesh,
        in_specs=(P("mp", "seq", None), P(), P(), P(), P()),
        out_specs=P("seq", None),
        check_vma=False,
    )
```

```python
import functools
import math

import jax
import jax.numpy as jnp
from jax import lax
from jax.experimental import pallas as pl
from jax.experimental.pallas import tpu as pltpu
from jax.sharding import PartitionSpec as P

HEADS = 32
HD = 128
FRAME_TOK = 64
NT = (((1,), (1,)), ((), ()))
LOG2_SCALE = math.log2(math.e) / math.sqrt(HD)
LOWEST = -1e30
NEXT_WAVE = 0
SMALL_VMEM = 24 * 1024 * 1024
LARGE_VMEM = 60 * 1024 * 1024
SMEM = pl.BlockSpec(memory_space=pltpu.SMEM)
VMEM = pl.BlockSpec(memory_space=pltpu.VMEM)
HBM = pl.BlockSpec(memory_space=pltpu.HBM)


def fold(readout, values):
    return lax.dot_general(readout, values, NT, preferred_element_type=jnp.float32).astype(jnp.bfloat16)


def value_place(h, count, lat):
    return (h * lat) % HD, count * 2 * HD + (h * lat // HD) * HD


def pack_kernel(k, me_ref, model_ref, qkv_ref, readout_ref, *refs):
    out_ref, values, readout, sems = refs[-4:]
    rows = out_ref.shape[0]
    count, lat = values.shape[0], readout.shape[0]
    first = (me_ref[0] ^ k) * count

    def columns(h, part, width):
        return pl.ds(pl.multiple_of(((first + h) * 3 + part) * HD, HD), width)

    copies = [
        pltpu.make_async_copy(
            readout_ref.at[model_ref[0], :, pl.ds(pl.multiple_of(first * HD, HD), count * HD)], readout, sems.at[2 * count]
        )
    ]
    for h in range(count):
        copies.append(pltpu.make_async_copy(qkv_ref.at[0, :, columns(h, 2, HD)], values.at[h], sems.at[h]))
    for h in range(count):
        target = out_ref.at[:, h * 2 * HD : (h + 1) * 2 * HD]
        copies.append(pltpu.make_async_copy(qkv_ref.at[0, :, columns(h, 0, 2 * HD)], target, sems.at[count + h]))
    for copy in copies:
        copy.start()
    copies[0].wait()
    for h in range(count):
        copies[1 + h].wait()
        row, column = value_place(h, count, lat)
        out_ref[row : row + lat, column : column + HD] = fold(readout[:, h * HD : (h + 1) * HD], values[h])
    for copy in copies[1 + count :]:
        copy.wait()


def pack(me, model, qkv, readout_t, k, count, after, wave=False, first=False):
    rows = qkv.shape[1]
    lat = readout_t.shape[1]
    width = count * 2 * HD + -(-count * lat // HD) * HD
    return pl.pallas_call(
        functools.partial(pack_kernel, k),
        in_specs=[SMEM, SMEM] + [HBM] * (2 + len(after)),
        out_specs=VMEM,
        out_shape=jax.ShapeDtypeStruct((rows, width), jnp.bfloat16),
        scratch_shapes=[
            pltpu.VMEM((count, rows, HD), jnp.bfloat16),
            pltpu.VMEM((lat, count * HD), jnp.bfloat16),
            pltpu.SemaphoreType.DMA((2 * count + 1,)),
        ],
        compiler_params=pltpu.CompilerParams(vmem_limit_bytes=LARGE_VMEM if first else SMALL_VMEM),
        cost_estimate=pl.CostEstimate(
            flops=NEXT_WAVE if wave else 0, bytes_accessed=rows * width * 4, transcendentals=0
        ),
        name="pack",
    )(me, model, qkv, readout_t, *after)


def mask_rows(frames_ref, me, rows, query_offsets, key_offsets):
    columns = lax.broadcasted_iota(jnp.int32, (1, rows), 1)
    places = jnp.concatenate([(me ^ k) * rows + columns for k in query_offsets], axis=1)
    end = frames_ref[0] * FRAME_TOK
    bound = jnp.full(places.shape, end, jnp.int32)
    for c in range(1, frames_ref.shape[0]):
        later = end + frames_ref[c] * FRAME_TOK
        bound = jnp.where(places >= end, later, bound)
        end = later
    return [
        jnp.where((me ^ k) * rows + start < bound, 0.0, -jnp.inf)
        for k in key_offsets
        for start in range(0, rows, FRAME_TOK)
    ]


def run_units(units, lat):
    frames = [tile() for tile in units[0][0]]
    for u, (_, values, shifts, finish) in enumerate(units):
        ahead = list(units[u + 1][0]) if u + 1 < len(units) else []
        peaks = [jnp.max(f, axis=0, keepdims=True) + s for f, s in zip(sum(frames, []), shifts)]
        peak = jnp.maximum(functools.reduce(jnp.maximum, peaks), LOWEST)
        following, summed, start = [], None, 0
        for t, tile in enumerate(frames):
            for _ in range(-(-(len(ahead) - len(following)) // (len(frames) - t))):
                following.append(ahead[len(following)]())
            weights = [
                jnp.exp2((f + (s - peak)) * LOG2_SCALE).astype(jnp.bfloat16)
                for f, s in zip(tile, shifts[start : start + len(tile)])
            ]
            start += len(tile)
            part = jnp.dot(values[t](), jnp.concatenate(weights, axis=0), preferred_element_type=jnp.float32)
            summed = part if summed is None else summed + part
        finish(summed[:lat], summed[lat : lat + 1], peak)
        frames = following


def score_tile(keys, queries):
    scores = lax.dot_general(keys(), queries(), NT, preferred_element_type=jnp.float32)
    return [scores[start : start + FRAME_TOK] for start in range(0, scores.shape[0], FRAME_TOK)]


def stage_values(folded, pieces, lat):
    count = folded.shape[0]
    rows = pieces[0].shape[0]
    for i in range(count):
        row, column = value_place(i, count, lat)
        for n, piece in enumerate(pieces):
            folded[i, :lat, n * rows : (n + 1) * rows] = piece[row : row + lat, column : column + HD]
        folded[i, lat:] = jnp.ones_like(folded[i, lat:])


def pairs_of(pieces, i, what):
    column = (2 * i + what) * HD

    def read(n):
        return lambda: jnp.concatenate([pieces[n][:, column : column + HD], pieces[n + 1][:, column : column + HD]], axis=0)

    return [read(n) for n in range(0, len(pieces), 2)]


def early_kernel(offsets, frames_ref, me_ref, timestep_ref, step_weight_ref, sign_ref, sample_ref, *refs):
    count_pieces = len(offsets)
    arrived = refs[:count_pieces]
    sums_ref, stats_ref, factor_ref, pieces, folded, asked, sems = refs[-7:]
    me = me_ref[0]
    rows = pieces.shape[1]
    lat = sums_ref.shape[2]
    count = folded.shape[0]
    blocks = count_pieces // 2
    copies = [pltpu.make_async_copy(arrived[n], pieces.at[n], sems.at[n]) for n in range(count_pieces)]
    for copy in copies:
        copy.start()
    factor_ref[...] = jnp.full(factor_ref.shape, sign_ref[0] * step_weight_ref[timestep_ref[sample_ref[0]]])
    for copy in copies:
        copy.wait()
    pieces = [pieces.at[n] for n in range(count_pieces)]
    stage_values(folded, pieces, lat)
    for i in range(count):
        for b, read in enumerate(pairs_of(pieces, i, 0)):
            asked[b, i] = read()
    half = count_pieces // 2 + 1

    def some_blocks(b, carry):
        q = [2 * b, 2 * b + 1]
        shifts = mask_rows(frames_ref, me, rows, [jnp.where(n < half, n, n + 2) for n in q], offsets)
        peaks, totals, units = [], [], []
        for i in range(count):

            def finish(summed, total, peak, i=i):
                sums_ref[b, i] = summed
                peaks.append(peak)
                totals.append(total)

            tiles = [
                functools.partial(score_tile, keys, lambda i=i: asked[b, i]) for keys in pairs_of(pieces, i, 1)
            ]
            values = [lambda i=i, t=t: folded[i, :, t * 2 * rows : (t + 1) * 2 * rows] for t in range(blocks)]
            units.append((tiles, values, shifts, finish))
        run_units(units, lat)
        rest = [jnp.ones_like(peaks[0])] * (stats_ref.shape[2] - count)
        stats_ref[b, 0] = jnp.concatenate(peaks + rest, axis=0)
        stats_ref[b, 1] = jnp.concatenate(totals + rest, axis=0)
        return carry

    lax.fori_loop(0, blocks, some_blocks, 0)


def late_kernel(offsets, late, frames_ref, me_ref, *refs):
    early = len(offsets)
    arrived = refs[:2]
    sums_ref, stats_ref, factor_ref, early_ref, early_folded, keep_ref, give_ref, late_pieces, folded, sems = refs[2:]
    copies = [pltpu.make_async_copy(arrived[n], late_pieces.at[n], sems.at[n]) for n in range(2)]
    for copy in copies:
        copy.start()
    me = me_ref[0]
    half, lat, rows = keep_ref.shape
    bits = half.bit_length()
    count = folded.shape[0]
    for copy in copies:
        copy.wait()
    pieces = [early_ref.at[n] for n in range(early)] + [late_pieces.at[n] for n in range(2)]
    stage_values(folded, pieces[early:], lat)
    factor = factor_ref[:1]
    every = list(offsets) + list(late)
    results = {}

    def add(b, part):
        results[b] = part if b not in results else results[b] + part

    def write(b):
        for j in range(2):
            k = every[2 * b + j]
            n = sum(((k >> bit) & 1) << (bits - 1 - bit) for bit in range(bits))
            part = results[b][:, j * rows : (j + 1) * rows] * factor
            if n < half:
                keep_ref[n] = part
            else:
                give_ref[n - half] = part.astype(jnp.bfloat16)

    units = []
    blocks = early // 2
    for b in [blocks] + list(range(blocks)):
        keys_in = range(blocks + 1) if b == blocks else [blocks]
        key_offsets = [every[2 * t + j] for t in keys_in for j in range(2)]
        shifts = mask_rows(frames_ref, me, rows, every[2 * b : 2 * b + 2], key_offsets)
        for i in range(count):

            def finish(summed, total, peak, b=b, i=i):
                if b < blocks:
                    before = stats_ref[b, 0, i : i + 1]
                    highest = jnp.maximum(before, peak)
                    old = jnp.exp2((before - highest) * LOG2_SCALE)
                    new = jnp.exp2((peak - highest) * LOG2_SCALE)
                    both = stats_ref[b, 1, i : i + 1] * old + total * new
                    add(b, sums_ref[b, i] * (old / both) + summed * (new / both))
                else:
                    add(b, summed / total)
                if i == count - 1:
                    write(b)

            queries = pairs_of(pieces, i, 0)[b]
            keys = pairs_of(pieces, i, 1)
            tiles = [functools.partial(score_tile, keys[t], queries) for t in keys_in]
            values = [
                lambda i=i, t=t: folded[i] if t == blocks else early_folded[i, :, t * 2 * rows : (t + 1) * 2 * rows]
                for t in keys_in
            ]
            units.append((tiles, values, shifts, finish))
    run_units(units, lat)


def attend_early(pieces, offsets, span_frames, me, timestep, step_weight, sign, sample, count, lat):
    rows, width = pieces[0].shape
    blocks = len(pieces) // 2
    tokens = len(pieces) * rows
    return pl.pallas_call(
        functools.partial(early_kernel, offsets),
        in_specs=[SMEM] * 6 + [HBM] * len(pieces),
        out_specs=[VMEM] * 5,
        out_shape=[
            jax.ShapeDtypeStruct((blocks, count, lat, 2 * rows), jnp.float32),
            jax.ShapeDtypeStruct((blocks, 2, 8, 2 * rows), jnp.float32),
            jax.ShapeDtypeStruct((8, rows), jnp.float32),
            jax.ShapeDtypeStruct((len(pieces), rows, width), jnp.bfloat16),
            jax.ShapeDtypeStruct((count, lat + 16, tokens), jnp.bfloat16),
        ],
        scratch_shapes=[
            pltpu.VMEM((blocks, count, 2 * rows, HD), jnp.bfloat16),
            pltpu.SemaphoreType.DMA((len(pieces),)),
        ],
        compiler_params=pltpu.CompilerParams(vmem_limit_bytes=SMALL_VMEM if len(pieces) <= 8 else LARGE_VMEM),
        cost_estimate=pl.CostEstimate(
            flops=count * tokens * tokens * 2 * (HD + lat),
            bytes_accessed=tokens * count * 3 * HD * 2,
            transcendentals=count * tokens * tokens,
        ),
        name="attend_early",
    )(span_frames, me, timestep, step_weight, sign, sample, *pieces)


def attend_late(pieces, offsets, late, early, span_frames, me, count, lat):
    rows, width = pieces[0].shape
    half = len(offsets) // 2 + 1
    tokens = 2 * half * rows
    return pl.pallas_call(
        functools.partial(late_kernel, offsets, late),
        in_specs=[SMEM] * 2 + [HBM] * 2 + [VMEM] * len(early),
        out_specs=[VMEM, VMEM],
        out_shape=[
            jax.ShapeDtypeStruct((half, lat, rows), jnp.float32),
            jax.ShapeDtypeStruct((half, lat, rows), jnp.bfloat16),
        ],
        scratch_shapes=[
            pltpu.VMEM((2, rows, width), jnp.bfloat16),
            pltpu.VMEM((count, lat + 16, 2 * rows), jnp.bfloat16),
            pltpu.SemaphoreType.DMA((2,)),
        ],
        compiler_params=pltpu.CompilerParams(vmem_limit_bytes=SMALL_VMEM if half <= 4 else LARGE_VMEM),
        cost_estimate=pl.CostEstimate(
            flops=count * tokens * rows * 4 * (HD + lat),
            bytes_accessed=tokens * count * 3 * HD * 2,
            transcendentals=count * tokens * rows * 2,
        ),
        name="attend_late",
    )(span_frames, me, *pieces, *early)


def swap(array, axis, offset):
    size = lax.axis_size(axis)
    return lax.ppermute(array, axis, [(i, i ^ offset) for i in range(size)])


def body(qkv, readout, step_weight, timestep, span_frames):
    seq_count = lax.axis_size("seq")
    mp_count = lax.axis_size("mp")
    half = seq_count // 2
    count = HEADS // seq_count
    lat = readout.shape[2]
    me = lax.axis_index("seq").astype(jnp.int32).reshape(1)
    mp_index = lax.axis_index("mp").astype(jnp.int32)
    sample_count = mp_count // 2
    model_index = mp_index // sample_count
    sample = (mp_index % sample_count).reshape(1)
    sign = jnp.where(model_index == 1, 1.0, -1.0).astype(jnp.float32).reshape(1)
    model = model_index.reshape(1)
    readout_t = jnp.swapaxes(readout, 1, 2)

    pieces = [None] * seq_count
    for n in range(half):
        k = seq_count - 1 - n
        pieces[k] = swap(pack(me, model, qkv, readout_t, k, count, [pieces[k + 2]] if n > 1 else [], n > 1, n == 0), "seq", k)
    for k in range(half - 1, 0, -1):
        after = [] if k == half - 1 else [pieces[k + 1], pieces[seq_count - 1]] if k > 1 else [pieces[half - 1]]
        pieces[k] = swap(pack(me, model, qkv, readout_t, k, count, after), "seq", k)
    pieces[0] = pack(me, model, qkv, readout_t, 0, count, [pieces[half - 1]])
    late = [half, half + 1]
    early = [k for k in range(seq_count) if k not in late]
    merged = attend_early(
        [pieces[k] for k in early], early, span_frames, me, timestep, step_weight, sign, sample, count, lat
    )
    keep, give = attend_late([pieces[k] for k in late], early, late, merged, span_frames, me, count, lat)

    keep = keep + swap(give, "seq", 1).astype(jnp.float32)
    offset = 2
    while offset < seq_count:
        radix = min(4, seq_count // offset)
        size = keep.shape[0] // radix
        parts = [keep[n * size : (n + 1) * size] for n in range(radix)]
        keep = parts[0]
        for n in range(radix - 1, 0, -1):
            bits_n = (n >> 1) | ((n & 1) << 1) if radix == 4 else n
            keep = keep + swap(parts[n], "seq", offset * bits_n)
        offset *= radix
    total = keep[0]
    offset = 1
    while offset < mp_count:
        radix = min(4, mp_count // offset)
        own = total
        for n in range(radix - 1, 0, -1):
            total = total + swap(own, "mp", offset * n)
        offset *= radix
    return total.T


def solution(mesh):
    return jax.shard_map(
        body,
        mesh=mesh,
        in_specs=(P("mp", "seq", None), P(), P(), P(), P()),
        out_specs=P("seq", None),
        check_vma=False,
    )
```

```python
import functools
import math

import jax
import jax.numpy as jnp
from jax import lax
from jax.experimental import pallas as pl
from jax.experimental.pallas import tpu as pltpu
from jax.sharding import PartitionSpec as P

HEADS = 32
HD = 128
FRAME_TOK = 64
NT = (((1,), (1,)), ((), ()))
LOG2_SCALE = math.log2(math.e) / math.sqrt(HD)
LOWEST = -1e30
NEXT_WAVE = 0
SMALL_VMEM = 24 * 1024 * 1024
LARGE_VMEM = 60 * 1024 * 1024
SMEM = pl.BlockSpec(memory_space=pltpu.SMEM)
VMEM = pl.BlockSpec(memory_space=pltpu.VMEM)
HBM = pl.BlockSpec(memory_space=pltpu.HBM)


def fold(readout, values):
    return lax.dot_general(readout, values, NT, preferred_element_type=jnp.float32).astype(jnp.bfloat16)


def value_place(h, count, lat):
    return (h * lat) % HD, count * 2 * HD + (h * lat // HD) * HD


def pack_kernel(k, me_ref, model_ref, qkv_ref, readout_ref, *refs):
    out_ref, values, readout, sems = refs[-4:]
    rows = out_ref.shape[0]
    count, lat = values.shape[0], readout.shape[0]
    first = (me_ref[0] ^ k) * count

    def columns(h, part, width):
        return pl.ds(pl.multiple_of(((first + h) * 3 + part) * HD, HD), width)

    copies = [
        pltpu.make_async_copy(
            readout_ref.at[model_ref[0], :, pl.ds(pl.multiple_of(first * HD, HD), count * HD)], readout, sems.at[2 * count]
        )
    ]
    for h in range(count):
        copies.append(pltpu.make_async_copy(qkv_ref.at[0, :, columns(h, 2, HD)], values.at[h], sems.at[h]))
    for h in range(count):
        target = out_ref.at[:, h * 2 * HD : (h + 1) * 2 * HD]
        copies.append(pltpu.make_async_copy(qkv_ref.at[0, :, columns(h, 0, 2 * HD)], target, sems.at[count + h]))
    for copy in copies:
        copy.start()
    copies[0].wait()
    for h in range(count):
        copies[1 + h].wait()
        row, column = value_place(h, count, lat)
        out_ref[row : row + lat, column : column + HD] = fold(readout[:, h * HD : (h + 1) * HD], values[h])
    for copy in copies[1 + count :]:
        copy.wait()


def pack(me, model, qkv, readout_t, k, count, after, wave=False, first=False):
    rows = qkv.shape[1]
    lat = readout_t.shape[1]
    width = count * 2 * HD + -(-count * lat // HD) * HD
    return pl.pallas_call(
        functools.partial(pack_kernel, k),
        in_specs=[SMEM, SMEM] + [HBM] * (2 + len(after)),
        out_specs=VMEM,
        out_shape=jax.ShapeDtypeStruct((rows, width), jnp.bfloat16),
        scratch_shapes=[
            pltpu.VMEM((count, rows, HD), jnp.bfloat16),
            pltpu.VMEM((lat, count * HD), jnp.bfloat16),
            pltpu.SemaphoreType.DMA((2 * count + 1,)),
        ],
        compiler_params=pltpu.CompilerParams(vmem_limit_bytes=LARGE_VMEM if first else SMALL_VMEM),
        cost_estimate=pl.CostEstimate(
            flops=NEXT_WAVE if wave else 0, bytes_accessed=rows * width * 4, transcendentals=0
        ),
        name="pack",
    )(me, model, qkv, readout_t, *after)


def mask_rows(frames_ref, me, rows, query_offsets, key_offsets):
    columns = lax.broadcasted_iota(jnp.int32, (1, rows), 1)
    places = jnp.concatenate([(me ^ k) * rows + columns for k in query_offsets], axis=1)
    end = frames_ref[0] * FRAME_TOK
    bound = jnp.full(places.shape, end, jnp.int32)
    for c in range(1, frames_ref.shape[0]):
        later = end + frames_ref[c] * FRAME_TOK
        bound = jnp.where(places >= end, later, bound)
        end = later
    return [
        jnp.where((me ^ k) * rows + start < bound, 0.0, -jnp.inf)
        for k in key_offsets
        for start in range(0, rows, FRAME_TOK)
    ]


def run_units(units, lat):
    frames = [tile() for tile in units[0][0]]
    for u, (_, values, shifts, finish) in enumerate(units):
        ahead = list(units[u + 1][0]) if u + 1 < len(units) else []
        peaks = [jnp.max(f, axis=0, keepdims=True) + s for f, s in zip(sum(frames, []), shifts)]
        peak = jnp.maximum(functools.reduce(jnp.maximum, peaks), LOWEST)
        following, summed, start = [], None, 0
        for t, tile in enumerate(frames):
            for _ in range(-(-(len(ahead) - len(following)) // (len(frames) - t))):
                following.append(ahead[len(following)]())
            weights = [
                jnp.exp2((f + (s - peak)) * LOG2_SCALE).astype(jnp.bfloat16)
                for f, s in zip(tile, shifts[start : start + len(tile)])
            ]
            start += len(tile)
            part = jnp.dot(values[t](), jnp.concatenate(weights, axis=0), preferred_element_type=jnp.float32)
            summed = part if summed is None else summed + part
        finish(summed[:lat], summed[lat : lat + 1], peak)
        frames = following


def score_tile(keys, queries):
    scores = lax.dot_general(keys(), queries(), NT, preferred_element_type=jnp.float32)
    return [scores[start : start + FRAME_TOK] for start in range(0, scores.shape[0], FRAME_TOK)]


def stage_values(folded, pieces, lat):
    count = folded.shape[0]
    rows = pieces[0].shape[0]
    for i in range(count):
        row, column = value_place(i, count, lat)
        for n, piece in enumerate(pieces):
            folded[i, :lat, n * rows : (n + 1) * rows] = piece[row : row + lat, column : column + HD]
        folded[i, lat:] = jnp.ones_like(folded[i, lat:])


def pairs_of(pieces, i, what):
    column = (2 * i + what) * HD

    def read(n):
        return lambda: jnp.concatenate([pieces[n][:, column : column + HD], pieces[n + 1][:, column : column + HD]], axis=0)

    return [read(n) for n in range(0, len(pieces), 2)]


def early_kernel(offsets, frames_ref, me_ref, timestep_ref, step_weight_ref, sign_ref, sample_ref, *refs):
    count_pieces = len(offsets)
    arrived = refs[:count_pieces]
    sums_ref, stats_ref, factor_ref, pieces, folded, asked, sems = refs[-7:]
    me = me_ref[0]
    rows = pieces.shape[1]
    lat = sums_ref.shape[2]
    count = folded.shape[0]
    blocks = count_pieces // 2
    copies = [pltpu.make_async_copy(arrived[n], pieces.at[n], sems.at[n]) for n in range(count_pieces)]
    for copy in copies:
        copy.start()
    factor_ref[...] = jnp.full(factor_ref.shape, sign_ref[0] * step_weight_ref[timestep_ref[sample_ref[0]]])
    for copy in copies:
        copy.wait()
    pieces = [pieces.at[n] for n in range(count_pieces)]
    stage_values(folded, pieces, lat)
    for i in range(count):
        for b, read in enumerate(pairs_of(pieces, i, 0)):
            asked[b, i] = read()
    half = count_pieces // 2 + 1

    def some_blocks(b, carry):
        q = [2 * b, 2 * b + 1]
        shifts = mask_rows(frames_ref, me, rows, [jnp.where(n < half, n, n + 2) for n in q], offsets)
        peaks, totals, units = [], [], []
        for i in range(count):

            def finish(summed, total, peak, i=i):
                sums_ref[b, i] = summed
                peaks.append(peak)
                totals.append(total)

            tiles = [
                functools.partial(score_tile, keys, lambda i=i: asked[b, i]) for keys in pairs_of(pieces, i, 1)
            ]
            values = [lambda i=i, t=t: folded[i, :, t * 2 * rows : (t + 1) * 2 * rows] for t in range(blocks)]
            units.append((tiles, values, shifts, finish))
        run_units(units, lat)
        rest = [jnp.ones_like(peaks[0])] * (stats_ref.shape[2] - count)
        stats_ref[b, 0] = jnp.concatenate(peaks + rest, axis=0)
        stats_ref[b, 1] = jnp.concatenate(totals + rest, axis=0)
        return carry

    lax.fori_loop(0, blocks, some_blocks, 0)


def late_kernel(offsets, late, chosen, groups, frames_ref, me_ref, *refs):
    early = len(offsets)
    arrived = refs[:2]
    sums_ref, stats_ref, factor_ref, early_ref, early_folded, *out_refs, late_pieces, folded, sems = refs[2:]
    copies = [pltpu.make_async_copy(arrived[n], late_pieces.at[n], sems.at[n]) for n in range(2)]
    for copy in copies:
        copy.start()
    me = me_ref[0]
    size, lat, rows = out_refs[0].shape
    count = folded.shape[0]
    for copy in copies:
        copy.wait()
    pieces = [early_ref.at[n] for n in range(early)] + [late_pieces.at[n] for n in range(2)]
    stage_values(folded, pieces[early:], lat)
    factor = factor_ref[:1]
    every = list(offsets) + list(late)
    results = {}

    def add(b, part):
        results[b] = part if b not in results else results[b] + part

    def write(b):
        for j in range(2):
            k = every[2 * b + j]
            out_ref = out_refs[groups.index(k // size)]
            out_ref[k % size] = (results[b][:, j * rows : (j + 1) * rows] * factor).astype(out_ref.dtype)

    units = []
    blocks = early // 2
    for b in chosen:
        keys_in = range(blocks + 1) if b == blocks else [blocks]
        key_offsets = [every[2 * t + j] for t in keys_in for j in range(2)]
        shifts = mask_rows(frames_ref, me, rows, every[2 * b : 2 * b + 2], key_offsets)
        for i in range(count):

            def finish(summed, total, peak, b=b, i=i):
                if b < blocks:
                    before = stats_ref[b, 0, i : i + 1]
                    highest = jnp.maximum(before, peak)
                    old = jnp.exp2((before - highest) * LOG2_SCALE)
                    new = jnp.exp2((peak - highest) * LOG2_SCALE)
                    both = stats_ref[b, 1, i : i + 1] * old + total * new
                    add(b, sums_ref[b, i] * (old / both) + summed * (new / both))
                else:
                    add(b, summed / total)
                if i == count - 1:
                    write(b)

            queries = pairs_of(pieces, i, 0)[b]
            keys = pairs_of(pieces, i, 1)
            tiles = [functools.partial(score_tile, keys[t], queries) for t in keys_in]
            values = [
                lambda i=i, t=t: folded[i] if t == blocks else early_folded[i, :, t * 2 * rows : (t + 1) * 2 * rows]
                for t in keys_in
            ]
            units.append((tiles, values, shifts, finish))
    run_units(units, lat)


def attend_early(pieces, offsets, span_frames, me, timestep, step_weight, sign, sample, count, lat):
    rows, width = pieces[0].shape
    blocks = len(pieces) // 2
    tokens = len(pieces) * rows
    return pl.pallas_call(
        functools.partial(early_kernel, offsets),
        in_specs=[SMEM] * 6 + [HBM] * len(pieces),
        out_specs=[VMEM] * 5,
        out_shape=[
            jax.ShapeDtypeStruct((blocks, count, lat, 2 * rows), jnp.float32),
            jax.ShapeDtypeStruct((blocks, 2, 8, 2 * rows), jnp.float32),
            jax.ShapeDtypeStruct((8, rows), jnp.float32),
            jax.ShapeDtypeStruct((len(pieces), rows, width), jnp.bfloat16),
            jax.ShapeDtypeStruct((count, lat + 16, tokens), jnp.bfloat16),
        ],
        scratch_shapes=[
            pltpu.VMEM((blocks, count, 2 * rows, HD), jnp.bfloat16),
            pltpu.SemaphoreType.DMA((len(pieces),)),
        ],
        compiler_params=pltpu.CompilerParams(vmem_limit_bytes=SMALL_VMEM if len(pieces) <= 8 else LARGE_VMEM),
        cost_estimate=pl.CostEstimate(
            flops=count * tokens * tokens * 2 * (HD + lat),
            bytes_accessed=tokens * count * 3 * HD * 2,
            transcendentals=count * tokens * tokens,
        ),
        name="attend_early",
    )(span_frames, me, timestep, step_weight, sign, sample, *pieces)


def attend_late(pieces, offsets, late, chosen, groups, early, span_frames, me, count, lat):
    rows, width = pieces[0].shape
    half = len(offsets) // 2 + 1
    tokens = 2 * half * rows
    return pl.pallas_call(
        functools.partial(late_kernel, offsets, late, chosen, groups),
        in_specs=[SMEM] * 2 + [HBM] * 2 + [VMEM] * len(early),
        out_specs=[VMEM] * len(groups),
        out_shape=[
            jax.ShapeDtypeStruct((half // 2, lat, rows), jnp.bfloat16 if g else jnp.float32) for g in groups
        ],
        scratch_shapes=[
            pltpu.VMEM((2, rows, width), jnp.bfloat16),
            pltpu.VMEM((count, lat + 16, 2 * rows), jnp.bfloat16),
            pltpu.SemaphoreType.DMA((2,)),
        ],
        compiler_params=pltpu.CompilerParams(vmem_limit_bytes=SMALL_VMEM if half <= 4 else LARGE_VMEM),
        cost_estimate=pl.CostEstimate(
            flops=count * tokens * rows * 2 * (HD + lat),
            bytes_accessed=tokens * count * 3 * HD * 2,
            transcendentals=count * tokens * rows,
        ),
        name="attend_late",
    )(span_frames, me, *pieces, *early)


def swap(array, axis, offset):
    size = lax.axis_size(axis)
    return lax.ppermute(array, axis, [(i, i ^ offset) for i in range(size)])


def body(qkv, readout, step_weight, timestep, span_frames):
    seq_count = lax.axis_size("seq")
    mp_count = lax.axis_size("mp")
    half = seq_count // 2
    count = HEADS // seq_count
    lat = readout.shape[2]
    me = lax.axis_index("seq").astype(jnp.int32).reshape(1)
    mp_index = lax.axis_index("mp").astype(jnp.int32)
    sample_count = mp_count // 2
    model_index = mp_index // sample_count
    sample = (mp_index % sample_count).reshape(1)
    sign = jnp.where(model_index == 1, 1.0, -1.0).astype(jnp.float32).reshape(1)
    model = model_index.reshape(1)
    readout_t = jnp.swapaxes(readout, 1, 2)

    pieces = [None] * seq_count
    for n in range(half):
        k = seq_count - 1 - n
        pieces[k] = swap(pack(me, model, qkv, readout_t, k, count, [pieces[k + 2]] if n > 1 else [], n > 1, n == 0), "seq", k)
    for k in range(half - 1, 0, -1):
        after = [] if k == half - 1 else [pieces[k + 1], pieces[seq_count - 1]] if k > 1 else [pieces[half - 1]]
        pieces[k] = swap(pack(me, model, qkv, readout_t, k, count, after), "seq", k)
    pieces[0] = pack(me, model, qkv, readout_t, 0, count, [pieces[half - 1]])
    late = [half, half + 1]
    early = [k for k in range(seq_count) if k not in late]
    merged = attend_early(
        [pieces[k] for k in early], early, span_frames, me, timestep, step_weight, sign, sample, count, lat
    )
    blocks = len(early) // 2
    far_blocks = [blocks] + list(range(half // 2, blocks))
    ends = [pieces[k] for k in late]
    given = attend_late(ends, early, late, far_blocks, [2, 3], merged, span_frames, me, count, lat)
    near_blocks = list(range(half // 2 - 1, -1, -1))
    given = attend_late(ends, early, late, near_blocks, [0, 1], merged, span_frames, me, count, lat) + given
    size = half // 2
    while True:
        keep = given[0]
        for n in range(len(given) - 1, 0, -1):
            keep = keep + swap(given[n], "seq", n * size).astype(jnp.float32)
        if size == 1:
            break
        radix = min(4, size)
        size //= radix
        given = [keep[n * size : (n + 1) * size] for n in range(radix)]
    total = keep[0]
    offset = 1
    while offset < mp_count:
        radix = min(4, mp_count // offset)
        own = total
        for n in range(radix - 1, 0, -1):
            total = total + swap(own, "mp", offset * n)
        offset *= radix
    return total.T


def solution(mesh):
    return jax.shard_map(
        body,
        mesh=mesh,
        in_specs=(P("mp", "seq", None), P(), P(), P(), P()),
        out_specs=P("seq", None),
        check_vma=False,
    )
```

```python
import functools
import math

import jax
import jax.numpy as jnp
from jax import lax
from jax.experimental import pallas as pl
from jax.experimental.pallas import tpu as pltpu
from jax.sharding import PartitionSpec as P

HEADS = 32
HD = 128
FRAME_TOK = 64
NT = (((1,), (1,)), ((), ()))
LOG2_SCALE = math.log2(math.e) / math.sqrt(HD)
LOWEST = -1e30
NEXT_WAVE = 0
SMALL_VMEM = 24 * 1024 * 1024
LARGE_VMEM = 60 * 1024 * 1024
SMEM = pl.BlockSpec(memory_space=pltpu.SMEM)
VMEM = pl.BlockSpec(memory_space=pltpu.VMEM)
HBM = pl.BlockSpec(memory_space=pltpu.HBM)


def fold(readout, values):
    return lax.dot_general(readout, values, NT, preferred_element_type=jnp.float32).astype(jnp.bfloat16)


def value_place(h, count, lat):
    return (h * lat) % HD, count * 2 * HD + (h * lat // HD) * HD


def pack_kernel(k, me_ref, model_ref, qkv_ref, readout_ref, *refs):
    out_ref, values, readout, sems = refs[-4:]
    rows = out_ref.shape[0]
    count, lat = values.shape[0], readout.shape[0]
    first = (me_ref[0] ^ k) * count

    def columns(h, part, width):
        return pl.ds(pl.multiple_of(((first + h) * 3 + part) * HD, HD), width)

    copies = [
        pltpu.make_async_copy(
            readout_ref.at[model_ref[0], :, pl.ds(pl.multiple_of(first * HD, HD), count * HD)], readout, sems.at[2 * count]
        )
    ]
    for h in range(count):
        copies.append(pltpu.make_async_copy(qkv_ref.at[0, :, columns(h, 2, HD)], values.at[h], sems.at[h]))
    for h in range(count):
        target = out_ref.at[:, h * 2 * HD : (h + 1) * 2 * HD]
        copies.append(pltpu.make_async_copy(qkv_ref.at[0, :, columns(h, 0, 2 * HD)], target, sems.at[count + h]))
    for copy in copies:
        copy.start()
    copies[0].wait()
    for h in range(count):
        copies[1 + h].wait()
        row, column = value_place(h, count, lat)
        out_ref[row : row + lat, column : column + HD] = fold(readout[:, h * HD : (h + 1) * HD], values[h])
    for copy in copies[1 + count :]:
        copy.wait()


def pack(me, model, qkv, readout_t, k, count, after, wave=False):
    rows = qkv.shape[1]
    lat = readout_t.shape[1]
    width = count * 2 * HD + -(-count * lat // HD) * HD
    return pl.pallas_call(
        functools.partial(pack_kernel, k),
        in_specs=[SMEM, SMEM] + [HBM] * (2 + len(after)),
        out_specs=VMEM,
        out_shape=jax.ShapeDtypeStruct((rows, width), jnp.bfloat16),
        scratch_shapes=[
            pltpu.VMEM((count, rows, HD), jnp.bfloat16),
            pltpu.VMEM((lat, count * HD), jnp.bfloat16),
            pltpu.SemaphoreType.DMA((2 * count + 1,)),
        ],
        compiler_params=pltpu.CompilerParams(vmem_limit_bytes=SMALL_VMEM),
        cost_estimate=pl.CostEstimate(
            flops=NEXT_WAVE if wave else 0, bytes_accessed=rows * width * 4, transcendentals=0
        ),
        name="pack",
    )(me, model, qkv, readout_t, *after)


def mask_rows(frames_ref, me, rows, query_offsets, key_offsets):
    columns = lax.broadcasted_iota(jnp.int32, (1, rows), 1)
    places = jnp.concatenate([(me ^ k) * rows + columns for k in query_offsets], axis=1)
    end = frames_ref[0] * FRAME_TOK
    bound = jnp.full(places.shape, end, jnp.int32)
    for c in range(1, frames_ref.shape[0]):
        later = end + frames_ref[c] * FRAME_TOK
        bound = jnp.where(places >= end, later, bound)
        end = later
    return [
        jnp.where((me ^ k) * rows + start < bound, 0.0, -jnp.inf)
        for k in key_offsets
        for start in range(0, rows, FRAME_TOK)
    ]


def run_units(units, lat):
    frames = [tile() for tile in units[0][0]]
    for u, (_, values, shifts, finish) in enumerate(units):
        ahead = list(units[u + 1][0]) if u + 1 < len(units) else []
        peaks = [jnp.max(f, axis=0, keepdims=True) + s for f, s in zip(sum(frames, []), shifts)]
        peak = jnp.maximum(functools.reduce(jnp.maximum, peaks), LOWEST)
        following, summed, start = [], None, 0
        for t, tile in enumerate(frames):
            for _ in range(-(-(len(ahead) - len(following)) // (len(frames) - t))):
                following.append(ahead[len(following)]())
            weights = [
                jnp.exp2((f + (s - peak)) * LOG2_SCALE).astype(jnp.bfloat16)
                for f, s in zip(tile, shifts[start : start + len(tile)])
            ]
            start += len(tile)
            part = jnp.dot(values[t](), jnp.concatenate(weights, axis=0), preferred_element_type=jnp.float32)
            summed = part if summed is None else summed + part
        finish(summed[:lat], summed[lat : lat + 1], peak)
        frames = following


def score_tile(keys, queries):
    scores = lax.dot_general(keys(), queries(), NT, preferred_element_type=jnp.float32)
    return [scores[start : start + FRAME_TOK] for start in range(0, scores.shape[0], FRAME_TOK)]


def stage_values(folded, pieces, lat):
    count = folded.shape[0]
    rows = pieces[0].shape[0]
    for i in range(count):
        row, column = value_place(i, count, lat)
        for n, piece in enumerate(pieces):
            folded[i, :lat, n * rows : (n + 1) * rows] = piece[row : row + lat, column : column + HD]
        folded[i, lat:] = jnp.ones_like(folded[i, lat:])


def pairs_of(pieces, i, what):
    column = (2 * i + what) * HD

    def read(n):
        return lambda: jnp.concatenate([pieces[n][:, column : column + HD], pieces[n + 1][:, column : column + HD]], axis=0)

    return [read(n) for n in range(0, len(pieces), 2)]


def early_kernel(offsets, frames_ref, me_ref, timestep_ref, step_weight_ref, sign_ref, sample_ref, *refs):
    count_pieces = len(offsets)
    arrived = refs[:count_pieces]
    sums_ref, stats_ref, factor_ref, pieces, folded, asked, sems = refs[-7:]
    me = me_ref[0]
    rows = pieces.shape[1]
    lat = sums_ref.shape[2]
    count = folded.shape[0]
    blocks = count_pieces // 2
    copies = [pltpu.make_async_copy(arrived[n], pieces.at[n], sems.at[n]) for n in range(count_pieces)]
    for copy in copies:
        copy.start()
    factor_ref[...] = jnp.full(factor_ref.shape, sign_ref[0] * step_weight_ref[timestep_ref[sample_ref[0]]])
    for copy in copies:
        copy.wait()
    pieces = [pieces.at[n] for n in range(count_pieces)]
    stage_values(folded, pieces, lat)
    for i in range(count):
        for b, read in enumerate(pairs_of(pieces, i, 0)):
            asked[b, i] = read()
    half = count_pieces // 2 + 1

    def some_blocks(b, carry):
        q = [2 * b, 2 * b + 1]
        shifts = mask_rows(frames_ref, me, rows, [jnp.where(n < half, n, n + 2) for n in q], offsets)
        peaks, totals, units = [], [], []
        for i in range(count):

            def finish(summed, total, peak, i=i):
                sums_ref[b, i] = summed
                peaks.append(peak)
                totals.append(total)

            tiles = [
                functools.partial(score_tile, keys, lambda i=i: asked[b, i]) for keys in pairs_of(pieces, i, 1)
            ]
            values = [lambda i=i, t=t: folded[i, :, t * 2 * rows : (t + 1) * 2 * rows] for t in range(blocks)]
            units.append((tiles, values, shifts, finish))
        run_units(units, lat)
        rest = [jnp.ones_like(peaks[0])] * (stats_ref.shape[2] - count)
        stats_ref[b, 0] = jnp.concatenate(peaks + rest, axis=0)
        stats_ref[b, 1] = jnp.concatenate(totals + rest, axis=0)
        return carry

    lax.fori_loop(0, blocks, some_blocks, 0)


def late_kernel(offsets, late, chosen, groups, frames_ref, me_ref, *refs):
    early = len(offsets)
    arrived = refs[:2]
    sums_ref, stats_ref, factor_ref, early_ref, early_folded, *out_refs, late_pieces, folded, sems = refs[2:]
    copies = [pltpu.make_async_copy(arrived[n], late_pieces.at[n], sems.at[n]) for n in range(2)]
    for copy in copies:
        copy.start()
    me = me_ref[0]
    size, lat, rows = out_refs[0].shape
    count = folded.shape[0]
    for copy in copies:
        copy.wait()
    pieces = [early_ref.at[n] for n in range(early)] + [late_pieces.at[n] for n in range(2)]
    stage_values(folded, pieces[early:], lat)
    factor = factor_ref[:1]
    every = list(offsets) + list(late)
    results = {}

    def add(b, part):
        results[b] = part if b not in results else results[b] + part

    def write(b):
        for j in range(2):
            k = every[2 * b + j]
            out_ref = out_refs[groups.index(k // size)]
            out_ref[k % size] = (results[b][:, j * rows : (j + 1) * rows] * factor).astype(out_ref.dtype)

    units = []
    blocks = early // 2
    for b in chosen:
        keys_in = range(blocks + 1) if b == blocks else [blocks]
        key_offsets = [every[2 * t + j] for t in keys_in for j in range(2)]
        shifts = mask_rows(frames_ref, me, rows, every[2 * b : 2 * b + 2], key_offsets)
        for i in range(count):

            def finish(summed, total, peak, b=b, i=i):
                if b < blocks:
                    before = stats_ref[b, 0, i : i + 1]
                    highest = jnp.maximum(before, peak)
                    old = jnp.exp2((before - highest) * LOG2_SCALE)
                    new = jnp.exp2((peak - highest) * LOG2_SCALE)
                    both = stats_ref[b, 1, i : i + 1] * old + total * new
                    add(b, sums_ref[b, i] * (old / both) + summed * (new / both))
                else:
                    add(b, summed / total)
                if i == count - 1:
                    write(b)

            queries = pairs_of(pieces, i, 0)[b]
            keys = pairs_of(pieces, i, 1)
            tiles = [functools.partial(score_tile, keys[t], queries) for t in keys_in]
            values = [
                lambda i=i, t=t: folded[i] if t == blocks else early_folded[i, :, t * 2 * rows : (t + 1) * 2 * rows]
                for t in keys_in
            ]
            units.append((tiles, values, shifts, finish))
    run_units(units, lat)


def attend_early(pieces, offsets, span_frames, me, timestep, step_weight, sign, sample, count, lat):
    rows, width = pieces[0].shape
    blocks = len(pieces) // 2
    tokens = len(pieces) * rows
    return pl.pallas_call(
        functools.partial(early_kernel, offsets),
        in_specs=[SMEM] * 6 + [HBM] * len(pieces),
        out_specs=[VMEM] * 5,
        out_shape=[
            jax.ShapeDtypeStruct((blocks, count, lat, 2 * rows), jnp.float32),
            jax.ShapeDtypeStruct((blocks, 2, 8, 2 * rows), jnp.float32),
            jax.ShapeDtypeStruct((8, rows), jnp.float32),
            jax.ShapeDtypeStruct((len(pieces), rows, width), jnp.bfloat16),
            jax.ShapeDtypeStruct((count, lat + 16, tokens), jnp.bfloat16),
        ],
        scratch_shapes=[
            pltpu.VMEM((blocks, count, 2 * rows, HD), jnp.bfloat16),
            pltpu.SemaphoreType.DMA((len(pieces),)),
        ],
        compiler_params=pltpu.CompilerParams(vmem_limit_bytes=SMALL_VMEM if len(pieces) <= 8 else LARGE_VMEM),
        cost_estimate=pl.CostEstimate(
            flops=count * tokens * tokens * 2 * (HD + lat),
            bytes_accessed=tokens * count * 3 * HD * 2,
            transcendentals=count * tokens * tokens,
        ),
        name="attend_early",
    )(span_frames, me, timestep, step_weight, sign, sample, *pieces)


def attend_late(pieces, offsets, late, chosen, groups, early, span_frames, me, count, lat):
    rows, width = pieces[0].shape
    half = len(offsets) // 2 + 1
    tokens = 2 * half * rows
    return pl.pallas_call(
        functools.partial(late_kernel, offsets, late, chosen, groups),
        in_specs=[SMEM] * 2 + [HBM] * 2 + [VMEM] * len(early),
        out_specs=[VMEM] * len(groups),
        out_shape=[
            jax.ShapeDtypeStruct((half // 2, lat, rows), jnp.bfloat16 if g else jnp.float32) for g in groups
        ],
        scratch_shapes=[
            pltpu.VMEM((2, rows, width), jnp.bfloat16),
            pltpu.VMEM((count, lat + 16, 2 * rows), jnp.bfloat16),
            pltpu.SemaphoreType.DMA((2,)),
        ],
        compiler_params=pltpu.CompilerParams(vmem_limit_bytes=SMALL_VMEM if half <= 4 else LARGE_VMEM),
        cost_estimate=pl.CostEstimate(
            flops=count * tokens * rows * 4 * (HD + lat),
            bytes_accessed=tokens * count * 3 * HD * 2,
            transcendentals=count * tokens * rows * 2,
        ),
        name="attend_late",
    )(span_frames, me, *pieces, *early)


def swap(array, axis, offset):
    size = lax.axis_size(axis)
    return lax.ppermute(array, axis, [(i, i ^ offset) for i in range(size)])


def body(qkv, readout, step_weight, timestep, span_frames):
    seq_count = lax.axis_size("seq")
    mp_count = lax.axis_size("mp")
    half = seq_count // 2
    count = HEADS // seq_count
    lat = readout.shape[2]
    me = lax.axis_index("seq").astype(jnp.int32).reshape(1)
    mp_index = lax.axis_index("mp").astype(jnp.int32)
    sample_count = mp_count // 2
    model_index = mp_index // sample_count
    sample = (mp_index % sample_count).reshape(1)
    sign = jnp.where(model_index == 1, 1.0, -1.0).astype(jnp.float32).reshape(1)
    model = model_index.reshape(1)
    readout_t = jnp.swapaxes(readout, 1, 2)

    pieces = [None] * seq_count
    for n in range(half):
        k = seq_count - 1 - n
        pieces[k] = swap(pack(me, model, qkv, readout_t, k, count, [pieces[k + 2]] if n > 1 else [], n > 1), "seq", k)
    pieces[0] = pack(me, model, qkv, readout_t, 0, count, [pieces[seq_count - 1]])
    for k in [half - 1] + list(range(1, half - 1)):
        after = [pieces[k - 1], pieces[half - 1], pieces[seq_count - 1]] if k not in (1, half - 1) else []
        pieces[k] = swap(pack(me, model, qkv, readout_t, k, count, after), "seq", k)
    late = [half, half + 1]
    early = [k for k in range(seq_count) if k not in late]
    merged = attend_early(
        [pieces[k] for k in early], early, span_frames, me, timestep, step_weight, sign, sample, count, lat
    )
    blocks = len(early) // 2
    ends = [pieces[k] for k in late]
    order = [blocks] + list(range(blocks))
    given = attend_late(ends, early, late, order, [0, 1, 2, 3], merged, span_frames, me, count, lat)
    size = half // 2
    while True:
        keep = given[0]
        for n in range(len(given) - 1, 0, -1):
            keep = keep + swap(given[n], "seq", n * size).astype(jnp.float32)
        if size == 1:
            break
        radix = min(4, size)
        size //= radix
        given = [keep[n * size : (n + 1) * size] for n in range(radix)]
    total = keep[0]
    offset = 1
    while offset < mp_count:
        radix = min(4, mp_count // offset)
        own = total
        for n in range(radix - 1, 0, -1):
            total = total + swap(own, "mp", offset * n)
        offset *= radix
    return total.T


def solution(mesh):
    return jax.shard_map(
        body,
        mesh=mesh,
        in_specs=(P("mp", "seq", None), P(), P(), P(), P()),
        out_specs=P("seq", None),
        check_vma=False,
    )
```

```python
import functools
import math

import jax
import jax.numpy as jnp
from jax import lax
from jax.experimental import pallas as pl
from jax.experimental.pallas import tpu as pltpu
from jax.sharding import PartitionSpec as P

HEADS = 32
HD = 128
FRAME_TOK = 64
NT = (((1,), (1,)), ((), ()))
LOG2_SCALE = math.log2(math.e) / math.sqrt(HD)
LOWEST = -1e30
SPLIT_COST = 0
SMALL_VMEM = 24 * 1024 * 1024
LARGE_VMEM = 60 * 1024 * 1024
SMEM = pl.BlockSpec(memory_space=pltpu.SMEM)
VMEM = pl.BlockSpec(memory_space=pltpu.VMEM)
HBM = pl.BlockSpec(memory_space=pltpu.HBM)


def fold(readout, values):
    return lax.dot_general(readout, values, NT, preferred_element_type=jnp.float32).astype(jnp.bfloat16)


def value_place(h, count, lat):
    return (h * lat) % HD, count * 2 * HD + (h * lat // HD) * HD


def pack_kernel(head_of, me_ref, model_ref, qkv_ref, readout_ref, *refs):
    out_ref, values, readout, sems = refs[-4:]
    rows = out_ref.shape[0]
    count, lat = values.shape[0], readout.shape[0]
    first = head_of(me_ref[0])

    def columns(h, part, width):
        return pl.ds(pl.multiple_of(((first + h) * 3 + part) * HD, HD), width)

    copies = [
        pltpu.make_async_copy(
            readout_ref.at[model_ref[0], :, pl.ds(pl.multiple_of(first * HD, HD), count * HD)], readout, sems.at[2 * count]
        )
    ]
    for h in range(count):
        copies.append(pltpu.make_async_copy(qkv_ref.at[0, :, columns(h, 2, HD)], values.at[h], sems.at[h]))
    for h in range(count):
        target = out_ref.at[:, h * 2 * HD : (h + 1) * 2 * HD]
        copies.append(pltpu.make_async_copy(qkv_ref.at[0, :, columns(h, 0, 2 * HD)], target, sems.at[count + h]))
    for copy in copies:
        copy.start()
    copies[0].wait()
    for h in range(count):
        copies[1 + h].wait()
        row, column = value_place(h, count, lat)
        out_ref[row : row + lat, column : column + HD] = fold(readout[:, h * HD : (h + 1) * HD], values[h])
    for copy in copies[1 + count :]:
        copy.wait()


def pack(me, model, qkv, readout_t, head_of, count, after):
    rows = qkv.shape[1]
    lat = readout_t.shape[1]
    width = count * 2 * HD + -(-count * lat // HD) * HD
    return pl.pallas_call(
        functools.partial(pack_kernel, head_of),
        in_specs=[SMEM, SMEM] + [HBM] * (2 + len(after)),
        out_specs=VMEM,
        out_shape=jax.ShapeDtypeStruct((rows, width), jnp.bfloat16),
        scratch_shapes=[
            pltpu.VMEM((count, rows, HD), jnp.bfloat16),
            pltpu.VMEM((lat, count * HD), jnp.bfloat16),
            pltpu.SemaphoreType.DMA((2 * count + 1,)),
        ],
        compiler_params=pltpu.CompilerParams(vmem_limit_bytes=SMALL_VMEM),
        cost_estimate=pl.CostEstimate(
            flops=0, bytes_accessed=rows * width * 4, transcendentals=0
        ),
        name="pack",
    )(me, model, qkv, readout_t, *after)


def queries_kernel(head_of, me_ref, qkv_ref, *refs):
    out_ref, sems = refs[-2:]
    count = out_ref.shape[1] // HD
    first = head_of(me_ref[0])
    copies = []
    for h in range(count):
        source = qkv_ref.at[0, :, pl.ds(pl.multiple_of((first + h) * 3 * HD, HD), HD)]
        copies.append(pltpu.make_async_copy(source, out_ref.at[:, h * HD : (h + 1) * HD], sems.at[h]))
    for copy in copies:
        copy.start()
    for copy in copies:
        copy.wait()


def pack_queries(me, qkv, head_of, count, after):
    rows = qkv.shape[1]
    return pl.pallas_call(
        functools.partial(queries_kernel, head_of),
        in_specs=[SMEM] + [HBM] * (1 + len(after)),
        out_specs=VMEM,
        out_shape=jax.ShapeDtypeStruct((rows, count * HD), jnp.bfloat16),
        scratch_shapes=[pltpu.SemaphoreType.DMA((count,))],
        compiler_params=pltpu.CompilerParams(vmem_limit_bytes=SMALL_VMEM),
        cost_estimate=pl.CostEstimate(flops=0, bytes_accessed=rows * count * HD * 4, transcendentals=0),
        name="pack_queries",
    )(me, qkv, *after)


def mask_rows(frames_ref, me, rows, query_offsets, key_offsets):
    columns = lax.broadcasted_iota(jnp.int32, (1, rows), 1)
    places = jnp.concatenate([(me ^ k) * rows + columns for k in query_offsets], axis=1)
    end = frames_ref[0] * FRAME_TOK
    bound = jnp.full(places.shape, end, jnp.int32)
    for c in range(1, frames_ref.shape[0]):
        later = end + frames_ref[c] * FRAME_TOK
        bound = jnp.where(places >= end, later, bound)
        end = later
    return [
        jnp.where((me ^ k) * rows + start < bound, 0.0, -jnp.inf)
        for k in key_offsets
        for start in range(0, rows, FRAME_TOK)
    ]


def run_units(units, lat):
    frames = [tile() for tile in units[0][0]]
    for u, (_, values, shifts, finish) in enumerate(units):
        ahead = list(units[u + 1][0]) if u + 1 < len(units) else []
        peaks = [jnp.max(f, axis=0, keepdims=True) + s for f, s in zip(sum(frames, []), shifts)]
        peak = jnp.maximum(functools.reduce(jnp.maximum, peaks), LOWEST)
        following, summed, start = [], None, 0
        for t, tile in enumerate(frames):
            for _ in range(-(-(len(ahead) - len(following)) // (len(frames) - t))):
                following.append(ahead[len(following)]())
            weights = [
                jnp.exp2((f + (s - peak)) * LOG2_SCALE).astype(jnp.bfloat16)
                for f, s in zip(tile, shifts[start : start + len(tile)])
            ]
            start += len(tile)
            part = jnp.dot(values[t](), jnp.concatenate(weights, axis=0), preferred_element_type=jnp.float32)
            summed = part if summed is None else summed + part
        finish(summed[:lat], summed[lat : lat + 1], peak)
        frames = following


def score_tile(keys, queries):
    scores = lax.dot_general(keys(), queries(), NT, preferred_element_type=jnp.float32)
    return [scores[start : start + FRAME_TOK] for start in range(0, scores.shape[0], FRAME_TOK)]


def stage_values(folded, pieces, lat):
    count = folded.shape[0]
    rows = pieces[0].shape[0]
    for i in range(count):
        row, column = value_place(i, count, lat)
        for n, piece in enumerate(pieces):
            folded[i, :lat, n * rows : (n + 1) * rows] = piece[row : row + lat, column : column + HD]
        folded[i, lat:] = jnp.ones_like(folded[i, lat:])


def pairs_of(pieces, i, what):
    column = (2 * i + what) * HD

    def read(n):
        return lambda: jnp.concatenate([pieces[n][:, column : column + HD], pieces[n + 1][:, column : column + HD]], axis=0)

    return [read(n) for n in range(0, len(pieces), 2)]


def early_kernel(offsets, frames_ref, me_ref, timestep_ref, step_weight_ref, sign_ref, sample_ref, *refs):
    count_pieces = len(offsets)
    arrived = refs[:count_pieces]
    sums_ref, stats_ref, factor_ref, pieces, folded, asked, sems = refs[-7:]
    me = me_ref[0]
    rows = pieces.shape[1]
    lat = sums_ref.shape[2]
    count = folded.shape[0]
    blocks = count_pieces // 2
    copies = [pltpu.make_async_copy(arrived[n], pieces.at[n], sems.at[n]) for n in range(count_pieces)]
    for copy in copies:
        copy.start()
    factor_ref[...] = jnp.full(factor_ref.shape, sign_ref[0] * step_weight_ref[timestep_ref[sample_ref[0]]])
    for copy in copies:
        copy.wait()
    pieces = [pieces.at[n] for n in range(count_pieces)]
    stage_values(folded, pieces, lat)
    for i in range(count):
        for b, read in enumerate(pairs_of(pieces, i, 0)):
            asked[b, i] = read()
    half = count_pieces // 2 + 1

    def some_blocks(b, carry):
        q = [2 * b, 2 * b + 1]
        shifts = mask_rows(frames_ref, me, rows, [jnp.where(n < half, n, n + 2) for n in q], offsets)
        peaks, totals, units = [], [], []
        for i in range(count):

            def finish(summed, total, peak, i=i):
                sums_ref[b, i] = summed
                peaks.append(peak)
                totals.append(total)

            tiles = [
                functools.partial(score_tile, keys, lambda i=i: asked[b, i]) for keys in pairs_of(pieces, i, 1)
            ]
            values = [lambda i=i, t=t: folded[i, :, t * 2 * rows : (t + 1) * 2 * rows] for t in range(blocks)]
            units.append((tiles, values, shifts, finish))
        run_units(units, lat)
        rest = [jnp.ones_like(peaks[0])] * (stats_ref.shape[2] - count)
        stats_ref[b, 0] = jnp.concatenate(peaks + rest, axis=0)
        stats_ref[b, 1] = jnp.concatenate(totals + rest, axis=0)
        return carry

    lax.fori_loop(0, blocks, some_blocks, 0)


def late_kernel(offsets, late, chosen, groups, frames_ref, me_ref, *refs):
    early = len(offsets)
    arrived = refs[:2]
    sums_ref, stats_ref, factor_ref, early_ref, early_folded, *out_refs, late_pieces, folded, sems = refs[2:]
    split_ref = out_refs.pop(0) if len(out_refs) > len(groups) else None
    copies = [pltpu.make_async_copy(arrived[n], late_pieces.at[n], sems.at[n]) for n in range(2)]
    for copy in copies:
        copy.start()
    me = me_ref[0]
    size, lat, rows = out_refs[0].shape
    count = folded.shape[0]
    for copy in copies:
        copy.wait()
    pieces = [early_ref.at[n] for n in range(early)] + [late_pieces.at[n] for n in range(2)]
    stage_values(folded, pieces[early:], lat)
    factor = factor_ref[:1]
    every = list(offsets) + list(late)
    results = {}

    def add(b, part):
        results[b] = part if b not in results else results[b] + part

    def write(b):
        for j in range(2):
            k = every[2 * b + j]
            out_ref = out_refs[groups.index(k // size)]
            part = results[b][:, j * rows : (j + 1) * rows]
            if split_ref is not None:
                part = part + split_ref[k]
            out_ref[k % size] = (part * factor).astype(out_ref.dtype)

    units = []
    blocks = early // 2
    for b in chosen:
        keys_in = range(blocks + 1) if b == blocks else [blocks]
        key_offsets = [every[2 * t + j] for t in keys_in for j in range(2)]
        shifts = mask_rows(frames_ref, me, rows, every[2 * b : 2 * b + 2], key_offsets)
        for i in range(count):

            def finish(summed, total, peak, b=b, i=i):
                if b < blocks:
                    before = stats_ref[b, 0, i : i + 1]
                    highest = jnp.maximum(before, peak)
                    old = jnp.exp2((before - highest) * LOG2_SCALE)
                    new = jnp.exp2((peak - highest) * LOG2_SCALE)
                    both = stats_ref[b, 1, i : i + 1] * old + total * new
                    add(b, sums_ref[b, i] * (old / both) + summed * (new / both))
                else:
                    add(b, summed / total)
                if i == count - 1:
                    write(b)

            queries = pairs_of(pieces, i, 0)[b]
            keys = pairs_of(pieces, i, 1)
            tiles = [functools.partial(score_tile, keys[t], queries) for t in keys_in]
            values = [
                lambda i=i, t=t: folded[i] if t == blocks else early_folded[i, :, t * 2 * rows : (t + 1) * 2 * rows]
                for t in keys_in
            ]
            units.append((tiles, values, shifts, finish))
    run_units(units, lat)


def split_kernel(half, frames_ref, me_ref, *refs):
    near, far = refs[:half], refs[half : 2 * half]
    sums_ref, stats_ref, near_pieces, far_pieces, folded, asked, sems = refs[-7:]
    copies = [pltpu.make_async_copy(near[k], near_pieces.at[k], sems.at[k]) for k in range(half)]
    copies += [pltpu.make_async_copy(far[k], far_pieces.at[k], sems.at[half + k]) for k in range(half)]
    for copy in copies:
        copy.start()
    for copy in copies:
        copy.wait()
    me = me_ref[0]
    rows = near_pieces.shape[1]
    lat = sums_ref.shape[2]
    count = folded.shape[0]
    pieces = [near_pieces.at[k] for k in range(half)]
    stage_values(folded, pieces, lat)
    for i in range(count):
        for b, read in enumerate(pairs_of(pieces, i, 0)):
            asked[b, i] = read()
        for k in range(half):
            asked[half // 2 + k // 2, i, (k % 2) * rows : (k % 2 + 1) * rows] = far_pieces[k, :, i * HD : (i + 1) * HD]

    def some_blocks(b, carry):
        shifts = mask_rows(frames_ref, me, rows, [2 * b, 2 * b + 1], range(half))
        peaks, totals, units = [], [], []
        for i in range(count):

            def finish(summed, total, peak, i=i):
                sums_ref[b, i] = summed
                peaks.append(peak)
                totals.append(total)

            tiles = [functools.partial(score_tile, keys, lambda i=i: asked[b, i]) for keys in pairs_of(pieces, i, 1)]
            values = [lambda i=i, t=t: folded[i, :, t * 2 * rows : (t + 1) * 2 * rows] for t in range(half // 2)]
            units.append((tiles, values, shifts, finish))
        run_units(units, lat)
        rest = [jnp.ones_like(peaks[0])] * (stats_ref.shape[2] - count)
        stats_ref[b, 0] = jnp.concatenate(peaks + rest, axis=0)
        stats_ref[b, 1] = jnp.concatenate(totals + rest, axis=0)
        return carry

    lax.fori_loop(0, half, some_blocks, 0)


def attend_split(near, far, span_frames, me, count, lat):
    half = len(near)
    rows, width = near[0].shape
    return pl.pallas_call(
        functools.partial(split_kernel, half),
        in_specs=[SMEM, SMEM] + [HBM] * (2 * half),
        out_specs=[VMEM, VMEM],
        out_shape=[
            jax.ShapeDtypeStruct((half, count, lat, 2 * rows), jnp.float32),
            jax.ShapeDtypeStruct((half, 2, 8, 2 * rows), jnp.float32),
        ],
        scratch_shapes=[
            pltpu.VMEM((half, rows, width), jnp.bfloat16),
            pltpu.VMEM((half, rows, count * HD), jnp.bfloat16),
            pltpu.VMEM((count, lat + 16, half * rows), jnp.bfloat16),
            pltpu.VMEM((half, count, 2 * rows, HD), jnp.bfloat16),
            pltpu.SemaphoreType.DMA((2 * half,)),
        ],
        compiler_params=pltpu.CompilerParams(vmem_limit_bytes=SMALL_VMEM),
        cost_estimate=pl.CostEstimate(
            flops=SPLIT_COST,
            bytes_accessed=0,
            transcendentals=0,
        ),
        name="attend_split",
    )(span_frames, me, *near, *far)


def combine_kernel(count, sums_ref, stats_ref, other_ref, out_ref):
    rows = out_ref.shape[2]
    blocks = sums_ref.shape[0]
    for b in range(blocks):
        o = b ^ (blocks // 2)
        peak, other_peak = stats_ref[b, 0], other_ref[o, 0]
        highest = jnp.maximum(peak, other_peak)
        own = jnp.exp2((peak - highest) * LOG2_SCALE)
        both = stats_ref[b, 1] * own + other_ref[o, 1] * jnp.exp2((other_peak - highest) * LOG2_SCALE)
        weight = own / both
        result = sums_ref[b, 0] * weight[:1]
        for i in range(1, count):
            result = result + sums_ref[b, i] * weight[i : i + 1]
        for j in range(2):
            out_ref[b * 2 + j] = result[:, j * rows : (j + 1) * rows]


def combine(sums, stats, other):
    half, count, lat, block = sums.shape
    return pl.pallas_call(
        functools.partial(combine_kernel, count),
        in_specs=[VMEM] * 3,
        out_specs=VMEM,
        out_shape=jax.ShapeDtypeStruct((2 * half, lat, block // 2), jnp.float32),
        compiler_params=pltpu.CompilerParams(vmem_limit_bytes=SMALL_VMEM),
        cost_estimate=pl.CostEstimate(flops=0, bytes_accessed=sums.size * 4, transcendentals=0),
        name="combine",
    )(sums, stats, other)


def attend_early(pieces, offsets, span_frames, me, timestep, step_weight, sign, sample, count, lat):
    rows, width = pieces[0].shape
    blocks = len(pieces) // 2
    tokens = len(pieces) * rows
    return pl.pallas_call(
        functools.partial(early_kernel, offsets),
        in_specs=[SMEM] * 6 + [HBM] * len(pieces),
        out_specs=[VMEM] * 5,
        out_shape=[
            jax.ShapeDtypeStruct((blocks, count, lat, 2 * rows), jnp.float32),
            jax.ShapeDtypeStruct((blocks, 2, 8, 2 * rows), jnp.float32),
            jax.ShapeDtypeStruct((8, rows), jnp.float32),
            jax.ShapeDtypeStruct((len(pieces), rows, width), jnp.bfloat16),
            jax.ShapeDtypeStruct((count, lat + 16, tokens), jnp.bfloat16),
        ],
        scratch_shapes=[
            pltpu.VMEM((blocks, count, 2 * rows, HD), jnp.bfloat16),
            pltpu.SemaphoreType.DMA((len(pieces),)),
        ],
        compiler_params=pltpu.CompilerParams(vmem_limit_bytes=SMALL_VMEM if len(pieces) <= 8 else LARGE_VMEM),
        cost_estimate=pl.CostEstimate(
            flops=count * tokens * tokens * 2 * (HD + lat),
            bytes_accessed=tokens * count * 3 * HD * 2,
            transcendentals=count * tokens * tokens,
        ),
        name="attend_early",
    )(span_frames, me, timestep, step_weight, sign, sample, *pieces)


def attend_late(pieces, offsets, late, chosen, groups, early, span_frames, me, count, lat):
    rows, width = pieces[0].shape
    half = len(offsets) // 2 + 1
    tokens = 2 * half * rows
    return pl.pallas_call(
        functools.partial(late_kernel, offsets, late, chosen, groups),
        in_specs=[SMEM] * 2 + [HBM] * 2 + [VMEM] * len(early),
        out_specs=[VMEM] * len(groups),
        out_shape=[
            jax.ShapeDtypeStruct((half // 2, lat, rows), jnp.bfloat16 if g else jnp.float32) for g in groups
        ],
        scratch_shapes=[
            pltpu.VMEM((2, rows, width), jnp.bfloat16),
            pltpu.VMEM((count, lat + 16, 2 * rows), jnp.bfloat16),
            pltpu.SemaphoreType.DMA((2,)),
        ],
        compiler_params=pltpu.CompilerParams(vmem_limit_bytes=SMALL_VMEM if half <= 4 else LARGE_VMEM),
        cost_estimate=pl.CostEstimate(
            flops=count * tokens * rows * 4 * (HD + lat),
            bytes_accessed=tokens * count * 3 * HD * 2,
            transcendentals=count * tokens * rows * 2,
        ),
        name="attend_late",
    )(span_frames, me, *pieces, *early)


def swap(array, axis, offset):
    size = lax.axis_size(axis)
    return lax.ppermute(array, axis, [(i, i ^ offset) for i in range(size)])


def body(qkv, readout, step_weight, timestep, span_frames):
    seq_count = lax.axis_size("seq")
    mp_count = lax.axis_size("mp")
    half = seq_count // 2
    pair_heads = 2 * HEADS // seq_count
    count = max(1, pair_heads // 4)
    split = pair_heads - 2 * count
    lat = readout.shape[2]
    me = lax.axis_index("seq").astype(jnp.int32).reshape(1)
    mp_index = lax.axis_index("mp").astype(jnp.int32)
    sample_count = mp_count // 2
    model_index = mp_index // sample_count
    sample = (mp_index % sample_count).reshape(1)
    sign = jnp.where(model_index == 1, 1.0, -1.0).astype(jnp.float32).reshape(1)
    model = model_index.reshape(1)
    readout_t = jnp.swapaxes(readout, 1, 2)

    def whole_head(k):
        return lambda m: ((m ^ k) & (half - 1)) * pair_heads + split + (m ^ k) // half * count

    def split_head(k):
        return lambda m: ((m ^ k) & (half - 1)) * pair_heads

    def send(k, after):
        packed = pack(me, model, qkv, readout_t, whole_head(k), count, after)
        return swap(packed, "seq", k) if k else packed

    pieces = [None] * seq_count
    near, far = [None] * half, [None] * half
    tops = range(seq_count - 1, half - 1, -1)
    if split:
        for k in tops:
            after = [far[k + 2 - half]] if k < seq_count - 2 else []
            far[k - half] = swap(pack_queries(me, qkv, split_head(k), split, after), "seq", k)
        for k in [half - 1] + list(range(1, half - 1)):
            after = [near[k - 1], near[half - 1], far[half - 1], far[half - 2]] if k not in (1, half - 1) else []
            near[k] = swap(pack(me, model, qkv, readout_t, split_head(k), split, after), "seq", k)
        near[0] = pack(me, model, qkv, readout_t, split_head(0), split, [far[half - 1]])
        sums, stats = attend_split(near, far, span_frames, me, split, lat)
    for k in tops:
        after = [pieces[k + 2], stats] if k < seq_count - 2 and split else [pieces[k + 2]] if k < seq_count - 2 else []
        pieces[k] = send(k, after if k < seq_count - 2 or not split else [far[k - half - 2]])
    pieces[0] = send(0, [pieces[seq_count - 1]])
    for k in [half - 1] + list(range(1, half - 1)):
        after = [pieces[k - 1], pieces[half - 1]] if k not in (1, half - 1) else [near[half - 2]] if split else []
        pieces[k] = send(k, after)
    late = [half, half + 1]
    early = [k for k in range(seq_count) if k not in late]
    merged = attend_early(
        [pieces[k] for k in early], early, span_frames, me, timestep, step_weight, sign, sample, count, lat
    )
    blocks = len(early) // 2
    if split:
        merged = list(merged) + [combine(sums, stats, swap(stats, "seq", half))]
    ends = [pieces[k] for k in late]
    order = [blocks] + list(range(blocks))
    given = attend_late(ends, early, late, order, [0, 1, 2, 3], merged, span_frames, me, count, lat)
    size = half // 2
    while True:
        keep = given[0]
        for n in range(len(given) - 1, 0, -1):
            keep = keep + swap(given[n], "seq", n * size).astype(jnp.float32)
        if size == 1:
            break
        radix = min(4, size)
        size //= radix
        given = [keep[n * size : (n + 1) * size] for n in range(radix)]
    total = keep[0]
    offset = 1
    while offset < mp_count:
        radix = min(4, mp_count // offset)
        own = total
        for n in range(radix - 1, 0, -1):
            total = total + swap(own, "mp", offset * n)
        offset *= radix
    return total.T


def solution(mesh):
    return jax.shard_map(
        body,
        mesh=mesh,
        in_specs=(P("mp", "seq", None), P(), P(), P(), P()),
        out_specs=P("seq", None),
        check_vma=False,
    )
```

```python
import functools
import math

import jax
import jax.numpy as jnp
from jax import lax
from jax.experimental import pallas as pl
from jax.experimental.pallas import tpu as pltpu
from jax.sharding import PartitionSpec as P

HEADS = 32
HD = 128
FRAME_TOK = 64
NT = (((1,), (1,)), ((), ()))
LOG2_SCALE = math.log2(math.e) / math.sqrt(HD)
LOWEST = -1e30
TAKE = 1000000000
SMALL_VMEM = 24 * 1024 * 1024
LARGE_VMEM = 60 * 1024 * 1024
SMEM = pl.BlockSpec(memory_space=pltpu.SMEM)
VMEM = pl.BlockSpec(memory_space=pltpu.VMEM)
HBM = pl.BlockSpec(memory_space=pltpu.HBM)


def fold(readout, values):
    return lax.dot_general(readout, values, NT, preferred_element_type=jnp.float32).astype(jnp.bfloat16)


def value_place(h, count, lat):
    return (h * lat) % HD, count * 2 * HD + (h * lat // HD) * HD


def pack_kernel(k, me_ref, model_ref, qkv_ref, readout_ref, *refs):
    out_ref, values, readout, sems = refs[-4:]
    rows = out_ref.shape[0]
    count, lat = values.shape[0], readout.shape[0]
    first = (me_ref[0] ^ k) * count

    def columns(h, part, width):
        return pl.ds(pl.multiple_of(((first + h) * 3 + part) * HD, HD), width)

    copies = [
        pltpu.make_async_copy(
            readout_ref.at[model_ref[0], :, pl.ds(pl.multiple_of(first * HD, HD), count * HD)], readout, sems.at[2 * count]
        )
    ]
    for h in range(count):
        copies.append(pltpu.make_async_copy(qkv_ref.at[0, :, columns(h, 2, HD)], values.at[h], sems.at[h]))
    for h in range(count):
        target = out_ref.at[:, h * 2 * HD : (h + 1) * 2 * HD]
        copies.append(pltpu.make_async_copy(qkv_ref.at[0, :, columns(h, 0, 2 * HD)], target, sems.at[count + h]))
    for copy in copies:
        copy.start()
    copies[0].wait()
    for h in range(count):
        copies[1 + h].wait()
        row, column = value_place(h, count, lat)
        out_ref[row : row + lat, column : column + HD] = fold(readout[:, h * HD : (h + 1) * HD], values[h])
    for copy in copies[1 + count :]:
        copy.wait()


def pack(me, model, qkv, readout_t, k, count, after):
    rows = qkv.shape[1]
    lat = readout_t.shape[1]
    width = count * 2 * HD + -(-count * lat // HD) * HD
    return pl.pallas_call(
        functools.partial(pack_kernel, k),
        in_specs=[SMEM, SMEM] + [HBM] * (2 + len(after)),
        out_specs=VMEM,
        out_shape=jax.ShapeDtypeStruct((rows, width), jnp.bfloat16),
        scratch_shapes=[
            pltpu.VMEM((count, rows, HD), jnp.bfloat16),
            pltpu.VMEM((lat, count * HD), jnp.bfloat16),
            pltpu.SemaphoreType.DMA((2 * count + 1,)),
        ],
        compiler_params=pltpu.CompilerParams(vmem_limit_bytes=SMALL_VMEM),
        cost_estimate=pl.CostEstimate(
            flops=0, bytes_accessed=rows * width * 4, transcendentals=0
        ),
        name="pack",
    )(me, model, qkv, readout_t, *after)


def mask_rows(frames_ref, me, rows, query_offsets, key_offsets):
    columns = lax.broadcasted_iota(jnp.int32, (1, rows), 1)
    places = jnp.concatenate([(me ^ k) * rows + columns for k in query_offsets], axis=1)
    end = frames_ref[0] * FRAME_TOK
    bound = jnp.full(places.shape, end, jnp.int32)
    for c in range(1, frames_ref.shape[0]):
        later = end + frames_ref[c] * FRAME_TOK
        bound = jnp.where(places >= end, later, bound)
        end = later
    return [
        jnp.where((me ^ k) * rows + start < bound, 0.0, -jnp.inf)
        for k in key_offsets
        for start in range(0, rows, FRAME_TOK)
    ]


def run_units(units, lat):
    frames = [tile() for tile in units[0][0]]
    for u, (_, values, shifts, finish) in enumerate(units):
        ahead = list(units[u + 1][0]) if u + 1 < len(units) else []
        peaks = [jnp.max(f, axis=0, keepdims=True) + s for f, s in zip(sum(frames, []), shifts)]
        peak = jnp.maximum(functools.reduce(jnp.maximum, peaks), LOWEST)
        following, summed, start = [], None, 0
        for t, tile in enumerate(frames):
            for _ in range(-(-(len(ahead) - len(following)) // (len(frames) - t))):
                following.append(ahead[len(following)]())
            weights = [
                jnp.exp2((f + (s - peak)) * LOG2_SCALE).astype(jnp.bfloat16)
                for f, s in zip(tile, shifts[start : start + len(tile)])
            ]
            start += len(tile)
            part = jnp.dot(values[t](), jnp.concatenate(weights, axis=0), preferred_element_type=jnp.float32)
            summed = part if summed is None else summed + part
        finish(summed[:lat], summed[lat : lat + 1], peak)
        frames = following


def score_tile(keys, queries):
    scores = lax.dot_general(keys(), queries(), NT, preferred_element_type=jnp.float32)
    return [scores[start : start + FRAME_TOK] for start in range(0, scores.shape[0], FRAME_TOK)]


def stage_values(folded, pieces, lat):
    count = folded.shape[0]
    rows = pieces[0].shape[0]
    for i in range(count):
        row, column = value_place(i, count, lat)
        for n, piece in enumerate(pieces):
            folded[i, :lat, n * rows : (n + 1) * rows] = piece[row : row + lat, column : column + HD]
        folded[i, lat:] = jnp.ones_like(folded[i, lat:])


def groups_of(count):
    return [tuple(range(n, min(n + 2, count))) for n in range(0, count, 2)]


def read_group(pieces, group, i, what):
    column = (2 * i + what) * HD
    parts = [pieces[n][:, column : column + HD] for n in group]
    return parts[0] if len(parts) == 1 else jnp.concatenate(parts, axis=0)


def early_kernel(offsets, frames_ref, me_ref, timestep_ref, step_weight_ref, sign_ref, sample_ref, *refs):
    number = len(offsets)
    arrived = refs[:number]
    sums_ref, stats_ref, factor_ref, held, folded, asked, sems = refs[-7:]
    me = me_ref[0]
    rows = held.shape[1]
    lat = sums_ref.shape[2]
    count = folded.shape[0]
    groups = groups_of(number)
    full = number // 2
    copies = [pltpu.make_async_copy(arrived[n], held.at[n], sems.at[n]) for n in range(number)]
    for copy in copies:
        copy.start()
    factor_ref[...] = jnp.full(factor_ref.shape, sign_ref[0] * step_weight_ref[timestep_ref[sample_ref[0]]])
    for copy in copies:
        copy.wait()
    pieces = [held.at[n] for n in range(number)]
    stage_values(folded, pieces, lat)
    for i in range(count):
        for b in range(full):
            asked[b, i] = read_group(pieces, groups[b], i, 0)
    half = (number + 1) // 2

    def block(b, queries_of, query_offsets):
        width = rows * len(query_offsets)
        shifts = mask_rows(frames_ref, me, rows, query_offsets, offsets)
        peaks, totals, units = [], [], []
        for i in range(count):

            def finish(summed, total, peak, i=i):
                sums_ref[b, i, :, :width] = summed
                peaks.append(peak)
                totals.append(total)

            tiles = [
                functools.partial(score_tile, lambda g=g, i=i: read_group(pieces, g, i, 1), lambda i=i: queries_of(i))
                for g in groups
            ]
            values = [lambda i=i, g=g: folded[i, :, g[0] * rows : (g[-1] + 1) * rows] for g in groups]
            units.append((tiles, values, shifts, finish))
        run_units(units, lat)
        rest = [jnp.ones_like(peaks[0])] * (stats_ref.shape[2] - count)
        stats_ref[b, 0, :, :width] = jnp.concatenate(peaks + rest, axis=0)
        stats_ref[b, 1, :, :width] = jnp.concatenate(totals + rest, axis=0)

    def some_blocks(b, carry):
        q = [2 * b, 2 * b + 1]
        block(b, lambda i: asked[b, i], [jnp.where(n < half, n, n + 2) for n in q])
        return carry

    lax.fori_loop(0, full, some_blocks, 0)
    block(full, lambda i: read_group(pieces, groups[full], i, 0), offsets[2 * full :])


def late_kernel(offsets, late, frames_ref, me_ref, late_ref, *refs):
    early = len(offsets)
    sums_ref, stats_ref, factor_ref, early_ref, early_folded, *out_refs, late_piece, folded, sem = refs
    copy = pltpu.make_async_copy(late_ref, late_piece, sem)
    copy.start()
    me = me_ref[0]
    size, lat, rows = out_refs[0].shape
    count = folded.shape[0]
    copy.wait()
    pieces = [early_ref.at[n] for n in range(early)] + [late_piece]
    stage_values(folded, pieces[early:], lat)
    factor = factor_ref[:1]
    every = list(offsets) + [late]
    groups = groups_of(early) + [(early,)]
    results = {}

    def write(b):
        for j, n in enumerate(groups[b]):
            k = every[n]
            out_ref = out_refs[k // size]
            out_ref[k % size] = (results[b][:, j * rows : (j + 1) * rows] * factor).astype(out_ref.dtype)

    def value_tile(i, g):
        return folded[i] if g[0] == early else early_folded[i, :, g[0] * rows : (g[-1] + 1) * rows]

    units = []
    last = len(groups) - 1
    for b in [last] + list(range(last)):
        key_groups = groups if b == last else groups[last:]
        key_offsets = [every[n] for g in key_groups for n in g]
        width = rows * len(groups[b])
        shifts = mask_rows(frames_ref, me, rows, [every[n] for n in groups[b]], key_offsets)
        for i in range(count):

            def finish(summed, total, peak, b=b, i=i, width=width):
                if b < last:
                    before = stats_ref[b, 0, i : i + 1, :width]
                    highest = jnp.maximum(before, peak)
                    old = jnp.exp2((before - highest) * LOG2_SCALE)
                    new = jnp.exp2((peak - highest) * LOG2_SCALE)
                    both = stats_ref[b, 1, i : i + 1, :width] * old + total * new
                    part = sums_ref[b, i, :, :width] * (old / both) + summed * (new / both)
                else:
                    part = summed / total
                results[b] = part if i == 0 else results[b] + part
                if i == count - 1:
                    write(b)

            tiles = [
                functools.partial(
                    score_tile,
                    lambda g=g, i=i: read_group(pieces, g, i, 1),
                    lambda b=b, i=i: read_group(pieces, groups[b], i, 0),
                )
                for g in key_groups
            ]
            values = [functools.partial(value_tile, i, g) for g in key_groups]
            units.append((tiles, values, shifts, finish))
    run_units(units, lat)


def attend_early(pieces, offsets, taken, span_frames, me, timestep, step_weight, sign, sample, count, lat):
    rows, width = pieces[0].shape
    blocks = len(groups_of(len(pieces)))
    tokens = len(pieces) * rows
    return pl.pallas_call(
        functools.partial(early_kernel, offsets),
        in_specs=[SMEM] * 6 + [HBM] * (len(pieces) + 1),
        out_specs=[VMEM] * 5,
        out_shape=[
            jax.ShapeDtypeStruct((blocks, count, lat, 2 * rows), jnp.float32),
            jax.ShapeDtypeStruct((blocks, 2, 8, 2 * rows), jnp.float32),
            jax.ShapeDtypeStruct((8, rows), jnp.float32),
            jax.ShapeDtypeStruct((len(pieces), rows, width), jnp.bfloat16),
            jax.ShapeDtypeStruct((count, lat + 16, tokens), jnp.bfloat16),
        ],
        scratch_shapes=[
            pltpu.VMEM((len(pieces) // 2, count, 2 * rows, HD), jnp.bfloat16),
            pltpu.SemaphoreType.DMA((len(pieces),)),
        ],
        compiler_params=pltpu.CompilerParams(vmem_limit_bytes=SMALL_VMEM if len(pieces) <= 8 else LARGE_VMEM),
        cost_estimate=pl.CostEstimate(
            flops=count * tokens * tokens * 2 * (HD + lat),
            bytes_accessed=tokens * count * 3 * HD * 2,
            transcendentals=count * tokens * tokens,
        ),
        name="attend_early",
    )(span_frames, me, timestep, step_weight, sign, sample, *pieces, taken)


def attend_late(piece, offsets, late, early, span_frames, me, count, lat):
    rows, width = piece.shape
    seq_count = len(offsets) + 1
    tokens = seq_count * rows
    return pl.pallas_call(
        functools.partial(late_kernel, offsets, late),
        in_specs=[SMEM] * 2 + [HBM] + [VMEM] * len(early),
        out_specs=[VMEM] * 4,
        out_shape=[
            jax.ShapeDtypeStruct((seq_count // 4, lat, rows), jnp.bfloat16 if g else jnp.float32) for g in range(4)
        ],
        scratch_shapes=[
            pltpu.VMEM((rows, width), jnp.bfloat16),
            pltpu.VMEM((count, lat + 16, rows), jnp.bfloat16),
            pltpu.SemaphoreType.DMA,
        ],
        compiler_params=pltpu.CompilerParams(vmem_limit_bytes=SMALL_VMEM if seq_count <= 8 else LARGE_VMEM),
        cost_estimate=pl.CostEstimate(
            flops=count * tokens * rows * 4 * (HD + lat),
            bytes_accessed=tokens * count * 3 * HD * 2,
            transcendentals=count * tokens * rows * 2,
        ),
        name="attend_late",
    )(span_frames, me, piece, *early)


def take_kernel(piece_ref, me_ref, out_ref):
    out_ref[...] = jnp.full(out_ref.shape, me_ref[0], jnp.int32)


def take(piece, me):
    return pl.pallas_call(
        take_kernel,
        in_specs=[HBM, SMEM],
        out_specs=VMEM,
        out_shape=jax.ShapeDtypeStruct((8, HD), jnp.int32),
        compiler_params=pltpu.CompilerParams(vmem_limit_bytes=SMALL_VMEM),
        cost_estimate=pl.CostEstimate(flops=TAKE, bytes_accessed=0, transcendentals=0),
        name="take",
    )(piece, me)


def swap(array, axis, offset):
    size = lax.axis_size(axis)
    return lax.ppermute(array, axis, [(i, i ^ offset) for i in range(size)])


def body(qkv, readout, step_weight, timestep, span_frames):
    seq_count = lax.axis_size("seq")
    mp_count = lax.axis_size("mp")
    half = seq_count // 2
    count = HEADS // seq_count
    lat = readout.shape[2]
    me = lax.axis_index("seq").astype(jnp.int32).reshape(1)
    mp_index = lax.axis_index("mp").astype(jnp.int32)
    sample_count = mp_count // 2
    model_index = mp_index // sample_count
    sample = (mp_index % sample_count).reshape(1)
    sign = jnp.where(model_index == 1, 1.0, -1.0).astype(jnp.float32).reshape(1)
    model = model_index.reshape(1)
    readout_t = jnp.swapaxes(readout, 1, 2)

    pieces = [None] * seq_count
    for n in range(half):
        k = seq_count - 1 - n
        packed = pack(me, model, qkv, readout_t, k, count, [pieces[k + 2]] if n > 1 else [])
        pieces[k] = swap(packed, "seq", k)
    pieces[0] = pack(me, model, qkv, readout_t, 0, count, [pieces[seq_count - 1]])
    for k in [half - 1] + list(range(1, half - 1)):
        after = [pieces[k - 1], pieces[half - 1], pieces[seq_count - 1]] if k not in (1, half - 1) else []
        pieces[k] = swap(pack(me, model, qkv, readout_t, k, count, after), "seq", k)
    early = [k for k in range(seq_count) if k not in (half, half + 1)] + [half + 1]
    merged = attend_early(
        [pieces[k] for k in early], early, take(pieces[half + 1], me), span_frames, me, timestep, step_weight, sign, sample, count, lat
    )
    given = attend_late(pieces[half], early, half, merged, span_frames, me, count, lat)
    size = half // 2
    while True:
        keep = given[0]
        for n in range(len(given) - 1, 0, -1):
            keep = keep + swap(given[n], "seq", n * size).astype(jnp.float32)
        if size == 1:
            break
        radix = min(4, size)
        size //= radix
        given = [keep[n * size : (n + 1) * size] for n in range(radix)]
    total = keep[0]
    offset = 1
    while offset < mp_count:
        radix = min(4, mp_count // offset)
        own = total
        for n in range(radix - 1, 0, -1):
            total = total + swap(own, "mp", offset * n)
        offset *= radix
    return total.T


def solution(mesh):
    return jax.shard_map(
        body,
        mesh=mesh,
        in_specs=(P("mp", "seq", None), P(), P(), P(), P()),
        out_specs=P("seq", None),
        check_vma=False,
    )
```

```python
import functools
import math

import jax
import jax.numpy as jnp
from jax import lax
from jax.experimental import pallas as pl
from jax.experimental.pallas import tpu as pltpu
from jax.sharding import PartitionSpec as P

HEADS = 32
HD = 128
FRAME_TOK = 64
NT = (((1,), (1,)), ((), ()))
LOG2_SCALE = math.log2(math.e) / math.sqrt(HD)
LOWEST = -1e30
PACK_VMEM = 4 * 1024 * 1024
SMALL_VMEM = 16 * 1024 * 1024
LARGE_VMEM = 60 * 1024 * 1024
SMEM = pl.BlockSpec(memory_space=pltpu.SMEM)
VMEM = pl.BlockSpec(memory_space=pltpu.VMEM)
HBM = pl.BlockSpec(memory_space=pltpu.HBM)


def fold(readout, values):
    return lax.dot_general(readout, values, NT, preferred_element_type=jnp.float32).astype(jnp.bfloat16)


def value_place(h, count, lat):
    return (h * lat) % HD, count * 2 * HD + (h * lat // HD) * HD


def pack_kernel(k, me_ref, model_ref, qkv_ref, readout_ref, *refs):
    out_ref, values, readout, sems = refs[-4:]
    rows = out_ref.shape[0]
    count, lat = values.shape[0], readout.shape[0]
    first = (me_ref[0] ^ k) * count

    def columns(h, part, width):
        return pl.ds(pl.multiple_of(((first + h) * 3 + part) * HD, HD), width)

    copies = [
        pltpu.make_async_copy(
            readout_ref.at[model_ref[0], :, pl.ds(pl.multiple_of(first * HD, HD), count * HD)], readout, sems.at[2 * count]
        )
    ]
    for h in range(count):
        copies.append(pltpu.make_async_copy(qkv_ref.at[0, :, columns(h, 2, HD)], values.at[h], sems.at[h]))
    for h in range(count):
        target = out_ref.at[:, h * 2 * HD : (h + 1) * 2 * HD]
        copies.append(pltpu.make_async_copy(qkv_ref.at[0, :, columns(h, 0, 2 * HD)], target, sems.at[count + h]))
    for copy in copies:
        copy.start()
    copies[0].wait()
    for h in range(count):
        copies[1 + h].wait()
        row, column = value_place(h, count, lat)
        out_ref[row : row + lat, column : column + HD] = fold(readout[:, h * HD : (h + 1) * HD], values[h])
    for copy in copies[1 + count :]:
        copy.wait()


def pack(me, model, qkv, readout_t, k, count, after, first=False):
    rows = qkv.shape[1]
    lat = readout_t.shape[1]
    width = count * 2 * HD + -(-count * lat // HD) * HD
    return pl.pallas_call(
        functools.partial(pack_kernel, k),
        in_specs=[SMEM, SMEM] + [HBM] * (2 + len(after)),
        out_specs=VMEM,
        out_shape=jax.ShapeDtypeStruct((rows, width), jnp.bfloat16),
        scratch_shapes=[
            pltpu.VMEM((count, rows, HD), jnp.bfloat16),
            pltpu.VMEM((lat, count * HD), jnp.bfloat16),
            pltpu.SemaphoreType.DMA((2 * count + 1,)),
        ],
        compiler_params=pltpu.CompilerParams(vmem_limit_bytes=LARGE_VMEM if first else PACK_VMEM),
        cost_estimate=pl.CostEstimate(
            flops=0, bytes_accessed=rows * width * 4, transcendentals=0
        ),
        name="pack",
    )(me, model, qkv, readout_t, *after)


def mask_rows(frames_ref, me, rows, query_offsets, key_offsets):
    columns = lax.broadcasted_iota(jnp.int32, (1, rows), 1)
    places = jnp.concatenate([(me ^ k) * rows + columns for k in query_offsets], axis=1)
    end = frames_ref[0] * FRAME_TOK
    bound = jnp.full(places.shape, end, jnp.int32)
    for c in range(1, frames_ref.shape[0]):
        later = end + frames_ref[c] * FRAME_TOK
        bound = jnp.where(places >= end, later, bound)
        end = later
    return [
        jnp.where((me ^ k) * rows + start < bound, 0.0, -jnp.inf)
        for k in key_offsets
        for start in range(0, rows, FRAME_TOK)
    ]


def run_units(units, lat):
    frames = [tile() for tile in units[0][0]]
    for u, (_, values, shifts, finish) in enumerate(units):
        ahead = list(units[u + 1][0]) if u + 1 < len(units) else []
        peaks = [jnp.max(f, axis=0, keepdims=True) + s for f, s in zip(sum(frames, []), shifts)]
        peak = jnp.maximum(functools.reduce(jnp.maximum, peaks), LOWEST)
        following, summed, start = [], None, 0
        for t, tile in enumerate(frames):
            for _ in range(-(-(len(ahead) - len(following)) // (len(frames) - t))):
                following.append(ahead[len(following)]())
            weights = [
                jnp.exp2((f + (s - peak)) * LOG2_SCALE).astype(jnp.bfloat16)
                for f, s in zip(tile, shifts[start : start + len(tile)])
            ]
            start += len(tile)
            part = jnp.dot(values[t](), jnp.concatenate(weights, axis=0), preferred_element_type=jnp.float32)
            summed = part if summed is None else summed + part
        finish(summed[:lat], summed[lat : lat + 1], peak)
        frames = following


def score_tile(keys, queries):
    scores = lax.dot_general(keys(), queries(), NT, preferred_element_type=jnp.float32)
    return [scores[start : start + FRAME_TOK] for start in range(0, scores.shape[0], FRAME_TOK)]


def stage_values(folded, pieces, lat):
    count = folded.shape[0]
    rows = pieces[0].shape[0]
    for i in range(count):
        row, column = value_place(i, count, lat)
        for n, piece in enumerate(pieces):
            folded[i, :lat, n * rows : (n + 1) * rows] = piece[row : row + lat, column : column + HD]
        folded[i, lat:] = jnp.ones_like(folded[i, lat:])


def pairs_of(pieces, i, what):
    column = (2 * i + what) * HD

    def read(n):
        return lambda: jnp.concatenate([pieces[n][:, column : column + HD], pieces[n + 1][:, column : column + HD]], axis=0)

    return [read(n) for n in range(0, len(pieces), 2)]


def early_kernel(offsets, frames_ref, me_ref, timestep_ref, step_weight_ref, sign_ref, sample_ref, *refs):
    count_pieces = len(offsets)
    arrived = refs[:count_pieces]
    sums_ref, stats_ref, factor_ref, pieces, folded, asked, sems = refs[-7:]
    me = me_ref[0]
    rows = pieces.shape[1]
    count, lat, _ = sums_ref.shape
    blocks = count_pieces // 2
    copies = [pltpu.make_async_copy(arrived[n], pieces.at[n], sems.at[n]) for n in range(count_pieces)]
    for copy in copies:
        copy.start()
    factor_ref[...] = jnp.full(factor_ref.shape, sign_ref[0] * step_weight_ref[timestep_ref[sample_ref[0]]])
    for copy in copies:
        copy.wait()
    pieces = [pieces.at[n] for n in range(count_pieces)]
    stage_values(folded, pieces, lat)
    for i in range(count):
        for b, read in enumerate(pairs_of(pieces, i, 0)):
            asked[b, i] = read()
    half = count_pieces // 2 + 1

    def some_blocks(b, carry):
        q = [2 * b, 2 * b + 1]
        span = pl.ds(pl.multiple_of(b * 2 * rows, 2 * rows), 2 * rows)
        shifts = mask_rows(frames_ref, me, rows, [jnp.where(n < half, n, n + 2) for n in q], offsets)
        peaks, totals, units = [], [], []
        for i in range(count):

            def finish(summed, total, peak, i=i):
                sums_ref[i, :, span] = summed
                peaks.append(peak)
                totals.append(total)

            tiles = [
                functools.partial(score_tile, keys, lambda i=i: asked[b, i]) for keys in pairs_of(pieces, i, 1)
            ]
            values = [lambda i=i, t=t: folded[i, :, t * 2 * rows : (t + 1) * 2 * rows] for t in range(blocks)]
            units.append((tiles, values, shifts, finish))
        run_units(units, lat)
        rest = [jnp.ones_like(peaks[0])] * (stats_ref.shape[1] - count)
        stats_ref[0, :, span] = jnp.concatenate(peaks + rest, axis=0)
        stats_ref[1, :, span] = jnp.concatenate(totals + rest, axis=0)
        return carry

    lax.fori_loop(0, blocks, some_blocks, 0)


def late_kernel(offsets, late, frames_ref, me_ref, *refs):
    early = len(offsets)
    arrived = refs[:2]
    sums_ref, stats_ref, factor_ref, early_ref, early_folded, *out_refs, late_pieces, folded, sems = refs[2:]
    copies = [pltpu.make_async_copy(arrived[n], late_pieces.at[n], sems.at[n]) for n in range(2)]
    for copy in copies:
        copy.start()
    me = me_ref[0]
    size, lat, rows = out_refs[0].shape
    count = folded.shape[0]
    for copy in copies:
        copy.wait()
    pieces = [early_ref.at[n] for n in range(early)] + [late_pieces.at[n] for n in range(2)]
    stage_values(folded, pieces[early:], lat)
    factor = factor_ref[:1]
    every = list(offsets) + list(late)
    blocks = early // 2
    results = {}

    def write(number, start):
        for j in range(number):
            k = every[start + j]
            out_ref = out_refs[k // size]
            out_ref[k % size] = (results[start][:, j * rows : (j + 1) * rows] * factor).astype(out_ref.dtype)

    units = []
    for start, number, tiles_in in ((0, early, [blocks]), (early, 2, range(blocks + 1))):
        key_offsets = [every[2 * t + j] for t in tiles_in for j in range(2)]
        shifts = mask_rows(frames_ref, me, rows, every[start : start + number], key_offsets)
        for i in range(count):

            def finish(summed, total, peak, start=start, number=number, i=i):
                if start == 0:
                    before = stats_ref[0, i : i + 1]
                    highest = jnp.maximum(before, peak)
                    old = jnp.exp2((before - highest) * LOG2_SCALE)
                    new = jnp.exp2((peak - highest) * LOG2_SCALE)
                    both = stats_ref[1, i : i + 1] * old + total * new
                    part = sums_ref[i] * (old / both) + summed * (new / both)
                else:
                    part = summed / total
                results[start] = part if i == 0 else results[start] + part
                if i == count - 1:
                    write(number, start)

            def queries(start=start, number=number, i=i):
                column = 2 * i * HD
                return jnp.concatenate([p[:, column : column + HD] for p in pieces[start : start + number]], axis=0)

            keys = pairs_of(pieces, i, 1)
            tiles = [functools.partial(score_tile, keys[t], queries) for t in tiles_in]
            values = [
                lambda i=i, t=t: folded[i] if t == blocks else early_folded[i, :, t * 2 * rows : (t + 1) * 2 * rows]
                for t in tiles_in
            ]
            units.append((tiles, values, shifts, finish))
    run_units(units, lat)


def attend_early(pieces, offsets, span_frames, me, timestep, step_weight, sign, sample, count, lat):
    rows, width = pieces[0].shape
    blocks = len(pieces) // 2
    tokens = len(pieces) * rows
    return pl.pallas_call(
        functools.partial(early_kernel, offsets),
        in_specs=[SMEM] * 6 + [HBM] * len(pieces),
        out_specs=[VMEM] * 5,
        out_shape=[
            jax.ShapeDtypeStruct((count, lat, tokens), jnp.float32),
            jax.ShapeDtypeStruct((2, 8, tokens), jnp.float32),
            jax.ShapeDtypeStruct((8, rows), jnp.float32),
            jax.ShapeDtypeStruct((len(pieces), rows, width), jnp.bfloat16),
            jax.ShapeDtypeStruct((count, lat + 16, tokens), jnp.bfloat16),
        ],
        scratch_shapes=[
            pltpu.VMEM((blocks, count, 2 * rows, HD), jnp.bfloat16),
            pltpu.SemaphoreType.DMA((len(pieces),)),
        ],
        compiler_params=pltpu.CompilerParams(vmem_limit_bytes=SMALL_VMEM if len(pieces) <= 8 else LARGE_VMEM),
        cost_estimate=pl.CostEstimate(
            flops=count * tokens * tokens * 2 * (HD + lat),
            bytes_accessed=tokens * count * 3 * HD * 2,
            transcendentals=count * tokens * tokens,
        ),
        name="attend_early",
    )(span_frames, me, timestep, step_weight, sign, sample, *pieces)


def attend_late(pieces, offsets, late, early, span_frames, me, count, lat):
    rows, width = pieces[0].shape
    half = len(offsets) // 2 + 1
    tokens = 2 * half * rows
    return pl.pallas_call(
        functools.partial(late_kernel, offsets, late),
        in_specs=[SMEM] * 2 + [HBM] * 2 + [VMEM] * len(early),
        out_specs=[VMEM] * 4,
        out_shape=[
            jax.ShapeDtypeStruct((half // 2, lat, rows), jnp.bfloat16 if g else jnp.float32) for g in range(4)
        ],
        scratch_shapes=[
            pltpu.VMEM((2, rows, width), jnp.bfloat16),
            pltpu.VMEM((count, lat + 16, 2 * rows), jnp.bfloat16),
            pltpu.SemaphoreType.DMA((2,)),
        ],
        compiler_params=pltpu.CompilerParams(vmem_limit_bytes=SMALL_VMEM if half <= 4 else LARGE_VMEM),
        cost_estimate=pl.CostEstimate(
            flops=count * tokens * rows * 4 * (HD + lat),
            bytes_accessed=tokens * count * 3 * HD * 2,
            transcendentals=count * tokens * rows * 2,
        ),
        name="attend_late",
    )(span_frames, me, *pieces, *early)


def swap(array, axis, offset):
    size = lax.axis_size(axis)
    return lax.ppermute(array, axis, [(i, i ^ offset) for i in range(size)])


def body(qkv, readout, step_weight, timestep, span_frames):
    seq_count = lax.axis_size("seq")
    mp_count = lax.axis_size("mp")
    half = seq_count // 2
    count = HEADS // seq_count
    lat = readout.shape[2]
    me = lax.axis_index("seq").astype(jnp.int32).reshape(1)
    mp_index = lax.axis_index("mp").astype(jnp.int32)
    sample_count = mp_count // 2
    model_index = mp_index // sample_count
    sample = (mp_index % sample_count).reshape(1)
    sign = jnp.where(model_index == 1, 1.0, -1.0).astype(jnp.float32).reshape(1)
    model = model_index.reshape(1)
    readout_t = jnp.swapaxes(readout, 1, 2)

    pieces = [None] * seq_count
    for n in range(half):
        k = seq_count - 1 - n
        pieces[k] = swap(pack(me, model, qkv, readout_t, k, count, [pieces[k + 2]] if n > 1 else [], n == 0), "seq", k)
    for k in range(half - 1, 0, -1):
        after = [] if k == half - 1 else [pieces[k + 1], pieces[seq_count - 1]] if k > 1 else [pieces[half - 1]]
        pieces[k] = swap(pack(me, model, qkv, readout_t, k, count, after), "seq", k)
    pieces[0] = pack(me, model, qkv, readout_t, 0, count, [pieces[half - 1]])
    late = [half, half + 1]
    early = [k for k in range(seq_count) if k not in late]
    merged = attend_early(
        [pieces[k] for k in early], early, span_frames, me, timestep, step_weight, sign, sample, count, lat
    )
    ends = [pieces[k] for k in late]
    given = attend_late(ends, early, late, merged, span_frames, me, count, lat)
    size = half // 2
    while True:
        keep = given[0]
        for n in range(len(given) - 1, 0, -1):
            keep = keep + swap(given[n], "seq", n * size).astype(jnp.float32)
        if size == 1:
            break
        radix = min(4, size)
        size //= radix
        given = [keep[n * size : (n + 1) * size] for n in range(radix)]
    total = keep[0]
    offset = 1
    while offset < mp_count:
        radix = min(4, mp_count // offset)
        own = total
        for n in range(radix - 1, 0, -1):
            total = total + swap(own, "mp", offset * n)
        offset *= radix
    return total.T


def solution(mesh):
    return jax.shard_map(
        body,
        mesh=mesh,
        in_specs=(P("mp", "seq", None), P(), P(), P(), P()),
        out_specs=P("seq", None),
        check_vma=False,
    )
```

```python
import functools
import math

import jax
import jax.numpy as jnp
from jax import lax
from jax.experimental import pallas as pl
from jax.experimental.pallas import tpu as pltpu
from jax.sharding import PartitionSpec as P

HEADS = 32
HD = 128
FRAME_TOK = 64
NT = (((1,), (1,)), ((), ()))
LOG2_SCALE = math.log2(math.e) / math.sqrt(HD)
LOWEST = -1e30
PACK_VMEM = 4 * 1024 * 1024
SMALL_VMEM = 16 * 1024 * 1024
LARGE_VMEM = 60 * 1024 * 1024
SMEM = pl.BlockSpec(memory_space=pltpu.SMEM)
VMEM = pl.BlockSpec(memory_space=pltpu.VMEM)
HBM = pl.BlockSpec(memory_space=pltpu.HBM)


def fold(readout, values):
    return lax.dot_general(readout, values, NT, preferred_element_type=jnp.float32).astype(jnp.bfloat16)


def value_place(h, count, lat):
    return (h * lat) % HD, count * 2 * HD + (h * lat // HD) * HD


def pack_kernel(k, me_ref, model_ref, qkv_ref, readout_ref, *refs):
    out_ref, values, readout, sems = refs[-4:]
    rows = out_ref.shape[0]
    count, lat = values.shape[0], readout.shape[0]
    first = (me_ref[0] ^ k) * count

    def columns(h, part, width):
        return pl.ds(pl.multiple_of(((first + h) * 3 + part) * HD, HD), width)

    copies = [
        pltpu.make_async_copy(
            readout_ref.at[model_ref[0], :, pl.ds(pl.multiple_of(first * HD, HD), count * HD)], readout, sems.at[2 * count]
        )
    ]
    for h in range(count):
        copies.append(pltpu.make_async_copy(qkv_ref.at[0, :, columns(h, 2, HD)], values.at[h], sems.at[h]))
    for h in range(count):
        target = out_ref.at[:, h * 2 * HD : (h + 1) * 2 * HD]
        copies.append(pltpu.make_async_copy(qkv_ref.at[0, :, columns(h, 0, 2 * HD)], target, sems.at[count + h]))
    for copy in copies:
        copy.start()
    copies[0].wait()
    for h in range(count):
        copies[1 + h].wait()
        row, column = value_place(h, count, lat)
        out_ref[row : row + lat, column : column + HD] = fold(readout[:, h * HD : (h + 1) * HD], values[h])
    for copy in copies[1 + count :]:
        copy.wait()


def pack(me, model, qkv, readout_t, k, count, after, first=False):
    rows = qkv.shape[1]
    lat = readout_t.shape[1]
    width = count * 2 * HD + -(-count * lat // HD) * HD
    return pl.pallas_call(
        functools.partial(pack_kernel, k),
        in_specs=[SMEM, SMEM] + [HBM] * (2 + len(after)),
        out_specs=VMEM,
        out_shape=jax.ShapeDtypeStruct((rows, width), jnp.bfloat16),
        scratch_shapes=[
            pltpu.VMEM((count, rows, HD), jnp.bfloat16),
            pltpu.VMEM((lat, count * HD), jnp.bfloat16),
            pltpu.SemaphoreType.DMA((2 * count + 1,)),
        ],
        compiler_params=pltpu.CompilerParams(vmem_limit_bytes=LARGE_VMEM if first else PACK_VMEM),
        cost_estimate=pl.CostEstimate(
            flops=0, bytes_accessed=rows * width * 4, transcendentals=0
        ),
        name="pack",
    )(me, model, qkv, readout_t, *after)


def mask_rows(frames_ref, me, rows, query_offsets, key_offsets):
    columns = lax.broadcasted_iota(jnp.int32, (1, rows), 1)
    places = jnp.concatenate([(me ^ k) * rows + columns for k in query_offsets], axis=1)
    end = frames_ref[0] * FRAME_TOK
    bound = jnp.full(places.shape, end, jnp.int32)
    for c in range(1, frames_ref.shape[0]):
        later = end + frames_ref[c] * FRAME_TOK
        bound = jnp.where(places >= end, later, bound)
        end = later
    return [
        jnp.where((me ^ k) * rows + start < bound, 0.0, -jnp.inf)
        for k in key_offsets
        for start in range(0, rows, FRAME_TOK)
    ]


def run_units(units, lat):
    frames = [tile() for tile in units[0][0]]
    for u, (_, values, shifts, finish) in enumerate(units):
        ahead = list(units[u + 1][0]) if u + 1 < len(units) else []
        peaks = [jnp.max(f, axis=0, keepdims=True) + s for f, s in zip(sum(frames, []), shifts)]
        peak = jnp.maximum(functools.reduce(jnp.maximum, peaks), LOWEST)
        following, summed, start = [], None, 0
        for t, tile in enumerate(frames):
            for _ in range(-(-(len(ahead) - len(following)) // (len(frames) - t))):
                following.append(ahead[len(following)]())
            weights = [
                jnp.exp2((f + (s - peak)) * LOG2_SCALE).astype(jnp.bfloat16)
                for f, s in zip(tile, shifts[start : start + len(tile)])
            ]
            start += len(tile)
            part = jnp.dot(values[t](), jnp.concatenate(weights, axis=0), preferred_element_type=jnp.float32)
            summed = part if summed is None else summed + part
        finish(summed[:lat], summed[lat : lat + 1], peak)
        frames = following


def score_tile(keys, queries):
    scores = lax.dot_general(keys(), queries(), NT, preferred_element_type=jnp.float32)
    return [scores[start : start + FRAME_TOK] for start in range(0, scores.shape[0], FRAME_TOK)]


def stage_values(folded, pieces, lat):
    count = folded.shape[0]
    rows = pieces[0].shape[0]
    for i in range(count):
        row, column = value_place(i, count, lat)
        for n, piece in enumerate(pieces):
            folded[i, :lat, n * rows : (n + 1) * rows] = piece[row : row + lat, column : column + HD]
        folded[i, lat:] = jnp.ones_like(folded[i, lat:])


def pairs_of(pieces, i, what):
    column = (2 * i + what) * HD

    def read(n):
        return lambda: jnp.concatenate([pieces[n][:, column : column + HD], pieces[n + 1][:, column : column + HD]], axis=0)

    return [read(n) for n in range(0, len(pieces), 2)]


def early_kernel(offsets, frames_ref, me_ref, timestep_ref, step_weight_ref, sign_ref, sample_ref, *refs):
    count_pieces = len(offsets)
    arrived = refs[:count_pieces]
    sums_ref, stats_ref, factor_ref, pieces, folded, asked, sems = refs[-7:]
    me = me_ref[0]
    rows = pieces.shape[1]
    count, lat, _ = sums_ref.shape
    blocks = count_pieces // 2
    copies = [pltpu.make_async_copy(arrived[n], pieces.at[n], sems.at[n]) for n in range(count_pieces)]
    for copy in copies:
        copy.start()
    factor_ref[...] = jnp.full(factor_ref.shape, sign_ref[0] * step_weight_ref[timestep_ref[sample_ref[0]]])
    for copy in copies:
        copy.wait()
    pieces = [pieces.at[n] for n in range(count_pieces)]
    stage_values(folded, pieces, lat)
    for i in range(count):
        for b, read in enumerate(pairs_of(pieces, i, 0)):
            asked[b, i] = read()
    half = count_pieces // 2 + 1

    def some_blocks(b, carry):
        q = [2 * b, 2 * b + 1]
        span = pl.ds(pl.multiple_of(b * 2 * rows, 2 * rows), 2 * rows)
        shifts = mask_rows(frames_ref, me, rows, [jnp.where(n < half, n, n + 2) for n in q], offsets)
        peaks, totals, units = [], [], []
        for i in range(count):

            def finish(summed, total, peak, i=i):
                sums_ref[i, :, span] = summed
                peaks.append(peak)
                totals.append(total)

            tiles = [
                functools.partial(score_tile, keys, lambda i=i: asked[b, i]) for keys in pairs_of(pieces, i, 1)
            ]
            values = [lambda i=i, t=t: folded[i, :, t * 2 * rows : (t + 1) * 2 * rows] for t in range(blocks)]
            units.append((tiles, values, shifts, finish))
        run_units(units, lat)
        rest = [jnp.ones_like(peaks[0])] * (stats_ref.shape[1] - count)
        stats_ref[0, :, span] = jnp.concatenate(peaks + rest, axis=0)
        stats_ref[1, :, span] = jnp.concatenate(totals + rest, axis=0)
        return carry

    lax.fori_loop(0, blocks, some_blocks, 0)


def late_kernel(offsets, late, frames_ref, me_ref, *refs):
    early = len(offsets)
    arrived = refs[:2]
    sums_ref, stats_ref, factor_ref, early_ref, early_folded, *out_refs, late_pieces, folded, sems = refs[2:]
    copies = [pltpu.make_async_copy(arrived[n], late_pieces.at[n], sems.at[n]) for n in range(2)]
    for copy in copies:
        copy.start()
    me = me_ref[0]
    size, lat, rows = out_refs[0].shape
    count = folded.shape[0]
    for copy in copies:
        copy.wait()
    pieces = [early_ref.at[n] for n in range(early)] + [late_pieces.at[n] for n in range(2)]
    stage_values(folded, pieces[early:], lat)
    factor = factor_ref[:1]
    every = list(offsets) + list(late)
    blocks = early // 2
    results = {}

    def write(number, start):
        for j in range(number):
            k = every[start + j]
            out_ref = out_refs[k // size]
            out_ref[k % size] = (results[start][:, j * rows : (j + 1) * rows] * factor).astype(out_ref.dtype)

    units = []
    for start, number, tiles_in in ((0, early, [blocks]), (early, 2, range(blocks + 1))):
        key_offsets = [every[2 * t + j] for t in tiles_in for j in range(2)]
        shifts = mask_rows(frames_ref, me, rows, every[start : start + number], key_offsets)
        for i in range(count):

            def finish(summed, total, peak, start=start, number=number, i=i):
                if start == 0:
                    before = stats_ref[0, i : i + 1]
                    highest = jnp.maximum(before, peak)
                    old = jnp.exp2((before - highest) * LOG2_SCALE)
                    new = jnp.exp2((peak - highest) * LOG2_SCALE)
                    both = stats_ref[1, i : i + 1] * old + total * new
                    part = sums_ref[i] * (old / both) + summed * (new / both)
                else:
                    part = summed / total
                results[start] = part if i == 0 else results[start] + part
                if i == count - 1:
                    write(number, start)

            def queries(start=start, number=number, i=i):
                column = 2 * i * HD
                return jnp.concatenate([p[:, column : column + HD] for p in pieces[start : start + number]], axis=0)

            keys = pairs_of(pieces, i, 1)
            tiles = [functools.partial(score_tile, keys[t], queries) for t in tiles_in]
            values = [
                lambda i=i, t=t: folded[i] if t == blocks else early_folded[i, :, t * 2 * rows : (t + 1) * 2 * rows]
                for t in tiles_in
            ]
            units.append((tiles, values, shifts, finish))
    run_units(units, lat)


def attend_early(pieces, offsets, span_frames, me, timestep, step_weight, sign, sample, count, lat):
    rows, width = pieces[0].shape
    blocks = len(pieces) // 2
    tokens = len(pieces) * rows
    return pl.pallas_call(
        functools.partial(early_kernel, offsets),
        in_specs=[SMEM] * 6 + [HBM] * len(pieces),
        out_specs=[VMEM] * 5,
        out_shape=[
            jax.ShapeDtypeStruct((count, lat, tokens), jnp.float32),
            jax.ShapeDtypeStruct((2, 8, tokens), jnp.float32),
            jax.ShapeDtypeStruct((8, rows), jnp.float32),
            jax.ShapeDtypeStruct((len(pieces), rows, width), jnp.bfloat16),
            jax.ShapeDtypeStruct((count, lat + 16, tokens), jnp.bfloat16),
        ],
        scratch_shapes=[
            pltpu.VMEM((blocks, count, 2 * rows, HD), jnp.bfloat16),
            pltpu.SemaphoreType.DMA((len(pieces),)),
        ],
        compiler_params=pltpu.CompilerParams(vmem_limit_bytes=SMALL_VMEM if len(pieces) <= 8 else LARGE_VMEM),
        cost_estimate=pl.CostEstimate(
            flops=count * tokens * tokens * 2 * (HD + lat),
            bytes_accessed=tokens * count * 3 * HD * 2,
            transcendentals=count * tokens * tokens,
        ),
        name="attend_early",
    )(span_frames, me, timestep, step_weight, sign, sample, *pieces)


def attend_late(pieces, offsets, late, early, span_frames, me, count, lat):
    rows, width = pieces[0].shape
    half = len(offsets) // 2 + 1
    tokens = 2 * half * rows
    return pl.pallas_call(
        functools.partial(late_kernel, offsets, late),
        in_specs=[SMEM] * 2 + [HBM] * 2 + [VMEM] * len(early),
        out_specs=[VMEM] * 4,
        out_shape=[
            jax.ShapeDtypeStruct((half // 2, lat, rows), jnp.bfloat16 if g else jnp.float32) for g in range(4)
        ],
        scratch_shapes=[
            pltpu.VMEM((2, rows, width), jnp.bfloat16),
            pltpu.VMEM((count, lat + 16, 2 * rows), jnp.bfloat16),
            pltpu.SemaphoreType.DMA((2,)),
        ],
        compiler_params=pltpu.CompilerParams(vmem_limit_bytes=SMALL_VMEM if half <= 4 else LARGE_VMEM),
        cost_estimate=pl.CostEstimate(
            flops=count * tokens * rows * 4 * (HD + lat),
            bytes_accessed=tokens * count * 3 * HD * 2,
            transcendentals=count * tokens * rows * 2,
        ),
        name="attend_late",
    )(span_frames, me, *pieces, *early)


def swap(array, axis, offset):
    size = lax.axis_size(axis)
    return lax.ppermute(array, axis, [(i, i ^ offset) for i in range(size)])


def body(qkv, readout, step_weight, timestep, span_frames):
    seq_count = lax.axis_size("seq")
    mp_count = lax.axis_size("mp")
    half = seq_count // 2
    count = HEADS // seq_count
    lat = readout.shape[2]
    me = lax.axis_index("seq").astype(jnp.int32).reshape(1)
    mp_index = lax.axis_index("mp").astype(jnp.int32)
    sample_count = mp_count // 2
    model_index = mp_index // sample_count
    sample = (mp_index % sample_count).reshape(1)
    sign = jnp.where(model_index == 1, 1.0, -1.0).astype(jnp.float32).reshape(1)
    model = model_index.reshape(1)
    readout_t = jnp.swapaxes(readout, 1, 2)

    pieces = [None] * seq_count
    for n in range(half):
        k = seq_count - 1 - n
        pieces[k] = swap(pack(me, model, qkv, readout_t, k, count, [pieces[k + 2]] if n > 1 else [], n == 0), "seq", k)
    for k in range(half - 1, 0, -1):
        after = [] if k == half - 1 else [pieces[k + 1], pieces[seq_count - 1]] if k > 1 else [pieces[half - 1]]
        pieces[k] = swap(pack(me, model, qkv, readout_t, k, count, after), "seq", k)
    pieces[0] = pack(me, model, qkv, readout_t, 0, count, [pieces[half - 1]])
    late = [half, half + 1]
    early = [k for k in range(seq_count) if k not in late]
    merged = attend_early(
        [pieces[k] for k in early], early, span_frames, me, timestep, step_weight, sign, sample, count, lat
    )
    ends = [pieces[k] for k in late]
    given = attend_late(ends, early, late, merged, span_frames, me, count, lat)
    size = half // 2
    while size > 1:
        keep = given[0]
        for n in range(len(given) - 1, 0, -1):
            keep = keep + swap(given[n], "seq", n * size).astype(jnp.float32)
        radix = min(4, size // 2)
        if radix == 1:
            break
        size //= radix
        given = [keep[n * size : (n + 1) * size] for n in range(radix)]
    together = min(4, mp_count)
    total = keep[0]
    for n in range(2 * together - 1, 0, -1):
        total = total + swap(keep[n // together], ("seq", "mp"), n // together * mp_count + n % together)
    offset = together
    while offset < mp_count:
        radix = min(4, mp_count // offset)
        own = total
        for n in range(radix - 1, 0, -1):
            total = total + swap(own, "mp", offset * n)
        offset *= radix
    return total.T


def solution(mesh):
    return jax.shard_map(
        body,
        mesh=mesh,
        in_specs=(P("mp", "seq", None), P(), P(), P(), P()),
        out_specs=P("seq", None),
        check_vma=False,
    )
```

```python
import functools
import math

import jax
import jax.numpy as jnp
from jax import lax
from jax.experimental import pallas as pl
from jax.experimental.pallas import tpu as pltpu
from jax.sharding import PartitionSpec as P

HEADS = 32
HD = 128
FRAME_TOK = 64
NT = (((1,), (1,)), ((), ()))
LOG2_SCALE = math.log2(math.e) / math.sqrt(HD)
LOWEST = -1e30
PACK_VMEM = 4 * 1024 * 1024
SMALL_VMEM = 16 * 1024 * 1024
LARGE_VMEM = 60 * 1024 * 1024
SMEM = pl.BlockSpec(memory_space=pltpu.SMEM)
VMEM = pl.BlockSpec(memory_space=pltpu.VMEM)
HBM = pl.BlockSpec(memory_space=pltpu.HBM)


def fold(readout, values):
    return lax.dot_general(readout, values, NT, preferred_element_type=jnp.float32).astype(jnp.bfloat16)


def value_place(h, count, lat):
    return (h * lat) % HD, count * 2 * HD + (h * lat // HD) * HD


def pack_kernel(k, me_ref, model_ref, qkv_ref, readout_ref, *refs):
    out_ref, values, readout, sems = refs[-4:]
    rows = out_ref.shape[0]
    count, lat = values.shape[0], readout.shape[0]
    first = (me_ref[0] ^ k) * count

    def columns(h, part, width):
        return pl.ds(pl.multiple_of(((first + h) * 3 + part) * HD, HD), width)

    copies = [
        pltpu.make_async_copy(
            readout_ref.at[model_ref[0], :, pl.ds(pl.multiple_of(first * HD, HD), count * HD)], readout, sems.at[2 * count]
        )
    ]
    for h in range(count):
        copies.append(pltpu.make_async_copy(qkv_ref.at[0, :, columns(h, 2, HD)], values.at[h], sems.at[h]))
    for h in range(count):
        target = out_ref.at[:, h * 2 * HD : (h + 1) * 2 * HD]
        copies.append(pltpu.make_async_copy(qkv_ref.at[0, :, columns(h, 0, 2 * HD)], target, sems.at[count + h]))
    for copy in copies:
        copy.start()
    copies[0].wait()
    for h in range(count):
        copies[1 + h].wait()
        row, column = value_place(h, count, lat)
        out_ref[row : row + lat, column : column + HD] = fold(readout[:, h * HD : (h + 1) * HD], values[h])
    for copy in copies[1 + count :]:
        copy.wait()


def pack(me, model, qkv, readout_t, k, count, after, first=False):
    rows = qkv.shape[1]
    lat = readout_t.shape[1]
    width = count * 2 * HD + -(-count * lat // HD) * HD
    return pl.pallas_call(
        functools.partial(pack_kernel, k),
        in_specs=[SMEM, SMEM] + [HBM] * (2 + len(after)),
        out_specs=VMEM,
        out_shape=jax.ShapeDtypeStruct((rows, width), jnp.bfloat16),
        scratch_shapes=[
            pltpu.VMEM((count, rows, HD), jnp.bfloat16),
            pltpu.VMEM((lat, count * HD), jnp.bfloat16),
            pltpu.SemaphoreType.DMA((2 * count + 1,)),
        ],
        compiler_params=pltpu.CompilerParams(vmem_limit_bytes=LARGE_VMEM if first else PACK_VMEM),
        cost_estimate=pl.CostEstimate(
            flops=0, bytes_accessed=rows * width * 4, transcendentals=0
        ),
        name="pack",
    )(me, model, qkv, readout_t, *after)


def mask_rows(frames_ref, me, rows, query_offsets, key_offsets):
    columns = lax.broadcasted_iota(jnp.int32, (1, rows), 1)
    places = jnp.concatenate([(me ^ k) * rows + columns for k in query_offsets], axis=1)
    end = frames_ref[0] * FRAME_TOK
    bound = jnp.full(places.shape, end, jnp.int32)
    for c in range(1, frames_ref.shape[0]):
        later = end + frames_ref[c] * FRAME_TOK
        bound = jnp.where(places >= end, later, bound)
        end = later
    return [
        jnp.where((me ^ k) * rows + start < bound, 0.0, -jnp.inf)
        for k in key_offsets
        for start in range(0, rows, FRAME_TOK)
    ]


def run_units(units, lat):
    frames = [tile() for tile in units[0][0]]
    for u, (_, values, shifts, finish) in enumerate(units):
        ahead = list(units[u + 1][0]) if u + 1 < len(units) else []
        peaks = [jnp.max(f, axis=0, keepdims=True) + s for f, s in zip(sum(frames, []), shifts)]
        peak = jnp.maximum(functools.reduce(jnp.maximum, peaks), LOWEST)
        following, summed, start = [], None, 0
        for t, tile in enumerate(frames):
            for _ in range(-(-(len(ahead) - len(following)) // (len(frames) - t))):
                following.append(ahead[len(following)]())
            weights = [
                jnp.exp2((f + (s - peak)) * LOG2_SCALE).astype(jnp.bfloat16)
                for f, s in zip(tile, shifts[start : start + len(tile)])
            ]
            start += len(tile)
            part = jnp.dot(values[t](), jnp.concatenate(weights, axis=0), preferred_element_type=jnp.float32)
            summed = part if summed is None else summed + part
        finish(summed[:lat], summed[lat : lat + 1], peak)
        frames = following


def score_tile(keys, queries):
    scores = lax.dot_general(keys(), queries(), NT, preferred_element_type=jnp.float32)
    return [scores[start : start + FRAME_TOK] for start in range(0, scores.shape[0], FRAME_TOK)]


def stage_values(folded, pieces, lat):
    count = folded.shape[0]
    rows = pieces[0].shape[0]
    for i in range(count):
        row, column = value_place(i, count, lat)
        for n, piece in enumerate(pieces):
            folded[i, :lat, n * rows : (n + 1) * rows] = piece[row : row + lat, column : column + HD]
        folded[i, lat:] = jnp.ones_like(folded[i, lat:])


def pairs_of(pieces, i, what):
    column = (2 * i + what) * HD

    def read(n):
        return lambda: jnp.concatenate([pieces[n][:, column : column + HD], pieces[n + 1][:, column : column + HD]], axis=0)

    return [read(n) for n in range(0, len(pieces), 2)]


def early_kernel(offsets, frames_ref, me_ref, timestep_ref, step_weight_ref, sign_ref, sample_ref, *refs):
    count_pieces = len(offsets)
    arrived = refs[:count_pieces]
    sums_ref, stats_ref, factor_ref, pieces, folded, asked, sems = refs[-7:]
    me = me_ref[0]
    rows = pieces.shape[1]
    count, lat, _ = sums_ref.shape
    blocks = count_pieces // 2
    copies = [pltpu.make_async_copy(arrived[n], pieces.at[n], sems.at[n]) for n in range(count_pieces)]
    for copy in copies:
        copy.start()
    factor_ref[...] = jnp.full(factor_ref.shape, sign_ref[0] * step_weight_ref[timestep_ref[sample_ref[0]]])
    for copy in copies:
        copy.wait()
    pieces = [pieces.at[n] for n in range(count_pieces)]
    stage_values(folded, pieces, lat)
    for i in range(count):
        for b, read in enumerate(pairs_of(pieces, i, 0)):
            asked[b, i] = read()
    half = count_pieces // 2 + 1

    def some_blocks(b, carry):
        q = [2 * b, 2 * b + 1]
        span = pl.ds(pl.multiple_of(b * 2 * rows, 2 * rows), 2 * rows)
        shifts = mask_rows(frames_ref, me, rows, [jnp.where(n < half, n, n + 2) for n in q], offsets)
        peaks, totals, units = [], [], []
        for i in range(count):

            def finish(summed, total, peak, i=i):
                sums_ref[i, :, span] = summed
                peaks.append(peak)
                totals.append(total)

            tiles = [
                functools.partial(score_tile, keys, lambda i=i: asked[b, i]) for keys in pairs_of(pieces, i, 1)
            ]
            values = [lambda i=i, t=t: folded[i, :, t * 2 * rows : (t + 1) * 2 * rows] for t in range(blocks)]
            units.append((tiles, values, shifts, finish))
        run_units(units, lat)
        rest = [jnp.ones_like(peaks[0])] * (stats_ref.shape[1] - count)
        stats_ref[0, :, span] = jnp.concatenate(peaks + rest, axis=0)
        stats_ref[1, :, span] = jnp.concatenate(totals + rest, axis=0)
        return carry

    lax.fori_loop(0, blocks, some_blocks, 0)


def late_kernel(offsets, late, frames_ref, me_ref, *refs):
    early = len(offsets)
    arrived = refs[:2]
    sums_ref, stats_ref, factor_ref, early_ref, early_folded, *out_refs, late_pieces, folded, sems = refs[2:]
    copies = [pltpu.make_async_copy(arrived[n], late_pieces.at[n], sems.at[n]) for n in range(2)]
    for copy in copies:
        copy.start()
    me = me_ref[0]
    size, lat, rows = out_refs[0].shape
    count = folded.shape[0]
    for copy in copies:
        copy.wait()
    pieces = [early_ref.at[n] for n in range(early)] + [late_pieces.at[n] for n in range(2)]
    stage_values(folded, pieces[early:], lat)
    factor = factor_ref[:1]
    every = list(offsets) + list(late)
    blocks = early // 2
    results = {}

    def write(number, start):
        for j in range(number):
            k = every[start + j]
            out_ref = out_refs[k // size]
            out_ref[k % size] = (results[start][:, j * rows : (j + 1) * rows] * factor).astype(out_ref.dtype)

    units = []
    for start, number, tiles_in in ((0, early, [blocks]), (early, 2, range(blocks + 1))):
        key_offsets = [every[2 * t + j] for t in tiles_in for j in range(2)]
        shifts = mask_rows(frames_ref, me, rows, every[start : start + number], key_offsets)
        for i in range(count):

            def finish(summed, total, peak, start=start, number=number, i=i):
                if start == 0:
                    before = stats_ref[0, i : i + 1]
                    highest = jnp.maximum(before, peak)
                    old = jnp.exp2((before - highest) * LOG2_SCALE)
                    new = jnp.exp2((peak - highest) * LOG2_SCALE)
                    both = stats_ref[1, i : i + 1] * old + total * new
                    part = sums_ref[i] * (old / both) + summed * (new / both)
                else:
                    part = summed / total
                results[start] = part if i == 0 else results[start] + part
                if i == count - 1:
                    write(number, start)

            def queries(start=start, number=number, i=i):
                column = 2 * i * HD
                return jnp.concatenate([p[:, column : column + HD] for p in pieces[start : start + number]], axis=0)

            keys = pairs_of(pieces, i, 1)
            tiles = [functools.partial(score_tile, keys[t], queries) for t in tiles_in]
            values = [
                lambda i=i, t=t: folded[i] if t == blocks else early_folded[i, :, t * 2 * rows : (t + 1) * 2 * rows]
                for t in tiles_in
            ]
            units.append((tiles, values, shifts, finish))
    run_units(units, lat)


def attend_early(pieces, offsets, span_frames, me, timestep, step_weight, sign, sample, count, lat):
    rows, width = pieces[0].shape
    blocks = len(pieces) // 2
    tokens = len(pieces) * rows
    return pl.pallas_call(
        functools.partial(early_kernel, offsets),
        in_specs=[SMEM] * 6 + [HBM] * len(pieces),
        out_specs=[VMEM] * 5,
        out_shape=[
            jax.ShapeDtypeStruct((count, lat, tokens), jnp.float32),
            jax.ShapeDtypeStruct((2, 8, tokens), jnp.float32),
            jax.ShapeDtypeStruct((8, rows), jnp.float32),
            jax.ShapeDtypeStruct((len(pieces), rows, width), jnp.bfloat16),
            jax.ShapeDtypeStruct((count, lat + 16, tokens), jnp.bfloat16),
        ],
        scratch_shapes=[
            pltpu.VMEM((blocks, count, 2 * rows, HD), jnp.bfloat16),
            pltpu.SemaphoreType.DMA((len(pieces),)),
        ],
        compiler_params=pltpu.CompilerParams(vmem_limit_bytes=SMALL_VMEM if len(pieces) <= 8 else LARGE_VMEM),
        cost_estimate=pl.CostEstimate(
            flops=count * tokens * tokens * 2 * (HD + lat),
            bytes_accessed=tokens * count * 3 * HD * 2,
            transcendentals=count * tokens * tokens,
        ),
        name="attend_early",
    )(span_frames, me, timestep, step_weight, sign, sample, *pieces)


def attend_late(pieces, offsets, late, early, span_frames, me, count, lat):
    rows, width = pieces[0].shape
    half = len(offsets) // 2 + 1
    tokens = 2 * half * rows
    return pl.pallas_call(
        functools.partial(late_kernel, offsets, late),
        in_specs=[SMEM] * 2 + [HBM] * 2 + [VMEM] * len(early),
        out_specs=[VMEM] * 4,
        out_shape=[
            jax.ShapeDtypeStruct((half // 2, lat, rows), jnp.bfloat16 if g else jnp.float32) for g in range(4)
        ],
        scratch_shapes=[
            pltpu.VMEM((2, rows, width), jnp.bfloat16),
            pltpu.VMEM((count, lat + 16, 2 * rows), jnp.bfloat16),
            pltpu.SemaphoreType.DMA((2,)),
        ],
        compiler_params=pltpu.CompilerParams(vmem_limit_bytes=SMALL_VMEM if half <= 4 else LARGE_VMEM),
        cost_estimate=pl.CostEstimate(
            flops=count * tokens * rows * 4 * (HD + lat),
            bytes_accessed=tokens * count * 3 * HD * 2,
            transcendentals=count * tokens * rows * 2,
        ),
        name="attend_late",
    )(span_frames, me, *pieces, *early)


def swap(array, axis, offset):
    size = lax.axis_size(axis)
    return lax.ppermute(array, axis, [(i, i ^ offset) for i in range(size)])


def body(qkv, readout, step_weight, timestep, span_frames):
    seq_count = lax.axis_size("seq")
    mp_count = lax.axis_size("mp")
    half = seq_count // 2
    count = HEADS // seq_count
    lat = readout.shape[2]
    me = lax.axis_index("seq").astype(jnp.int32).reshape(1)
    mp_index = lax.axis_index("mp").astype(jnp.int32)
    sample_count = mp_count // 2
    model_index = mp_index // sample_count
    sample = (mp_index % sample_count).reshape(1)
    sign = jnp.where(model_index == 1, 1.0, -1.0).astype(jnp.float32).reshape(1)
    model = model_index.reshape(1)
    readout_t = jnp.swapaxes(readout, 1, 2)

    pieces = [None] * seq_count
    for n in range(half):
        k = seq_count - 1 - n
        packed = pack(me, model, qkv, readout_t, k, count, [pieces[k + 2]] if n > 1 else [], n < 2)
        pieces[k] = swap(packed, "seq", k)
    for k in range(half - 1, 0, -1):
        after = [] if k == half - 1 else [pieces[k + 1], pieces[seq_count - 1]] if k > 1 else [pieces[half - 1]]
        pieces[k] = swap(pack(me, model, qkv, readout_t, k, count, after, k == half - 1), "seq", k)
    pieces[0] = pack(me, model, qkv, readout_t, 0, count, [pieces[half - 1]])
    late = [half, half + 1]
    early = [k for k in range(seq_count) if k not in late]
    merged = attend_early(
        [pieces[k] for k in early], early, span_frames, me, timestep, step_weight, sign, sample, count, lat
    )
    ends = [pieces[k] for k in late]
    given = attend_late(ends, early, late, merged, span_frames, me, count, lat)
    size = half // 2
    while True:
        keep = given[0]
        for n in range(len(given) - 1, 0, -1):
            keep = keep + swap(given[n], "seq", n * size).astype(jnp.float32)
        if size == 1:
            break
        radix = min(4, size)
        size //= radix
        given = [keep[n * size : (n + 1) * size] for n in range(radix)]
    total = keep[0]
    offset = 1
    while offset < mp_count:
        radix = min(4, mp_count // offset)
        own = total
        for n in range(radix - 1, 0, -1):
            total = total + swap(own, "mp", offset * n)
        offset *= radix
    return total.T


def solution(mesh):
    return jax.shard_map(
        body,
        mesh=mesh,
        in_specs=(P("mp", "seq", None), P(), P(), P(), P()),
        out_specs=P("seq", None),
        check_vma=False,
    )
```

```python
import functools
import math

import jax
import jax.numpy as jnp
from jax import lax
from jax.experimental import pallas as pl
from jax.experimental.pallas import tpu as pltpu
from jax.sharding import PartitionSpec as P

HEADS = 32
HD = 128
FRAME_TOK = 64
NT = (((1,), (1,)), ((), ()))
LOG2_SCALE = math.log2(math.e) / math.sqrt(HD)
LOWEST = -1e30
PACK_VMEM = 4 * 1024 * 1024
SMALL_VMEM = 16 * 1024 * 1024
LARGE_VMEM = 60 * 1024 * 1024
SMEM = pl.BlockSpec(memory_space=pltpu.SMEM)
VMEM = pl.BlockSpec(memory_space=pltpu.VMEM)
HBM = pl.BlockSpec(memory_space=pltpu.HBM)


def fold(readout, values):
    return lax.dot_general(readout, values, NT, preferred_element_type=jnp.float32).astype(jnp.bfloat16)


def value_place(h, count, lat):
    return (h * lat) % HD, count * 2 * HD + (h * lat // HD) * HD


def pack_kernel(k, me_ref, model_ref, qkv_ref, readout_ref, *refs):
    out_ref, values, readout, sems = refs[-4:]
    rows = out_ref.shape[0]
    count, lat = values.shape[0], readout.shape[0]
    first = (me_ref[0] ^ k) * count

    def columns(h, part, width):
        return pl.ds(pl.multiple_of(((first + h) * 3 + part) * HD, HD), width)

    copies = [
        pltpu.make_async_copy(
            readout_ref.at[model_ref[0], :, pl.ds(pl.multiple_of(first * HD, HD), count * HD)], readout, sems.at[2 * count]
        )
    ]
    for h in range(count):
        copies.append(pltpu.make_async_copy(qkv_ref.at[0, :, columns(h, 2, HD)], values.at[h], sems.at[h]))
    for h in range(count):
        target = out_ref.at[:, h * 2 * HD : (h + 1) * 2 * HD]
        copies.append(pltpu.make_async_copy(qkv_ref.at[0, :, columns(h, 0, 2 * HD)], target, sems.at[count + h]))
    for copy in copies:
        copy.start()
    copies[0].wait()
    for h in range(count):
        copies[1 + h].wait()
        row, column = value_place(h, count, lat)
        out_ref[row : row + lat, column : column + HD] = fold(readout[:, h * HD : (h + 1) * HD], values[h])
    for copy in copies[1 + count :]:
        copy.wait()


def pack(me, model, qkv, readout_t, k, count, after, first=False):
    rows = qkv.shape[1]
    lat = readout_t.shape[1]
    width = count * 2 * HD + -(-count * lat // HD) * HD
    return pl.pallas_call(
        functools.partial(pack_kernel, k),
        in_specs=[SMEM, SMEM] + [HBM] * (2 + len(after)),
        out_specs=VMEM,
        out_shape=jax.ShapeDtypeStruct((rows, width), jnp.bfloat16),
        scratch_shapes=[
            pltpu.VMEM((count, rows, HD), jnp.bfloat16),
            pltpu.VMEM((lat, count * HD), jnp.bfloat16),
            pltpu.SemaphoreType.DMA((2 * count + 1,)),
        ],
        compiler_params=pltpu.CompilerParams(vmem_limit_bytes=LARGE_VMEM if first else PACK_VMEM),
        cost_estimate=pl.CostEstimate(
            flops=0, bytes_accessed=rows * width * 4, transcendentals=0
        ),
        name="pack",
    )(me, model, qkv, readout_t, *after)


def mask_rows(frames_ref, me, rows, query_offsets, key_offsets):
    columns = lax.broadcasted_iota(jnp.int32, (1, rows), 1)
    places = jnp.concatenate([(me ^ k) * rows + columns for k in query_offsets], axis=1)
    end = frames_ref[0] * FRAME_TOK
    bound = jnp.full(places.shape, end, jnp.int32)
    for c in range(1, frames_ref.shape[0]):
        later = end + frames_ref[c] * FRAME_TOK
        bound = jnp.where(places >= end, later, bound)
        end = later
    return [
        jnp.where((me ^ k) * rows + start < bound, 0.0, -jnp.inf)
        for k in key_offsets
        for start in range(0, rows, FRAME_TOK)
    ]


def run_units(units, lat):
    frames = [tile() for tile in units[0][0]]
    for u, (_, values, shifts, finish) in enumerate(units):
        ahead = list(units[u + 1][0]) if u + 1 < len(units) else []
        peaks = [jnp.max(f, axis=0, keepdims=True) + s for f, s in zip(sum(frames, []), shifts)]
        peak = jnp.maximum(functools.reduce(jnp.maximum, peaks), LOWEST)
        following, summed, start = [], None, 0
        for t, tile in enumerate(frames):
            for _ in range(-(-(len(ahead) - len(following)) // (len(frames) - t))):
                following.append(ahead[len(following)]())
            weights = [
                jnp.exp2((f + (s - peak)) * LOG2_SCALE).astype(jnp.bfloat16)
                for f, s in zip(tile, shifts[start : start + len(tile)])
            ]
            start += len(tile)
            part = jnp.dot(values[t](), jnp.concatenate(weights, axis=0), preferred_element_type=jnp.float32)
            summed = part if summed is None else summed + part
        finish(summed[:lat], summed[lat : lat + 1], peak)
        frames = following


def score_tile(keys, queries):
    scores = lax.dot_general(keys(), queries(), NT, preferred_element_type=jnp.float32)
    return [scores[start : start + FRAME_TOK] for start in range(0, scores.shape[0], FRAME_TOK)]


def stage_values(folded, pieces, lat):
    count = folded.shape[0]
    rows = pieces[0].shape[0]
    for i in range(count):
        row, column = value_place(i, count, lat)
        for n, piece in enumerate(pieces):
            folded[i, :lat, n * rows : (n + 1) * rows] = piece[row : row + lat, column : column + HD]
        folded[i, lat:] = jnp.ones_like(folded[i, lat:])


def pairs_of(pieces, i, what):
    column = (2 * i + what) * HD

    def read(n):
        return lambda: jnp.concatenate([pieces[n][:, column : column + HD], pieces[n + 1][:, column : column + HD]], axis=0)

    return [read(n) for n in range(0, len(pieces), 2)]


def early_kernel(offsets, frames_ref, me_ref, timestep_ref, step_weight_ref, sign_ref, sample_ref, *refs):
    count_pieces = len(offsets)
    arrived = refs[:count_pieces]
    sums_ref, stats_ref, factor_ref, pieces, folded, asked, sems = refs[-7:]
    me = me_ref[0]
    rows = pieces.shape[1]
    count, lat, _ = sums_ref.shape
    blocks = count_pieces // 2
    copies = [pltpu.make_async_copy(arrived[n], pieces.at[n], sems.at[n]) for n in range(count_pieces)]
    for copy in copies:
        copy.start()
    factor_ref[...] = jnp.full(factor_ref.shape, sign_ref[0] * step_weight_ref[timestep_ref[sample_ref[0]]])
    for copy in copies:
        copy.wait()
    pieces = [pieces.at[n] for n in range(count_pieces)]
    stage_values(folded, pieces, lat)
    for i in range(count):
        for b, read in enumerate(pairs_of(pieces, i, 0)):
            asked[b, i] = read()

    def some_blocks(b, carry):
        q = [2 * b, 2 * b + 1]
        span = pl.ds(pl.multiple_of(b * 2 * rows, 2 * rows), 2 * rows)
        shifts = mask_rows(frames_ref, me, rows, [sum(jnp.where(n == j, k, 0) for j, k in enumerate(offsets)) for n in q], offsets)
        peaks, totals, units = [], [], []
        for i in range(count):

            def finish(summed, total, peak, i=i):
                sums_ref[i, :, span] = summed
                peaks.append(peak)
                totals.append(total)

            tiles = [
                functools.partial(score_tile, keys, lambda i=i: asked[b, i]) for keys in pairs_of(pieces, i, 1)
            ]
            values = [lambda i=i, t=t: folded[i, :, t * 2 * rows : (t + 1) * 2 * rows] for t in range(blocks)]
            units.append((tiles, values, shifts, finish))
        run_units(units, lat)
        rest = [jnp.ones_like(peaks[0])] * (stats_ref.shape[1] - count)
        stats_ref[0, :, span] = jnp.concatenate(peaks + rest, axis=0)
        stats_ref[1, :, span] = jnp.concatenate(totals + rest, axis=0)
        return carry

    lax.fori_loop(0, blocks, some_blocks, 0)


def late_kernel(offsets, late, frames_ref, me_ref, *refs):
    early = len(offsets)
    arrived = refs[:2]
    sums_ref, stats_ref, factor_ref, early_ref, early_folded, *out_refs, late_pieces, folded, sems = refs[2:]
    copies = [pltpu.make_async_copy(arrived[n], late_pieces.at[n], sems.at[n]) for n in range(2)]
    for copy in copies:
        copy.start()
    me = me_ref[0]
    size, lat, rows = out_refs[0].shape
    count = folded.shape[0]
    for copy in copies:
        copy.wait()
    pieces = [early_ref.at[n] for n in range(early)] + [late_pieces.at[n] for n in range(2)]
    stage_values(folded, pieces[early:], lat)
    factor = factor_ref[:1]
    every = list(offsets) + list(late)
    blocks = early // 2
    results = {}

    def write(number, start):
        for j in range(number):
            k = every[start + j]
            out_ref = out_refs[k // size]
            out_ref[k % size] = (results[start][:, j * rows : (j + 1) * rows] * factor).astype(out_ref.dtype)

    units = []
    for start, number, tiles_in in ((0, early, [blocks]), (early, 2, range(blocks + 1))):
        key_offsets = [every[2 * t + j] for t in tiles_in for j in range(2)]
        shifts = mask_rows(frames_ref, me, rows, every[start : start + number], key_offsets)
        for i in range(count):

            def finish(summed, total, peak, start=start, number=number, i=i):
                if start == 0:
                    before = stats_ref[0, i : i + 1]
                    highest = jnp.maximum(before, peak)
                    old = jnp.exp2((before - highest) * LOG2_SCALE)
                    new = jnp.exp2((peak - highest) * LOG2_SCALE)
                    both = stats_ref[1, i : i + 1] * old + total * new
                    part = sums_ref[i] * (old / both) + summed * (new / both)
                else:
                    part = summed / total
                results[start] = part if i == 0 else results[start] + part
                if i == count - 1:
                    write(number, start)

            def queries(start=start, number=number, i=i):
                column = 2 * i * HD
                return jnp.concatenate([p[:, column : column + HD] for p in pieces[start : start + number]], axis=0)

            keys = pairs_of(pieces, i, 1)
            tiles = [functools.partial(score_tile, keys[t], queries) for t in tiles_in]
            values = [
                lambda i=i, t=t: folded[i] if t == blocks else early_folded[i, :, t * 2 * rows : (t + 1) * 2 * rows]
                for t in tiles_in
            ]
            units.append((tiles, values, shifts, finish))
    run_units(units, lat)


def attend_early(pieces, offsets, span_frames, me, timestep, step_weight, sign, sample, count, lat):
    rows, width = pieces[0].shape
    blocks = len(pieces) // 2
    tokens = len(pieces) * rows
    return pl.pallas_call(
        functools.partial(early_kernel, offsets),
        in_specs=[SMEM] * 6 + [HBM] * len(pieces),
        out_specs=[VMEM] * 5,
        out_shape=[
            jax.ShapeDtypeStruct((count, lat, tokens), jnp.float32),
            jax.ShapeDtypeStruct((2, 8, tokens), jnp.float32),
            jax.ShapeDtypeStruct((8, rows), jnp.float32),
            jax.ShapeDtypeStruct((len(pieces), rows, width), jnp.bfloat16),
            jax.ShapeDtypeStruct((count, lat + 16, tokens), jnp.bfloat16),
        ],
        scratch_shapes=[
            pltpu.VMEM((blocks, count, 2 * rows, HD), jnp.bfloat16),
            pltpu.SemaphoreType.DMA((len(pieces),)),
        ],
        compiler_params=pltpu.CompilerParams(vmem_limit_bytes=SMALL_VMEM if len(pieces) <= 8 else LARGE_VMEM),
        cost_estimate=pl.CostEstimate(
            flops=count * tokens * tokens * 2 * (HD + lat),
            bytes_accessed=tokens * count * 3 * HD * 2,
            transcendentals=count * tokens * tokens,
        ),
        name="attend_early",
    )(span_frames, me, timestep, step_weight, sign, sample, *pieces)


def attend_late(pieces, offsets, late, early, span_frames, me, count, lat):
    rows, width = pieces[0].shape
    half = len(offsets) // 2 + 1
    tokens = 2 * half * rows
    return pl.pallas_call(
        functools.partial(late_kernel, offsets, late),
        in_specs=[SMEM] * 2 + [HBM] * 2 + [VMEM] * len(early),
        out_specs=[VMEM] * 4,
        out_shape=[
            jax.ShapeDtypeStruct((half // 2, lat, rows), jnp.bfloat16 if g else jnp.float32) for g in range(4)
        ],
        scratch_shapes=[
            pltpu.VMEM((2, rows, width), jnp.bfloat16),
            pltpu.VMEM((count, lat + 16, 2 * rows), jnp.bfloat16),
            pltpu.SemaphoreType.DMA((2,)),
        ],
        compiler_params=pltpu.CompilerParams(vmem_limit_bytes=SMALL_VMEM if half <= 4 else LARGE_VMEM),
        cost_estimate=pl.CostEstimate(
            flops=count * tokens * rows * 4 * (HD + lat),
            bytes_accessed=tokens * count * 3 * HD * 2,
            transcendentals=count * tokens * rows * 2,
        ),
        name="attend_late",
    )(span_frames, me, *pieces, *early)


def swap(array, axis, offset):
    size = lax.axis_size(axis)
    return lax.ppermute(array, axis, [(i, i ^ offset) for i in range(size)])


def body(qkv, readout, step_weight, timestep, span_frames):
    seq_count = lax.axis_size("seq")
    mp_count = lax.axis_size("mp")
    half = seq_count // 2
    count = HEADS // seq_count
    lat = readout.shape[2]
    me = lax.axis_index("seq").astype(jnp.int32).reshape(1)
    mp_index = lax.axis_index("mp").astype(jnp.int32)
    sample_count = mp_count // 2
    model_index = mp_index // sample_count
    sample = (mp_index % sample_count).reshape(1)
    sign = jnp.where(model_index == 1, 1.0, -1.0).astype(jnp.float32).reshape(1)
    model = model_index.reshape(1)
    readout_t = jnp.swapaxes(readout, 1, 2)

    pieces = [None] * seq_count
    tops = [seq_count - 1, half] + list(range(seq_count - 2, half, -1))
    for n, k in enumerate(tops):
        after = [pieces[tops[n - 2]]] if n > 1 else []
        pieces[k] = swap(pack(me, model, qkv, readout_t, k, count, after, n == 0), "seq", k)
    for k in range(half - 1, 0, -1):
        after = [] if k == half - 1 else [pieces[k + 1], pieces[tops[0]]] if k > 1 else [pieces[half - 1]]
        pieces[k] = swap(pack(me, model, qkv, readout_t, k, count, after), "seq", k)
    pieces[0] = pack(me, model, qkv, readout_t, 0, count, [pieces[half - 1]])
    late = sorted(tops[-2:])
    early = [k for k in range(seq_count) if k not in late]
    merged = attend_early(
        [pieces[k] for k in early], early, span_frames, me, timestep, step_weight, sign, sample, count, lat
    )
    ends = [pieces[k] for k in late]
    given = attend_late(ends, early, late, merged, span_frames, me, count, lat)
    size = half // 2
    while True:
        keep = given[0]
        for n in range(len(given) - 1, 0, -1):
            keep = keep + swap(given[n], "seq", n * size).astype(jnp.float32)
        if size == 1:
            break
        radix = min(4, size)
        size //= radix
        given = [keep[n * size : (n + 1) * size] for n in range(radix)]
    total = keep[0]
    offset = 1
    while offset < mp_count:
        radix = min(4, mp_count // offset)
        own = total
        for n in range(radix - 1, 0, -1):
            total = total + swap(own, "mp", offset * n)
        offset *= radix
    return total.T


def solution(mesh):
    return jax.shard_map(
        body,
        mesh=mesh,
        in_specs=(P("mp", "seq", None), P(), P(), P(), P()),
        out_specs=P("seq", None),
        check_vma=False,
    )
```

```python
import functools
import math

import jax
import jax.numpy as jnp
from jax import lax
from jax.experimental import pallas as pl
from jax.experimental.pallas import tpu as pltpu
from jax.sharding import PartitionSpec as P

HEADS = 32
HD = 128
FRAME_TOK = 64
NT = (((1,), (1,)), ((), ()))
LOG2_SCALE = math.log2(math.e) / math.sqrt(HD)
LOWEST = -1e30
PACK_VMEM = 4 * 1024 * 1024
SMALL_VMEM = 16 * 1024 * 1024
LARGE_VMEM = 60 * 1024 * 1024
SMEM = pl.BlockSpec(memory_space=pltpu.SMEM)
VMEM = pl.BlockSpec(memory_space=pltpu.VMEM)
HBM = pl.BlockSpec(memory_space=pltpu.HBM)


def fold(readout, values):
    return lax.dot_general(readout, values, NT, preferred_element_type=jnp.float32).astype(jnp.bfloat16)


def value_place(h, count, lat):
    return (h * lat) % HD, count * 2 * HD + (h * lat // HD) * HD


def pack_kernel(k, me_ref, model_ref, qkv_ref, readout_ref, *refs):
    out_ref, values, readout, sems = refs[-4:]
    rows = out_ref.shape[0]
    count, lat = values.shape[0], readout.shape[0]
    first = (me_ref[0] ^ k) * count

    def columns(h, part, width):
        return pl.ds(pl.multiple_of(((first + h) * 3 + part) * HD, HD), width)

    copies = [
        pltpu.make_async_copy(
            readout_ref.at[model_ref[0], :, pl.ds(pl.multiple_of(first * HD, HD), count * HD)], readout, sems.at[2 * count]
        )
    ]
    for h in range(count):
        copies.append(pltpu.make_async_copy(qkv_ref.at[0, :, columns(h, 2, HD)], values.at[h], sems.at[h]))
    for h in range(count):
        target = out_ref.at[:, h * 2 * HD : (h + 1) * 2 * HD]
        copies.append(pltpu.make_async_copy(qkv_ref.at[0, :, columns(h, 0, 2 * HD)], target, sems.at[count + h]))
    for copy in copies:
        copy.start()
    copies[0].wait()
    for h in range(count):
        copies[1 + h].wait()
        row, column = value_place(h, count, lat)
        out_ref[row : row + lat, column : column + HD] = fold(readout[:, h * HD : (h + 1) * HD], values[h])
    for copy in copies[1 + count :]:
        copy.wait()


def pack(me, model, qkv, readout_t, k, count, after, first=False):
    rows = qkv.shape[1]
    lat = readout_t.shape[1]
    width = count * 2 * HD + -(-count * lat // HD) * HD
    return pl.pallas_call(
        functools.partial(pack_kernel, k),
        in_specs=[SMEM, SMEM] + [HBM] * (2 + len(after)),
        out_specs=VMEM,
        out_shape=jax.ShapeDtypeStruct((rows, width), jnp.bfloat16),
        scratch_shapes=[
            pltpu.VMEM((count, rows, HD), jnp.bfloat16),
            pltpu.VMEM((lat, count * HD), jnp.bfloat16),
            pltpu.SemaphoreType.DMA((2 * count + 1,)),
        ],
        compiler_params=pltpu.CompilerParams(vmem_limit_bytes=LARGE_VMEM if first else PACK_VMEM),
        cost_estimate=pl.CostEstimate(
            flops=0, bytes_accessed=rows * width * 4, transcendentals=0
        ),
        name="pack",
    )(me, model, qkv, readout_t, *after)


def mask_rows(frames_ref, me, rows, query_offsets, key_offsets):
    columns = lax.broadcasted_iota(jnp.int32, (1, rows), 1)
    places = jnp.concatenate([(me ^ k) * rows + columns for k in query_offsets], axis=1)
    end = frames_ref[0] * FRAME_TOK
    bound = jnp.full(places.shape, end, jnp.int32)
    for c in range(1, frames_ref.shape[0]):
        later = end + frames_ref[c] * FRAME_TOK
        bound = jnp.where(places >= end, later, bound)
        end = later
    return [
        jnp.where((me ^ k) * rows + start < bound, 0.0, -jnp.inf)
        for k in key_offsets
        for start in range(0, rows, FRAME_TOK)
    ]


def run_units(units, lat):
    frames = [tile() for tile in units[0][0]]
    for u, (_, values, shifts, finish) in enumerate(units):
        ahead = list(units[u + 1][0]) if u + 1 < len(units) else []
        peaks = [jnp.max(f, axis=0, keepdims=True) + s for f, s in zip(sum(frames, []), shifts)]
        peak = jnp.maximum(functools.reduce(jnp.maximum, peaks), LOWEST)
        following, summed, start = [], None, 0
        for t, tile in enumerate(frames):
            for _ in range(-(-(len(ahead) - len(following)) // (len(frames) - t))):
                following.append(ahead[len(following)]())
            weights = [
                jnp.exp2((f + (s - peak)) * LOG2_SCALE).astype(jnp.bfloat16)
                for f, s in zip(tile, shifts[start : start + len(tile)])
            ]
            start += len(tile)
            part = jnp.dot(values[t](), jnp.concatenate(weights, axis=0), preferred_element_type=jnp.float32)
            summed = part if summed is None else summed + part
        finish(summed[:lat], summed[lat : lat + 1], peak)
        frames = following


def score_tile(keys, queries):
    scores = lax.dot_general(keys(), queries(), NT, preferred_element_type=jnp.float32)
    return [scores[start : start + FRAME_TOK] for start in range(0, scores.shape[0], FRAME_TOK)]


def stage_values(folded, pieces, lat):
    count = folded.shape[0]
    rows = pieces[0].shape[0]
    for i in range(count):
        row, column = value_place(i, count, lat)
        for n, piece in enumerate(pieces):
            folded[i, :lat, n * rows : (n + 1) * rows] = piece[row : row + lat, column : column + HD]
        folded[i, lat:] = jnp.ones_like(folded[i, lat:])


def pairs_of(pieces, i, what):
    column = (2 * i + what) * HD

    def read(n):
        return lambda: jnp.concatenate([pieces[n][:, column : column + HD], pieces[n + 1][:, column : column + HD]], axis=0)

    return [read(n) for n in range(0, len(pieces), 2)]


def early_kernel(offsets, frames_ref, me_ref, timestep_ref, step_weight_ref, sign_ref, sample_ref, *refs):
    count_pieces = len(offsets)
    arrived = refs[:count_pieces]
    sums_ref, stats_ref, factor_ref, pieces, folded, asked, sems = refs[-7:]
    me = me_ref[0]
    rows = pieces.shape[1]
    count, lat, _ = sums_ref.shape
    blocks = count_pieces // 2
    copies = [pltpu.make_async_copy(arrived[n], pieces.at[n], sems.at[n]) for n in range(count_pieces)]
    for copy in copies:
        copy.start()
    factor_ref[...] = jnp.full(factor_ref.shape, sign_ref[0] * step_weight_ref[timestep_ref[sample_ref[0]]])
    for copy in copies:
        copy.wait()
    pieces = [pieces.at[n] for n in range(count_pieces)]
    stage_values(folded, pieces, lat)
    for i in range(count):
        for b, read in enumerate(pairs_of(pieces, i, 0)):
            asked[b, i] = read()

    def some_blocks(b, carry):
        q = [2 * b, 2 * b + 1]
        span = pl.ds(pl.multiple_of(b * 2 * rows, 2 * rows), 2 * rows)
        shifts = mask_rows(frames_ref, me, rows, [sum(jnp.where(n == j, k, 0) for j, k in enumerate(offsets)) for n in q], offsets)
        peaks, totals, units = [], [], []
        for i in range(count):

            def finish(summed, total, peak, i=i):
                sums_ref[i, :, span] = summed
                peaks.append(peak)
                totals.append(total)

            tiles = [
                functools.partial(score_tile, keys, lambda i=i: asked[b, i]) for keys in pairs_of(pieces, i, 1)
            ]
            values = [lambda i=i, t=t: folded[i, :, t * 2 * rows : (t + 1) * 2 * rows] for t in range(blocks)]
            units.append((tiles, values, shifts, finish))
        run_units(units, lat)
        rest = [jnp.ones_like(peaks[0])] * (stats_ref.shape[1] - count)
        stats_ref[0, :, span] = jnp.concatenate(peaks + rest, axis=0)
        stats_ref[1, :, span] = jnp.concatenate(totals + rest, axis=0)
        return carry

    lax.fori_loop(0, blocks, some_blocks, 0)


def join_kernel(every, early, last, frames_ref, me_ref, *refs):
    known = len(every) - 1
    new_ref, early_ref, early_folded, sums_ref, stats_ref, *refs = refs
    if last:
        joined_ref, joined_folded, factor_ref, *out_refs, piece, folded, sem = refs
        size = out_refs[0].shape[0]
        factor = factor_ref[:1]
    else:
        new_sums, new_stats, piece, folded, sem = refs
    lat = sums_ref.shape[1]
    rows = piece.shape[0]
    count = folded.shape[0]
    copy = pltpu.make_async_copy(new_ref, piece, sem)
    copy.start()
    me = me_ref[0]
    copy.wait()
    pieces = [early_ref.at[n] for n in range(early)] + ([joined_ref] if last else []) + [piece]
    stage_values(folded, [piece], lat)
    results, peaks, totals = {}, {0: [], known: []}, {0: [], known: []}

    def read(numbers, i, what):
        column = (2 * i + what) * HD
        parts = [pieces[n][:, column : column + HD] for n in numbers]
        return parts[0] if len(parts) == 1 else jnp.concatenate(parts, axis=0)

    def value_tile(numbers, i):
        if numbers[0] < early:
            return early_folded[i, :, numbers[0] * rows : (numbers[-1] + 1) * rows]
        parts = [folded[i] if n == known else joined_folded[i] for n in numbers]
        return parts[0] if len(parts) == 1 else jnp.concatenate(parts, axis=1)

    def write(start, number):
        for j in range(number):
            k = every[start + j]
            out_ref = out_refs[k // size]
            out_ref[k % size] = (results[start][:, j * rows : (j + 1) * rows] * factor).astype(out_ref.dtype)

    units = []
    all_tiles = [tuple(range(n, min(n + 2, known + 1))) for n in range(0, known + 1, 2)]
    for start, number, key_tiles in ((0, known, [(known,)]), (known, 1, all_tiles)):
        shifts = mask_rows(
            frames_ref, me, rows, every[start : start + number], [every[n] for tile in key_tiles for n in tile]
        )
        for i in range(count):

            def finish(summed, total, peak, start=start, number=number, i=i):
                part = summed
                if start == 0:
                    before = stats_ref[0, i : i + 1]
                    highest = jnp.maximum(before, peak)
                    old = jnp.exp2((before - highest) * LOG2_SCALE)
                    new = jnp.exp2((peak - highest) * LOG2_SCALE)
                    peak, total = highest, stats_ref[1, i : i + 1] * old + total * new
                    if last:
                        old, new = old / total, new / total
                    part = sums_ref[i] * old + summed * new
                elif last:
                    part = summed / total
                if last:
                    results[start] = part if i == 0 else results[start] + part
                    if i == count - 1:
                        write(start, number)
                    return
                span = slice(start * rows, (start + number) * rows)
                new_sums[i, :, span] = part
                peaks[start].append(peak)
                totals[start].append(total)
                if i == count - 1:
                    rest = [jnp.ones_like(peak)] * (new_stats.shape[1] - count)
                    new_stats[0, :, span] = jnp.concatenate(peaks[start] + rest, axis=0)
                    new_stats[1, :, span] = jnp.concatenate(totals[start] + rest, axis=0)

            queries = functools.partial(read, range(start, start + number), i, 0)
            tiles = [functools.partial(score_tile, functools.partial(read, t, i, 1), queries) for t in key_tiles]
            units.append((tiles, [functools.partial(value_tile, t, i) for t in key_tiles], shifts, finish))
    run_units(units, lat)


def attend_early(pieces, offsets, span_frames, me, timestep, step_weight, sign, sample, count, lat):
    rows, width = pieces[0].shape
    blocks = len(pieces) // 2
    tokens = len(pieces) * rows
    return pl.pallas_call(
        functools.partial(early_kernel, offsets),
        in_specs=[SMEM] * 6 + [HBM] * len(pieces),
        out_specs=[VMEM] * 5,
        out_shape=[
            jax.ShapeDtypeStruct((count, lat, tokens), jnp.float32),
            jax.ShapeDtypeStruct((2, 8, tokens), jnp.float32),
            jax.ShapeDtypeStruct((8, rows), jnp.float32),
            jax.ShapeDtypeStruct((len(pieces), rows, width), jnp.bfloat16),
            jax.ShapeDtypeStruct((count, lat + 16, tokens), jnp.bfloat16),
        ],
        scratch_shapes=[
            pltpu.VMEM((blocks, count, 2 * rows, HD), jnp.bfloat16),
            pltpu.SemaphoreType.DMA((len(pieces),)),
        ],
        compiler_params=pltpu.CompilerParams(vmem_limit_bytes=SMALL_VMEM if len(pieces) <= 8 else LARGE_VMEM),
        cost_estimate=pl.CostEstimate(
            flops=count * tokens * tokens * 2 * (HD + lat),
            bytes_accessed=tokens * count * 3 * HD * 2,
            transcendentals=count * tokens * tokens,
        ),
        name="attend_early",
    )(span_frames, me, timestep, step_weight, sign, sample, *pieces)


def join(piece, every, early, state, joined, span_frames, me, count, lat):
    last = bool(joined)
    rows, width = piece.shape
    tokens = len(every) * rows
    if last:
        shape = (len(every) // 4, lat, rows)
        out_shape = [jax.ShapeDtypeStruct(shape, jnp.bfloat16 if g else jnp.float32) for g in range(4)]
    else:
        out_shape = [
            jax.ShapeDtypeStruct((count, lat, tokens), jnp.float32),
            jax.ShapeDtypeStruct((2, 8, tokens), jnp.float32),
            jax.ShapeDtypeStruct((rows, width), jnp.bfloat16),
            jax.ShapeDtypeStruct((count, lat + 16, rows), jnp.bfloat16),
        ]
    held = [pltpu.VMEM((rows, width), jnp.bfloat16), pltpu.VMEM((count, lat + 16, rows), jnp.bfloat16)]
    return pl.pallas_call(
        functools.partial(join_kernel, every, early, last),
        in_specs=[SMEM] * 2 + [HBM] + [VMEM] * (len(state) + len(joined)),
        out_specs=[VMEM] * 4,
        out_shape=out_shape,
        scratch_shapes=(held if last else []) + [pltpu.SemaphoreType.DMA],
        compiler_params=pltpu.CompilerParams(vmem_limit_bytes=SMALL_VMEM if len(every) <= 8 else LARGE_VMEM),
        cost_estimate=pl.CostEstimate(
            flops=0, bytes_accessed=rows * width * 2, transcendentals=0
        ),
        name="join",
    )(span_frames, me, piece, *state, *joined)


def swap(array, axis, offset):
    size = lax.axis_size(axis)
    return lax.ppermute(array, axis, [(i, i ^ offset) for i in range(size)])


def body(qkv, readout, step_weight, timestep, span_frames):
    seq_count = lax.axis_size("seq")
    mp_count = lax.axis_size("mp")
    half = seq_count // 2
    count = HEADS // seq_count
    lat = readout.shape[2]
    me = lax.axis_index("seq").astype(jnp.int32).reshape(1)
    mp_index = lax.axis_index("mp").astype(jnp.int32)
    sample_count = mp_count // 2
    model_index = mp_index // sample_count
    sample = (mp_index % sample_count).reshape(1)
    sign = jnp.where(model_index == 1, 1.0, -1.0).astype(jnp.float32).reshape(1)
    model = model_index.reshape(1)
    readout_t = jnp.swapaxes(readout, 1, 2)

    pieces = [None] * seq_count
    tops = [seq_count - 1, half] + list(range(seq_count - 2, half, -1))
    for n, k in enumerate(tops):
        after = [pieces[tops[n - 2]]] if n > 1 else []
        pieces[k] = swap(pack(me, model, qkv, readout_t, k, count, after, n == 0), "seq", k)
    for k in range(half - 1, 0, -1):
        after = [] if k == half - 1 else [pieces[k + 1]] if k > 1 else [pieces[tops[0]]]
        pieces[k] = swap(pack(me, model, qkv, readout_t, k, count, after), "seq", k)
    pieces[0] = pack(me, model, qkv, readout_t, 0, count, [pieces[half - 1]])
    early = [k for k in range(seq_count) if k not in tops[-2:]]
    sums, stats, factor, held, folded = attend_early(
        [pieces[k] for k in early], early, span_frames, me, timestep, step_weight, sign, sample, count, lat
    )
    every = early + tops[-2:]
    state = [held, folded, sums, stats]
    sums, stats, third, third_folded = join(pieces[every[-2]], every[:-1], len(early), state, [], span_frames, me, count, lat)
    state = [held, folded, sums, stats]
    joined = [third, third_folded, factor]
    given = join(pieces[every[-1]], every, len(early), state, joined, span_frames, me, count, lat)
    size = half // 2
    while True:
        keep = given[0]
        for n in range(len(given) - 1, 0, -1):
            keep = keep + swap(given[n], "seq", n * size).astype(jnp.float32)
        if size == 1:
            break
        radix = min(4, size)
        size //= radix
        given = [keep[n * size : (n + 1) * size] for n in range(radix)]
    total = keep[0]
    offset = 1
    while offset < mp_count:
        radix = min(4, mp_count // offset)
        own = total
        for n in range(radix - 1, 0, -1):
            total = total + swap(own, "mp", offset * n)
        offset *= radix
    return total.T


def solution(mesh):
    return jax.shard_map(
        body,
        mesh=mesh,
        in_specs=(P("mp", "seq", None), P(), P(), P(), P()),
        out_specs=P("seq", None),
        check_vma=False,
    )
```

```python
import functools
import math

import jax
import jax.numpy as jnp
from jax import lax
from jax.experimental import pallas as pl
from jax.experimental.pallas import tpu as pltpu
from jax.sharding import PartitionSpec as P

HEADS = 32
HD = 128
FRAME_TOK = 64
NT = (((1,), (1,)), ((), ()))
LOG2_SCALE = math.log2(math.e) / math.sqrt(HD)
LOWEST = -1e30
PACK_VMEM = 4 * 1024 * 1024
SMALL_VMEM = 16 * 1024 * 1024
LARGE_VMEM = 60 * 1024 * 1024
SMEM = pl.BlockSpec(memory_space=pltpu.SMEM)
VMEM = pl.BlockSpec(memory_space=pltpu.VMEM)
HBM = pl.BlockSpec(memory_space=pltpu.HBM)


def fold(readout, values):
    return lax.dot_general(readout, values, NT, preferred_element_type=jnp.float32).astype(jnp.bfloat16)


def value_place(h, count, lat):
    return (h * lat) % HD, count * 2 * HD + (h * lat // HD) * HD


def pack_kernel(k, me_ref, model_ref, qkv_ref, readout_ref, *refs):
    out_ref, values, readout, sems = refs[-4:]
    rows = out_ref.shape[0]
    count, lat = values.shape[0], readout.shape[0]
    first = (me_ref[0] ^ k) * count

    def columns(h, part, width):
        return pl.ds(pl.multiple_of(((first + h) * 3 + part) * HD, HD), width)

    copies = [
        pltpu.make_async_copy(
            readout_ref.at[model_ref[0], :, pl.ds(pl.multiple_of(first * HD, HD), count * HD)], readout, sems.at[2 * count]
        )
    ]
    for h in range(count):
        copies.append(pltpu.make_async_copy(qkv_ref.at[0, :, columns(h, 2, HD)], values.at[h], sems.at[h]))
    for h in range(count):
        target = out_ref.at[:, h * 2 * HD : (h + 1) * 2 * HD]
        copies.append(pltpu.make_async_copy(qkv_ref.at[0, :, columns(h, 0, 2 * HD)], target, sems.at[count + h]))
    for copy in copies:
        copy.start()
    copies[0].wait()
    for h in range(count):
        copies[1 + h].wait()
        row, column = value_place(h, count, lat)
        out_ref[row : row + lat, column : column + HD] = fold(readout[:, h * HD : (h + 1) * HD], values[h])
    for copy in copies[1 + count :]:
        copy.wait()


def pack(me, model, qkv, readout_t, k, count, after, first=False):
    rows = qkv.shape[1]
    lat = readout_t.shape[1]
    width = count * 2 * HD + -(-count * lat // HD) * HD
    return pl.pallas_call(
        functools.partial(pack_kernel, k),
        in_specs=[SMEM, SMEM] + [HBM] * (2 + len(after)),
        out_specs=VMEM,
        out_shape=jax.ShapeDtypeStruct((rows, width), jnp.bfloat16),
        scratch_shapes=[
            pltpu.VMEM((count, rows, HD), jnp.bfloat16),
            pltpu.VMEM((lat, count * HD), jnp.bfloat16),
            pltpu.SemaphoreType.DMA((2 * count + 1,)),
        ],
        compiler_params=pltpu.CompilerParams(vmem_limit_bytes=LARGE_VMEM if first else PACK_VMEM),
        cost_estimate=pl.CostEstimate(
            flops=0, bytes_accessed=rows * width * 4, transcendentals=0
        ),
        name="pack",
    )(me, model, qkv, readout_t, *after)


def mask_rows(frames_ref, me, rows, query_offsets, key_offsets):
    columns = lax.broadcasted_iota(jnp.int32, (1, rows), 1)
    places = jnp.concatenate([(me ^ k) * rows + columns for k in query_offsets], axis=1)
    end = frames_ref[0] * FRAME_TOK
    bound = jnp.full(places.shape, end, jnp.int32)
    for c in range(1, frames_ref.shape[0]):
        later = end + frames_ref[c] * FRAME_TOK
        bound = jnp.where(places >= end, later, bound)
        end = later
    return [
        jnp.where((me ^ k) * rows + start < bound, 0.0, -jnp.inf)
        for k in key_offsets
        for start in range(0, rows, FRAME_TOK)
    ]


def run_units(units, lat):
    frames = [tile() for tile in units[0][0]]
    for u, (_, values, shifts, finish) in enumerate(units):
        ahead = list(units[u + 1][0]) if u + 1 < len(units) else []
        peaks = [jnp.max(f, axis=0, keepdims=True) + s for f, s in zip(sum(frames, []), shifts)]
        peak = jnp.maximum(functools.reduce(jnp.maximum, peaks), LOWEST)
        following, summed, start = [], None, 0
        for t, tile in enumerate(frames):
            for _ in range(-(-(len(ahead) - len(following)) // (len(frames) - t))):
                following.append(ahead[len(following)]())
            weights = [
                jnp.exp2((f + (s - peak)) * LOG2_SCALE).astype(jnp.bfloat16)
                for f, s in zip(tile, shifts[start : start + len(tile)])
            ]
            start += len(tile)
            part = jnp.dot(values[t](), jnp.concatenate(weights, axis=0), preferred_element_type=jnp.float32)
            summed = part if summed is None else summed + part
        finish(summed[:lat], summed[lat : lat + 1], peak)
        frames = following


def score_tile(keys, queries):
    scores = lax.dot_general(keys(), queries(), NT, preferred_element_type=jnp.float32)
    return [scores[start : start + FRAME_TOK] for start in range(0, scores.shape[0], FRAME_TOK)]


def stage_values(folded, pieces, lat):
    count = folded.shape[0]
    rows = pieces[0].shape[0]
    for i in range(count):
        row, column = value_place(i, count, lat)
        for n, piece in enumerate(pieces):
            folded[i, :lat, n * rows : (n + 1) * rows] = piece[row : row + lat, column : column + HD]
        folded[i, lat:] = jnp.ones_like(folded[i, lat:])


def pairs_of(pieces, i, what):
    column = (2 * i + what) * HD

    def read(n):
        return lambda: jnp.concatenate([pieces[n][:, column : column + HD], pieces[n + 1][:, column : column + HD]], axis=0)

    return [read(n) for n in range(0, len(pieces), 2)]


def early_kernel(offsets, late, frames_ref, me_ref, timestep_ref, step_weight_ref, sign_ref, sample_ref, *refs):
    count_pieces = len(offsets)
    arrived = refs[:count_pieces]
    sums_ref, stats_ref, factor_ref, pieces, folded, wide_ref, late_ref, asked, sems = refs[-9:]
    me = me_ref[0]
    rows = pieces.shape[1]
    count, lat, _ = sums_ref.shape
    blocks = count_pieces // 2
    copies = [pltpu.make_async_copy(arrived[n], pieces.at[n], sems.at[n]) for n in range(count_pieces)]
    for copy in copies:
        copy.start()
    factor_ref[...] = jnp.full(factor_ref.shape, sign_ref[0] * step_weight_ref[timestep_ref[sample_ref[0]]])
    for ref, queries, keys in ((wide_ref, offsets, late), (late_ref, late, list(offsets) + list(late))):
        for n, row in enumerate(mask_rows(frames_ref, me, rows, queries, keys)):
            ref[n : n + 1] = row
    for copy in copies:
        copy.wait()
    pieces = [pieces.at[n] for n in range(count_pieces)]
    stage_values(folded, pieces, lat)
    for i in range(count):
        for b, read in enumerate(pairs_of(pieces, i, 0)):
            asked[b, i] = read()
    half = count_pieces // 2 + 1

    def some_blocks(b, carry):
        q = [2 * b, 2 * b + 1]
        span = pl.ds(pl.multiple_of(b * 2 * rows, 2 * rows), 2 * rows)
        shifts = mask_rows(frames_ref, me, rows, [jnp.where(n < half, n, n + 2) for n in q], offsets)
        peaks, totals, units = [], [], []
        for i in range(count):

            def finish(summed, total, peak, i=i):
                sums_ref[i, :, span] = summed
                peaks.append(peak)
                totals.append(total)

            tiles = [
                functools.partial(score_tile, keys, lambda i=i: asked[b, i]) for keys in pairs_of(pieces, i, 1)
            ]
            values = [lambda i=i, t=t: folded[i, :, t * 2 * rows : (t + 1) * 2 * rows] for t in range(blocks)]
            units.append((tiles, values, shifts, finish))
        run_units(units, lat)
        rest = [jnp.ones_like(peaks[0])] * (stats_ref.shape[1] - count)
        stats_ref[0, :, span] = jnp.concatenate(peaks + rest, axis=0)
        stats_ref[1, :, span] = jnp.concatenate(totals + rest, axis=0)
        return carry

    lax.fori_loop(0, blocks, some_blocks, 0)


def late_kernel(offsets, late, *refs):
    early = len(offsets)
    arrived = refs[:2]
    sums_ref, stats_ref, factor_ref, early_ref, early_folded, wide_ref, late_ref, *out_refs, folded = refs[2:]
    size, lat, rows = out_refs[0].shape
    count = folded.shape[0]
    pieces = [early_ref.at[n] for n in range(early)] + list(arrived)
    stage_values(folded, pieces[early:], lat)
    factor = factor_ref[:1]
    every = list(offsets) + list(late)
    blocks = early // 2
    results = {}

    def write(number, start):
        for j in range(number):
            k = every[start + j]
            out_ref = out_refs[k // size]
            out_ref[k % size] = (results[start][:, j * rows : (j + 1) * rows] * factor).astype(out_ref.dtype)

    units = []
    for start, number, tiles_in in ((0, early, [blocks]), (early, 2, range(blocks + 1))):
        rows_ref = late_ref if start else wide_ref
        shifts = [rows_ref[n : n + 1] for n in range(rows_ref.shape[0])]
        for i in range(count):

            def finish(summed, total, peak, start=start, number=number, i=i):
                if start == 0:
                    before = stats_ref[0, i : i + 1]
                    highest = jnp.maximum(before, peak)
                    old = jnp.exp2((before - highest) * LOG2_SCALE)
                    new = jnp.exp2((peak - highest) * LOG2_SCALE)
                    both = stats_ref[1, i : i + 1] * old + total * new
                    part = sums_ref[i] * (old / both) + summed * (new / both)
                else:
                    part = summed / total
                results[start] = part if i == 0 else results[start] + part
                if i == count - 1:
                    write(number, start)

            def queries(start=start, number=number, i=i):
                column = 2 * i * HD
                return jnp.concatenate([p[:, column : column + HD] for p in pieces[start : start + number]], axis=0)

            keys = pairs_of(pieces, i, 1)
            tiles = [functools.partial(score_tile, keys[t], queries) for t in tiles_in]
            values = [
                lambda i=i, t=t: folded[i] if t == blocks else early_folded[i, :, t * 2 * rows : (t + 1) * 2 * rows]
                for t in tiles_in
            ]
            units.append((tiles, values, shifts, finish))
    run_units(units, lat)


def attend_early(pieces, offsets, late, span_frames, me, timestep, step_weight, sign, sample, count, lat):
    rows, width = pieces[0].shape
    blocks = len(pieces) // 2
    tokens = len(pieces) * rows
    frames = rows // FRAME_TOK
    return pl.pallas_call(
        functools.partial(early_kernel, offsets, late),
        in_specs=[SMEM] * 6 + [HBM] * len(pieces),
        out_specs=[VMEM] * 7,
        out_shape=[
            jax.ShapeDtypeStruct((count, lat, tokens), jnp.float32),
            jax.ShapeDtypeStruct((2, 8, tokens), jnp.float32),
            jax.ShapeDtypeStruct((8, rows), jnp.float32),
            jax.ShapeDtypeStruct((len(pieces), rows, width), jnp.bfloat16),
            jax.ShapeDtypeStruct((count, lat + 16, tokens), jnp.bfloat16),
            jax.ShapeDtypeStruct((2 * frames, tokens), jnp.float32),
            jax.ShapeDtypeStruct(((len(pieces) + 2) * frames, 2 * rows), jnp.float32),
        ],
        scratch_shapes=[
            pltpu.VMEM((blocks, count, 2 * rows, HD), jnp.bfloat16),
            pltpu.SemaphoreType.DMA((len(pieces),)),
        ],
        compiler_params=pltpu.CompilerParams(vmem_limit_bytes=SMALL_VMEM if len(pieces) <= 8 else LARGE_VMEM),
        cost_estimate=pl.CostEstimate(
            flops=count * tokens * tokens * 2 * (HD + lat),
            bytes_accessed=tokens * count * 3 * HD * 2,
            transcendentals=count * tokens * tokens,
        ),
        name="attend_early",
    )(span_frames, me, timestep, step_weight, sign, sample, *pieces)


def attend_late(pieces, offsets, late, early, count, lat):
    rows, width = pieces[0].shape
    half = len(offsets) // 2 + 1
    tokens = 2 * half * rows
    return pl.pallas_call(
        functools.partial(late_kernel, offsets, late),
        in_specs=[VMEM] * (2 + len(early)),
        out_specs=[VMEM] * 4,
        out_shape=[
            jax.ShapeDtypeStruct((half // 2, lat, rows), jnp.bfloat16 if g else jnp.float32) for g in range(4)
        ],
        scratch_shapes=[pltpu.VMEM((count, lat + 16, 2 * rows), jnp.bfloat16)],
        compiler_params=pltpu.CompilerParams(vmem_limit_bytes=SMALL_VMEM if half <= 4 else LARGE_VMEM),
        cost_estimate=pl.CostEstimate(
            flops=count * tokens * rows * 4 * (HD + lat),
            bytes_accessed=tokens * count * 3 * HD * 2,
            transcendentals=count * tokens * rows * 2,
        ),
        name="attend_late",
    )(*pieces, *early)


def swap(array, axis, offset):
    size = lax.axis_size(axis)
    return lax.ppermute(array, axis, [(i, i ^ offset) for i in range(size)])


def body(qkv, readout, step_weight, timestep, span_frames):
    seq_count = lax.axis_size("seq")
    mp_count = lax.axis_size("mp")
    half = seq_count // 2
    count = HEADS // seq_count
    lat = readout.shape[2]
    me = lax.axis_index("seq").astype(jnp.int32).reshape(1)
    mp_index = lax.axis_index("mp").astype(jnp.int32)
    sample_count = mp_count // 2
    model_index = mp_index // sample_count
    sample = (mp_index % sample_count).reshape(1)
    sign = jnp.where(model_index == 1, 1.0, -1.0).astype(jnp.float32).reshape(1)
    model = model_index.reshape(1)
    readout_t = jnp.swapaxes(readout, 1, 2)

    pieces = [None] * seq_count
    for n in range(half):
        k = seq_count - 1 - n
        pieces[k] = swap(pack(me, model, qkv, readout_t, k, count, [pieces[k + 2]] if n > 1 else [], n == 0), "seq", k)
    for k in range(half - 1, 0, -1):
        after = [] if k == half - 1 else [pieces[k + 1], pieces[seq_count - 1]] if k > 1 else [pieces[half - 1]]
        pieces[k] = swap(pack(me, model, qkv, readout_t, k, count, after), "seq", k)
    pieces[0] = pack(me, model, qkv, readout_t, 0, count, [pieces[half - 1]])
    late = [half, half + 1]
    early = [k for k in range(seq_count) if k not in late]
    merged = attend_early(
        [pieces[k] for k in early], early, late, span_frames, me, timestep, step_weight, sign, sample, count, lat
    )
    ends = [pieces[k] for k in late]
    given = attend_late(ends, early, late, merged, count, lat)
    size = half // 2
    while True:
        keep = given[0]
        for n in range(len(given) - 1, 0, -1):
            keep = keep + swap(given[n], "seq", n * size).astype(jnp.float32)
        if size == 1:
            break
        radix = min(4, size)
        size //= radix
        given = [keep[n * size : (n + 1) * size] for n in range(radix)]
    total = keep[0]
    offset = 1
    while offset < mp_count:
        radix = min(4, mp_count // offset)
        own = total
        for n in range(radix - 1, 0, -1):
            total = total + swap(own, "mp", offset * n)
        offset *= radix
    return total.T


def solution(mesh):
    return jax.shard_map(
        body,
        mesh=mesh,
        in_specs=(P("mp", "seq", None), P(), P(), P(), P()),
        out_specs=P("seq", None),
        check_vma=False,
    )
```

```python
import functools
import math

import jax
import jax.numpy as jnp
from jax import lax
from jax.experimental import pallas as pl
from jax.experimental.pallas import tpu as pltpu
from jax.sharding import PartitionSpec as P

HEADS = 32
HD = 128
FRAME_TOK = 64
NT = (((1,), (1,)), ((), ()))
LOG2_SCALE = math.log2(math.e) / math.sqrt(HD)
LOWEST = -1e30
PACK_VMEM = 4 * 1024 * 1024
SMALL_VMEM = 16 * 1024 * 1024
LARGE_VMEM = 60 * 1024 * 1024
SMEM = pl.BlockSpec(memory_space=pltpu.SMEM)
VMEM = pl.BlockSpec(memory_space=pltpu.VMEM)
HBM = pl.BlockSpec(memory_space=pltpu.HBM)


def fold(readout, values):
    return lax.dot_general(readout, values, NT, preferred_element_type=jnp.float32).astype(jnp.bfloat16)


def value_place(h, count, lat):
    return (h * lat) % HD, count * 2 * HD + (h * lat // HD) * HD


def pack_kernel(k, me_ref, model_ref, qkv_ref, readout_ref, *refs):
    out_ref, values, readout, sems = refs[-4:]
    rows = out_ref.shape[0]
    count, lat = values.shape[0], readout.shape[0]
    first = (me_ref[0] ^ k) * count

    def columns(h, part, width):
        return pl.ds(pl.multiple_of(((first + h) * 3 + part) * HD, HD), width)

    copies = [
        pltpu.make_async_copy(
            readout_ref.at[model_ref[0], :, pl.ds(pl.multiple_of(first * HD, HD), count * HD)], readout, sems.at[2 * count]
        )
    ]
    for h in range(count):
        copies.append(pltpu.make_async_copy(qkv_ref.at[0, :, columns(h, 2, HD)], values.at[h], sems.at[h]))
    for h in range(count):
        target = out_ref.at[:, h * 2 * HD : (h + 1) * 2 * HD]
        copies.append(pltpu.make_async_copy(qkv_ref.at[0, :, columns(h, 0, 2 * HD)], target, sems.at[count + h]))
    for copy in copies:
        copy.start()
    copies[0].wait()
    for h in range(count):
        copies[1 + h].wait()
        row, column = value_place(h, count, lat)
        out_ref[row : row + lat, column : column + HD] = fold(readout[:, h * HD : (h + 1) * HD], values[h])
    for copy in copies[1 + count :]:
        copy.wait()


def pack(me, model, qkv, readout_t, k, count, after, first=False):
    rows = qkv.shape[1]
    lat = readout_t.shape[1]
    width = count * 2 * HD + -(-count * lat // HD) * HD
    return pl.pallas_call(
        functools.partial(pack_kernel, k),
        in_specs=[SMEM, SMEM] + [HBM] * (2 + len(after)),
        out_specs=VMEM,
        out_shape=jax.ShapeDtypeStruct((rows, width), jnp.bfloat16),
        scratch_shapes=[
            pltpu.VMEM((count, rows, HD), jnp.bfloat16),
            pltpu.VMEM((lat, count * HD), jnp.bfloat16),
            pltpu.SemaphoreType.DMA((2 * count + 1,)),
        ],
        compiler_params=pltpu.CompilerParams(vmem_limit_bytes=LARGE_VMEM if first else PACK_VMEM),
        cost_estimate=pl.CostEstimate(
            flops=0, bytes_accessed=rows * width * 4, transcendentals=0
        ),
        name="pack",
    )(me, model, qkv, readout_t, *after)


def mask_rows(frames_ref, me, rows, query_offsets, key_offsets):
    columns = lax.broadcasted_iota(jnp.int32, (1, rows), 1)
    places = jnp.concatenate([(me ^ k) * rows + columns for k in query_offsets], axis=1)
    end = frames_ref[0] * FRAME_TOK
    bound = jnp.full(places.shape, end, jnp.int32)
    for c in range(1, frames_ref.shape[0]):
        later = end + frames_ref[c] * FRAME_TOK
        bound = jnp.where(places >= end, later, bound)
        end = later
    return [
        jnp.where((me ^ k) * rows + start < bound, 0.0, -jnp.inf)
        for k in key_offsets
        for start in range(0, rows, FRAME_TOK)
    ]


def run_units(units, lat):
    frames = [tile() for tile in units[0][0]]
    for u, (_, values, shifts, finish) in enumerate(units):
        ahead = list(units[u + 1][0]) if u + 1 < len(units) else []
        peaks = [jnp.max(f, axis=0, keepdims=True) + s for f, s in zip(sum(frames, []), shifts)]
        peak = jnp.maximum(functools.reduce(jnp.maximum, peaks), LOWEST)
        following, summed, start = [], None, 0
        for t, tile in enumerate(frames):
            for _ in range(-(-(len(ahead) - len(following)) // (len(frames) - t))):
                following.append(ahead[len(following)]())
            weights = [
                jnp.exp2((f + (s - peak)) * LOG2_SCALE).astype(jnp.bfloat16)
                for f, s in zip(tile, shifts[start : start + len(tile)])
            ]
            start += len(tile)
            part = jnp.dot(values[t](), jnp.concatenate(weights, axis=0), preferred_element_type=jnp.float32)
            summed = part if summed is None else summed + part
        finish(summed[:lat], summed[lat : lat + 1], peak)
        frames = following


def score_tile(keys, queries):
    scores = lax.dot_general(keys(), queries(), NT, preferred_element_type=jnp.float32)
    return [scores[start : start + FRAME_TOK] for start in range(0, scores.shape[0], FRAME_TOK)]


def stage_values(folded, pieces, lat):
    count = folded.shape[0]
    rows = pieces[0].shape[0]
    for i in range(count):
        row, column = value_place(i, count, lat)
        for n, piece in enumerate(pieces):
            folded[i, :lat, n * rows : (n + 1) * rows] = piece[row : row + lat, column : column + HD]
        folded[i, lat:] = jnp.ones_like(folded[i, lat:])


def pairs_of(pieces, i, what):
    column = (2 * i + what) * HD

    def read(n):
        return lambda: jnp.concatenate([pieces[n][:, column : column + HD], pieces[n + 1][:, column : column + HD]], axis=0)

    return [read(n) for n in range(0, len(pieces), 2)]


def early_kernel(offsets, late, frames_ref, me_ref, timestep_ref, step_weight_ref, sign_ref, sample_ref, *refs):
    count_pieces = len(offsets)
    arrived = refs[:count_pieces]
    sums_ref, stats_ref, factor_ref, pieces, folded, wide_ref, late_ref, asked, sems = refs[-9:]
    me = me_ref[0]
    rows = pieces.shape[1]
    count, lat, _ = sums_ref.shape
    blocks = count_pieces // 2
    copies = [pltpu.make_async_copy(arrived[n], pieces.at[n], sems.at[n]) for n in range(count_pieces)]
    for copy in copies:
        copy.start()
    factor_ref[...] = jnp.full(factor_ref.shape, sign_ref[0] * step_weight_ref[timestep_ref[sample_ref[0]]])
    for ref, queries, keys in ((wide_ref, offsets, late), (late_ref, late, list(offsets) + list(late))):
        for n, row in enumerate(mask_rows(frames_ref, me, rows, queries, keys)):
            ref[n : n + 1] = row
    for copy in copies:
        copy.wait()
    pieces = [pieces.at[n] for n in range(count_pieces)]
    stage_values(folded, pieces, lat)
    for i in range(count):
        for b, read in enumerate(pairs_of(pieces, i, 0)):
            asked[b, i] = read()
    half = count_pieces // 2 + 1

    def some_blocks(b, carry):
        q = [2 * b, 2 * b + 1]
        span = pl.ds(pl.multiple_of(b * 2 * rows, 2 * rows), 2 * rows)
        shifts = mask_rows(frames_ref, me, rows, [jnp.where(n < half, n, n + 2) for n in q], offsets)
        peaks, totals, units = [], [], []
        for i in range(count):

            def finish(summed, total, peak, i=i):
                sums_ref[i, :, span] = summed
                peaks.append(peak)
                totals.append(total)

            tiles = [
                functools.partial(score_tile, keys, lambda i=i: asked[b, i]) for keys in pairs_of(pieces, i, 1)
            ]
            values = [lambda i=i, t=t: folded[i, :, t * 2 * rows : (t + 1) * 2 * rows] for t in range(blocks)]
            units.append((tiles, values, shifts, finish))
        run_units(units, lat)
        rest = [jnp.ones_like(peaks[0])] * (stats_ref.shape[1] - count)
        stats_ref[0, :, span] = jnp.concatenate(peaks + rest, axis=0)
        stats_ref[1, :, span] = jnp.concatenate(totals + rest, axis=0)
        return carry

    lax.fori_loop(0, blocks, some_blocks, 0)


def late_kernel(offsets, late, *refs):
    early = len(offsets)
    arrived = refs[:2]
    sums_ref, stats_ref, factor_ref, early_ref, early_folded, wide_ref, late_ref, *out_refs, folded = refs[2:]
    size, lat, rows = out_refs[0].shape
    count = folded.shape[0]
    pieces = [early_ref.at[n] for n in range(early)] + list(arrived)
    stage_values(folded, pieces[early:], lat)
    factor = factor_ref[:1]
    every = list(offsets) + list(late)
    blocks = early // 2
    results = {}

    def write(number, start):
        for j in range(number):
            k = every[start + j]
            out_ref = out_refs[k // size]
            out_ref[k % size] = (results[start][:, j * rows : (j + 1) * rows] * factor).astype(out_ref.dtype)

    units = []
    for start, number, tiles_in in ((0, early, [blocks]), (early, 2, range(blocks + 1))):
        rows_ref = late_ref if start else wide_ref
        shifts = [rows_ref[n : n + 1] for n in range(rows_ref.shape[0])]
        for i in range(count):

            def finish(summed, total, peak, start=start, number=number, i=i):
                if start == 0:
                    before = stats_ref[0, i : i + 1]
                    highest = jnp.maximum(before, peak)
                    old = jnp.exp2((before - highest) * LOG2_SCALE)
                    new = jnp.exp2((peak - highest) * LOG2_SCALE)
                    both = stats_ref[1, i : i + 1] * old + total * new
                    part = sums_ref[i] * (old / both) + summed * (new / both)
                else:
                    part = summed / total
                results[start] = part if i == 0 else results[start] + part
                if i == count - 1:
                    write(number, start)

            def queries(start=start, number=number, i=i):
                column = 2 * i * HD
                return jnp.concatenate([p[:, column : column + HD] for p in pieces[start : start + number]], axis=0)

            keys = pairs_of(pieces, i, 1)
            tiles = [functools.partial(score_tile, keys[t], queries) for t in tiles_in]
            values = [
                lambda i=i, t=t: folded[i] if t == blocks else early_folded[i, :, t * 2 * rows : (t + 1) * 2 * rows]
                for t in tiles_in
            ]
            units.append((tiles, values, shifts, finish))
    run_units(units, lat)


def attend_early(pieces, offsets, late, span_frames, me, timestep, step_weight, sign, sample, count, lat):
    rows, width = pieces[0].shape
    blocks = len(pieces) // 2
    tokens = len(pieces) * rows
    frames = rows // FRAME_TOK
    return pl.pallas_call(
        functools.partial(early_kernel, offsets, late),
        in_specs=[SMEM] * 6 + [HBM] * len(pieces),
        out_specs=[VMEM] * 7,
        out_shape=[
            jax.ShapeDtypeStruct((count, lat, tokens), jnp.float32),
            jax.ShapeDtypeStruct((2, 8, tokens), jnp.float32),
            jax.ShapeDtypeStruct((8, rows), jnp.float32),
            jax.ShapeDtypeStruct((len(pieces), rows, width), jnp.bfloat16),
            jax.ShapeDtypeStruct((count, lat + 16, tokens), jnp.bfloat16),
            jax.ShapeDtypeStruct((2 * frames, tokens), jnp.float32),
            jax.ShapeDtypeStruct(((len(pieces) + 2) * frames, 2 * rows), jnp.float32),
        ],
        scratch_shapes=[
            pltpu.VMEM((blocks, count, 2 * rows, HD), jnp.bfloat16),
            pltpu.SemaphoreType.DMA((len(pieces),)),
        ],
        compiler_params=pltpu.CompilerParams(vmem_limit_bytes=SMALL_VMEM if len(pieces) <= 8 else LARGE_VMEM),
        cost_estimate=pl.CostEstimate(
            flops=count * tokens * tokens * 2 * (HD + lat),
            bytes_accessed=tokens * count * 3 * HD * 2,
            transcendentals=count * tokens * tokens,
        ),
        name="attend_early",
    )(span_frames, me, timestep, step_weight, sign, sample, *pieces)


def attend_late(pieces, offsets, late, early, count, lat):
    rows, width = pieces[0].shape
    half = len(offsets) // 2 + 1
    tokens = 2 * half * rows
    return pl.pallas_call(
        functools.partial(late_kernel, offsets, late),
        in_specs=[VMEM] * (2 + len(early)),
        out_specs=[VMEM] * 4,
        out_shape=[
            jax.ShapeDtypeStruct((half // 2, lat, rows), jnp.bfloat16 if g else jnp.float32) for g in range(4)
        ],
        scratch_shapes=[pltpu.VMEM((count, lat + 16, 2 * rows), jnp.bfloat16)],
        compiler_params=pltpu.CompilerParams(vmem_limit_bytes=SMALL_VMEM if half <= 4 else LARGE_VMEM),
        cost_estimate=pl.CostEstimate(
            flops=count * tokens * rows * 4 * (HD + lat),
            bytes_accessed=tokens * count * 3 * HD * 2,
            transcendentals=count * tokens * rows * 2,
        ),
        name="attend_late",
    )(*pieces, *early)


def swap(array, axis, offset):
    size = lax.axis_size(axis)
    return lax.ppermute(array, axis, [(i, i ^ offset) for i in range(size)])


def body(qkv, readout, step_weight, timestep, span_frames):
    seq_count = lax.axis_size("seq")
    mp_count = lax.axis_size("mp")
    half = seq_count // 2
    count = HEADS // seq_count
    lat = readout.shape[2]
    me = lax.axis_index("seq").astype(jnp.int32).reshape(1)
    mp_index = lax.axis_index("mp").astype(jnp.int32)
    sample_count = mp_count // 2
    model_index = mp_index // sample_count
    sample = (mp_index % sample_count).reshape(1)
    sign = jnp.where(model_index == 1, 1.0, -1.0).astype(jnp.float32).reshape(1)
    model = model_index.reshape(1)
    readout_t = jnp.swapaxes(readout, 1, 2)

    pieces = [None] * seq_count
    for n in range(half):
        k = seq_count - 1 - n
        pieces[k] = swap(pack(me, model, qkv, readout_t, k, count, [pieces[k + 2]] if n > 1 else [], n == 0), "seq", k)
    for k in range(half - 1, 0, -1):
        after = [] if k == half - 1 else [pieces[k + 1], pieces[seq_count - 1]] if k > 1 else [pieces[half - 1]]
        pieces[k] = swap(pack(me, model, qkv, readout_t, k, count, after), "seq", k)
    pieces[0] = pack(me, model, qkv, readout_t, 0, count, [pieces[half - 1]])
    late = [half, half + 1]
    early = [k for k in range(seq_count) if k not in late]
    merged = attend_early(
        [pieces[k] for k in early], early, late, span_frames, me, timestep, step_weight, sign, sample, count, lat
    )
    ends = [pieces[k] for k in late]
    given = attend_late(ends, early, late, merged, count, lat)
    size = half // 2
    while True:
        keep = given[0]
        for n in [2, 3, 1] if len(given) == 4 else range(1, len(given)):
            keep = keep + swap(given[n], "seq", n * size).astype(jnp.float32)
        if size == 1:
            break
        radix = min(4, size)
        size //= radix
        given = [keep[n * size : (n + 1) * size] for n in range(radix)]
    total = keep[0]
    offset = 1
    while offset < mp_count:
        radix = min(4, mp_count // offset)
        own = total
        for n in range(radix - 1, 0, -1):
            total = total + swap(own, "mp", offset * n)
        offset *= radix
    return total.T


def solution(mesh):
    return jax.shard_map(
        body,
        mesh=mesh,
        in_specs=(P("mp", "seq", None), P(), P(), P(), P()),
        out_specs=P("seq", None),
        check_vma=False,
    )
```

```python
import functools
import math

import jax
import jax.numpy as jnp
from jax import lax
from jax.experimental import pallas as pl
from jax.experimental.pallas import tpu as pltpu
from jax.sharding import PartitionSpec as P

HEADS = 32
HD = 128
FRAME_TOK = 64
NT = (((1,), (1,)), ((), ()))
LOG2_SCALE = math.log2(math.e) / math.sqrt(HD)
LOWEST = -1e30
PACK_VMEM = 4 * 1024 * 1024
SMALL_VMEM = 16 * 1024 * 1024
LARGE_VMEM = 60 * 1024 * 1024
SMEM = pl.BlockSpec(memory_space=pltpu.SMEM)
VMEM = pl.BlockSpec(memory_space=pltpu.VMEM)
HBM = pl.BlockSpec(memory_space=pltpu.HBM)


def fold(readout, values):
    return lax.dot_general(readout, values, NT, preferred_element_type=jnp.float32).astype(jnp.bfloat16)


def value_place(h, count, lat):
    return (h * lat) % HD, count * 2 * HD + (h * lat // HD) * HD


def pack_kernel(k, me_ref, model_ref, qkv_ref, readout_ref, *refs):
    out_ref, values, readout, sems = refs[-4:]
    rows = out_ref.shape[0]
    count, lat = values.shape[0], readout.shape[0]
    first = (me_ref[0] ^ k) * count

    def columns(h, part, width):
        return pl.ds(pl.multiple_of(((first + h) * 3 + part) * HD, HD), width)

    copies = [
        pltpu.make_async_copy(
            readout_ref.at[model_ref[0], :, pl.ds(pl.multiple_of(first * HD, HD), count * HD)], readout, sems.at[2 * count]
        )
    ]
    for h in range(count):
        copies.append(pltpu.make_async_copy(qkv_ref.at[0, :, columns(h, 2, HD)], values.at[h], sems.at[h]))
    for h in range(count):
        target = out_ref.at[:, h * 2 * HD : (h + 1) * 2 * HD]
        copies.append(pltpu.make_async_copy(qkv_ref.at[0, :, columns(h, 0, 2 * HD)], target, sems.at[count + h]))
    for copy in copies:
        copy.start()
    copies[0].wait()
    for h in range(count):
        copies[1 + h].wait()
        row, column = value_place(h, count, lat)
        out_ref[row : row + lat, column : column + HD] = fold(readout[:, h * HD : (h + 1) * HD], values[h])
    for copy in copies[1 + count :]:
        copy.wait()


def pack(me, model, qkv, readout_t, k, count, after, first=False):
    rows = qkv.shape[1]
    lat = readout_t.shape[1]
    width = count * 2 * HD + -(-count * lat // HD) * HD
    return pl.pallas_call(
        functools.partial(pack_kernel, k),
        in_specs=[SMEM, SMEM] + [HBM] * (2 + len(after)),
        out_specs=VMEM,
        out_shape=jax.ShapeDtypeStruct((rows, width), jnp.bfloat16),
        scratch_shapes=[
            pltpu.VMEM((count, rows, HD), jnp.bfloat16),
            pltpu.VMEM((lat, count * HD), jnp.bfloat16),
            pltpu.SemaphoreType.DMA((2 * count + 1,)),
        ],
        compiler_params=pltpu.CompilerParams(vmem_limit_bytes=LARGE_VMEM if first else PACK_VMEM),
        cost_estimate=pl.CostEstimate(
            flops=0, bytes_accessed=rows * width * 4, transcendentals=0
        ),
        name="pack",
    )(me, model, qkv, readout_t, *after)


def mask_rows(frames_ref, me, rows, query_offsets, key_offsets):
    columns = lax.broadcasted_iota(jnp.int32, (1, rows), 1)
    places = jnp.concatenate([(me ^ k) * rows + columns for k in query_offsets], axis=1)
    end = frames_ref[0] * FRAME_TOK
    bound = jnp.full(places.shape, end, jnp.int32)
    for c in range(1, frames_ref.shape[0]):
        later = end + frames_ref[c] * FRAME_TOK
        bound = jnp.where(places >= end, later, bound)
        end = later
    return [
        jnp.where((me ^ k) * rows + start < bound, 0.0, -jnp.inf)
        for k in key_offsets
        for start in range(0, rows, FRAME_TOK)
    ]


def run_units(units, lat):
    frames = [tile() for tile in units[0][0]]
    for u, (_, values, shifts, finish) in enumerate(units):
        ahead = list(units[u + 1][0]) if u + 1 < len(units) else []
        peaks = [jnp.max(f, axis=0, keepdims=True) + s for f, s in zip(sum(frames, []), shifts)]
        peak = jnp.maximum(functools.reduce(jnp.maximum, peaks), LOWEST)
        following, summed, start = [], None, 0
        for t, tile in enumerate(frames):
            for _ in range(-(-(len(ahead) - len(following)) // (len(frames) - t))):
                following.append(ahead[len(following)]())
            weights = [
                jnp.exp2((f + (s - peak)) * LOG2_SCALE).astype(jnp.bfloat16)
                for f, s in zip(tile, shifts[start : start + len(tile)])
            ]
            start += len(tile)
            part = jnp.dot(values[t](), jnp.concatenate(weights, axis=0), preferred_element_type=jnp.float32)
            summed = part if summed is None else summed + part
        finish(summed[:lat], summed[lat : lat + 1], peak)
        frames = following


def score_tile(keys, queries):
    scores = lax.dot_general(keys(), queries(), NT, preferred_element_type=jnp.float32)
    return [scores[start : start + FRAME_TOK] for start in range(0, scores.shape[0], FRAME_TOK)]


def stage_values(folded, pieces, lat):
    count = folded.shape[0]
    rows = pieces[0].shape[0]
    for i in range(count):
        row, column = value_place(i, count, lat)
        for n, piece in enumerate(pieces):
            folded[i, :lat, n * rows : (n + 1) * rows] = piece[row : row + lat, column : column + HD]
        folded[i, lat:] = jnp.ones_like(folded[i, lat:])


def pairs_of(pieces, i, what):
    column = (2 * i + what) * HD

    def read(n):
        return lambda: jnp.concatenate([pieces[n][:, column : column + HD], pieces[n + 1][:, column : column + HD]], axis=0)

    return [read(n) for n in range(0, len(pieces), 2)]


def early_kernel(offsets, late, frames_ref, me_ref, timestep_ref, step_weight_ref, sign_ref, sample_ref, *refs):
    count_pieces = len(offsets)
    arrived = refs[:count_pieces]
    sums_ref, stats_ref, factor_ref, pieces, folded, wide_ref, late_ref, asked, sems = refs[-9:]
    me = me_ref[0]
    rows = pieces.shape[1]
    count, lat, _ = sums_ref.shape
    blocks = count_pieces // 2
    copies = [pltpu.make_async_copy(arrived[n], pieces.at[n], sems.at[n]) for n in range(count_pieces)]
    for copy in copies:
        copy.start()
    factor_ref[...] = jnp.full(factor_ref.shape, sign_ref[0] * step_weight_ref[timestep_ref[sample_ref[0]]])
    for ref, queries, keys in ((wide_ref, offsets, late), (late_ref, late, list(offsets) + list(late))):
        for n, row in enumerate(mask_rows(frames_ref, me, rows, queries, keys)):
            ref[n : n + 1] = row
    for copy in copies:
        copy.wait()
    pieces = [pieces.at[n] for n in range(count_pieces)]
    stage_values(folded, pieces, lat)
    for i in range(count):
        for b, read in enumerate(pairs_of(pieces, i, 0)):
            asked[b, i] = read()
    half = count_pieces // 2 + 1

    def some_blocks(b, carry):
        q = [2 * b, 2 * b + 1]
        span = pl.ds(pl.multiple_of(b * 2 * rows, 2 * rows), 2 * rows)
        shifts = mask_rows(frames_ref, me, rows, [jnp.where(n < half, n, n + 2) for n in q], offsets)
        peaks, totals, units = [], [], []
        for i in range(count):

            def finish(summed, total, peak, i=i):
                sums_ref[i, :, span] = summed
                peaks.append(peak)
                totals.append(total)

            tiles = [
                functools.partial(score_tile, keys, lambda i=i: asked[b, i]) for keys in pairs_of(pieces, i, 1)
            ]
            values = [lambda i=i, t=t: folded[i, :, t * 2 * rows : (t + 1) * 2 * rows] for t in range(blocks)]
            units.append((tiles, values, shifts, finish))
        run_units(units, lat)
        rest = [jnp.ones_like(peaks[0])] * (stats_ref.shape[1] - count)
        stats_ref[0, :, span] = jnp.concatenate(peaks + rest, axis=0)
        stats_ref[1, :, span] = jnp.concatenate(totals + rest, axis=0)
        return carry

    lax.fori_loop(0, blocks, some_blocks, 0)


def late_kernel(offsets, late, *refs):
    early = len(offsets)
    arrived = refs[:2]
    sums_ref, stats_ref, factor_ref, early_ref, early_folded, wide_ref, late_ref, *out_refs, folded = refs[2:]
    size, lat, rows = out_refs[0].shape
    count = folded.shape[0]
    pieces = [early_ref.at[n] for n in range(early)] + list(arrived)
    stage_values(folded, pieces[early:], lat)
    factor = factor_ref[:1]
    every = list(offsets) + list(late)
    blocks = early // 2
    results = {}

    def write(number, start):
        for j in range(number):
            k = every[start + j]
            out_ref = out_refs[k // size]
            out_ref[k % size] = (results[start][:, j * rows : (j + 1) * rows] * factor).astype(out_ref.dtype)

    units = []
    for start, number, tiles_in in ((0, early, [blocks]), (early, 2, range(blocks + 1))):
        rows_ref = late_ref if start else wide_ref
        shifts = [rows_ref[n : n + 1] for n in range(rows_ref.shape[0])]
        for i in range(count):

            def finish(summed, total, peak, start=start, number=number, i=i):
                if start == 0:
                    before = stats_ref[0, i : i + 1]
                    highest = jnp.maximum(before, peak)
                    old = jnp.exp2((before - highest) * LOG2_SCALE)
                    new = jnp.exp2((peak - highest) * LOG2_SCALE)
                    both = stats_ref[1, i : i + 1] * old + total * new
                    part = sums_ref[i] * (old / both) + summed * (new / both)
                else:
                    part = summed / total
                results[start] = part if i == 0 else results[start] + part
                if i == count - 1:
                    write(number, start)

            def queries(start=start, number=number, i=i):
                column = 2 * i * HD
                return jnp.concatenate([p[:, column : column + HD] for p in pieces[start : start + number]], axis=0)

            keys = pairs_of(pieces, i, 1)
            tiles = [functools.partial(score_tile, keys[t], queries) for t in tiles_in]
            values = [
                lambda i=i, t=t: folded[i] if t == blocks else early_folded[i, :, t * 2 * rows : (t + 1) * 2 * rows]
                for t in tiles_in
            ]
            units.append((tiles, values, shifts, finish))
    run_units(units, lat)


def attend_early(pieces, offsets, late, span_frames, me, timestep, step_weight, sign, sample, count, lat):
    rows, width = pieces[0].shape
    blocks = len(pieces) // 2
    tokens = len(pieces) * rows
    frames = rows // FRAME_TOK
    return pl.pallas_call(
        functools.partial(early_kernel, offsets, late),
        in_specs=[SMEM] * 6 + [HBM] * len(pieces),
        out_specs=[VMEM] * 7,
        out_shape=[
            jax.ShapeDtypeStruct((count, lat, tokens), jnp.float32),
            jax.ShapeDtypeStruct((2, 8, tokens), jnp.float32),
            jax.ShapeDtypeStruct((8, rows), jnp.float32),
            jax.ShapeDtypeStruct((len(pieces), rows, width), jnp.bfloat16),
            jax.ShapeDtypeStruct((count, lat + 16, tokens), jnp.bfloat16),
            jax.ShapeDtypeStruct((2 * frames, tokens), jnp.float32),
            jax.ShapeDtypeStruct(((len(pieces) + 2) * frames, 2 * rows), jnp.float32),
        ],
        scratch_shapes=[
            pltpu.VMEM((blocks, count, 2 * rows, HD), jnp.bfloat16),
            pltpu.SemaphoreType.DMA((len(pieces),)),
        ],
        compiler_params=pltpu.CompilerParams(vmem_limit_bytes=SMALL_VMEM if len(pieces) <= 8 else LARGE_VMEM),
        cost_estimate=pl.CostEstimate(
            flops=count * tokens * tokens * 2 * (HD + lat),
            bytes_accessed=tokens * count * 3 * HD * 2,
            transcendentals=count * tokens * tokens,
        ),
        name="attend_early",
    )(span_frames, me, timestep, step_weight, sign, sample, *pieces)


def attend_late(pieces, offsets, late, early, count, lat):
    rows, width = pieces[0].shape
    half = len(offsets) // 2 + 1
    tokens = 2 * half * rows
    return pl.pallas_call(
        functools.partial(late_kernel, offsets, late),
        in_specs=[VMEM] * (2 + len(early)),
        out_specs=[VMEM] * 4,
        out_shape=[
            jax.ShapeDtypeStruct((half // 2, lat, rows), jnp.bfloat16 if g else jnp.float32) for g in range(4)
        ],
        scratch_shapes=[pltpu.VMEM((count, lat + 16, 2 * rows), jnp.bfloat16)],
        compiler_params=pltpu.CompilerParams(vmem_limit_bytes=SMALL_VMEM if half <= 4 else LARGE_VMEM),
        cost_estimate=pl.CostEstimate(
            flops=count * tokens * rows * 4 * (HD + lat),
            bytes_accessed=tokens * count * 3 * HD * 2,
            transcendentals=count * tokens * rows * 2,
        ),
        name="attend_late",
    )(*pieces, *early)


def swap(array, axis, offset):
    size = lax.axis_size(axis)
    return lax.ppermute(array, axis, [(i, i ^ offset) for i in range(size)])


def body(qkv, readout, step_weight, timestep, span_frames):
    seq_count = lax.axis_size("seq")
    mp_count = lax.axis_size("mp")
    half = seq_count // 2
    count = HEADS // seq_count
    lat = readout.shape[2]
    me = lax.axis_index("seq").astype(jnp.int32).reshape(1)
    mp_index = lax.axis_index("mp").astype(jnp.int32)
    sample_count = mp_count // 2
    model_index = mp_index // sample_count
    sample = (mp_index % sample_count).reshape(1)
    sign = jnp.where(model_index == 1, 1.0, -1.0).astype(jnp.float32).reshape(1)
    model = model_index.reshape(1)
    readout_t = jnp.swapaxes(readout, 1, 2)

    pieces = [None] * seq_count
    for n in range(half):
        k = seq_count - 1 - n
        pieces[k] = swap(pack(me, model, qkv, readout_t, k, count, [pieces[k + 2]] if n > 1 else [], n == 0), "seq", k)
    for k in range(half - 1, 0, -1):
        after = [] if k == half - 1 else [pieces[k + 1], pieces[seq_count - 1]] if k > 1 else [pieces[half - 1]]
        pieces[k] = swap(pack(me, model, qkv, readout_t, k, count, after), "seq", k)
    pieces[0] = pack(me, model, qkv, readout_t, 0, count, [pieces[half - 1]])
    late = [half, half + 1]
    early = [k for k in range(seq_count) if k not in late]
    merged = attend_early(
        [pieces[k] for k in early], early, late, span_frames, me, timestep, step_weight, sign, sample, count, lat
    )
    ends = [pieces[k] for k in late]
    given = attend_late(ends, early, late, merged, count, lat)
    size = half // 2
    while True:
        keep = given[0]
        for n in [2, 1, 3] if len(given) == 4 else range(1, len(given)):
            keep = keep + swap(given[n], "seq", n * size).astype(jnp.float32)
        if size == 1:
            break
        radix = min(4, size)
        size //= radix
        given = [keep[n * size : (n + 1) * size] for n in range(radix)]
    total = keep[0]
    offset = 1
    while offset < mp_count:
        radix = min(4, mp_count // offset)
        own = total
        for n in range(radix - 1, 0, -1):
            total = total + swap(own, "mp", offset * n)
        offset *= radix
    return total.T


def solution(mesh):
    return jax.shard_map(
        body,
        mesh=mesh,
        in_specs=(P("mp", "seq", None), P(), P(), P(), P()),
        out_specs=P("seq", None),
        check_vma=False,
    )
```

```python
import functools
import math

import jax
import jax.numpy as jnp
from jax import lax
from jax.experimental import pallas as pl
from jax.experimental.pallas import tpu as pltpu
from jax.sharding import PartitionSpec as P

HEADS = 32
HD = 128
FRAME_TOK = 64
NT = (((1,), (1,)), ((), ()))
LOG2_SCALE = math.log2(math.e) / math.sqrt(HD)
LOWEST = -1e30
PACK_VMEM = 4 * 1024 * 1024
SMALL_VMEM = 16 * 1024 * 1024
LARGE_VMEM = 60 * 1024 * 1024
SMEM = pl.BlockSpec(memory_space=pltpu.SMEM)
VMEM = pl.BlockSpec(memory_space=pltpu.VMEM)
HBM = pl.BlockSpec(memory_space=pltpu.HBM)


def fold(readout, values):
    return lax.dot_general(readout, values, NT, preferred_element_type=jnp.float32).astype(jnp.bfloat16)


def value_place(h, count, lat):
    return (h * lat) % HD, count * 2 * HD + (h * lat // HD) * HD


def pack_kernel(k, me_ref, model_ref, qkv_ref, readout_ref, *refs):
    out_ref, slab, readout, sems = refs[-4:]
    lat = readout.shape[0]
    count = readout.shape[1] // HD
    target = me_ref[0] ^ k

    def columns(width):
        return pl.ds(pl.multiple_of(target * count * width, HD), count * width)

    copies = [
        pltpu.make_async_copy(qkv_ref.at[0, :, columns(3 * HD)], slab, sems.at[0]),
        pltpu.make_async_copy(readout_ref.at[model_ref[0], :, columns(HD)], readout, sems.at[1]),
    ]
    for copy in copies:
        copy.start()
    for copy in copies:
        copy.wait()
    for h in range(count):
        base = h * 3 * HD
        out_ref[:, h * 2 * HD : (h + 1) * 2 * HD] = slab[:, base : base + 2 * HD]
        row, column = value_place(h, count, lat)
        out_ref[row : row + lat, column : column + HD] = fold(
            readout[:, h * HD : (h + 1) * HD], slab[:, base + 2 * HD : base + 3 * HD]
        )


def pack(me, model, qkv, readout_t, k, count, after, first=False):
    rows = qkv.shape[1]
    lat = readout_t.shape[1]
    width = count * 2 * HD + -(-count * lat // HD) * HD
    return pl.pallas_call(
        functools.partial(pack_kernel, k),
        in_specs=[SMEM, SMEM] + [HBM] * (2 + len(after)),
        out_specs=VMEM,
        out_shape=jax.ShapeDtypeStruct((rows, width), jnp.bfloat16),
        scratch_shapes=[
            pltpu.VMEM((rows, count * 3 * HD), jnp.bfloat16),
            pltpu.VMEM((lat, count * HD), jnp.bfloat16),
            pltpu.SemaphoreType.DMA((2,)),
        ],
        compiler_params=pltpu.CompilerParams(vmem_limit_bytes=LARGE_VMEM if first else PACK_VMEM),
        cost_estimate=pl.CostEstimate(
            flops=0, bytes_accessed=rows * width * 4, transcendentals=0
        ),
        name="pack",
    )(me, model, qkv, readout_t, *after)


def mask_rows(frames_ref, me, rows, query_offsets, key_offsets):
    columns = lax.broadcasted_iota(jnp.int32, (1, rows), 1)
    places = jnp.concatenate([(me ^ k) * rows + columns for k in query_offsets], axis=1)
    end = frames_ref[0] * FRAME_TOK
    bound = jnp.full(places.shape, end, jnp.int32)
    for c in range(1, frames_ref.shape[0]):
        later = end + frames_ref[c] * FRAME_TOK
        bound = jnp.where(places >= end, later, bound)
        end = later
    return [
        jnp.where((me ^ k) * rows + start < bound, 0.0, -jnp.inf)
        for k in key_offsets
        for start in range(0, rows, FRAME_TOK)
    ]


def run_units(units, lat):
    frames = [tile() for tile in units[0][0]]
    for u, (_, values, shifts, finish) in enumerate(units):
        ahead = list(units[u + 1][0]) if u + 1 < len(units) else []
        peaks = [jnp.max(f, axis=0, keepdims=True) + s for f, s in zip(sum(frames, []), shifts)]
        peak = jnp.maximum(functools.reduce(jnp.maximum, peaks), LOWEST)
        following, summed, start = [], None, 0
        for t, tile in enumerate(frames):
            for _ in range(-(-(len(ahead) - len(following)) // (len(frames) - t))):
                following.append(ahead[len(following)]())
            weights = [
                jnp.exp2((f + (s - peak)) * LOG2_SCALE).astype(jnp.bfloat16)
                for f, s in zip(tile, shifts[start : start + len(tile)])
            ]
            start += len(tile)
            part = jnp.dot(values[t](), jnp.concatenate(weights, axis=0), preferred_element_type=jnp.float32)
            summed = part if summed is None else summed + part
        finish(summed[:lat], summed[lat : lat + 1], peak)
        frames = following


def score_tile(keys, queries):
    scores = lax.dot_general(keys(), queries(), NT, preferred_element_type=jnp.float32)
    return [scores[start : start + FRAME_TOK] for start in range(0, scores.shape[0], FRAME_TOK)]


def stage_values(folded, pieces, lat):
    count = folded.shape[0]
    rows = pieces[0].shape[0]
    for i in range(count):
        row, column = value_place(i, count, lat)
        for n, piece in enumerate(pieces):
            folded[i, :lat, n * rows : (n + 1) * rows] = piece[row : row + lat, column : column + HD]
        folded[i, lat:] = jnp.ones_like(folded[i, lat:])


def pairs_of(pieces, i, what):
    column = (2 * i + what) * HD

    def read(n):
        return lambda: jnp.concatenate([pieces[n][:, column : column + HD], pieces[n + 1][:, column : column + HD]], axis=0)

    return [read(n) for n in range(0, len(pieces), 2)]


def early_kernel(offsets, late, frames_ref, me_ref, timestep_ref, step_weight_ref, sign_ref, sample_ref, *refs):
    count_pieces = len(offsets)
    arrived = refs[:count_pieces]
    sums_ref, stats_ref, factor_ref, pieces, folded, wide_ref, late_ref, asked, sems = refs[-9:]
    me = me_ref[0]
    rows = pieces.shape[1]
    count, lat, _ = sums_ref.shape
    blocks = count_pieces // 2
    copies = [pltpu.make_async_copy(arrived[n], pieces.at[n], sems.at[n]) for n in range(count_pieces)]
    for copy in copies:
        copy.start()
    factor_ref[...] = jnp.full(factor_ref.shape, sign_ref[0] * step_weight_ref[timestep_ref[sample_ref[0]]])
    for ref, queries, keys in ((wide_ref, offsets, late), (late_ref, late, list(offsets) + list(late))):
        for n, row in enumerate(mask_rows(frames_ref, me, rows, queries, keys)):
            ref[n : n + 1] = row
    for copy in copies:
        copy.wait()
    pieces = [pieces.at[n] for n in range(count_pieces)]
    stage_values(folded, pieces, lat)
    for i in range(count):
        for b, read in enumerate(pairs_of(pieces, i, 0)):
            asked[b, i] = read()
    half = count_pieces // 2 + 1

    def some_blocks(b, carry):
        q = [2 * b, 2 * b + 1]
        span = pl.ds(pl.multiple_of(b * 2 * rows, 2 * rows), 2 * rows)
        shifts = mask_rows(frames_ref, me, rows, [jnp.where(n < half, n, n + 2) for n in q], offsets)
        peaks, totals, units = [], [], []
        for i in range(count):

            def finish(summed, total, peak, i=i):
                sums_ref[i, :, span] = summed
                peaks.append(peak)
                totals.append(total)

            tiles = [
                functools.partial(score_tile, keys, lambda i=i: asked[b, i]) for keys in pairs_of(pieces, i, 1)
            ]
            values = [lambda i=i, t=t: folded[i, :, t * 2 * rows : (t + 1) * 2 * rows] for t in range(blocks)]
            units.append((tiles, values, shifts, finish))
        run_units(units, lat)
        rest = [jnp.ones_like(peaks[0])] * (stats_ref.shape[1] - count)
        stats_ref[0, :, span] = jnp.concatenate(peaks + rest, axis=0)
        stats_ref[1, :, span] = jnp.concatenate(totals + rest, axis=0)
        return carry

    lax.fori_loop(0, blocks, some_blocks, 0)


def late_kernel(offsets, late, *refs):
    early = len(offsets)
    arrived = refs[:2]
    sums_ref, stats_ref, factor_ref, early_ref, early_folded, wide_ref, late_ref, *out_refs, folded = refs[2:]
    size, lat, rows = out_refs[0].shape
    count = folded.shape[0]
    pieces = [early_ref.at[n] for n in range(early)] + list(arrived)
    stage_values(folded, pieces[early:], lat)
    factor = factor_ref[:1]
    every = list(offsets) + list(late)
    blocks = early // 2
    results = {}

    def write(number, start):
        for j in range(number):
            k = every[start + j]
            out_ref = out_refs[k // size]
            out_ref[k % size] = (results[start][:, j * rows : (j + 1) * rows] * factor).astype(out_ref.dtype)

    units = []
    for start, number, tiles_in in ((0, early, [blocks]), (early, 2, range(blocks + 1))):
        rows_ref = late_ref if start else wide_ref
        shifts = [rows_ref[n : n + 1] for n in range(rows_ref.shape[0])]
        for i in range(count):

            def finish(summed, total, peak, start=start, number=number, i=i):
                if start == 0:
                    before = stats_ref[0, i : i + 1]
                    highest = jnp.maximum(before, peak)
                    old = jnp.exp2((before - highest) * LOG2_SCALE)
                    new = jnp.exp2((peak - highest) * LOG2_SCALE)
                    both = stats_ref[1, i : i + 1] * old + total * new
                    part = sums_ref[i] * (old / both) + summed * (new / both)
                else:
                    part = summed / total
                results[start] = part if i == 0 else results[start] + part
                if i == count - 1:
                    write(number, start)

            def queries(start=start, number=number, i=i):
                column = 2 * i * HD
                return jnp.concatenate([p[:, column : column + HD] for p in pieces[start : start + number]], axis=0)

            keys = pairs_of(pieces, i, 1)
            tiles = [functools.partial(score_tile, keys[t], queries) for t in tiles_in]
            values = [
                lambda i=i, t=t: folded[i] if t == blocks else early_folded[i, :, t * 2 * rows : (t + 1) * 2 * rows]
                for t in tiles_in
            ]
            units.append((tiles, values, shifts, finish))
    run_units(units, lat)


def attend_early(pieces, offsets, late, span_frames, me, timestep, step_weight, sign, sample, count, lat):
    rows, width = pieces[0].shape
    blocks = len(pieces) // 2
    tokens = len(pieces) * rows
    frames = rows // FRAME_TOK
    return pl.pallas_call(
        functools.partial(early_kernel, offsets, late),
        in_specs=[SMEM] * 6 + [HBM] * len(pieces),
        out_specs=[VMEM] * 7,
        out_shape=[
            jax.ShapeDtypeStruct((count, lat, tokens), jnp.float32),
            jax.ShapeDtypeStruct((2, 8, tokens), jnp.float32),
            jax.ShapeDtypeStruct((8, rows), jnp.float32),
            jax.ShapeDtypeStruct((len(pieces), rows, width), jnp.bfloat16),
            jax.ShapeDtypeStruct((count, lat + 16, tokens), jnp.bfloat16),
            jax.ShapeDtypeStruct((2 * frames, tokens), jnp.float32),
            jax.ShapeDtypeStruct(((len(pieces) + 2) * frames, 2 * rows), jnp.float32),
        ],
        scratch_shapes=[
            pltpu.VMEM((blocks, count, 2 * rows, HD), jnp.bfloat16),
            pltpu.SemaphoreType.DMA((len(pieces),)),
        ],
        compiler_params=pltpu.CompilerParams(vmem_limit_bytes=SMALL_VMEM if len(pieces) <= 8 else LARGE_VMEM),
        cost_estimate=pl.CostEstimate(
            flops=count * tokens * tokens * 2 * (HD + lat),
            bytes_accessed=tokens * count * 3 * HD * 2,
            transcendentals=count * tokens * tokens,
        ),
        name="attend_early",
    )(span_frames, me, timestep, step_weight, sign, sample, *pieces)


def attend_late(pieces, offsets, late, early, count, lat):
    rows, width = pieces[0].shape
    half = len(offsets) // 2 + 1
    tokens = 2 * half * rows
    return pl.pallas_call(
        functools.partial(late_kernel, offsets, late),
        in_specs=[VMEM] * (2 + len(early)),
        out_specs=[VMEM] * 4,
        out_shape=[
            jax.ShapeDtypeStruct((half // 2, lat, rows), jnp.bfloat16 if g else jnp.float32) for g in range(4)
        ],
        scratch_shapes=[pltpu.VMEM((count, lat + 16, 2 * rows), jnp.bfloat16)],
        compiler_params=pltpu.CompilerParams(vmem_limit_bytes=SMALL_VMEM if half <= 4 else LARGE_VMEM),
        cost_estimate=pl.CostEstimate(
            flops=count * tokens * rows * 4 * (HD + lat),
            bytes_accessed=tokens * count * 3 * HD * 2,
            transcendentals=count * tokens * rows * 2,
        ),
        name="attend_late",
    )(*pieces, *early)


def swap(array, axis, offset):
    size = lax.axis_size(axis)
    return lax.ppermute(array, axis, [(i, i ^ offset) for i in range(size)])


def body(qkv, readout, step_weight, timestep, span_frames):
    seq_count = lax.axis_size("seq")
    mp_count = lax.axis_size("mp")
    half = seq_count // 2
    count = HEADS // seq_count
    lat = readout.shape[2]
    me = lax.axis_index("seq").astype(jnp.int32).reshape(1)
    mp_index = lax.axis_index("mp").astype(jnp.int32)
    sample_count = mp_count // 2
    model_index = mp_index // sample_count
    sample = (mp_index % sample_count).reshape(1)
    sign = jnp.where(model_index == 1, 1.0, -1.0).astype(jnp.float32).reshape(1)
    model = model_index.reshape(1)
    readout_t = jnp.swapaxes(readout, 1, 2)

    pieces = [None] * seq_count
    for n in range(half):
        k = seq_count - 1 - n
        pieces[k] = swap(pack(me, model, qkv, readout_t, k, count, [pieces[k + 2]] if n > 1 else [], n == 0), "seq", k)
    for k in range(half - 1, 0, -1):
        after = [] if k == half - 1 else [pieces[k + 1], pieces[seq_count - 1]] if k > 1 else [pieces[half - 1]]
        pieces[k] = swap(pack(me, model, qkv, readout_t, k, count, after), "seq", k)
    pieces[0] = pack(me, model, qkv, readout_t, 0, count, [pieces[half - 1]])
    late = [half, half + 1]
    early = [k for k in range(seq_count) if k not in late]
    merged = attend_early(
        [pieces[k] for k in early], early, late, span_frames, me, timestep, step_weight, sign, sample, count, lat
    )
    ends = [pieces[k] for k in late]
    given = attend_late(ends, early, late, merged, count, lat)
    size = half // 2
    while True:
        keep = given[0]
        for n in [2, 3, 1] if len(given) == 4 else range(1, len(given)):
            keep = keep + swap(given[n], "seq", n * size).astype(jnp.float32)
        if size == 1:
            break
        radix = min(4, size)
        size //= radix
        given = [keep[n * size : (n + 1) * size] for n in range(radix)]
    total = keep[0]
    offset = 1
    while offset < mp_count:
        radix = min(4, mp_count // offset)
        own = total
        for n in range(radix - 1, 0, -1):
            total = total + swap(own, "mp", offset * n)
        offset *= radix
    return total.T


def solution(mesh):
    return jax.shard_map(
        body,
        mesh=mesh,
        in_specs=(P("mp", "seq", None), P(), P(), P(), P()),
        out_specs=P("seq", None),
        check_vma=False,
    )
```

```python
import functools
import math

import jax
import jax.numpy as jnp
from jax import lax
from jax.experimental import pallas as pl
from jax.experimental.pallas import tpu as pltpu
from jax.sharding import PartitionSpec as P

HEADS = 32
HD = 128
FRAME_TOK = 64
NT = (((1,), (1,)), ((), ()))
LOG2_SCALE = math.log2(math.e) / math.sqrt(HD)
LOWEST = -1e30
PACK_VMEM = 4 * 1024 * 1024
SMALL_VMEM = 16 * 1024 * 1024
LARGE_VMEM = 60 * 1024 * 1024
SMEM = pl.BlockSpec(memory_space=pltpu.SMEM)
VMEM = pl.BlockSpec(memory_space=pltpu.VMEM)
HBM = pl.BlockSpec(memory_space=pltpu.HBM)


def fold(readout, values):
    return lax.dot_general(readout, values, NT, preferred_element_type=jnp.float32).astype(jnp.bfloat16)


def value_place(h, count, lat):
    return (h * lat) % HD, count * 2 * HD + (h * lat // HD) * HD


def pack_kernel(k, me_ref, model_ref, qkv_ref, readout_ref, *refs):
    out_ref, slab, readout, sems = refs[-4:]
    lat = readout.shape[0]
    count = readout.shape[1] // HD
    target = me_ref[0] ^ k

    def columns(width):
        return pl.ds(pl.multiple_of(target * count * width, HD), count * width)

    copies = [
        pltpu.make_async_copy(qkv_ref.at[0, :, columns(3 * HD)], slab, sems.at[0]),
        pltpu.make_async_copy(readout_ref.at[model_ref[0], :, columns(HD)], readout, sems.at[1]),
    ]
    for copy in copies:
        copy.start()
    for copy in copies:
        copy.wait()
    for h in range(count):
        base = h * 3 * HD
        out_ref[:, h * 2 * HD : (h + 1) * 2 * HD] = slab[:, base : base + 2 * HD]
        row, column = value_place(h, count, lat)
        out_ref[row : row + lat, column : column + HD] = fold(
            readout[:, h * HD : (h + 1) * HD], slab[:, base + 2 * HD : base + 3 * HD]
        )


def pack(me, model, qkv, readout_t, k, count, after, first=False):
    rows = qkv.shape[1]
    lat = readout_t.shape[1]
    width = count * 2 * HD + -(-count * lat // HD) * HD
    return pl.pallas_call(
        functools.partial(pack_kernel, k),
        in_specs=[SMEM, SMEM] + [HBM] * (2 + len(after)),
        out_specs=VMEM,
        out_shape=jax.ShapeDtypeStruct((rows, width), jnp.bfloat16),
        scratch_shapes=[
            pltpu.VMEM((rows, count * 3 * HD), jnp.bfloat16),
            pltpu.VMEM((lat, count * HD), jnp.bfloat16),
            pltpu.SemaphoreType.DMA((2,)),
        ],
        compiler_params=pltpu.CompilerParams(vmem_limit_bytes=LARGE_VMEM if first else PACK_VMEM),
        cost_estimate=pl.CostEstimate(
            flops=0, bytes_accessed=rows * width * 4, transcendentals=0
        ),
        name="pack",
    )(me, model, qkv, readout_t, *after)


def mask_rows(frames_ref, me, rows, query_offsets, key_offsets):
    columns = lax.broadcasted_iota(jnp.int32, (1, rows), 1)
    places = jnp.concatenate([(me ^ k) * rows + columns for k in query_offsets], axis=1)
    end = frames_ref[0] * FRAME_TOK
    bound = jnp.full(places.shape, end, jnp.int32)
    for c in range(1, frames_ref.shape[0]):
        later = end + frames_ref[c] * FRAME_TOK
        bound = jnp.where(places >= end, later, bound)
        end = later
    return [
        jnp.where((me ^ k) * rows + start < bound, 0.0, -jnp.inf)
        for k in key_offsets
        for start in range(0, rows, FRAME_TOK)
    ]


def run_units(units, lat):
    frames = [tile() for tile in units[0][0]]
    for u, (_, values, shifts, finish) in enumerate(units):
        ahead = list(units[u + 1][0]) if u + 1 < len(units) else []
        peaks = [jnp.max(f, axis=0, keepdims=True) + s for f, s in zip(sum(frames, []), shifts)]
        peak = jnp.maximum(functools.reduce(jnp.maximum, peaks), LOWEST)
        following, summed, start = [], None, 0
        for t, tile in enumerate(frames):
            for _ in range(-(-(len(ahead) - len(following)) // (len(frames) - t))):
                following.append(ahead[len(following)]())
            weights = [
                jnp.exp2((f + (s - peak)) * LOG2_SCALE).astype(jnp.bfloat16)
                for f, s in zip(tile, shifts[start : start + len(tile)])
            ]
            start += len(tile)
            part = jnp.dot(values[t](), jnp.concatenate(weights, axis=0), preferred_element_type=jnp.float32)
            summed = part if summed is None else summed + part
        finish(summed[:lat], summed[lat : lat + 1], peak)
        frames = following


def score_tile(keys, queries):
    scores = lax.dot_general(keys(), queries(), NT, preferred_element_type=jnp.float32)
    return [scores[start : start + FRAME_TOK] for start in range(0, scores.shape[0], FRAME_TOK)]


def stage_values(folded, pieces, lat):
    count = folded.shape[0]
    rows = pieces[0].shape[0]
    for i in range(count):
        row, column = value_place(i, count, lat)
        for n, piece in enumerate(pieces):
            folded[i, :lat, n * rows : (n + 1) * rows] = piece[row : row + lat, column : column + HD]
        folded[i, lat:] = jnp.ones_like(folded[i, lat:])


def pairs_of(pieces, i, what):
    column = (2 * i + what) * HD

    def read(n):
        return lambda: jnp.concatenate([pieces[n][:, column : column + HD], pieces[n + 1][:, column : column + HD]], axis=0)

    return [read(n) for n in range(0, len(pieces), 2)]


def early_kernel(offsets, late, frames_ref, me_ref, timestep_ref, step_weight_ref, sign_ref, sample_ref, *refs):
    count_pieces = len(offsets)
    arrived = refs[:count_pieces]
    sums_ref, stats_ref, factor_ref, pieces, folded, wide_ref, late_ref, asked, sems = refs[-9:]
    me = me_ref[0]
    rows = pieces.shape[1]
    count, lat, _ = sums_ref.shape
    blocks = count_pieces // 2
    copies = [pltpu.make_async_copy(arrived[n], pieces.at[n], sems.at[n]) for n in range(count_pieces)]
    for copy in copies:
        copy.start()
    factor_ref[...] = jnp.full(factor_ref.shape, sign_ref[0] * step_weight_ref[timestep_ref[sample_ref[0]]])
    for ref, queries, keys in ((wide_ref, offsets, late), (late_ref, late, list(offsets) + list(late))):
        for n, row in enumerate(mask_rows(frames_ref, me, rows, queries, keys)):
            ref[n : n + 1] = row
    for copy in copies:
        copy.wait()
    pieces = [pieces.at[n] for n in range(count_pieces)]
    stage_values(folded, pieces, lat)
    for i in range(count):
        for b, read in enumerate(pairs_of(pieces, i, 0)):
            asked[b, i] = read()
    half = count_pieces // 2 + 1

    def some_blocks(b, carry):
        q = [2 * b, 2 * b + 1]
        span = pl.ds(pl.multiple_of(b * 2 * rows, 2 * rows), 2 * rows)
        shifts = mask_rows(frames_ref, me, rows, [jnp.where(n < half, n, n + 2) for n in q], offsets)
        peaks, totals, units = [], [], []
        for i in range(count):

            def finish(summed, total, peak, i=i):
                sums_ref[i, :, span] = summed
                peaks.append(peak)
                totals.append(total)

            tiles = [
                functools.partial(score_tile, keys, lambda i=i: asked[b, i]) for keys in pairs_of(pieces, i, 1)
            ]
            values = [lambda i=i, t=t: folded[i, :, t * 2 * rows : (t + 1) * 2 * rows] for t in range(blocks)]
            units.append((tiles, values, shifts, finish))
        run_units(units, lat)
        rest = [jnp.ones_like(peaks[0])] * (stats_ref.shape[1] - count)
        stats_ref[0, :, span] = jnp.concatenate(peaks + rest, axis=0)
        stats_ref[1, :, span] = jnp.concatenate(totals + rest, axis=0)
        return carry

    lax.fori_loop(0, blocks, some_blocks, 0)


def late_kernel(offsets, late, *refs):
    early = len(offsets)
    arrived = refs[:2]
    sums_ref, stats_ref, factor_ref, early_ref, early_folded, wide_ref, late_ref, *out_refs, folded = refs[2:]
    size, lat, rows = out_refs[0].shape
    count = folded.shape[0]
    pieces = [early_ref.at[n] for n in range(early)] + list(arrived)
    stage_values(folded, pieces[early:], lat)
    factor = factor_ref[:1]
    every = list(offsets) + list(late)
    blocks = early // 2
    results = {}

    def write(number, start):
        for j in range(number):
            k = every[start + j]
            out_ref = out_refs[k // size]
            out_ref[k % size] = (results[start][:, j * rows : (j + 1) * rows] * factor).astype(out_ref.dtype)

    units = []
    for start, number, tiles_in in ((0, early, [blocks]), (early, 2, range(blocks + 1))):
        rows_ref = late_ref if start else wide_ref
        shifts = [rows_ref[n : n + 1] for n in range(rows_ref.shape[0])]
        for i in range(count):

            def finish(summed, total, peak, start=start, number=number, i=i):
                if start == 0:
                    before = stats_ref[0, i : i + 1]
                    highest = jnp.maximum(before, peak)
                    old = jnp.exp2((before - highest) * LOG2_SCALE)
                    new = jnp.exp2((peak - highest) * LOG2_SCALE)
                    both = stats_ref[1, i : i + 1] * old + total * new
                    part = sums_ref[i] * (old / both) + summed * (new / both)
                else:
                    part = summed / total
                results[start] = part if i == 0 else results[start] + part
                if i == count - 1:
                    write(number, start)

            def queries(start=start, number=number, i=i):
                column = 2 * i * HD
                return jnp.concatenate([p[:, column : column + HD] for p in pieces[start : start + number]], axis=0)

            keys = pairs_of(pieces, i, 1)
            tiles = [functools.partial(score_tile, keys[t], queries) for t in tiles_in]
            values = [
                lambda i=i, t=t: folded[i] if t == blocks else early_folded[i, :, t * 2 * rows : (t + 1) * 2 * rows]
                for t in tiles_in
            ]
            units.append((tiles, values, shifts, finish))
    run_units(units, lat)


def attend_early(pieces, offsets, late, span_frames, me, timestep, step_weight, sign, sample, count, lat):
    rows, width = pieces[0].shape
    blocks = len(pieces) // 2
    tokens = len(pieces) * rows
    frames = rows // FRAME_TOK
    return pl.pallas_call(
        functools.partial(early_kernel, offsets, late),
        in_specs=[SMEM] * 6 + [HBM] * len(pieces),
        out_specs=[VMEM] * 7,
        out_shape=[
            jax.ShapeDtypeStruct((count, lat, tokens), jnp.float32),
            jax.ShapeDtypeStruct((2, 8, tokens), jnp.float32),
            jax.ShapeDtypeStruct((8, rows), jnp.float32),
            jax.ShapeDtypeStruct((len(pieces), rows, width), jnp.bfloat16),
            jax.ShapeDtypeStruct((count, lat + 16, tokens), jnp.bfloat16),
            jax.ShapeDtypeStruct((2 * frames, tokens), jnp.float32),
            jax.ShapeDtypeStruct(((len(pieces) + 2) * frames, 2 * rows), jnp.float32),
        ],
        scratch_shapes=[
            pltpu.VMEM((blocks, count, 2 * rows, HD), jnp.bfloat16),
            pltpu.SemaphoreType.DMA((len(pieces),)),
        ],
        compiler_params=pltpu.CompilerParams(vmem_limit_bytes=SMALL_VMEM if len(pieces) <= 8 else LARGE_VMEM),
        cost_estimate=pl.CostEstimate(
            flops=count * tokens * tokens * 2 * (HD + lat),
            bytes_accessed=tokens * count * 3 * HD * 2,
            transcendentals=count * tokens * tokens,
        ),
        name="attend_early",
    )(span_frames, me, timestep, step_weight, sign, sample, *pieces)


def attend_late(pieces, offsets, late, early, count, lat):
    rows, width = pieces[0].shape
    half = len(offsets) // 2 + 1
    tokens = 2 * half * rows
    return pl.pallas_call(
        functools.partial(late_kernel, offsets, late),
        in_specs=[VMEM] * (2 + len(early)),
        out_specs=[VMEM] * 4,
        out_shape=[
            jax.ShapeDtypeStruct((half // 2, lat, rows), jnp.bfloat16 if g else jnp.float32) for g in range(4)
        ],
        scratch_shapes=[pltpu.VMEM((count, lat + 16, 2 * rows), jnp.bfloat16)],
        compiler_params=pltpu.CompilerParams(vmem_limit_bytes=SMALL_VMEM if half <= 4 else LARGE_VMEM),
        cost_estimate=pl.CostEstimate(
            flops=count * tokens * rows * 4 * (HD + lat),
            bytes_accessed=tokens * count * 3 * HD * 2,
            transcendentals=count * tokens * rows * 2,
        ),
        name="attend_late",
    )(*pieces, *early)


def swap(array, axis, offset):
    size = lax.axis_size(axis)
    return lax.ppermute(array, axis, [(i, i ^ offset) for i in range(size)])


def body(qkv, readout, step_weight, timestep, span_frames):
    seq_count = lax.axis_size("seq")
    mp_count = lax.axis_size("mp")
    half = seq_count // 2
    count = HEADS // seq_count
    lat = readout.shape[2]
    me = lax.axis_index("seq").astype(jnp.int32).reshape(1)
    mp_index = lax.axis_index("mp").astype(jnp.int32)
    sample_count = mp_count // 2
    model_index = mp_index // sample_count
    sample = (mp_index % sample_count).reshape(1)
    sign = jnp.where(model_index == 1, 1.0, -1.0).astype(jnp.float32).reshape(1)
    model = model_index.reshape(1)
    readout_t = jnp.swapaxes(readout, 1, 2)

    pieces = [None] * seq_count
    for n in range(half):
        k = seq_count - 1 - n
        pieces[k] = swap(pack(me, model, qkv, readout_t, k, count, [pieces[k + 2]] if n > 1 else [], n < 2), "seq", k)
    for k in range(half - 1, 0, -1):
        after = [] if k == half - 1 else [pieces[k + 1], pieces[seq_count - 1]] if k > 1 else [pieces[half - 1]]
        pieces[k] = swap(pack(me, model, qkv, readout_t, k, count, after, k == half - 1), "seq", k)
    pieces[0] = pack(me, model, qkv, readout_t, 0, count, [pieces[half - 1]])
    late = [half, half + 1]
    early = [k for k in range(seq_count) if k not in late]
    merged = attend_early(
        [pieces[k] for k in early], early, late, span_frames, me, timestep, step_weight, sign, sample, count, lat
    )
    ends = [pieces[k] for k in late]
    given = attend_late(ends, early, late, merged, count, lat)
    size = half // 2
    while True:
        keep = given[0]
        for n in [2, 3, 1] if len(given) == 4 else range(1, len(given)):
            keep = keep + swap(given[n], "seq", n * size).astype(jnp.float32)
        if size == 1:
            break
        radix = min(4, size)
        size //= radix
        given = [keep[n * size : (n + 1) * size] for n in range(radix)]
    total = keep[0]
    offset = 1
    while offset < mp_count:
        radix = min(4, mp_count // offset)
        own = total
        for n in range(radix - 1, 0, -1):
            total = total + swap(own, "mp", offset * n)
        offset *= radix
    return total.T


def solution(mesh):
    return jax.shard_map(
        body,
        mesh=mesh,
        in_specs=(P("mp", "seq", None), P(), P(), P(), P()),
        out_specs=P("seq", None),
        check_vma=False,
    )
```

```python
import functools
import math

import jax
import jax.numpy as jnp
from jax import lax
from jax.experimental import pallas as pl
from jax.experimental.pallas import tpu as pltpu
from jax.sharding import PartitionSpec as P

HEADS = 32
HD = 128
FRAME_TOK = 64
NT = (((1,), (1,)), ((), ()))
LOG2_SCALE = math.log2(math.e) / math.sqrt(HD)
LOWEST = -1e30
PACK_VMEM = 4 * 1024 * 1024
SMALL_VMEM = 16 * 1024 * 1024
LARGE_VMEM = 60 * 1024 * 1024
SMEM = pl.BlockSpec(memory_space=pltpu.SMEM)
VMEM = pl.BlockSpec(memory_space=pltpu.VMEM)
HBM = pl.BlockSpec(memory_space=pltpu.HBM)


def fold(readout, values):
    return lax.dot_general(readout, values, NT, preferred_element_type=jnp.float32).astype(jnp.bfloat16)


def value_place(h, count, lat):
    return (h * lat) % HD, count * 2 * HD + (h * lat // HD) * HD


def pack_kernel(k, members, qkv_ref, readout_ref, *refs):
    out_ref, slab, readout, sems = refs[-4:]
    lat = readout.shape[0]
    count = readout.shape[1] // HD
    target = lax.axis_index("seq") ^ k
    model = lax.axis_index("mp") // members

    def columns(width):
        return pl.ds(pl.multiple_of(target * count * width, HD), count * width)

    copies = [
        pltpu.make_async_copy(qkv_ref.at[0, :, columns(3 * HD)], slab, sems.at[0]),
        pltpu.make_async_copy(readout_ref.at[model, :, columns(HD)], readout, sems.at[1]),
    ]
    for copy in copies:
        copy.start()
    for copy in copies:
        copy.wait()
    for h in range(count):
        base = h * 3 * HD
        out_ref[:, h * 2 * HD : (h + 1) * 2 * HD] = slab[:, base : base + 2 * HD]
        row, column = value_place(h, count, lat)
        out_ref[row : row + lat, column : column + HD] = fold(
            readout[:, h * HD : (h + 1) * HD], slab[:, base + 2 * HD : base + 3 * HD]
        )


def pack(members, qkv, readout_t, k, count, after, first=False):
    rows = qkv.shape[1]
    lat = readout_t.shape[1]
    width = count * 2 * HD + -(-count * lat // HD) * HD
    return pl.pallas_call(
        functools.partial(pack_kernel, k, members),
        in_specs=[HBM] * (2 + len(after)),
        out_specs=VMEM,
        out_shape=jax.ShapeDtypeStruct((rows, width), jnp.bfloat16),
        scratch_shapes=[
            pltpu.VMEM((rows, count * 3 * HD), jnp.bfloat16),
            pltpu.VMEM((lat, count * HD), jnp.bfloat16),
            pltpu.SemaphoreType.DMA((2,)),
        ],
        compiler_params=pltpu.CompilerParams(vmem_limit_bytes=LARGE_VMEM if first else PACK_VMEM),
        cost_estimate=pl.CostEstimate(
            flops=0, bytes_accessed=rows * width * 4, transcendentals=0
        ),
        name="pack",
    )(qkv, readout_t, *after)


def mask_rows(frames_ref, me, rows, query_offsets, key_offsets):
    columns = lax.broadcasted_iota(jnp.int32, (1, rows), 1)
    places = jnp.concatenate([(me ^ k) * rows + columns for k in query_offsets], axis=1)
    end = frames_ref[0] * FRAME_TOK
    bound = jnp.full(places.shape, end, jnp.int32)
    for c in range(1, frames_ref.shape[0]):
        later = end + frames_ref[c] * FRAME_TOK
        bound = jnp.where(places >= end, later, bound)
        end = later
    return [
        jnp.where((me ^ k) * rows + start < bound, 0.0, -jnp.inf)
        for k in key_offsets
        for start in range(0, rows, FRAME_TOK)
    ]


def run_units(units, lat):
    frames = [tile() for tile in units[0][0]]
    for u, (_, values, shifts, finish) in enumerate(units):
        ahead = list(units[u + 1][0]) if u + 1 < len(units) else []
        peaks = [jnp.max(f, axis=0, keepdims=True) + s for f, s in zip(sum(frames, []), shifts)]
        peak = jnp.maximum(functools.reduce(jnp.maximum, peaks), LOWEST)
        following, summed, start = [], None, 0
        for t, tile in enumerate(frames):
            for _ in range(-(-(len(ahead) - len(following)) // (len(frames) - t))):
                following.append(ahead[len(following)]())
            weights = [
                jnp.exp2((f + (s - peak)) * LOG2_SCALE).astype(jnp.bfloat16)
                for f, s in zip(tile, shifts[start : start + len(tile)])
            ]
            start += len(tile)
            part = jnp.dot(values[t](), jnp.concatenate(weights, axis=0), preferred_element_type=jnp.float32)
            summed = part if summed is None else summed + part
        finish(summed[:lat], summed[lat : lat + 1], peak)
        frames = following


def score_tile(keys, queries):
    scores = lax.dot_general(keys(), queries(), NT, preferred_element_type=jnp.float32)
    return [scores[start : start + FRAME_TOK] for start in range(0, scores.shape[0], FRAME_TOK)]


def stage_values(folded, pieces, lat):
    count = folded.shape[0]
    rows = pieces[0].shape[0]
    for i in range(count):
        row, column = value_place(i, count, lat)
        for n, piece in enumerate(pieces):
            folded[i, :lat, n * rows : (n + 1) * rows] = piece[row : row + lat, column : column + HD]
        folded[i, lat:] = jnp.ones_like(folded[i, lat:])


def pairs_of(pieces, i, what):
    column = (2 * i + what) * HD

    def read(n):
        return lambda: jnp.concatenate([pieces[n][:, column : column + HD], pieces[n + 1][:, column : column + HD]], axis=0)

    return [read(n) for n in range(0, len(pieces), 2)]


def early_kernel(offsets, late, frames_ref, me_ref, timestep_ref, step_weight_ref, sign_ref, sample_ref, *refs):
    count_pieces = len(offsets)
    arrived = refs[:count_pieces]
    sums_ref, stats_ref, factor_ref, pieces, folded, wide_ref, late_ref, asked, sems = refs[-9:]
    me = me_ref[0]
    rows = pieces.shape[1]
    count, lat, _ = sums_ref.shape
    blocks = count_pieces // 2
    copies = [pltpu.make_async_copy(arrived[n], pieces.at[n], sems.at[n]) for n in range(count_pieces)]
    for copy in copies:
        copy.start()
    factor_ref[...] = jnp.full(factor_ref.shape, sign_ref[0] * step_weight_ref[timestep_ref[sample_ref[0]]])
    for ref, queries, keys in ((wide_ref, offsets, late), (late_ref, late, list(offsets) + list(late))):
        for n, row in enumerate(mask_rows(frames_ref, me, rows, queries, keys)):
            ref[n : n + 1] = row
    for copy in copies:
        copy.wait()
    pieces = [pieces.at[n] for n in range(count_pieces)]
    stage_values(folded, pieces, lat)
    for i in range(count):
        for b, read in enumerate(pairs_of(pieces, i, 0)):
            asked[b, i] = read()
    half = count_pieces // 2 + 1

    def some_blocks(b, carry):
        q = [2 * b, 2 * b + 1]
        span = pl.ds(pl.multiple_of(b * 2 * rows, 2 * rows), 2 * rows)
        shifts = mask_rows(frames_ref, me, rows, [jnp.where(n < half, n, n + 2) for n in q], offsets)
        peaks, totals, units = [], [], []
        for i in range(count):

            def finish(summed, total, peak, i=i):
                sums_ref[i, :, span] = summed
                peaks.append(peak)
                totals.append(total)

            tiles = [
                functools.partial(score_tile, keys, lambda i=i: asked[b, i]) for keys in pairs_of(pieces, i, 1)
            ]
            values = [lambda i=i, t=t: folded[i, :, t * 2 * rows : (t + 1) * 2 * rows] for t in range(blocks)]
            units.append((tiles, values, shifts, finish))
        run_units(units, lat)
        rest = [jnp.ones_like(peaks[0])] * (stats_ref.shape[1] - count)
        stats_ref[0, :, span] = jnp.concatenate(peaks + rest, axis=0)
        stats_ref[1, :, span] = jnp.concatenate(totals + rest, axis=0)
        return carry

    lax.fori_loop(0, blocks, some_blocks, 0)


def late_kernel(offsets, late, *refs):
    early = len(offsets)
    arrived = refs[:2]
    sums_ref, stats_ref, factor_ref, early_ref, early_folded, wide_ref, late_ref, *out_refs, folded = refs[2:]
    size, lat, rows = out_refs[0].shape
    count = folded.shape[0]
    pieces = [early_ref.at[n] for n in range(early)] + list(arrived)
    stage_values(folded, pieces[early:], lat)
    factor = factor_ref[:1]
    every = list(offsets) + list(late)
    blocks = early // 2
    results = {}

    def write(number, start):
        for j in range(number):
            k = every[start + j]
            out_ref = out_refs[k // size]
            out_ref[k % size] = (results[start][:, j * rows : (j + 1) * rows] * factor).astype(out_ref.dtype)

    units = []
    for start, number, tiles_in in ((0, early, [blocks]), (early, 2, range(blocks + 1))):
        rows_ref = late_ref if start else wide_ref
        shifts = [rows_ref[n : n + 1] for n in range(rows_ref.shape[0])]
        for i in range(count):

            def finish(summed, total, peak, start=start, number=number, i=i):
                if start == 0:
                    before = stats_ref[0, i : i + 1]
                    highest = jnp.maximum(before, peak)
                    old = jnp.exp2((before - highest) * LOG2_SCALE)
                    new = jnp.exp2((peak - highest) * LOG2_SCALE)
                    both = stats_ref[1, i : i + 1] * old + total * new
                    part = sums_ref[i] * (old / both) + summed * (new / both)
                else:
                    part = summed / total
                results[start] = part if i == 0 else results[start] + part
                if i == count - 1:
                    write(number, start)

            def queries(start=start, number=number, i=i):
                column = 2 * i * HD
                return jnp.concatenate([p[:, column : column + HD] for p in pieces[start : start + number]], axis=0)

            keys = pairs_of(pieces, i, 1)
            tiles = [functools.partial(score_tile, keys[t], queries) for t in tiles_in]
            values = [
                lambda i=i, t=t: folded[i] if t == blocks else early_folded[i, :, t * 2 * rows : (t + 1) * 2 * rows]
                for t in tiles_in
            ]
            units.append((tiles, values, shifts, finish))
    run_units(units, lat)


def attend_early(pieces, offsets, late, span_frames, me, timestep, step_weight, sign, sample, count, lat):
    rows, width = pieces[0].shape
    blocks = len(pieces) // 2
    tokens = len(pieces) * rows
    frames = rows // FRAME_TOK
    return pl.pallas_call(
        functools.partial(early_kernel, offsets, late),
        in_specs=[SMEM] * 6 + [HBM] * len(pieces),
        out_specs=[VMEM] * 7,
        out_shape=[
            jax.ShapeDtypeStruct((count, lat, tokens), jnp.float32),
            jax.ShapeDtypeStruct((2, 8, tokens), jnp.float32),
            jax.ShapeDtypeStruct((8, rows), jnp.float32),
            jax.ShapeDtypeStruct((len(pieces), rows, width), jnp.bfloat16),
            jax.ShapeDtypeStruct((count, lat + 16, tokens), jnp.bfloat16),
            jax.ShapeDtypeStruct((2 * frames, tokens), jnp.float32),
            jax.ShapeDtypeStruct(((len(pieces) + 2) * frames, 2 * rows), jnp.float32),
        ],
        scratch_shapes=[
            pltpu.VMEM((blocks, count, 2 * rows, HD), jnp.bfloat16),
            pltpu.SemaphoreType.DMA((len(pieces),)),
        ],
        compiler_params=pltpu.CompilerParams(vmem_limit_bytes=SMALL_VMEM if len(pieces) <= 8 else LARGE_VMEM),
        cost_estimate=pl.CostEstimate(
            flops=count * tokens * tokens * 2 * (HD + lat),
            bytes_accessed=tokens * count * 3 * HD * 2,
            transcendentals=count * tokens * tokens,
        ),
        name="attend_early",
    )(span_frames, me, timestep, step_weight, sign, sample, *pieces)


def attend_late(pieces, offsets, late, early, count, lat):
    rows, width = pieces[0].shape
    half = len(offsets) // 2 + 1
    tokens = 2 * half * rows
    return pl.pallas_call(
        functools.partial(late_kernel, offsets, late),
        in_specs=[VMEM] * (2 + len(early)),
        out_specs=[VMEM] * 4,
        out_shape=[
            jax.ShapeDtypeStruct((half // 2, lat, rows), jnp.bfloat16 if g else jnp.float32) for g in range(4)
        ],
        scratch_shapes=[pltpu.VMEM((count, lat + 16, 2 * rows), jnp.bfloat16)],
        compiler_params=pltpu.CompilerParams(vmem_limit_bytes=SMALL_VMEM if half <= 4 else LARGE_VMEM),
        cost_estimate=pl.CostEstimate(
            flops=count * tokens * rows * 4 * (HD + lat),
            bytes_accessed=tokens * count * 3 * HD * 2,
            transcendentals=count * tokens * rows * 2,
        ),
        name="attend_late",
    )(*pieces, *early)


def swap(array, axis, offset):
    size = lax.axis_size(axis)
    return lax.ppermute(array, axis, [(i, i ^ offset) for i in range(size)])


def body(qkv, readout, step_weight, timestep, span_frames):
    seq_count = lax.axis_size("seq")
    mp_count = lax.axis_size("mp")
    half = seq_count // 2
    count = HEADS // seq_count
    lat = readout.shape[2]
    me = lax.axis_index("seq").astype(jnp.int32).reshape(1)
    mp_index = lax.axis_index("mp").astype(jnp.int32)
    sample_count = mp_count // 2
    model_index = mp_index // sample_count
    sample = (mp_index % sample_count).reshape(1)
    sign = jnp.where(model_index == 1, 1.0, -1.0).astype(jnp.float32).reshape(1)
    readout_t = jnp.swapaxes(readout, 1, 2)

    pieces = [None] * seq_count
    for n in range(half):
        k = seq_count - 1 - n
        pieces[k] = swap(pack(sample_count, qkv, readout_t, k, count, [pieces[k + 2]] if n > 1 else [], n == 0), "seq", k)
    for k in range(half - 1, 0, -1):
        after = [] if k == half - 1 else [pieces[seq_count - 1], pieces[k + 1]] if k > 1 else [pieces[half - 1], pieces[seq_count - 1]]
        pieces[k] = swap(pack(sample_count, qkv, readout_t, k, count, after), "seq", k)
    pieces[0] = pack(sample_count, qkv, readout_t, 0, count, [pieces[half - 1]])
    late = [half, half + 1]
    early = [k for k in range(seq_count) if k not in late]
    merged = attend_early(
        [pieces[k] for k in early], early, late, span_frames, me, timestep, step_weight, sign, sample, count, lat
    )
    ends = [pieces[k] for k in late]
    given = attend_late(ends, early, late, merged, count, lat)
    size = half // 2
    while True:
        keep = given[0]
        for n in [2, 3, 1] if len(given) == 4 else range(1, len(given)):
            keep = keep + swap(given[n], "seq", n * size).astype(jnp.float32)
        if size == 1:
            break
        radix = min(4, size)
        size //= radix
        given = [keep[n * size : (n + 1) * size] for n in range(radix)]
    total = keep[0]
    offset = 1
    while offset < mp_count:
        radix = min(4, mp_count // offset)
        own = total
        for n in range(radix - 1, 0, -1):
            total = total + swap(own, "mp", offset * n)
        offset *= radix
    return total.T


def solution(mesh):
    return jax.shard_map(
        body,
        mesh=mesh,
        in_specs=(P("mp", "seq", None), P(), P(), P(), P()),
        out_specs=P("seq", None),
        check_vma=False,
    )
```

```python
import functools
import math

import jax
import jax.numpy as jnp
from jax import lax
from jax.experimental import pallas as pl
from jax.experimental.pallas import tpu as pltpu
from jax.sharding import PartitionSpec as P

HEADS = 32
HD = 128
FRAME_TOK = 64
NT = (((1,), (1,)), ((), ()))
LOG2_SCALE = math.log2(math.e) / math.sqrt(HD)
LOWEST = -1e30
PACK_VMEM = 4 * 1024 * 1024
SMALL_VMEM = 16 * 1024 * 1024
LARGE_VMEM = 60 * 1024 * 1024
SMEM = pl.BlockSpec(memory_space=pltpu.SMEM)
VMEM = pl.BlockSpec(memory_space=pltpu.VMEM)
HBM = pl.BlockSpec(memory_space=pltpu.HBM)


def fold(readout, values):
    return lax.dot_general(readout, values, NT, preferred_element_type=jnp.float32).astype(jnp.bfloat16)


def value_place(h, count, lat):
    return (h * lat) % HD, count * 2 * HD + (h * lat // HD) * HD


def pack_kernel(k, me_ref, model_ref, qkv_ref, readout_ref, *refs):
    out_ref, slab, readout, sems = refs[-4:]
    lat = readout.shape[0]
    count = readout.shape[1] // HD
    target = me_ref[0] ^ k

    def columns(width):
        return pl.ds(pl.multiple_of(target * count * width, HD), count * width)

    copies = [
        pltpu.make_async_copy(qkv_ref.at[0, :, columns(3 * HD)], slab, sems.at[0]),
        pltpu.make_async_copy(readout_ref.at[model_ref[0], :, columns(HD)], readout, sems.at[1]),
    ]
    for copy in copies:
        copy.start()
    for copy in copies:
        copy.wait()
    for h in range(count):
        base = h * 3 * HD
        out_ref[:, h * 2 * HD : (h + 1) * 2 * HD] = slab[:, base : base + 2 * HD]
        row, column = value_place(h, count, lat)
        out_ref[row : row + lat, column : column + HD] = fold(
            readout[:, h * HD : (h + 1) * HD], slab[:, base + 2 * HD : base + 3 * HD]
        )


def pack(me, model, qkv, readout_t, k, count, after, first=False):
    rows = qkv.shape[1]
    lat = readout_t.shape[1]
    width = count * 2 * HD + -(-count * lat // HD) * HD
    return pl.pallas_call(
        functools.partial(pack_kernel, k),
        in_specs=[SMEM, SMEM] + [HBM] * (2 + len(after)),
        out_specs=VMEM,
        out_shape=jax.ShapeDtypeStruct((rows, width), jnp.bfloat16),
        scratch_shapes=[
            pltpu.VMEM((rows, count * 3 * HD), jnp.bfloat16),
            pltpu.VMEM((lat, count * HD), jnp.bfloat16),
            pltpu.SemaphoreType.DMA((2,)),
        ],
        compiler_params=pltpu.CompilerParams(vmem_limit_bytes=LARGE_VMEM if first else PACK_VMEM),
        cost_estimate=pl.CostEstimate(
            flops=0, bytes_accessed=rows * width * 4, transcendentals=0
        ),
        name="pack",
    )(me, model, qkv, readout_t, *after)


def mask_rows(frames_ref, me, rows, query_offsets, key_offsets):
    columns = lax.broadcasted_iota(jnp.int32, (1, rows), 1)
    places = jnp.concatenate([(me ^ k) * rows + columns for k in query_offsets], axis=1)
    end = frames_ref[0] * FRAME_TOK
    bound = jnp.full(places.shape, end, jnp.int32)
    for c in range(1, frames_ref.shape[0]):
        later = end + frames_ref[c] * FRAME_TOK
        bound = jnp.where(places >= end, later, bound)
        end = later
    return [
        jnp.where((me ^ k) * rows + start < bound, 0.0, -jnp.inf)
        for k in key_offsets
        for start in range(0, rows, FRAME_TOK)
    ]


def run_units(units, lat):
    frames = [tile() for tile in units[0][0]]
    for u, (_, values, shifts, finish) in enumerate(units):
        ahead = list(units[u + 1][0]) if u + 1 < len(units) else []
        peaks = [jnp.max(f, axis=0, keepdims=True) + s for f, s in zip(sum(frames, []), shifts)]
        peak = jnp.maximum(functools.reduce(jnp.maximum, peaks), LOWEST)
        following, summed, start = [], None, 0
        for t, tile in enumerate(frames):
            for _ in range(-(-(len(ahead) - len(following)) // (len(frames) - t))):
                following.append(ahead[len(following)]())
            weights = [
                jnp.exp2((f + (s - peak)) * LOG2_SCALE).astype(jnp.bfloat16)
                for f, s in zip(tile, shifts[start : start + len(tile)])
            ]
            start += len(tile)
            part = jnp.dot(values[t](), jnp.concatenate(weights, axis=0), preferred_element_type=jnp.float32)
            summed = part if summed is None else summed + part
        finish(summed[:lat], summed[lat : lat + 1], peak)
        frames = following


def score_tile(keys, queries):
    scores = lax.dot_general(keys(), queries(), NT, preferred_element_type=jnp.float32)
    return [scores[start : start + FRAME_TOK] for start in range(0, scores.shape[0], FRAME_TOK)]


def stage_values(folded, pieces, lat):
    count = folded.shape[0]
    rows = pieces[0].shape[0]
    for i in range(count):
        row, column = value_place(i, count, lat)
        for n, piece in enumerate(pieces):
            folded[i, :lat, n * rows : (n + 1) * rows] = piece[row : row + lat, column : column + HD]
        folded[i, lat:] = jnp.ones_like(folded[i, lat:])


def pairs_of(pieces, i, what):
    column = (2 * i + what) * HD

    def read(n):
        return lambda: jnp.concatenate([pieces[n][:, column : column + HD], pieces[n + 1][:, column : column + HD]], axis=0)

    return [read(n) for n in range(0, len(pieces), 2)]


def early_kernel(offsets, late, frames_ref, me_ref, timestep_ref, step_weight_ref, sign_ref, sample_ref, *refs):
    count_pieces = len(offsets)
    arrived = refs[:count_pieces]
    sums_ref, stats_ref, factor_ref, pieces, folded, wide_ref, late_ref, asked, sems = refs[-9:]
    me = me_ref[0]
    rows = pieces.shape[1]
    count, lat, _ = sums_ref.shape
    blocks = count_pieces // 2
    copies = [pltpu.make_async_copy(arrived[n], pieces.at[n], sems.at[n]) for n in range(count_pieces)]
    for copy in copies:
        copy.start()
    factor_ref[...] = jnp.full(factor_ref.shape, sign_ref[0] * step_weight_ref[timestep_ref[sample_ref[0]]])
    for ref, queries, keys in ((wide_ref, offsets, late), (late_ref, late, list(offsets) + list(late))):
        for n, row in enumerate(mask_rows(frames_ref, me, rows, queries, keys)):
            ref[n : n + 1] = row
    for copy in copies:
        copy.wait()
    pieces = [pieces.at[n] for n in range(count_pieces)]
    stage_values(folded, pieces, lat)
    for i in range(count):
        for b, read in enumerate(pairs_of(pieces, i, 0)):
            asked[b, i] = read()
    half = count_pieces // 2 + 1

    def some_blocks(b, carry):
        q = [2 * b, 2 * b + 1]
        span = pl.ds(pl.multiple_of(b * 2 * rows, 2 * rows), 2 * rows)
        shifts = mask_rows(frames_ref, me, rows, [jnp.where(n < half, n, n + 2) for n in q], offsets)
        peaks, totals, units = [], [], []
        for i in range(count):

            def finish(summed, total, peak, i=i):
                sums_ref[i, :, span] = summed
                peaks.append(peak)
                totals.append(total)

            tiles = [
                functools.partial(score_tile, keys, lambda i=i: asked[b, i]) for keys in pairs_of(pieces, i, 1)
            ]
            values = [lambda i=i, t=t: folded[i, :, t * 2 * rows : (t + 1) * 2 * rows] for t in range(blocks)]
            units.append((tiles, values, shifts, finish))
        run_units(units, lat)
        rest = [jnp.ones_like(peaks[0])] * (stats_ref.shape[1] - count)
        stats_ref[0, :, span] = jnp.concatenate(peaks + rest, axis=0)
        stats_ref[1, :, span] = jnp.concatenate(totals + rest, axis=0)
        return carry

    lax.fori_loop(0, blocks, some_blocks, 0)


def late_kernel(offsets, late, *refs):
    early = len(offsets)
    arrived = refs[:2]
    sums_ref, stats_ref, factor_ref, early_ref, early_folded, wide_ref, late_ref, *out_refs, folded = refs[2:]
    size, lat, rows = out_refs[0].shape
    count = folded.shape[0]
    pieces = [early_ref.at[n] for n in range(early)] + list(arrived)
    stage_values(folded, pieces[early:], lat)
    factor = factor_ref[:1]
    every = list(offsets) + list(late)
    blocks = early // 2
    results = {}

    def write(number, start):
        for j in range(number):
            k = every[start + j]
            out_ref = out_refs[k // size]
            out_ref[k % size] = (results[start][:, j * rows : (j + 1) * rows] * factor).astype(out_ref.dtype)

    units = []
    for start, number, tiles_in in ((0, early, [blocks]), (early, 2, range(blocks + 1))):
        rows_ref = late_ref if start else wide_ref
        shifts = [rows_ref[n : n + 1] for n in range(rows_ref.shape[0])]
        for i in range(count):

            def finish(summed, total, peak, start=start, number=number, i=i):
                if start == 0:
                    before = stats_ref[0, i : i + 1]
                    highest = jnp.maximum(before, peak)
                    old = jnp.exp2((before - highest) * LOG2_SCALE)
                    new = jnp.exp2((peak - highest) * LOG2_SCALE)
                    both = stats_ref[1, i : i + 1] * old + total * new
                    part = sums_ref[i] * (old / both) + summed * (new / both)
                else:
                    part = summed / total
                results[start] = part if i == 0 else results[start] + part
                if i == count - 1:
                    write(number, start)

            def queries(start=start, number=number, i=i):
                column = 2 * i * HD
                return jnp.concatenate([p[:, column : column + HD] for p in pieces[start : start + number]], axis=0)

            keys = pairs_of(pieces, i, 1)
            tiles = [functools.partial(score_tile, keys[t], queries) for t in tiles_in]
            values = [
                lambda i=i, t=t: folded[i] if t == blocks else early_folded[i, :, t * 2 * rows : (t + 1) * 2 * rows]
                for t in tiles_in
            ]
            units.append((tiles, values, shifts, finish))
    run_units(units, lat)


def attend_early(pieces, offsets, late, span_frames, me, timestep, step_weight, sign, sample, count, lat):
    rows, width = pieces[0].shape
    blocks = len(pieces) // 2
    tokens = len(pieces) * rows
    frames = rows // FRAME_TOK
    return pl.pallas_call(
        functools.partial(early_kernel, offsets, late),
        in_specs=[SMEM] * 6 + [HBM] * len(pieces),
        out_specs=[VMEM] * 7,
        out_shape=[
            jax.ShapeDtypeStruct((count, lat, tokens), jnp.float32),
            jax.ShapeDtypeStruct((2, 8, tokens), jnp.float32),
            jax.ShapeDtypeStruct((8, rows), jnp.float32),
            jax.ShapeDtypeStruct((len(pieces), rows, width), jnp.bfloat16),
            jax.ShapeDtypeStruct((count, lat + 16, tokens), jnp.bfloat16),
            jax.ShapeDtypeStruct((2 * frames, tokens), jnp.float32),
            jax.ShapeDtypeStruct(((len(pieces) + 2) * frames, 2 * rows), jnp.float32),
        ],
        scratch_shapes=[
            pltpu.VMEM((blocks, count, 2 * rows, HD), jnp.bfloat16),
            pltpu.SemaphoreType.DMA((len(pieces),)),
        ],
        compiler_params=pltpu.CompilerParams(vmem_limit_bytes=SMALL_VMEM if len(pieces) <= 8 else LARGE_VMEM),
        cost_estimate=pl.CostEstimate(
            flops=count * tokens * tokens * 2 * (HD + lat),
            bytes_accessed=tokens * count * 3 * HD * 2,
            transcendentals=count * tokens * tokens,
        ),
        name="attend_early",
    )(span_frames, me, timestep, step_weight, sign, sample, *pieces)


def attend_late(pieces, offsets, late, early, count, lat):
    rows, width = pieces[0].shape
    half = len(offsets) // 2 + 1
    tokens = 2 * half * rows
    return pl.pallas_call(
        functools.partial(late_kernel, offsets, late),
        in_specs=[VMEM] * (2 + len(early)),
        out_specs=[VMEM] * 4,
        out_shape=[
            jax.ShapeDtypeStruct((half // 2, lat, rows), jnp.bfloat16 if g else jnp.float32) for g in range(4)
        ],
        scratch_shapes=[pltpu.VMEM((count, lat + 16, 2 * rows), jnp.bfloat16)],
        compiler_params=pltpu.CompilerParams(vmem_limit_bytes=SMALL_VMEM if half <= 4 else LARGE_VMEM),
        cost_estimate=pl.CostEstimate(
            flops=count * tokens * rows * 4 * (HD + lat),
            bytes_accessed=tokens * count * 3 * HD * 2,
            transcendentals=count * tokens * rows * 2,
        ),
        name="attend_late",
    )(*pieces, *early)


def swap(array, axis, offset):
    size = lax.axis_size(axis)
    return lax.ppermute(array, axis, [(i, i ^ offset) for i in range(size)])


def body(qkv, readout, step_weight, timestep, span_frames):
    seq_count = lax.axis_size("seq")
    mp_count = lax.axis_size("mp")
    half = seq_count // 2
    count = HEADS // seq_count
    lat = readout.shape[2]
    me = lax.axis_index("seq").astype(jnp.int32).reshape(1)
    mp_index = lax.axis_index("mp").astype(jnp.int32)
    sample_count = mp_count // 2
    model_index = mp_index // sample_count
    sample = (mp_index % sample_count).reshape(1)
    sign = jnp.where(model_index == 1, 1.0, -1.0).astype(jnp.float32).reshape(1)
    model = model_index.reshape(1)
    readout_t = jnp.swapaxes(readout, 1, 2)

    pieces = [None] * seq_count
    for n in range(half):
        k = seq_count - 1 - n
        pieces[k] = swap(pack(me, model, qkv, readout_t, k, count, [pieces[k + 2]] if n > 1 else [], n == 0), "seq", k)
    for k in range(half - 1, 0, -1):
        after = [] if k == half - 1 else [pieces[k + 1]] if k > 1 else [pieces[seq_count - 1]]
        pieces[k] = swap(pack(me, model, qkv, readout_t, k, count, after), "seq", k)
    pieces[0] = pack(me, model, qkv, readout_t, 0, count, [pieces[half - 1]])
    late = [half, half + 1]
    early = [k for k in range(seq_count) if k not in late]
    merged = attend_early(
        [pieces[k] for k in early], early, late, span_frames, me, timestep, step_weight, sign, sample, count, lat
    )
    ends = [pieces[k] for k in late]
    given = attend_late(ends, early, late, merged, count, lat)
    size = half // 2
    while True:
        keep = given[0]
        for n in [2, 3, 1] if len(given) == 4 else range(1, len(given)):
            keep = keep + swap(given[n], "seq", n * size).astype(jnp.float32)
        if size == 1:
            break
        radix = min(4, size)
        size //= radix
        given = [keep[n * size : (n + 1) * size] for n in range(radix)]
    total = keep[0]
    offset = 1
    while offset < mp_count:
        radix = min(4, mp_count // offset)
        own = total
        for n in range(radix - 1, 0, -1):
            total = total + swap(own, "mp", offset * n)
        offset *= radix
    return total.T


def solution(mesh):
    return jax.shard_map(
        body,
        mesh=mesh,
        in_specs=(P("mp", "seq", None), P(), P(), P(), P()),
        out_specs=P("seq", None),
        check_vma=False,
    )
```

```python
import functools
import math

import jax
import jax.numpy as jnp
from jax import lax
from jax.experimental import pallas as pl
from jax.experimental.pallas import tpu as pltpu
from jax.sharding import PartitionSpec as P

HEADS = 32
HD = 128
FRAME_TOK = 64
NT = (((1,), (1,)), ((), ()))
LOG2_SCALE = math.log2(math.e) / math.sqrt(HD)
LOWEST = -1e30
PACK_VMEM = 4 * 1024 * 1024
SMALL_VMEM = 16 * 1024 * 1024
LARGE_VMEM = 60 * 1024 * 1024
SMEM = pl.BlockSpec(memory_space=pltpu.SMEM)
VMEM = pl.BlockSpec(memory_space=pltpu.VMEM)
HBM = pl.BlockSpec(memory_space=pltpu.HBM)


def fold(readout, values):
    return lax.dot_general(readout, values, NT, preferred_element_type=jnp.float32).astype(jnp.bfloat16)


def value_place(h, count, lat):
    return (h * lat) % HD, count * 2 * HD + (h * lat // HD) * HD


def pack_kernel(k, me_ref, model_ref, qkv_ref, readout_ref, *refs):
    out_ref, slab, readout, sems = refs[-4:]
    lat = readout.shape[0]
    count = readout.shape[1] // HD
    target = me_ref[0] ^ k

    def columns(width):
        return pl.ds(pl.multiple_of(target * count * width, HD), count * width)

    copies = [
        pltpu.make_async_copy(qkv_ref.at[0, :, columns(3 * HD)], slab, sems.at[0]),
        pltpu.make_async_copy(readout_ref.at[model_ref[0], :, columns(HD)], readout, sems.at[1]),
    ]
    for copy in copies:
        copy.start()
    for copy in copies:
        copy.wait()
    for h in range(count):
        base = h * 3 * HD
        out_ref[:, h * 2 * HD : (h + 1) * 2 * HD] = slab[:, base : base + 2 * HD]
        row, column = value_place(h, count, lat)
        out_ref[row : row + lat, column : column + HD] = fold(
            readout[:, h * HD : (h + 1) * HD], slab[:, base + 2 * HD : base + 3 * HD]
        )


def pack(me, model, qkv, readout_t, k, count, after, first=False):
    rows = qkv.shape[1]
    lat = readout_t.shape[1]
    width = count * 2 * HD + -(-count * lat // HD) * HD
    return pl.pallas_call(
        functools.partial(pack_kernel, k),
        in_specs=[SMEM, SMEM] + [HBM] * (2 + len(after)),
        out_specs=VMEM,
        out_shape=jax.ShapeDtypeStruct((rows, width), jnp.bfloat16),
        scratch_shapes=[
            pltpu.VMEM((rows, count * 3 * HD), jnp.bfloat16),
            pltpu.VMEM((lat, count * HD), jnp.bfloat16),
            pltpu.SemaphoreType.DMA((2,)),
        ],
        compiler_params=pltpu.CompilerParams(vmem_limit_bytes=LARGE_VMEM if first else PACK_VMEM),
        cost_estimate=pl.CostEstimate(
            flops=0, bytes_accessed=rows * width * 4, transcendentals=0
        ),
        name="pack",
    )(me, model, qkv, readout_t, *after)


def mask_rows(frames_ref, me, rows, query_offsets, key_offsets):
    columns = lax.broadcasted_iota(jnp.int32, (1, rows), 1)
    places = jnp.concatenate([(me ^ k) * rows + columns for k in query_offsets], axis=1)
    end = frames_ref[0] * FRAME_TOK
    bound = jnp.full(places.shape, end, jnp.int32)
    for c in range(1, frames_ref.shape[0]):
        later = end + frames_ref[c] * FRAME_TOK
        bound = jnp.where(places >= end, later, bound)
        end = later
    return [
        jnp.where((me ^ k) * rows + start < bound, 0.0, -jnp.inf)
        for k in key_offsets
        for start in range(0, rows, FRAME_TOK)
    ]


def run_units(units, lat):
    frames = [tile() for tile in units[0][0]]
    for u, (_, values, shifts, finish) in enumerate(units):
        ahead = list(units[u + 1][0]) if u + 1 < len(units) else []
        peaks = [jnp.max(f, axis=0, keepdims=True) + s for f, s in zip(sum(frames, []), shifts)]
        peak = jnp.maximum(functools.reduce(jnp.maximum, peaks), LOWEST)
        following, summed, start = [], None, 0
        for t, tile in enumerate(frames):
            for _ in range(-(-(len(ahead) - len(following)) // (len(frames) - t))):
                following.append(ahead[len(following)]())
            weights = [
                jnp.exp2((f + (s - peak)) * LOG2_SCALE).astype(jnp.bfloat16)
                for f, s in zip(tile, shifts[start : start + len(tile)])
            ]
            start += len(tile)
            part = jnp.dot(values[t](), jnp.concatenate(weights, axis=0), preferred_element_type=jnp.float32)
            summed = part if summed is None else summed + part
        finish(summed[:lat], summed[lat : lat + 1], peak)
        frames = following


def score_tile(keys, queries):
    scores = lax.dot_general(keys(), queries(), NT, preferred_element_type=jnp.float32)
    return [scores[start : start + FRAME_TOK] for start in range(0, scores.shape[0], FRAME_TOK)]


def stage_values(folded, pieces, lat):
    count = folded.shape[0]
    rows = pieces[0].shape[0]
    for i in range(count):
        row, column = value_place(i, count, lat)
        for n, piece in enumerate(pieces):
            folded[i, :lat, n * rows : (n + 1) * rows] = piece[row : row + lat, column : column + HD]
        folded[i, lat:] = jnp.ones_like(folded[i, lat:])


def pairs_of(pieces, i, what):
    column = (2 * i + what) * HD

    def read(n):
        return lambda: jnp.concatenate([pieces[n][:, column : column + HD], pieces[n + 1][:, column : column + HD]], axis=0)

    return [read(n) for n in range(0, len(pieces), 2)]


def early_kernel(offsets, late, frames_ref, me_ref, timestep_ref, step_weight_ref, sign_ref, sample_ref, *refs):
    count_pieces = len(offsets)
    arrived = refs[:count_pieces]
    sums_ref, stats_ref, factor_ref, pieces, folded, wide_ref, late_ref, asked, sems = refs[-9:]
    me = me_ref[0]
    rows = pieces.shape[1]
    count, lat, _ = sums_ref.shape
    blocks = count_pieces // 2
    copies = [pltpu.make_async_copy(arrived[n], pieces.at[n], sems.at[n]) for n in range(count_pieces)]
    for copy in copies:
        copy.start()
    factor_ref[...] = jnp.full(factor_ref.shape, sign_ref[0] * step_weight_ref[timestep_ref[sample_ref[0]]])
    for ref, queries, keys in ((wide_ref, offsets, late), (late_ref, late, list(offsets) + list(late))):
        for n, row in enumerate(mask_rows(frames_ref, me, rows, queries, keys)):
            ref[n : n + 1] = row
    for copy in copies:
        copy.wait()
    pieces = [pieces.at[n] for n in range(count_pieces)]
    stage_values(folded, pieces, lat)
    for i in range(count):
        for b, read in enumerate(pairs_of(pieces, i, 0)):
            asked[b, i] = read()
    half = count_pieces // 2 + 1

    def some_blocks(b, carry):
        q = [2 * b, 2 * b + 1]
        span = pl.ds(pl.multiple_of(b * 2 * rows, 2 * rows), 2 * rows)
        shifts = mask_rows(frames_ref, me, rows, [jnp.where(n < half, n, n + 2) for n in q], offsets)
        peaks, totals, units = [], [], []
        for i in range(count):

            def finish(summed, total, peak, i=i):
                sums_ref[i, :, span] = summed
                peaks.append(peak)
                totals.append(total)

            tiles = [
                functools.partial(score_tile, keys, lambda i=i: asked[b, i]) for keys in pairs_of(pieces, i, 1)
            ]
            values = [lambda i=i, t=t: folded[i, :, t * 2 * rows : (t + 1) * 2 * rows] for t in range(blocks)]
            units.append((tiles, values, shifts, finish))
        run_units(units, lat)
        rest = [jnp.ones_like(peaks[0])] * (stats_ref.shape[1] - count)
        stats_ref[0, :, span] = jnp.concatenate(peaks + rest, axis=0)
        stats_ref[1, :, span] = jnp.concatenate(totals + rest, axis=0)
        return carry

    lax.fori_loop(0, blocks, some_blocks, 0)


def late_kernel(offsets, late, *refs):
    early = len(offsets)
    arrived = refs[:2]
    sums_ref, stats_ref, factor_ref, early_ref, early_folded, wide_ref, late_ref, *out_refs, folded = refs[2:]
    size, lat, rows = out_refs[0].shape
    count = folded.shape[0]
    pieces = [early_ref.at[n] for n in range(early)] + list(arrived)
    stage_values(folded, pieces[early:], lat)
    factor = factor_ref[:1]
    every = list(offsets) + list(late)
    blocks = early // 2
    results = {}

    def write(number, start):
        for j in range(number):
            k = every[start + j]
            out_ref = out_refs[k // size]
            out_ref[k % size] = (results[start][:, j * rows : (j + 1) * rows] * factor).astype(out_ref.dtype)

    units = []
    for start, number, tiles_in in ((0, early, [blocks]), (early, 2, range(blocks + 1))):
        rows_ref = late_ref if start else wide_ref
        shifts = [rows_ref[n : n + 1] for n in range(rows_ref.shape[0])]
        for i in range(count):

            def finish(summed, total, peak, start=start, number=number, i=i):
                if start == 0:
                    before = stats_ref[0, i : i + 1]
                    highest = jnp.maximum(before, peak)
                    old = jnp.exp2((before - highest) * LOG2_SCALE)
                    new = jnp.exp2((peak - highest) * LOG2_SCALE)
                    both = stats_ref[1, i : i + 1] * old + total * new
                    part = sums_ref[i] * (old / both) + summed * (new / both)
                else:
                    part = summed / total
                results[start] = part if i == 0 else results[start] + part
                if i == count - 1:
                    write(number, start)

            def queries(start=start, number=number, i=i):
                column = 2 * i * HD
                return jnp.concatenate([p[:, column : column + HD] for p in pieces[start : start + number]], axis=0)

            keys = pairs_of(pieces, i, 1)
            tiles = [functools.partial(score_tile, keys[t], queries) for t in tiles_in]
            values = [
                lambda i=i, t=t: folded[i] if t == blocks else early_folded[i, :, t * 2 * rows : (t + 1) * 2 * rows]
                for t in tiles_in
            ]
            if start == 0:
                column = (2 * i + 1) * HD
                tiles = [
                    functools.partial(score_tile, lambda n=n, c=column: pieces[n][:, c : c + HD], queries)
                    for n in (early, early + 1)
                ]
                values = [lambda i=i, n=n: folded[i, :, n * rows : (n + 1) * rows] for n in range(2)]
            units.append((tiles, values, shifts, finish))
    run_units(units, lat)


def attend_early(pieces, offsets, late, span_frames, me, timestep, step_weight, sign, sample, count, lat):
    rows, width = pieces[0].shape
    blocks = len(pieces) // 2
    tokens = len(pieces) * rows
    frames = rows // FRAME_TOK
    return pl.pallas_call(
        functools.partial(early_kernel, offsets, late),
        in_specs=[SMEM] * 6 + [HBM] * len(pieces),
        out_specs=[VMEM] * 7,
        out_shape=[
            jax.ShapeDtypeStruct((count, lat, tokens), jnp.float32),
            jax.ShapeDtypeStruct((2, 8, tokens), jnp.float32),
            jax.ShapeDtypeStruct((8, rows), jnp.float32),
            jax.ShapeDtypeStruct((len(pieces), rows, width), jnp.bfloat16),
            jax.ShapeDtypeStruct((count, lat + 16, tokens), jnp.bfloat16),
            jax.ShapeDtypeStruct((2 * frames, tokens), jnp.float32),
            jax.ShapeDtypeStruct(((len(pieces) + 2) * frames, 2 * rows), jnp.float32),
        ],
        scratch_shapes=[
            pltpu.VMEM((blocks, count, 2 * rows, HD), jnp.bfloat16),
            pltpu.SemaphoreType.DMA((len(pieces),)),
        ],
        compiler_params=pltpu.CompilerParams(vmem_limit_bytes=SMALL_VMEM if len(pieces) <= 8 else LARGE_VMEM),
        cost_estimate=pl.CostEstimate(
            flops=count * tokens * tokens * 2 * (HD + lat),
            bytes_accessed=tokens * count * 3 * HD * 2,
            transcendentals=count * tokens * tokens,
        ),
        name="attend_early",
    )(span_frames, me, timestep, step_weight, sign, sample, *pieces)


def attend_late(pieces, offsets, late, early, count, lat):
    rows, width = pieces[0].shape
    half = len(offsets) // 2 + 1
    tokens = 2 * half * rows
    return pl.pallas_call(
        functools.partial(late_kernel, offsets, late),
        in_specs=[VMEM] * (2 + len(early)),
        out_specs=[VMEM] * 4,
        out_shape=[
            jax.ShapeDtypeStruct((half // 2, lat, rows), jnp.bfloat16 if g else jnp.float32) for g in range(4)
        ],
        scratch_shapes=[pltpu.VMEM((count, lat + 16, 2 * rows), jnp.bfloat16)],
        compiler_params=pltpu.CompilerParams(vmem_limit_bytes=SMALL_VMEM if half <= 4 else LARGE_VMEM),
        cost_estimate=pl.CostEstimate(
            flops=count * tokens * rows * 4 * (HD + lat),
            bytes_accessed=tokens * count * 3 * HD * 2,
            transcendentals=count * tokens * rows * 2,
        ),
        name="attend_late",
    )(*pieces, *early)


def swap(array, axis, offset):
    size = lax.axis_size(axis)
    return lax.ppermute(array, axis, [(i, i ^ offset) for i in range(size)])


def body(qkv, readout, step_weight, timestep, span_frames):
    seq_count = lax.axis_size("seq")
    mp_count = lax.axis_size("mp")
    half = seq_count // 2
    count = HEADS // seq_count
    lat = readout.shape[2]
    me = lax.axis_index("seq").astype(jnp.int32).reshape(1)
    mp_index = lax.axis_index("mp").astype(jnp.int32)
    sample_count = mp_count // 2
    model_index = mp_index // sample_count
    sample = (mp_index % sample_count).reshape(1)
    sign = jnp.where(model_index == 1, 1.0, -1.0).astype(jnp.float32).reshape(1)
    model = model_index.reshape(1)
    readout_t = jnp.swapaxes(readout, 1, 2)

    pieces = [None] * seq_count
    for n in range(half):
        k = seq_count - 1 - n
        pieces[k] = swap(pack(me, model, qkv, readout_t, k, count, [pieces[k + 2]] if n > 1 else [], n == 0), "seq", k)
    for k in range(half - 1, 0, -1):
        after = [] if k == half - 1 else [pieces[k + 1], pieces[seq_count - 1]] if k > 1 else [pieces[half - 1]]
        pieces[k] = swap(pack(me, model, qkv, readout_t, k, count, after), "seq", k)
    pieces[0] = pack(me, model, qkv, readout_t, 0, count, [pieces[half - 1]])
    late = [half, half + 1]
    early = [k for k in range(seq_count) if k not in late]
    merged = attend_early(
        [pieces[k] for k in early], early, late, span_frames, me, timestep, step_weight, sign, sample, count, lat
    )
    ends = [pieces[k] for k in late]
    given = attend_late(ends, early, late, merged, count, lat)
    size = half // 2
    while True:
        keep = given[0]
        for n in [2, 3, 1] if len(given) == 4 else range(1, len(given)):
            keep = keep + swap(given[n], "seq", n * size).astype(jnp.float32)
        if size == 1:
            break
        radix = min(4, size)
        size //= radix
        given = [keep[n * size : (n + 1) * size] for n in range(radix)]
    total = keep[0]
    offset = 1
    while offset < mp_count:
        radix = min(4, mp_count // offset)
        own = total
        for n in range(radix - 1, 0, -1):
            total = total + swap(own, "mp", offset * n)
        offset *= radix
    return total.T


def solution(mesh):
    return jax.shard_map(
        body,
        mesh=mesh,
        in_specs=(P("mp", "seq", None), P(), P(), P(), P()),
        out_specs=P("seq", None),
        check_vma=False,
    )
```

```python
import functools
import math

import jax
import jax.numpy as jnp
from jax import lax
from jax.experimental import pallas as pl
from jax.experimental.pallas import tpu as pltpu
from jax.sharding import PartitionSpec as P

HEADS = 32
HD = 128
FRAME_TOK = 64
NT = (((1,), (1,)), ((), ()))
LOG2_SCALE = math.log2(math.e) / math.sqrt(HD)
LOWEST = -1e30
PACK_VMEM = 4 * 1024 * 1024
SMALL_VMEM = 16 * 1024 * 1024
LARGE_VMEM = 60 * 1024 * 1024
SMEM = pl.BlockSpec(memory_space=pltpu.SMEM)
VMEM = pl.BlockSpec(memory_space=pltpu.VMEM)
HBM = pl.BlockSpec(memory_space=pltpu.HBM)


def fold(readout, values):
    return lax.dot_general(readout, values, NT, preferred_element_type=jnp.float32).astype(jnp.bfloat16)


def value_place(h, count, lat):
    return (h * lat) % HD, count * 2 * HD + (h * lat // HD) * HD


def pack_kernel(k, me_ref, model_ref, qkv_ref, readout_ref, *refs):
    out_ref, slab, readout, sems = refs[-4:]
    lat = readout.shape[0]
    count = readout.shape[1] // HD
    target = me_ref[0] ^ k

    def columns(width):
        return pl.ds(pl.multiple_of(target * count * width, HD), count * width)

    copies = [
        pltpu.make_async_copy(qkv_ref.at[0, :, columns(3 * HD)], slab, sems.at[0]),
        pltpu.make_async_copy(readout_ref.at[model_ref[0], :, columns(HD)], readout, sems.at[1]),
    ]
    for copy in copies:
        copy.start()
    for copy in copies:
        copy.wait()
    for h in range(count):
        base = h * 3 * HD
        out_ref[:, h * 2 * HD : (h + 1) * 2 * HD] = slab[:, base : base + 2 * HD]
        row, column = value_place(h, count, lat)
        out_ref[row : row + lat, column : column + HD] = fold(
            readout[:, h * HD : (h + 1) * HD], slab[:, base + 2 * HD : base + 3 * HD]
        )


def pack(me, model, qkv, readout_t, k, count, after, first=False):
    rows = qkv.shape[1]
    lat = readout_t.shape[1]
    width = count * 2 * HD + -(-count * lat // HD) * HD
    return pl.pallas_call(
        functools.partial(pack_kernel, k),
        in_specs=[SMEM, SMEM] + [HBM] * (2 + len(after)),
        out_specs=VMEM,
        out_shape=jax.ShapeDtypeStruct((rows, width), jnp.bfloat16),
        scratch_shapes=[
            pltpu.VMEM((rows, count * 3 * HD), jnp.bfloat16),
            pltpu.VMEM((lat, count * HD), jnp.bfloat16),
            pltpu.SemaphoreType.DMA((2,)),
        ],
        compiler_params=pltpu.CompilerParams(vmem_limit_bytes=LARGE_VMEM if first else PACK_VMEM),
        cost_estimate=pl.CostEstimate(
            flops=0, bytes_accessed=rows * width * 4, transcendentals=0
        ),
        name="pack",
    )(me, model, qkv, readout_t, *after)


def mask_rows(frames_ref, me, rows, query_offsets, key_offsets):
    columns = lax.broadcasted_iota(jnp.int32, (1, rows), 1)
    places = jnp.concatenate([(me ^ k) * rows + columns for k in query_offsets], axis=1)
    end = frames_ref[0] * FRAME_TOK
    bound = jnp.full(places.shape, end, jnp.int32)
    for c in range(1, frames_ref.shape[0]):
        later = end + frames_ref[c] * FRAME_TOK
        bound = jnp.where(places >= end, later, bound)
        end = later
    return [
        jnp.where((me ^ k) * rows + start < bound, 0.0, -jnp.inf)
        for k in key_offsets
        for start in range(0, rows, FRAME_TOK)
    ]


def run_units(units, lat):
    frames = [tile() for tile in units[0][0]]
    for u, (_, values, shifts, finish) in enumerate(units):
        ahead = list(units[u + 1][0]) if u + 1 < len(units) else []
        peaks = [jnp.max(f, axis=0, keepdims=True) + s for f, s in zip(sum(frames, []), shifts)]
        peak = jnp.maximum(functools.reduce(jnp.maximum, peaks), LOWEST)
        following, summed, start = [], None, 0
        for t, tile in enumerate(frames):
            for _ in range(-(-(len(ahead) - len(following)) // (len(frames) - t))):
                following.append(ahead[len(following)]())
            weights = [
                jnp.exp2((f + (s - peak)) * LOG2_SCALE).astype(jnp.bfloat16)
                for f, s in zip(tile, shifts[start : start + len(tile)])
            ]
            start += len(tile)
            part = jnp.dot(values[t](), jnp.concatenate(weights, axis=0), preferred_element_type=jnp.float32)
            summed = part if summed is None else summed + part
        finish(summed[:lat], summed[lat : lat + 1], peak)
        frames = following


def score_tile(keys, queries):
    scores = lax.dot_general(keys(), queries(), NT, preferred_element_type=jnp.float32)
    return [scores[start : start + FRAME_TOK] for start in range(0, scores.shape[0], FRAME_TOK)]


def stage_values(folded, pieces, lat):
    count = folded.shape[0]
    rows = pieces[0].shape[0]
    for i in range(count):
        row, column = value_place(i, count, lat)
        for n, piece in enumerate(pieces):
            folded[i, :lat, n * rows : (n + 1) * rows] = piece[row : row + lat, column : column + HD]
        folded[i, lat:] = jnp.ones_like(folded[i, lat:])


def pairs_of(pieces, i, what):
    column = (2 * i + what) * HD

    def read(n):
        return lambda: jnp.concatenate([pieces[n][:, column : column + HD], pieces[n + 1][:, column : column + HD]], axis=0)

    return [read(n) for n in range(0, len(pieces), 2)]


def early_kernel(offsets, late, frames_ref, me_ref, timestep_ref, step_weight_ref, sign_ref, sample_ref, *refs):
    count_pieces = len(offsets)
    arrived = refs[:count_pieces]
    sums_ref, stats_ref, factor_ref, pieces, folded, wide_ref, late_ref, asked, sems = refs[-9:]
    me = me_ref[0]
    rows = pieces.shape[1]
    count, lat, _ = sums_ref.shape
    blocks = count_pieces // 2
    copies = [pltpu.make_async_copy(arrived[n], pieces.at[n], sems.at[n]) for n in range(count_pieces)]
    for copy in copies:
        copy.start()
    factor_ref[...] = jnp.full(factor_ref.shape, sign_ref[0] * step_weight_ref[timestep_ref[sample_ref[0]]])
    for ref, queries, keys in ((wide_ref, offsets, late), (late_ref, late, list(offsets) + list(late))):
        for n, row in enumerate(mask_rows(frames_ref, me, rows, queries, keys)):
            ref[n : n + 1] = row
    for copy in copies:
        copy.wait()
    pieces = [pieces.at[n] for n in range(count_pieces)]
    stage_values(folded, pieces, lat)
    for i in range(count):
        for b, read in enumerate(pairs_of(pieces, i, 0)):
            asked[b, i] = read()
    half = count_pieces // 2 + 1

    def some_blocks(b, carry):
        q = [2 * b, 2 * b + 1]
        span = pl.ds(pl.multiple_of(b * 2 * rows, 2 * rows), 2 * rows)
        shifts = mask_rows(frames_ref, me, rows, [jnp.where(n < half, n, n + 2) for n in q], offsets)
        peaks, totals, units = [], [], []
        for i in range(count):

            def finish(summed, total, peak, i=i):
                sums_ref[i, :, span] = summed
                peaks.append(peak)
                totals.append(total)

            tiles = [
                functools.partial(score_tile, keys, lambda i=i: asked[b, i]) for keys in pairs_of(pieces, i, 1)
            ]
            values = [lambda i=i, t=t: folded[i, :, t * 2 * rows : (t + 1) * 2 * rows] for t in range(blocks)]
            units.append((tiles, values, shifts, finish))
        run_units(units, lat)
        rest = [jnp.ones_like(peaks[0])] * (stats_ref.shape[1] - count)
        stats_ref[0, :, span] = jnp.concatenate(peaks + rest, axis=0)
        stats_ref[1, :, span] = jnp.concatenate(totals + rest, axis=0)
        return carry

    lax.fori_loop(0, blocks, some_blocks, 0)


def late_kernel(offsets, late, *refs):
    early = len(offsets)
    arrived = refs[:2]
    sums_ref, stats_ref, factor_ref, early_ref, early_folded, wide_ref, late_ref, *out_refs, folded = refs[2:]
    size, lat, rows = out_refs[0].shape
    count = folded.shape[0]
    pieces = [early_ref.at[n] for n in range(early)] + list(arrived)
    stage_values(folded, pieces[early:], lat)
    factor = factor_ref[:1]
    every = list(offsets) + list(late)
    blocks = early // 2
    results = {}

    def write(number, start):
        for j in range(number):
            k = every[start + j]
            out_ref = out_refs[k // size]
            out_ref[k % size] = (results[start][:, j * rows : (j + 1) * rows] * factor).astype(out_ref.dtype)

    units = []
    for start, number, tiles_in in ((early, 2, range(blocks + 1)), (0, early, [blocks])):
        rows_ref = late_ref if start else wide_ref
        shifts = [rows_ref[n : n + 1] for n in range(rows_ref.shape[0])]
        for i in range(count):

            def finish(summed, total, peak, start=start, number=number, i=i):
                if start == 0:
                    before = stats_ref[0, i : i + 1]
                    highest = jnp.maximum(before, peak)
                    old = jnp.exp2((before - highest) * LOG2_SCALE)
                    new = jnp.exp2((peak - highest) * LOG2_SCALE)
                    both = stats_ref[1, i : i + 1] * old + total * new
                    part = sums_ref[i] * (old / both) + summed * (new / both)
                else:
                    part = summed / total
                results[start] = part if i == 0 else results[start] + part
                if i == count - 1:
                    write(number, start)

            def queries(start=start, number=number, i=i):
                column = 2 * i * HD
                return jnp.concatenate([p[:, column : column + HD] for p in pieces[start : start + number]], axis=0)

            keys = pairs_of(pieces, i, 1)
            tiles = [functools.partial(score_tile, keys[t], queries) for t in tiles_in]
            values = [
                lambda i=i, t=t: folded[i] if t == blocks else early_folded[i, :, t * 2 * rows : (t + 1) * 2 * rows]
                for t in tiles_in
            ]
            if start == 0:
                column = (2 * i + 1) * HD
                tiles = [
                    functools.partial(score_tile, lambda n=n, c=column: pieces[n][:, c : c + HD], queries)
                    for n in (early, early + 1)
                ]
                values = [lambda i=i, n=n: folded[i, :, n * rows : (n + 1) * rows] for n in range(2)]
            units.append((tiles, values, shifts, finish))
    run_units(units, lat)


def attend_early(pieces, offsets, late, span_frames, me, timestep, step_weight, sign, sample, count, lat):
    rows, width = pieces[0].shape
    blocks = len(pieces) // 2
    tokens = len(pieces) * rows
    frames = rows // FRAME_TOK
    return pl.pallas_call(
        functools.partial(early_kernel, offsets, late),
        in_specs=[SMEM] * 6 + [HBM] * len(pieces),
        out_specs=[VMEM] * 7,
        out_shape=[
            jax.ShapeDtypeStruct((count, lat, tokens), jnp.float32),
            jax.ShapeDtypeStruct((2, 8, tokens), jnp.float32),
            jax.ShapeDtypeStruct((8, rows), jnp.float32),
            jax.ShapeDtypeStruct((len(pieces), rows, width), jnp.bfloat16),
            jax.ShapeDtypeStruct((count, lat + 16, tokens), jnp.bfloat16),
            jax.ShapeDtypeStruct((2 * frames, tokens), jnp.float32),
            jax.ShapeDtypeStruct(((len(pieces) + 2) * frames, 2 * rows), jnp.float32),
        ],
        scratch_shapes=[
            pltpu.VMEM((blocks, count, 2 * rows, HD), jnp.bfloat16),
            pltpu.SemaphoreType.DMA((len(pieces),)),
        ],
        compiler_params=pltpu.CompilerParams(vmem_limit_bytes=SMALL_VMEM if len(pieces) <= 8 else LARGE_VMEM),
        cost_estimate=pl.CostEstimate(
            flops=count * tokens * tokens * 2 * (HD + lat),
            bytes_accessed=tokens * count * 3 * HD * 2,
            transcendentals=count * tokens * tokens,
        ),
        name="attend_early",
    )(span_frames, me, timestep, step_weight, sign, sample, *pieces)


def attend_late(pieces, offsets, late, early, count, lat):
    rows, width = pieces[0].shape
    half = len(offsets) // 2 + 1
    tokens = 2 * half * rows
    return pl.pallas_call(
        functools.partial(late_kernel, offsets, late),
        in_specs=[VMEM] * (2 + len(early)),
        out_specs=[VMEM] * 4,
        out_shape=[
            jax.ShapeDtypeStruct((half // 2, lat, rows), jnp.bfloat16 if g else jnp.float32) for g in range(4)
        ],
        scratch_shapes=[pltpu.VMEM((count, lat + 16, 2 * rows), jnp.bfloat16)],
        compiler_params=pltpu.CompilerParams(vmem_limit_bytes=SMALL_VMEM if half <= 4 else LARGE_VMEM),
        cost_estimate=pl.CostEstimate(
            flops=count * tokens * rows * 4 * (HD + lat),
            bytes_accessed=tokens * count * 3 * HD * 2,
            transcendentals=count * tokens * rows * 2,
        ),
        name="attend_late",
    )(*pieces, *early)


def swap(array, axis, offset):
    size = lax.axis_size(axis)
    return lax.ppermute(array, axis, [(i, i ^ offset) for i in range(size)])


def body(qkv, readout, step_weight, timestep, span_frames):
    seq_count = lax.axis_size("seq")
    mp_count = lax.axis_size("mp")
    half = seq_count // 2
    count = HEADS // seq_count
    lat = readout.shape[2]
    me = lax.axis_index("seq").astype(jnp.int32).reshape(1)
    mp_index = lax.axis_index("mp").astype(jnp.int32)
    sample_count = mp_count // 2
    model_index = mp_index // sample_count
    sample = (mp_index % sample_count).reshape(1)
    sign = jnp.where(model_index == 1, 1.0, -1.0).astype(jnp.float32).reshape(1)
    model = model_index.reshape(1)
    readout_t = jnp.swapaxes(readout, 1, 2)

    pieces = [None] * seq_count
    for n in range(half):
        k = seq_count - 1 - n
        pieces[k] = swap(pack(me, model, qkv, readout_t, k, count, [pieces[k + 2]] if n > 1 else [], n == 0), "seq", k)
    for k in range(half - 1, 0, -1):
        after = [] if k == half - 1 else [pieces[k + 1], pieces[seq_count - 1]] if k > 1 else [pieces[half - 1]]
        pieces[k] = swap(pack(me, model, qkv, readout_t, k, count, after), "seq", k)
    pieces[0] = pack(me, model, qkv, readout_t, 0, count, [pieces[half - 1]])
    late = [half, half + 1]
    early = [k for k in range(seq_count) if k not in late]
    merged = attend_early(
        [pieces[k] for k in early], early, late, span_frames, me, timestep, step_weight, sign, sample, count, lat
    )
    ends = [pieces[k] for k in late]
    given = attend_late(ends, early, late, merged, count, lat)
    size = half // 2
    while True:
        keep = given[0]
        for n in [2, 3, 1] if len(given) == 4 else range(1, len(given)):
            keep = keep + swap(given[n], "seq", n * size).astype(jnp.float32)
        if size == 1:
            break
        radix = min(4, size)
        size //= radix
        given = [keep[n * size : (n + 1) * size] for n in range(radix)]
    total = keep[0]
    offset = 1
    while offset < mp_count:
        radix = min(4, mp_count // offset)
        own = total
        for n in range(radix - 1, 0, -1):
            total = total + swap(own, "mp", offset * n)
        offset *= radix
    return total.T


def solution(mesh):
    return jax.shard_map(
        body,
        mesh=mesh,
        in_specs=(P("mp", "seq", None), P(), P(), P(), P()),
        out_specs=P("seq", None),
        check_vma=False,
    )
```
